32 devices in a mesh: frame: 4 (over y, x), head: 4 (over z), dp: 2 (over core).
Axes of the slice: x: 2, y: 2, z: 4, core: 2. Of those that a mesh axis runs over, the one named last changes fastest.
Arguments:
- latent: bfloat16 [16, 8, 24, 5120], P(('dp', 'frame'), 'head'), parts along dimension 0, may hold values from -6 to 6, as said below
- pose_maps: bfloat16 [16, 16, 48, 256], P(('dp', 'frame'), 'head'), parts along dimension 0, may hold values from -6 to 6
- conv_weight: bfloat16 [3, 3, 3, 256, 320], replicated, may hold values from -0.078125 to 0.078125
- conv_bias: float32 [320], replicated, may hold values from -3 to 3
- pose_proj: bfloat16 [320, 5120], replicated, may hold values from -0.3125 to 0.3125
- w_qkv: bfloat16 [5120, 20, 3, 128], P('frame', 'head'), may hold values from -2 to 2
- w_out: bfloat16 [20, 128, 5120], P('head'), may hold values from -1 to 1
- clip_lengths: int32 [6], P('dp'), parts along dimension 0, may hold values from 1 to 4, 8 in all
- block_ids: int32 [16], P('dp'), parts along dimension 0, may hold values from 0 to 3, never falling along the last dimension, each value on 1 to 3 neighbouring positions
Outputs:
- attended: bfloat16 [16, 8, 24, 5120], P(('dp', 'frame'), 'head'), parts along dimension 0
The draws below stay inside these ranges and needn't reach their ends.
There are 2 independent parts, one for each index of `dp`. The reference program is written for one: setup_inputs(seed, part) draws one part's arguments, and reference() takes and returns one part's arrays. A program takes and returns all parts, laid end to end along the dimension named above; an argument that names none is the same for every part. Nothing has to cross between parts.
Inputs may be any that keep to these rules, and one draw needn't show every extreme that they name: `clip_lengths`: the clips together cover all 8 frames; the longest clip has exactly 4 frames. `block_ids`: never falls along the frames; every block id in the range is used, by at most 3 consecutive frames. `latent`: activations of order one.
All inputs are finite; a program needn't handle non-finite values.
Results may differ from the reference program's by a relative error of at most 0.017.
Values may be sent and summed in bfloat16 or wider, within the bound.
No kernel may reach another device: no remote copies, remote signals or barrier semaphores. Data moves between devices by JAX's collectives and lax.ppermute only.
A program may use at most 128 MiB of HBM per device.

```python
import math
import jax
import jax.numpy as jnp
import numpy as np
from jax import lax

D = 5120
HEAD_DIM = 128
HEADS_DEV = 5
C_IN = 256
C_OUT = 320
HL = 8
WL = 24
CLIPS = 3
BLOCK_MOST = 3
FRAMES = 8
HEADS = 20
TOKENS = 1536
N_HEAD = 4


def draw_latent(key, part):
    shape_all = (FRAMES, HL, WL, D)
    normal_part = jax.random.normal(jax.random.fold_in(key, 11), shape_all, jnp.float32)
    return jnp.clip(normal_part, -6.0, 6.0).astype(jnp.bfloat16)


def draw_w_qkv(key, part):
    base_draw = jnp.clip(jax.random.normal(jax.random.fold_in(key, 21), (D, HEADS, 3, HEAD_DIM), jnp.float32), -4.0, 4.0) * D ** (-0.5)
    return base_draw.astype(jnp.bfloat16)


def steps_of(key, extent, split, smallest, high):
    def one(dim, shards_of):
        steps = jax.random.uniform(jax.random.fold_in(jax.random.fold_in(key, 6), dim), (shards_of,), jnp.float32, smallest / len(split), high / len(split))
        return jnp.repeat(jnp.exp(steps), extent[dim] // shards_of).reshape((-1,) + (1,) * (len(extent) - dim - 1))

    gain = one(*split[0])
    for cut in split[1:]:
        gain = gain * one(*cut)
    return gain


def length_profile(amount, total, limit, skew):
    portions = [(1 << 20) // math.isqrt(rank ** skew) + 1 for rank in range(2, amount + 1)]
    rest, counts = total - limit - (amount - 1), [1] * (amount - 1)
    while rest > 0:
        movable = [i for i in range(amount - 1) if counts[i] < limit]
        pool, budget = sum([portions[i] for i in movable]), rest
        for i in movable:
            more = min(limit - counts[i], max(1, budget * portions[i] // pool), rest)
            counts[i] = counts[i] + more
            rest = rest - more
    return np.array([limit] + counts)


def uneven_parts(key, number_of, total, reach, slope):
    if number_of == 2:
        one = jax.random.randint(key, (), max(1, total - reach), min(reach, total - 1) + 1)
        return jnp.stack([one, total - one])
    tallies = jnp.asarray(length_profile(number_of, total, reach, slope), jnp.int32)
    twos = (number_of - 1) // 2
    giver, receiver = tallies[1:1 + 2 * twos:2], tallies[2:2 + 2 * twos:2]
    margin = jnp.minimum(giver - 1, reach - receiver)
    passed = jax.random.randint(jax.random.fold_in(key, 1), (twos,), 0, 1 << 20) % (margin + 1)
    tallies = tallies.at[1:1 + 2 * twos:2].set(giver - passed).at[2:2 + 2 * twos:2].set(receiver + passed)
    return tallies[jax.random.permutation(jax.random.fold_in(key, 2), number_of)]


def noise(stream_key, dims, deviation, limit, split=(), held_as=jnp.bfloat16):
    entries = deviation * jax.random.normal(stream_key, dims, jnp.float32)
    if split:
        entries = entries * steps_of(stream_key, dims, split, -0.22, 0.18)
    return jnp.clip(entries, -limit, limit).astype(held_as)


def setup_inputs(seed: int = 0, part: int = 0) -> dict:
    keys = jax.random.split(jax.random.key(seed), 10)
    own_keys = jax.random.split(jax.random.fold_in(keys[9], part), 10)
    latent = draw_latent(jax.random.fold_in(jax.random.fold_in(keys[9], part), 71), part)
    pose_maps = noise(own_keys[1], (FRAMES, 2 * HL, 2 * WL, C_IN), 1.0, 6.0, ((0, 4), (1, 4)))
    conv_weight = noise(keys[2], (3, 3, 3, C_IN, C_OUT), (27 * C_IN) ** -0.5, 0.078125)
    conv_bias = noise(keys[3], (C_OUT,), 0.5, 3.0, (), jnp.float32)
    pose_proj = noise(keys[4], (C_OUT, D), C_OUT ** -0.5, 0.3125)
    w_qkv = draw_w_qkv(jax.random.fold_in(keys[9], 71), part)
    w_out = noise(keys[6], (HEADS, HEAD_DIM, D), (HEAD_DIM // 4) ** -0.5, 1.0, ((0, 4),))
    clip_lengths = uneven_parts(own_keys[7], CLIPS, FRAMES, FRAMES - 4, 2).astype(jnp.int32)
    block_ids = jnp.searchsorted(jnp.cumsum(uneven_parts(own_keys[8], FRAMES // 2, FRAMES, BLOCK_MOST, 0)), jnp.arange(FRAMES), side="right").astype(jnp.int32)
    return dict(latent=latent, pose_maps=pose_maps, conv_weight=conv_weight, conv_bias=conv_bias, pose_proj=pose_proj, w_qkv=w_qkv, w_out=w_out, clip_lengths=clip_lengths, block_ids=block_ids)


NEG_FILL = -1.0e30


def frame_tables(clip_lengths, frame_count):
    clip_ends = jnp.cumsum(clip_lengths).astype(jnp.int32)
    clip_starts = (clip_ends - clip_lengths).astype(jnp.int32)
    frame_index = jnp.arange(frame_count, dtype=jnp.int32)
    clip_of = jnp.sum((frame_index[:, None] >= clip_ends[None, :]).astype(jnp.int32), axis=1).astype(jnp.int32)
    clip_match = clip_of[:, None] == jnp.arange(clip_lengths.shape[0], dtype=jnp.int32)[None, :]
    start_of = jnp.sum(jnp.where(clip_match, clip_starts[None, :], 0), axis=1).astype(jnp.int32)
    return clip_of, start_of


def reference(latent, pose_maps, conv_weight, conv_bias, pose_proj, w_qkv, w_out, clip_lengths, block_ids):
    clip_of, start_of = frame_tables(clip_lengths, FRAMES)
    padded = jnp.pad(pose_maps, ((2, 0), (1, 0), (1, 0), (0, 0)))
    frame_ids = jnp.arange(FRAMES, dtype=jnp.int32)
    tap_list = []
    for step_a in range(3):
        keep_mask = (frame_ids - 2 + step_a >= start_of).astype(pose_maps.dtype)[:, None, None, None]
        frames_tap = padded[step_a:step_a + FRAMES] * keep_mask
        for step_b in range(3):
            for step_e in range(3):
                tap_list.append(frames_tap[:, step_b:step_b + 2 * HL - 1:2, step_e:step_e + 2 * WL - 1:2])
    stacked = jnp.concatenate(tap_list, axis=3)
    summed = jnp.dot(stacked, conv_weight.reshape(27 * C_IN, C_OUT), preferred_element_type=jnp.float32) + conv_bias
    feature = jax.nn.silu(summed).astype(jnp.bfloat16)
    guided = (latent.astype(jnp.float32) + jnp.dot(feature, pose_proj, preferred_element_type=jnp.float32)).astype(jnp.bfloat16)

    tokens = guided.reshape(TOKENS, D)
    projected = jnp.dot(tokens, w_qkv.reshape(D, HEADS * 3 * HEAD_DIM), preferred_element_type=jnp.float32)
    projected = projected.astype(jnp.bfloat16).reshape(TOKENS, HEADS, 3, HEAD_DIM)

    row_frame = jnp.arange(TOKENS, dtype=jnp.int32) // (HL * WL)
    frame_visible = (clip_of[:, None] == clip_of[None, :]) & (block_ids[None, :] <= block_ids[:, None])
    visible = jnp.take(jnp.take(frame_visible, row_frame, axis=0), row_frame, axis=1)

    def one_head(head_parts):
        query_rows, key_rows, value_rows = head_parts
        scores = jnp.dot(query_rows, key_rows.T, preferred_element_type=jnp.float32) * HEAD_DIM ** -0.5
        scores = jnp.where(visible, scores, NEG_FILL)
        row_top = jnp.max(scores, axis=1, keepdims=True)
        weights = jnp.where(visible, jnp.exp(scores - row_top), 0.0)
        row_total = jnp.sum(weights, axis=1, keepdims=True)
        mixed_rows = jnp.dot(weights.astype(jnp.bfloat16), value_rows, preferred_element_type=jnp.float32)
        return (mixed_rows / row_total).astype(jnp.bfloat16)

    heads_major = jnp.transpose(projected, (1, 2, 0, 3))
    attended = lax.map(one_head, (heads_major[:, 0], heads_major[:, 1], heads_major[:, 2]))

    grouped_rows = attended.reshape(N_HEAD, HEADS_DEV, TOKENS, HEAD_DIM)
    grouped_rows = jnp.transpose(grouped_rows, (0, 2, 1, 3)).reshape(N_HEAD, TOKENS, HEADS_DEV * HEAD_DIM)
    grouped_weight = w_out.reshape(N_HEAD, HEADS_DEV * HEAD_DIM, D)

    def add_group(running, group_item):
        rows_group, weight_group = group_item
        partial_low = jnp.dot(rows_group, weight_group, preferred_element_type=jnp.float32).astype(jnp.bfloat16)
        partial_low = lax.optimization_barrier(partial_low)
        return running + partial_low.astype(jnp.float32), None

    summed_out, unused = lax.scan(add_group, jnp.zeros((TOKENS, D), jnp.float32), (grouped_rows, grouped_weight))
    return summed_out.astype(jnp.bfloat16).reshape(FRAMES, HL, WL, D)
```

```python
import jax
import jax.numpy as jnp
from jax import lax
from jax.experimental import pallas as pl
from jax.experimental.pallas import tpu as pltpu
from jax.sharding import PartitionSpec as P

NEG_FILL = -1e30
MIB = 1 << 20
F32 = jnp.float32
BF16 = jnp.bfloat16


def cost(flops, moved, exps=0):
    return pl.CostEstimate(flops=int(flops), bytes_accessed=int(moved), transcendentals=int(exps))


def frame_tables(clip_lengths, frame_count):
    clip_ends = jnp.cumsum(clip_lengths)
    clip_starts = clip_ends - clip_lengths
    frame_index = jnp.arange(frame_count, dtype=jnp.int32)
    clip_of = jnp.sum((frame_index[:, None] >= clip_ends[None, :]).astype(jnp.int32), axis=1)
    clip_match = clip_of[:, None] == jnp.arange(clip_lengths.shape[0], dtype=jnp.int32)[None, :]
    start_of = jnp.sum(jnp.where(clip_match, clip_starts[None, :], 0), axis=1)
    return (clip_of, start_of)


def shift_up(value, axis):
    count = lax.axis_size(axis)
    return lax.ppermute(value, axis, [(i, i + 1) for i in range(count - 1)])


def turn(value, axis, steps):
    count = lax.axis_size(axis)
    return lax.ppermute(value, axis, [(i, (i + steps) % count) for i in range(count)])


def across(value, axis, bits):
    count = lax.axis_size(axis)
    return lax.ppermute(value, axis, [(i, i ^ bits) for i in range(count)])


def line_chains(value, axis):
    count = lax.axis_size(axis)
    lower, upper = [value], [value]
    for s in range(1, count):
        lower.append(lax.ppermute(lower[-1], axis, [(i, i + 1) for i in range(s - 1, count - 1)]))
        upper.append(lax.ppermute(upper[-1], axis, [(i, i - 1) for i in range(1, count - s + 1)]))
    return lower, upper


def conv_kernel(keep_ref, cols_ref, weight_ref, bias_ref, out_ref, acc_ref):
    step = pl.program_id(0)
    tap_a, tap_b = step // 3, step % 3
    frames, strip_rows, width = out_ref.shape[0], out_ref.shape[1], cols_ref.shape[2]
    pieces = []
    for t in range(frames):
        keep = keep_ref[tap_a * frames + t]
        for r in range(strip_rows):
            rows = cols_ref[tap_a + t, tap_b + 2 * r].astype(F32)
            pieces.append(jnp.where(keep > 0, rows, 0.0))
    lhs = jnp.concatenate(pieces, axis=0).astype(BF16)
    channels = weight_ref.shape[3]
    total = None
    for e in range(3):
        part = lax.dot_general(
            lhs[:, e * channels : (e + 1) * channels],
            weight_ref[0, e],
            (((1,), (1,)), ((), ())),
            preferred_element_type=F32,
        )
        total = part if total is None else total + part

    @pl.when(step == 0)
    def _():
        acc_ref[...] = total

    @pl.when(step > 0)
    def _():
        acc_ref[...] += total

    @pl.when(step == 8)
    def _():
        summed = acc_ref[...] + bias_ref[...]
        feature = summed / (1.0 + jnp.exp(-summed))
        for t in range(frames):
            for r in range(strip_rows):
                at = (t * strip_rows + r) * width
                out_ref[t, r] = feature[at : at + width].astype(BF16)


def pose_feature(pose_maps, conv_weight, conv_bias, start_of, first_frame):
    frames, rows, columns, channels = pose_maps.shape
    out_channels = conv_weight.shape[-1]
    upper_row = shift_up(pose_maps[:, -1:], "head")
    rows_ext = jnp.concatenate([upper_row, pose_maps], axis=1)
    earlier = shift_up(rows_ext, "frame")
    extended = jnp.concatenate([earlier, rows_ext], axis=0)
    pairs = extended.reshape(2 * frames, rows + 1, columns // 2, 2 * channels)
    before = jnp.pad(pairs[:, :, :-1, channels:], ((0, 0), (0, 0), (1, 0), (0, 0)))
    cols = jnp.concatenate([before, pairs], axis=3)
    taps = jnp.transpose(conv_weight, (0, 1, 2, 4, 3)).reshape(9, 3, out_channels, channels)
    frame_ids = first_frame + jnp.arange(frames, dtype=jnp.int32)
    starts_here = lax.dynamic_slice_in_dim(start_of, first_frame, frames)
    keep = (frame_ids[None, :] - 2 + jnp.arange(3, dtype=jnp.int32)[:, None] >= starts_here[None, :])
    keep = keep.astype(jnp.int32).reshape(-1)
    out_shape = (frames, rows // 2, columns // 2, out_channels)
    tokens = frames * (rows // 2) * (columns // 2)
    feature = pl.pallas_call(
        conv_kernel,
        out_shape=jax.ShapeDtypeStruct(out_shape, BF16),
        grid_spec=pltpu.PrefetchScalarGridSpec(
            num_scalar_prefetch=1,
            grid=(9,),
            in_specs=[
                pl.BlockSpec(cols.shape, lambda i, k: (0, 0, 0, 0)),
                pl.BlockSpec((1, 3, out_channels, channels), lambda i, k: (i, 0, 0, 0)),
                pl.BlockSpec((1, out_channels), lambda i, k: (0, 0)),
            ],
            out_specs=pl.BlockSpec(out_shape, lambda i, k: (0, 0, 0, 0)),
            scratch_shapes=[pltpu.VMEM((tokens, out_channels), F32)],
        ),
        compiler_params=pltpu.CompilerParams(vmem_limit_bytes=24 * MIB),
        cost_estimate=cost(2 * tokens * 27 * channels * out_channels, conv_weight.size * 2),
        name="pose_conv",
    )(keep, cols, taps, conv_bias.reshape(1, -1))
    return feature.reshape(tokens, out_channels)


def guide_kernel(strips, frames, *refs):
    own_ref = refs[0]
    lower_refs, upper_refs = refs[1:strips], refs[strips : 2 * strips - 1]
    feature_refs = refs[2 * strips - 1 : 3 * strips - 1]
    proj_ref, out_ref = refs[-2], refs[-1]
    features = jnp.concatenate([ref[...] for ref in feature_refs], axis=0)
    added = jnp.dot(features, proj_ref[...], preferred_element_type=F32)
    tokens = own_ref.shape[0]
    per_frame = tokens // frames
    for s in range(strips):
        if s == 0:
            latent = own_ref[...].astype(F32)
        else:
            latent = lower_refs[s - 1][...].astype(F32) + upper_refs[strips - s - 1][...].astype(F32)
        guided = (latent + added[s * tokens : (s + 1) * tokens]).astype(BF16)
        for t in range(frames):
            at = (t * strips + s) * per_frame
            out_ref[0, at : at + per_frame] = guided[t * per_frame : (t + 1) * per_frame]


def guide(own, lower, upper, features, pose_proj, frames, blocks):
    strips = len(features)
    tokens, width = own.shape
    wide = width // blocks
    channels = pose_proj.shape[0]
    rows = strips * tokens

    def body(*refs):
        guide_kernel(strips, frames, *refs)

    piece = pl.BlockSpec((tokens, wide), lambda i: (0, i))
    whole = pl.BlockSpec((tokens, channels), lambda i: (0, 0))
    return pl.pallas_call(
        body,
        out_shape=jax.ShapeDtypeStruct((blocks, rows, wide), BF16),
        grid=(blocks,),
        in_specs=[piece] * (2 * strips - 1)
        + [whole] * strips
        + [pl.BlockSpec((channels, wide), lambda i: (0, i))],
        out_specs=pl.BlockSpec((1, rows, wide), lambda i: (i, 0, 0)),
        compiler_params=pltpu.CompilerParams(vmem_limit_bytes=32 * MIB),
        cost_estimate=cost(2 * rows * channels * width, 2 * (3 * rows + channels) * width),
        name="guide",
    )(own, *lower, *upper, *features, pose_proj)


def project(guided, order, groups, total, heads, head_size, frames):
    blocks, rows, wide = guided.shape
    group_rows = [sum(piece.shape[2] for piece in group) for group in groups]
    counts = [amount // wide for amount in group_rows]
    used = sum(counts)
    flat = [piece for group in groups for piece in group]
    per_frame = rows // frames

    def body(order_ref, *refs):
        guided_refs = refs[:used]
        weight_refs = refs[used : used + len(flat)]
        rest = refs[used + len(flat) :]
        summed = None
        at, first = 0, 0
        for group, count in zip(groups, counts):
            lhs = jnp.concatenate([ref[0] for ref in guided_refs[first : first + count]], axis=1)
            held = weight_refs[at : at + len(group)]
            rhs = jnp.concatenate(
                [jnp.concatenate([ref[0, j] for ref in held], axis=0) for j in range(3)], axis=1
            )
            part = jnp.dot(lhs, rhs, preferred_element_type=F32)
            summed = part if summed is None else summed + part
            at, first = at + len(group), first + count
        if total is None:
            for j in range(3):
                rest[0][0, j] = summed[:, j * head_size : (j + 1) * head_size]
            return
        total_ref, query_ref, keyval_ref = rest
        for j in range(3):
            value = (total_ref[0, j] + summed[:, j * head_size : (j + 1) * head_size]).astype(BF16)
            for t in range(frames):
                part = value[t * per_frame : (t + 1) * per_frame]
                if j == 0:
                    query_ref[t, 0] = part
                else:
                    keyval_ref[t, 0, j - 1] = part

    def pick(i):
        return lambda h, order: (order[i], 0, 0)

    in_specs = [pl.BlockSpec((1, rows, wide), pick(i)) for i in range(used)]
    in_specs += [
        pl.BlockSpec((1, 3, piece.shape[2], head_size), lambda h, order: (h, 0, 0, 0)) for piece in flat
    ]
    operands = [order] + [guided] * used + flat
    sums = pl.BlockSpec((1, 3, rows, head_size), lambda h, order: (h, 0, 0, 0))
    if total is None:
        out_shape = jax.ShapeDtypeStruct((heads, 3, rows, head_size), F32)
        out_specs = sums
    else:
        in_specs.append(sums)
        operands.append(total)
        out_shape = (
            jax.ShapeDtypeStruct((frames, heads, per_frame, head_size), BF16),
            jax.ShapeDtypeStruct((frames, heads, 2, per_frame, head_size), BF16),
        )
        out_specs = (
            pl.BlockSpec((frames, 1, per_frame, head_size), lambda h, order: (0, h, 0, 0)),
            pl.BlockSpec((frames, 1, 2, per_frame, head_size), lambda h, order: (0, h, 0, 0, 0)),
        )
    columns = heads * 3 * head_size
    return pl.pallas_call(
        body,
        out_shape=out_shape,
        grid_spec=pltpu.PrefetchScalarGridSpec(
            num_scalar_prefetch=1, grid=(heads,), in_specs=in_specs, out_specs=out_specs
        ),
        compiler_params=pltpu.CompilerParams(vmem_limit_bytes=48 * MIB),
        cost_estimate=cost(
            2 * rows * sum(group_rows) * columns,
            2 * sum(group_rows) * (columns + rows) + 4 * rows * columns,
        ),
        name="project",
    )(*operands)


def attend(queries, pieces, bases, spans, frame_count, strips):
    frames, heads, rows, size = queries.shape
    window = frame_count - 4 if frame_count > 4 else frame_count
    strip = rows // strips
    lengths = [piece.shape[0] for piece in pieces]
    table = jnp.concatenate([jnp.stack(bases).astype(jnp.int32), spans.reshape(-1).astype(jnp.int32)])
    scale = size ** (-0.5)

    def body(table_ref, query_ref, *refs):
        piece_refs, out_ref, held_ref = refs[: len(pieces)], refs[-2], refs[-1]
        for p, ref in enumerate(piece_refs):
            for t in range(lengths[p]):
                held_ref[table_ref[p] + t] = ref[t, 0]
        for t in range(frames):
            at = len(pieces) + 3 * t
            begin, low, high = table_ref[at], table_ref[at + 1], table_ref[at + 2]
            keys = held_ref[pl.ds(begin, window), 0].reshape(window * rows, size)
            values = held_ref[pl.ds(begin, window), 1].reshape(window * rows, size)
            scores = lax.dot_general(
                query_ref[t, 0], keys, (((1,), (1,)), ((), ())), preferred_element_type=F32
            )
            place = lax.broadcasted_iota(jnp.int32, (1, window * rows), 1)
            seen = (place >= low * rows) & (place < high * rows)
            scores = jnp.where(seen, scores * scale, NEG_FILL)
            weights = jnp.exp(scores - jnp.max(scores, axis=1, keepdims=True))
            totals = jnp.sum(weights, axis=1, keepdims=True)
            mixed = jnp.dot(weights.astype(BF16), values, preferred_element_type=F32)
            result = (mixed / totals).astype(BF16)
            for s in range(strips):
                out_ref[s, t] = result[s * strip : (s + 1) * strip]

    in_specs = [pl.BlockSpec((frames, 1, rows, size), lambda h, table: (0, h, 0, 0))]
    in_specs += [
        pl.BlockSpec((length, 1, 2, rows, size), lambda h, table: (0, h, 0, 0, 0)) for length in lengths
    ]
    return pl.pallas_call(
        body,
        out_shape=jax.ShapeDtypeStruct((strips, frames, strip, heads * size), BF16),
        grid_spec=pltpu.PrefetchScalarGridSpec(
            num_scalar_prefetch=1,
            grid=(heads,),
            in_specs=in_specs,
            out_specs=pl.BlockSpec((strips, frames, strip, size), lambda h, table: (0, 0, 0, h)),
            scratch_shapes=[pltpu.VMEM((frame_count, 2, rows, size), BF16)],
        ),
        compiler_params=pltpu.CompilerParams(vmem_limit_bytes=48 * MIB),
        cost_estimate=cost(
            4 * heads * frames * rows * rows * window * size,
            4 * heads * frame_count * rows * size,
            heads * frames * rows * rows * window,
        ),
        name="attend",
    )(table, queries, *pieces)


def out_project(rows_in, weight, place, groups, parts):
    tokens, depth = rows_in[0][0].shape[1:]
    columns = weight.shape[3]
    amount = len(rows_in)
    flat = [piece for pieces in rows_in for piece in pieces]

    def body(place_ref, *refs):
        step = pl.program_id(0)
        weight_ref, out_ref, acc_ref = refs[len(flat)], refs[-2], refs[-1]
        at, found = 0, []
        for pieces in rows_in:
            held = refs[at : at + len(pieces)]
            at += len(pieces)
            if len(held) == 1:
                found.append(held[0][step])
                continue
            first = pieces[0].shape[0]
            near = held[0][jnp.minimum(step, first - 1)]
            far = held[1][jnp.maximum(step - first, 0)]
            found.append(jnp.where(step < first, near, far))
        lhs = jnp.concatenate(found, axis=0)
        part = jnp.dot(lhs, weight_ref[:, 0].reshape(depth, columns), preferred_element_type=F32)
        part = part.astype(BF16).astype(F32)

        @pl.when(step == 0)
        def _():
            acc_ref[...] = part

        @pl.when(step > 0)
        def _():
            acc_ref[...] += part

        @pl.when(step == groups - 1)
        def _():
            for r in range(amount):
                out_ref[r] = acc_ref[r * tokens : (r + 1) * tokens].astype(BF16)

    in_specs = [pl.BlockSpec(piece.shape, lambda g, place: (0, 0, 0)) for piece in flat]
    in_specs.append(
        pl.BlockSpec(
            (parts, 1, depth // parts, columns), lambda g, place: (0, lax.rem(place[0] + g, groups), 0, 0)
        )
    )
    return pl.pallas_call(
        body,
        out_shape=jax.ShapeDtypeStruct((amount, tokens, columns), BF16),
        grid_spec=pltpu.PrefetchScalarGridSpec(
            num_scalar_prefetch=1,
            grid=(groups,),
            in_specs=in_specs,
            out_specs=pl.BlockSpec((amount, tokens, columns), lambda g, place: (0, 0, 0)),
            scratch_shapes=[pltpu.VMEM((amount * tokens, columns), F32)],
        ),
        compiler_params=pltpu.CompilerParams(vmem_limit_bytes=32 * MIB),
        cost_estimate=cost(
            2 * amount * tokens * groups * depth * columns, 2 * groups * depth * (columns + amount * tokens)
        ),
        name="out_project",
    )(place, *flat, weight)


def place_columns(pieces, me):
    tokens, columns = pieces[0].shape
    amount = len(pieces)

    def body(me_ref, *refs):
        step = pl.program_id(0)
        for r in range(amount):

            @pl.when(step == r)
            def _(r=r):
                refs[-1][...] = refs[r][...]

    return pl.pallas_call(
        body,
        out_shape=jax.ShapeDtypeStruct((tokens, amount * columns), BF16),
        grid_spec=pltpu.PrefetchScalarGridSpec(
            num_scalar_prefetch=1,
            grid=(amount,),
            in_specs=[pl.BlockSpec((tokens, columns), lambda i, me: (0, 0))] * amount,
            out_specs=pl.BlockSpec((tokens, columns), lambda i, me: (0, me[0] ^ i)),
        ),
        cost_estimate=cost(0, 4 * tokens * amount * columns),
        name="place_columns",
    )(me, *pieces)


def shards(
    latent, pose_maps, conv_weight, conv_bias, pose_proj, w_qkv, w_out, clip_lengths, block_ids
):
    frame_count = block_ids.shape[0]
    frames, strip_rows, width_grid, model_width = latent.shape
    heads, head_size = w_qkv.shape[1], w_qkv.shape[3]
    strips = lax.axis_size("head")
    frame_devices = lax.axis_size("frame")
    strip = strip_rows * width_grid
    tokens = frames * strip
    per_frame = strips * strip
    here = lax.axis_index("frame").astype(jnp.int32)
    group = lax.axis_index("head").astype(jnp.int32)
    core = lax.axis_index("dp").astype(jnp.int32)
    first_frame = here * frames
    clip_of, start_of = frame_tables(clip_lengths, frame_count)

    own = latent.reshape(tokens, model_width)
    lower, upper = line_chains(own, "head")

    weight = jnp.transpose(w_qkv, (1, 2, 0, 3))
    plane = frame_devices == 4
    half_rows = weight.shape[2] // 2
    if plane:
        half = lax.dynamic_slice_in_dim(weight, core * half_rows, half_rows, axis=2)
        from_x, from_y = across(half, "frame", 1), across(half, "frame", 2)
        quarter = half_rows // 2
        far_x = across(from_y[:, :, :quarter], "frame", 1)
        far_y = across(from_x[:, :, quarter:], "frame", 2)
        other_x, other_y = across(from_x, "dp", 1), across(from_y, "dp", 1)
        other_far_x, other_far_y = across(far_x, "dp", 1), across(far_y, "dp", 1)

    feature = pose_feature(pose_maps, conv_weight, conv_bias, start_of, first_frame)
    features = [feature] + [turn(feature, "head", s) for s in range(1, strips)]
    blocks = 8
    guided = guide(own, lower[1:], upper[1:], features, pose_proj, frames, blocks)

    if plane:
        order = []
        for near in (here, here ^ 1, here ^ 2, here ^ 3):
            order += [2 * near, 2 * near + 1] if near is here else [2 * near + core, 2 * near + 1 - core]
        order = jnp.stack(order)
        total = project(
            guided,
            order[:6],
            [(weight,), (from_x, other_x), (from_y, other_y)],
            None,
            heads,
            head_size,
            frames,
        )
        queries, keyvals = project(
            guided,
            order[6:],
            [(far_x, far_y, other_far_x, other_far_y)],
            total,
            heads,
            head_size,
            frames,
        )
    else:
        whole = lax.all_gather(weight, "frame", axis=2, tiled=True)
        flat = jnp.transpose(guided, (1, 0, 2)).reshape(-1, model_width)
        projected = jnp.einsum("mk,hjkd->hjmd", flat, whole, preferred_element_type=F32).astype(BF16)
        projected = projected.reshape(heads, 3, frames, per_frame, head_size)
        queries = jnp.transpose(projected[:, 0], (1, 0, 2, 3))
        keyvals = jnp.transpose(projected[:, 1:], (2, 0, 1, 3, 4))

    same_clip = clip_of[:, None] == clip_of[None, :]
    counts = jnp.sum((same_clip & (block_ids[None, :] <= block_ids[:, None])).astype(jnp.int32), axis=1)
    window = frame_count - 4 if frame_count > 4 else frame_count
    begins = jnp.minimum(start_of, frame_count - window)
    spans = jnp.stack([begins, start_of - begins, start_of - begins + counts], axis=1)
    spans = lax.dynamic_slice_in_dim(spans, first_frame, frames)
    if plane:
        near_x, near_y = across(keyvals, "frame", 1), across(keyvals, "frame", 2)
        middle = frames // 2
        diag_x = across(near_y[:middle], "frame", 1)
        diag_y = across(near_x[middle:], "frame", 2)
        pieces = [keyvals, near_x, near_y, diag_x, diag_y]
        bases = [here, here ^ 1, here ^ 2, here ^ 3, here ^ 3]
        bases = [base * frames for base in bases]
        bases[4] = bases[4] + middle
    else:
        pieces = [lax.all_gather(keyvals, "frame", axis=0, tiled=True)]
        bases = [jnp.int32(0)]
    head_out = attend(queries, pieces, bases, spans, frame_count, strips)
    head_out = head_out.reshape(strips, tokens, heads * head_size)

    flat_out = w_out.reshape(heads * head_size, model_width)
    if not plane:
        flat_rows = jnp.take(head_out, (group - jnp.arange(strips, dtype=jnp.int32)) % strips, axis=0)
        partial = jnp.dot(flat_rows, flat_out, preferred_element_type=F32).astype(BF16)
        summed = lax.psum_scatter(partial, "head", scatter_dimension=0, tiled=True)
        return summed.reshape(latent.shape)

    columns = model_width // frame_devices
    half_depth = heads * head_size // 2
    out_half = lax.dynamic_slice(flat_out, (core * half_depth, here * columns), (half_depth, columns))
    out_half, unused = lax.optimization_barrier((out_half, lower[-1][:16, :128]))
    out_weight = lax.all_gather(out_half, "head")
    out_weight = lax.all_gather(out_weight, "dp")

    strip_heads = [head_out[0]] + [turn(head_out[s], "head", -s) for s in range(1, strips)]
    strip_heads = jnp.stack(strip_heads)
    rows_x, rows_y = across(strip_heads, "frame", 1), across(strip_heads, "frame", 2)
    middle = strips // 2
    far = [across(rows_y[:middle], "frame", 1), across(rows_x[middle:], "frame", 2)]
    done = out_project(
        [[strip_heads], [rows_x], [rows_y], far], out_weight, group.reshape(1), strips, 2
    )
    mine = [done[0]] + [across(done[r], "frame", r) for r in range(1, frame_devices)]
    return place_columns(mine, here.reshape(1)).reshape(latent.shape)


def solution(mesh):
    return jax.shard_map(
        shards,
        mesh=mesh,
        in_specs=(
            P(("dp", "frame"), "head", None, None),
            P(("dp", "frame"), "head", None, None),
            P(),
            P(),
            P(),
            P("frame", "head", None, None),
            P("head", None, None),
            P("dp"),
            P("dp"),
        ),
        out_specs=P(("dp", "frame"), "head", None, None),
        check_vma=False,
    )
```

```python
import jax
import jax.numpy as jnp
from jax import lax
from jax.experimental import pallas as pl
from jax.experimental.pallas import tpu as pltpu
from jax.sharding import PartitionSpec as P

NEG_FILL = -1e30
MIB = 1 << 20
F32 = jnp.float32
BF16 = jnp.bfloat16


def cost(flops, moved, exps=0):
    return pl.CostEstimate(flops=int(flops), bytes_accessed=int(moved), transcendentals=int(exps))


def frame_tables(clip_lengths, frame_count):
    clip_ends = jnp.cumsum(clip_lengths)
    clip_starts = clip_ends - clip_lengths
    frame_index = jnp.arange(frame_count, dtype=jnp.int32)
    clip_of = jnp.sum((frame_index[:, None] >= clip_ends[None, :]).astype(jnp.int32), axis=1)
    clip_match = clip_of[:, None] == jnp.arange(clip_lengths.shape[0], dtype=jnp.int32)[None, :]
    start_of = jnp.sum(jnp.where(clip_match, clip_starts[None, :], 0), axis=1)
    return (clip_of, start_of)


def shift_up(value, axis):
    count = lax.axis_size(axis)
    return lax.ppermute(value, axis, [(i, i + 1) for i in range(count - 1)])


def turn(value, axis, steps):
    count = lax.axis_size(axis)
    return lax.ppermute(value, axis, [(i, (i + steps) % count) for i in range(count)])


def across(value, axis, bits):
    count = lax.axis_size(axis)
    return lax.ppermute(value, axis, [(i, i ^ bits) for i in range(count)])


def hop(lower, upper, axis, s):
    count = lax.axis_size(axis)
    lower = lax.ppermute(lower, axis, [(i, i + 1) for i in range(s - 1, count - 1)])
    upper = lax.ppermute(upper, axis, [(i, i - 1) for i in range(1, count - s + 1)])
    return lower, upper


def after(value, *others):
    def body(*refs):
        del refs

    anywhere = pl.BlockSpec(memory_space=pl.ANY)
    return pl.pallas_call(
        body,
        out_shape=jax.ShapeDtypeStruct(value.shape, value.dtype),
        in_specs=[anywhere] * (1 + len(others)),
        out_specs=anywhere,
        input_output_aliases={0: 0},
        name="after",
    )(value, *others)


def take_rows(weight, core):
    heads, kinds, rows, size = weight.shape
    half = rows // 2

    def body(core_ref, weight_ref, out_ref):
        out_ref[...] = weight_ref[...]

    return pl.pallas_call(
        body,
        out_shape=jax.ShapeDtypeStruct((heads, kinds, half, size), weight.dtype),
        grid_spec=pltpu.PrefetchScalarGridSpec(
            num_scalar_prefetch=1,
            grid=(heads,),
            in_specs=[pl.BlockSpec((1, kinds, half, size), lambda h, core: (h, 0, core[0], 0))],
            out_specs=pl.BlockSpec((1, kinds, half, size), lambda h, core: (h, 0, 0, 0)),
        ),
        cost_estimate=cost(0, 4 * heads * kinds * half * size),
        name="take_rows",
    )(core.reshape(1), weight)


def take_block(weight, row, column, shape, ready):
    def body(at_ref, weight_ref, ready_ref, out_ref):
        out_ref[...] = weight_ref[...]

    return pl.pallas_call(
        body,
        out_shape=jax.ShapeDtypeStruct(shape, weight.dtype),
        grid_spec=pltpu.PrefetchScalarGridSpec(
            num_scalar_prefetch=1,
            grid=(1,),
            in_specs=[
                pl.BlockSpec(shape, lambda i, at: (at[0], at[1])),
                pl.BlockSpec(memory_space=pl.ANY),
            ],
            out_specs=pl.BlockSpec(shape, lambda i, at: (0, 0)),
        ),
        cost_estimate=cost(0, 4 * shape[0] * shape[1]),
        name="take_block",
    )(jnp.stack([row, column]), weight, ready)


def conv_kernel(keep_ref, cols_ref, weight_ref, bias_ref, out_ref, acc_ref):
    step = pl.program_id(0)
    tap_a, tap_b = step // 3, step % 3
    frames, strip_rows, width = out_ref.shape[0], out_ref.shape[1], cols_ref.shape[2]
    pieces = []
    for t in range(frames):
        keep = keep_ref[tap_a * frames + t]
        for r in range(strip_rows):
            rows = cols_ref[tap_a + t, tap_b + 2 * r].astype(F32)
            pieces.append(jnp.where(keep > 0, rows, 0.0))
    lhs = jnp.concatenate(pieces, axis=0).astype(BF16)
    channels = weight_ref.shape[3]
    total = None
    for e in range(3):
        part = lax.dot_general(
            lhs[:, e * channels : (e + 1) * channels],
            weight_ref[0, e],
            (((1,), (1,)), ((), ())),
            preferred_element_type=F32,
        )
        total = part if total is None else total + part

    @pl.when(step == 0)
    def _():
        acc_ref[...] = total

    @pl.when(step > 0)
    def _():
        acc_ref[...] += total

    @pl.when(step == 8)
    def _():
        summed = acc_ref[...] + bias_ref[...]
        feature = summed / (1.0 + jnp.exp(-summed))
        for t in range(frames):
            for r in range(strip_rows):
                at = (t * strip_rows + r) * width
                out_ref[t, r] = feature[at : at + width].astype(BF16)


def pose_feature(pose_maps, conv_weight, conv_bias, start_of, first_frame):
    frames, rows, columns, channels = pose_maps.shape
    out_channels = conv_weight.shape[-1]
    upper_row = shift_up(pose_maps[:, -1:], "head")
    rows_ext = jnp.concatenate([upper_row, pose_maps], axis=1)
    earlier = shift_up(rows_ext, "frame")
    extended = jnp.concatenate([earlier, rows_ext], axis=0)
    pairs = extended.reshape(2 * frames, rows + 1, columns // 2, 2 * channels)
    before = jnp.pad(pairs[:, :, :-1, channels:], ((0, 0), (0, 0), (1, 0), (0, 0)))
    cols = jnp.concatenate([before, pairs], axis=3)
    taps = jnp.transpose(conv_weight, (0, 1, 2, 4, 3)).reshape(9, 3, out_channels, channels)
    frame_ids = first_frame + jnp.arange(frames, dtype=jnp.int32)
    starts_here = lax.dynamic_slice_in_dim(start_of, first_frame, frames)
    keep = (frame_ids[None, :] - 2 + jnp.arange(3, dtype=jnp.int32)[:, None] >= starts_here[None, :])
    keep = keep.astype(jnp.int32).reshape(-1)
    out_shape = (frames, rows // 2, columns // 2, out_channels)
    tokens = frames * (rows // 2) * (columns // 2)
    feature = pl.pallas_call(
        conv_kernel,
        out_shape=jax.ShapeDtypeStruct(out_shape, BF16),
        grid_spec=pltpu.PrefetchScalarGridSpec(
            num_scalar_prefetch=1,
            grid=(9,),
            in_specs=[
                pl.BlockSpec(cols.shape, lambda i, k: (0, 0, 0, 0)),
                pl.BlockSpec((1, 3, out_channels, channels), lambda i, k: (i, 0, 0, 0)),
                pl.BlockSpec((1, out_channels), lambda i, k: (0, 0)),
            ],
            out_specs=pl.BlockSpec(out_shape, lambda i, k: (0, 0, 0, 0)),
            scratch_shapes=[pltpu.VMEM((tokens, out_channels), F32)],
        ),
        compiler_params=pltpu.CompilerParams(vmem_limit_bytes=24 * MIB),
        cost_estimate=cost(2 * tokens * 27 * channels * out_channels, conv_weight.size * 2),
        name="pose_conv",
    )(keep, cols, taps, conv_bias.reshape(1, -1))
    return feature.reshape(tokens, out_channels)


def guide_kernel(strips, frames, *refs):
    own_ref = refs[0]
    lower_refs, upper_refs = refs[1:strips], refs[strips : 2 * strips - 1]
    feature_refs = refs[2 * strips - 1 : 3 * strips - 1]
    proj_ref, out_ref = refs[-2], refs[-1]
    features = jnp.concatenate([ref[...] for ref in feature_refs], axis=0)
    added = jnp.dot(features, proj_ref[...], preferred_element_type=F32)
    tokens = own_ref.shape[0]
    per_frame = tokens // frames
    for s in range(strips):
        if s == 0:
            latent = own_ref[...].astype(F32)
        else:
            latent = lower_refs[s - 1][...].astype(F32) + upper_refs[strips - s - 1][...].astype(F32)
        guided = (latent + added[s * tokens : (s + 1) * tokens]).astype(BF16)
        for t in range(frames):
            at = (t * strips + s) * per_frame
            out_ref[0, at : at + per_frame] = guided[t * per_frame : (t + 1) * per_frame]


def guide(own, lower, upper, features, pose_proj, frames, blocks):
    strips = len(features)
    tokens, width = own.shape
    wide = width // blocks
    channels = pose_proj.shape[0]
    rows = strips * tokens

    def body(*refs):
        guide_kernel(strips, frames, *refs)

    piece = pl.BlockSpec((tokens, wide), lambda i: (0, i))
    whole = pl.BlockSpec((tokens, channels), lambda i: (0, 0))
    return pl.pallas_call(
        body,
        out_shape=jax.ShapeDtypeStruct((blocks, rows, wide), BF16),
        grid=(blocks,),
        in_specs=[piece] * (2 * strips - 1)
        + [whole] * strips
        + [pl.BlockSpec((channels, wide), lambda i: (0, i))],
        out_specs=pl.BlockSpec((1, rows, wide), lambda i: (i, 0, 0)),
        compiler_params=pltpu.CompilerParams(vmem_limit_bytes=32 * MIB),
        cost_estimate=cost(2 * rows * channels * width, 2 * (3 * rows + channels) * width),
        name="guide",
    )(own, *lower, *upper, *features, pose_proj)


def project(guided, order, groups, total, heads, head_size, frames):
    blocks, rows, wide = guided.shape
    group_rows = [sum(piece.shape[2] for piece in group) for group in groups]
    counts = [amount // wide for amount in group_rows]
    used = sum(counts)
    flat = [piece for group in groups for piece in group]
    per_frame = rows // frames

    def body(order_ref, *refs):
        guided_refs = refs[:used]
        weight_refs = refs[used : used + len(flat)]
        rest = refs[used + len(flat) :]
        summed = None
        at, first = 0, 0
        for group, count in zip(groups, counts):
            lhs = jnp.concatenate([ref[0] for ref in guided_refs[first : first + count]], axis=1)
            held = weight_refs[at : at + len(group)]
            rhs = jnp.concatenate(
                [jnp.concatenate([ref[0, j] for ref in held], axis=0) for j in range(3)], axis=1
            )
            part = jnp.dot(lhs, rhs, preferred_element_type=F32)
            summed = part if summed is None else summed + part
            at, first = at + len(group), first + count
        if total is None:
            for j in range(3):
                rest[0][0, j] = summed[:, j * head_size : (j + 1) * head_size]
            return
        total_ref, query_ref, keyval_ref = rest
        for j in range(3):
            value = (total_ref[0, j] + summed[:, j * head_size : (j + 1) * head_size]).astype(BF16)
            for t in range(frames):
                part = value[t * per_frame : (t + 1) * per_frame]
                if j == 0:
                    query_ref[t, 0] = part
                else:
                    keyval_ref[t, 0, j - 1] = part

    def pick(i):
        return lambda h, order: (order[i], 0, 0)

    in_specs = [pl.BlockSpec((1, rows, wide), pick(i)) for i in range(used)]
    in_specs += [
        pl.BlockSpec((1, 3, piece.shape[2], head_size), lambda h, order: (h, 0, 0, 0)) for piece in flat
    ]
    operands = [order] + [guided] * used + flat
    sums = pl.BlockSpec((1, 3, rows, head_size), lambda h, order: (h, 0, 0, 0))
    if total is None:
        out_shape = jax.ShapeDtypeStruct((heads, 3, rows, head_size), F32)
        out_specs = sums
    else:
        in_specs.append(sums)
        operands.append(total)
        out_shape = (
            jax.ShapeDtypeStruct((frames, heads, per_frame, head_size), BF16),
            jax.ShapeDtypeStruct((frames, heads, 2, per_frame, head_size), BF16),
        )
        out_specs = (
            pl.BlockSpec((frames, 1, per_frame, head_size), lambda h, order: (0, h, 0, 0)),
            pl.BlockSpec((frames, 1, 2, per_frame, head_size), lambda h, order: (0, h, 0, 0, 0)),
        )
    columns = heads * 3 * head_size
    return pl.pallas_call(
        body,
        out_shape=out_shape,
        grid_spec=pltpu.PrefetchScalarGridSpec(
            num_scalar_prefetch=1, grid=(heads,), in_specs=in_specs, out_specs=out_specs
        ),
        compiler_params=pltpu.CompilerParams(vmem_limit_bytes=48 * MIB),
        cost_estimate=cost(
            2 * rows * sum(group_rows) * columns,
            2 * sum(group_rows) * (columns + rows) + 4 * rows * columns,
        ),
        name="project",
    )(*operands)


def attend(queries, pieces, bases, spans, frame_count, strips):
    frames, heads, rows, size = queries.shape
    window = frame_count - 4 if frame_count > 4 else frame_count
    strip = rows // strips
    lengths = [piece.shape[0] for piece in pieces]
    table = jnp.concatenate([jnp.stack(bases).astype(jnp.int32), spans.reshape(-1).astype(jnp.int32)])
    scale = size ** (-0.5)

    def body(table_ref, query_ref, *refs):
        piece_refs, out_ref, held_ref = refs[: len(pieces)], refs[-2], refs[-1]
        for p, ref in enumerate(piece_refs):
            for t in range(lengths[p]):
                held_ref[table_ref[p] + t] = ref[t, 0]
        for t in range(frames):
            at = len(pieces) + 3 * t
            begin, low, high = table_ref[at], table_ref[at + 1], table_ref[at + 2]
            keys = held_ref[pl.ds(begin, window), 0].reshape(window * rows, size)
            values = held_ref[pl.ds(begin, window), 1].reshape(window * rows, size)
            scores = lax.dot_general(
                query_ref[t, 0], keys, (((1,), (1,)), ((), ())), preferred_element_type=F32
            )
            place = lax.broadcasted_iota(jnp.int32, (1, window * rows), 1)
            seen = (place >= low * rows) & (place < high * rows)
            scores = jnp.where(seen, scores * scale, NEG_FILL)
            weights = jnp.exp(scores - jnp.max(scores, axis=1, keepdims=True))
            totals = jnp.sum(weights, axis=1, keepdims=True)
            mixed = jnp.dot(weights.astype(BF16), values, preferred_element_type=F32)
            result = (mixed / totals).astype(BF16)
            for s in range(strips):
                out_ref[s, t] = result[s * strip : (s + 1) * strip]

    in_specs = [pl.BlockSpec((frames, 1, rows, size), lambda h, table: (0, h, 0, 0))]
    in_specs += [
        pl.BlockSpec((length, 1, 2, rows, size), lambda h, table: (0, h, 0, 0, 0)) for length in lengths
    ]
    return pl.pallas_call(
        body,
        out_shape=jax.ShapeDtypeStruct((strips, frames, strip, heads * size), BF16),
        grid_spec=pltpu.PrefetchScalarGridSpec(
            num_scalar_prefetch=1,
            grid=(heads,),
            in_specs=in_specs,
            out_specs=pl.BlockSpec((strips, frames, strip, size), lambda h, table: (0, 0, 0, h)),
            scratch_shapes=[pltpu.VMEM((frame_count, 2, rows, size), BF16)],
        ),
        compiler_params=pltpu.CompilerParams(vmem_limit_bytes=48 * MIB),
        cost_estimate=cost(
            4 * heads * frames * rows * rows * window * size,
            4 * heads * frame_count * rows * size,
            heads * frames * rows * rows * window,
        ),
        name="attend",
    )(table, queries, *pieces)


def out_project(rows_in, weight, place, groups, parts):
    tokens, depth = rows_in[0][0].shape[1:]
    columns = weight.shape[3]
    amount = len(rows_in)
    flat = [piece for pieces in rows_in for piece in pieces]

    def body(place_ref, *refs):
        step = pl.program_id(0)
        weight_ref, out_ref, acc_ref = refs[len(flat)], refs[-2], refs[-1]
        at, found = 0, []
        for pieces in rows_in:
            held = refs[at : at + len(pieces)]
            at += len(pieces)
            if len(held) == 1:
                found.append(held[0][step])
                continue
            first = pieces[0].shape[0]
            near = held[0][jnp.minimum(step, first - 1)]
            far = held[1][jnp.maximum(step - first, 0)]
            found.append(jnp.where(step < first, near, far))
        lhs = jnp.concatenate(found, axis=0)
        part = jnp.dot(lhs, weight_ref[:, 0].reshape(depth, columns), preferred_element_type=F32)
        part = part.astype(BF16).astype(F32)

        @pl.when(step == 0)
        def _():
            acc_ref[...] = part

        @pl.when(step > 0)
        def _():
            acc_ref[...] += part

        @pl.when(step == groups - 1)
        def _():
            for r in range(amount):
                out_ref[r] = acc_ref[r * tokens : (r + 1) * tokens].astype(BF16)

    in_specs = [pl.BlockSpec(piece.shape, lambda g, place: (0, 0, 0)) for piece in flat]
    in_specs.append(
        pl.BlockSpec(
            (parts, 1, depth // parts, columns), lambda g, place: (0, lax.rem(place[0] + g, groups), 0, 0)
        )
    )
    return pl.pallas_call(
        body,
        out_shape=jax.ShapeDtypeStruct((amount, tokens, columns), BF16),
        grid_spec=pltpu.PrefetchScalarGridSpec(
            num_scalar_prefetch=1,
            grid=(groups,),
            in_specs=in_specs,
            out_specs=pl.BlockSpec((amount, tokens, columns), lambda g, place: (0, 0, 0)),
            scratch_shapes=[pltpu.VMEM((amount * tokens, columns), F32)],
        ),
        compiler_params=pltpu.CompilerParams(vmem_limit_bytes=32 * MIB),
        cost_estimate=cost(
            2 * amount * tokens * groups * depth * columns, 2 * groups * depth * (columns + amount * tokens)
        ),
        name="out_project",
    )(place, *flat, weight)


def place_columns(pieces, me):
    tokens, columns = pieces[0].shape
    amount = len(pieces)

    def body(me_ref, *refs):
        step = pl.program_id(0)
        for r in range(amount):

            @pl.when(step == r)
            def _(r=r):
                refs[-1][...] = refs[r][...]

    return pl.pallas_call(
        body,
        out_shape=jax.ShapeDtypeStruct((tokens, amount * columns), BF16),
        grid_spec=pltpu.PrefetchScalarGridSpec(
            num_scalar_prefetch=1,
            grid=(amount,),
            in_specs=[pl.BlockSpec((tokens, columns), lambda i, me: (0, 0))] * amount,
            out_specs=pl.BlockSpec((tokens, columns), lambda i, me: (0, me[0] ^ i)),
        ),
        cost_estimate=cost(0, 4 * tokens * amount * columns),
        name="place_columns",
    )(me, *pieces)


def shards(
    latent, pose_maps, conv_weight, conv_bias, pose_proj, w_qkv, w_out, clip_lengths, block_ids
):
    frame_count = block_ids.shape[0]
    frames, strip_rows, width_grid, model_width = latent.shape
    heads, head_size = w_qkv.shape[1], w_qkv.shape[3]
    strips = lax.axis_size("head")
    frame_devices = lax.axis_size("frame")
    strip = strip_rows * width_grid
    tokens = frames * strip
    per_frame = strips * strip
    here = lax.axis_index("frame").astype(jnp.int32)
    group = lax.axis_index("head").astype(jnp.int32)
    core = lax.axis_index("dp").astype(jnp.int32)
    first_frame = here * frames
    clip_of, start_of = frame_tables(clip_lengths, frame_count)

    own = latent.reshape(tokens, model_width)
    lower, upper = hop(own, own, "head", 1)
    lower, upper = [lower], [upper]

    weight = jnp.transpose(w_qkv, (1, 2, 0, 3))
    plane = frame_devices == 4
    half_rows = weight.shape[2] // 2
    if plane:
        half = take_rows(weight, core)
        from_x, from_y = across(half, "frame", 1), across(half, "frame", 2)

    feature = pose_feature(pose_maps, conv_weight, conv_bias, start_of, first_frame)
    features = [feature] + [turn(feature, "head", s) for s in range(1, strips)]
    lower[0], upper[0] = after(lower[0], *features), after(upper[0], *features)
    for s in range(2, strips):
        below, above = hop(lower[-1], upper[-1], "head", s)
        lower.append(below)
        upper.append(above)
    if plane:
        from_x, from_y = after(from_x, lower[1]), after(from_y, upper[1])
        quarter = half_rows // 2
        far_x = across(from_y[:, :, :quarter], "frame", 1)
        far_y = across(from_x[:, :, quarter:], "frame", 2)
        other_x, other_y = across(from_x, "dp", 1), across(from_y, "dp", 1)
        other_far_x, other_far_y = across(far_x, "dp", 1), across(far_y, "dp", 1)
    blocks = 8
    guided = guide(own, lower, upper, features, pose_proj, frames, blocks)

    if plane:
        order = []
        for near in (here, here ^ 1, here ^ 2, here ^ 3):
            order += [2 * near, 2 * near + 1] if near is here else [2 * near + core, 2 * near + 1 - core]
        order = jnp.stack(order)
        total = project(
            guided,
            order[:6],
            [(weight,), (from_x, other_x), (from_y, other_y)],
            None,
            heads,
            head_size,
            frames,
        )
        queries, keyvals = project(
            guided,
            order[6:],
            [(far_x, far_y, other_far_x, other_far_y)],
            total,
            heads,
            head_size,
            frames,
        )
    else:
        whole = lax.all_gather(weight, "frame", axis=2, tiled=True)
        flat = jnp.transpose(guided, (1, 0, 2)).reshape(-1, model_width)
        projected = jnp.einsum("mk,hjkd->hjmd", flat, whole, preferred_element_type=F32).astype(BF16)
        projected = projected.reshape(heads, 3, frames, per_frame, head_size)
        queries = jnp.transpose(projected[:, 0], (1, 0, 2, 3))
        keyvals = jnp.transpose(projected[:, 1:], (2, 0, 1, 3, 4))

    same_clip = clip_of[:, None] == clip_of[None, :]
    counts = jnp.sum((same_clip & (block_ids[None, :] <= block_ids[:, None])).astype(jnp.int32), axis=1)
    window = frame_count - 4 if frame_count > 4 else frame_count
    begins = jnp.minimum(start_of, frame_count - window)
    spans = jnp.stack([begins, start_of - begins, start_of - begins + counts], axis=1)
    spans = lax.dynamic_slice_in_dim(spans, first_frame, frames)
    if plane:
        near_x, near_y = across(keyvals, "frame", 1), across(keyvals, "frame", 2)
        middle = frames // 2
        diag_x = across(near_y[:middle], "frame", 1)
        diag_y = across(near_x[middle:], "frame", 2)
        pieces = [keyvals, near_x, near_y, diag_x, diag_y]
        bases = [here, here ^ 1, here ^ 2, here ^ 3, here ^ 3]
        bases = [base * frames for base in bases]
        bases[4] = bases[4] + middle
    else:
        pieces = [lax.all_gather(keyvals, "frame", axis=0, tiled=True)]
        bases = [jnp.int32(0)]
    head_out = attend(queries, pieces, bases, spans, frame_count, strips)
    head_out = head_out.reshape(strips, tokens, heads * head_size)

    flat_out = w_out.reshape(heads * head_size, model_width)
    if not plane:
        flat_rows = jnp.take(head_out, (group - jnp.arange(strips, dtype=jnp.int32)) % strips, axis=0)
        partial = jnp.dot(flat_rows, flat_out, preferred_element_type=F32).astype(BF16)
        summed = lax.psum_scatter(partial, "head", scatter_dimension=0, tiled=True)
        return summed.reshape(latent.shape)

    columns = model_width // frame_devices
    half_depth = heads * head_size // 2
    out_half = take_block(flat_out, core, here, (half_depth, columns), guided)
    out_weight = lax.all_gather(out_half, "head")
    out_weight = lax.all_gather(after(out_weight, head_out), "dp")

    strip_heads = [head_out[0]] + [turn(head_out[s], "head", -s) for s in range(1, strips)]
    strip_heads = jnp.stack(strip_heads)
    rows_x, rows_y = across(strip_heads, "frame", 1), across(strip_heads, "frame", 2)
    middle = strips // 2
    far = [across(rows_y[:middle], "frame", 1), across(rows_x[middle:], "frame", 2)]
    done = out_project(
        [[strip_heads], [rows_x], [rows_y], far], out_weight, group.reshape(1), strips, 2
    )
    mine = [done[0]] + [across(done[r], "frame", r) for r in range(1, frame_devices)]
    return place_columns(mine, here.reshape(1)).reshape(latent.shape)


def solution(mesh):
    return jax.shard_map(
        shards,
        mesh=mesh,
        in_specs=(
            P(("dp", "frame"), "head", None, None),
            P(("dp", "frame"), "head", None, None),
            P(),
            P(),
            P(),
            P("frame", "head", None, None),
            P("head", None, None),
            P("dp"),
            P("dp"),
        ),
        out_specs=P(("dp", "frame"), "head", None, None),
        check_vma=False,
    )
```

```python
import jax
import jax.numpy as jnp
from jax import lax
from jax.experimental import pallas as pl
from jax.experimental.pallas import tpu as pltpu
from jax.sharding import PartitionSpec as P

NEG_FILL = -1e30
MIB = 1 << 20
F32 = jnp.float32
BF16 = jnp.bfloat16
PLANE = 4


def cost(flops, moved, exps=0):
    return pl.CostEstimate(flops=int(flops), bytes_accessed=int(moved), transcendentals=int(exps))


def shifted(value, axis, steps):
    count = lax.axis_size(axis)
    leading, last = (max(0, -steps), min(count, count - steps))
    return lax.ppermute(value, axis, [(source, source + steps) for source in range(leading, last)])


def frame_tables(clip_lengths, frame_count):
    clip_ends = jnp.cumsum(clip_lengths)
    clip_starts = clip_ends - clip_lengths
    frame_index = jnp.arange(frame_count, dtype=jnp.int32)
    clip_of = jnp.sum((frame_index[:, None] >= clip_ends[None, :]).astype(jnp.int32), axis=1)
    clip_match = clip_of[:, None] == jnp.arange(clip_lengths.shape[0], dtype=jnp.int32)[None, :]
    start_of = jnp.sum(jnp.where(clip_match, clip_starts[None, :], 0), axis=1)
    return (clip_of, start_of)


def guide_features(latent, pose_maps, conv_weight, conv_bias, pose_proj, start_of, first_frame):
    frames_dev = pose_maps.shape[0]
    upper_row = shifted(pose_maps[:, -1:], "head", 1)
    rows_ext = jnp.concatenate([upper_row, pose_maps], axis=1)
    left_column = jnp.zeros(rows_ext.shape[:2] + (1, rows_ext.shape[3]), rows_ext.dtype)
    cols_ext = jnp.concatenate([left_column, rows_ext], axis=2)
    earlier = shifted(cols_ext, "frame", 1)
    extended = jnp.concatenate([earlier, cols_ext], axis=0)
    out_rows = pose_maps.shape[1] // 2
    out_cols = pose_maps.shape[2] // 2
    frame_ids = first_frame + jnp.arange(frames_dev, dtype=jnp.int32)
    starts_here = lax.dynamic_slice_in_dim(start_of, first_frame, frames_dev)
    tap_list = []
    for step_a in range(3):
        keep_mask = (frame_ids - 2 + step_a >= starts_here).astype(pose_maps.dtype)[
            :, None, None, None
        ]
        frames_tap = extended[step_a : step_a + frames_dev] * keep_mask
        for step_b in range(3):
            for step_e in range(3):
                tap_list.append(
                    frames_tap[
                        :,
                        step_b : step_b + 2 * out_rows - 1 : 2,
                        step_e : step_e + 2 * out_cols - 1 : 2,
                    ]
                )
    stacked = jnp.concatenate(tap_list, axis=3)
    kernel = conv_weight.reshape(-1, conv_weight.shape[-1])
    summed = jnp.dot(stacked, kernel, preferred_element_type=jnp.float32) + conv_bias
    feature = jax.nn.silu(summed).astype(jnp.bfloat16)
    guided = latent.astype(jnp.float32) + jnp.dot(
        feature, pose_proj, preferred_element_type=jnp.float32
    )
    return guided.astype(jnp.bfloat16)


def attend_rows(queries, query_clip, query_block, keyvals, clip_of, block_ids):
    heads_dev = queries.shape[1]
    rows_query = queries.shape[0]
    head_size = queries.shape[2]
    score_scale = head_size ** (-0.5)
    start_carry = (
        jnp.full((heads_dev, rows_query), NEG_FILL, jnp.float32),
        jnp.zeros((heads_dev, rows_query), jnp.float32),
        jnp.zeros((heads_dev, rows_query, head_size), jnp.float32),
    )

    def one_frame(running, frame_item):
        frame_kv, frame_id = frame_item
        key_clip = clip_of[frame_id]
        key_block = block_ids[frame_id]
        visible = (query_clip == key_clip) & (key_block <= query_block)
        run_max, run_total, run_acc = running
        scores = (
            jnp.einsum(
                "qhd,khd->hqk", queries, frame_kv[:, :, 0], preferred_element_type=jnp.float32
            )
            * score_scale
        )
        scores = jnp.where(visible[None, :, None], scores, NEG_FILL)
        new_max = jnp.maximum(run_max, jnp.max(scores, axis=2))
        factor = jnp.exp(run_max - new_max)
        weights = jnp.where(visible[None, :, None], jnp.exp(scores - new_max[:, :, None]), 0.0)
        new_total = run_total * factor + jnp.sum(weights, axis=2)
        new_acc = run_acc * factor[:, :, None] + jnp.einsum(
            "hqk,khd->hqd",
            weights.astype(jnp.bfloat16),
            frame_kv[:, :, 1],
            preferred_element_type=jnp.float32,
        )
        running = (new_max, new_total, new_acc)
        return (running, None)

    running = start_carry
    shard_piece = lax.all_gather(keyvals, "frame", axis=0, tiled=True)
    piece_frames = shard_piece.shape[0]
    frame_list = jnp.arange(piece_frames, dtype=jnp.int32)
    running, unused = lax.scan(one_frame, running, (shard_piece, frame_list))
    run_max, run_total, run_acc = running
    normalized = run_acc / run_total[:, :, None]
    return jnp.transpose(normalized, (1, 0, 2)).astype(jnp.bfloat16)


def plain_shards(
    latent, pose_maps, conv_weight, conv_bias, pose_proj, w_qkv, w_out, clip_lengths, block_ids
):
    frame_count = block_ids.shape[0]
    clip_of, start_of = frame_tables(clip_lengths, frame_count)
    frames_dev = latent.shape[0]
    first_frame = lax.axis_index("frame") * frames_dev
    guided = guide_features(
        latent, pose_maps, conv_weight, conv_bias, pose_proj, start_of, first_frame
    )
    whole_rows = lax.all_gather(guided, "head", axis=1, tiled=True)
    height = whole_rows.shape[1]
    width_grid = whole_rows.shape[2]
    model_width = whole_rows.shape[3]
    flat_tokens = whole_rows.reshape(-1, model_width)
    qkv_local = w_qkv.reshape(w_qkv.shape[0], -1)
    projected = jnp.dot(
        flat_tokens,
        lax.all_gather(qkv_local, "frame", axis=0, tiled=True),
        preferred_element_type=jnp.float32,
    ).astype(jnp.bfloat16)
    per_frame = height * width_grid
    heads_dev = w_qkv.shape[1]
    head_size = w_qkv.shape[3]
    grouped = projected.reshape(frames_dev, per_frame, heads_dev, 3, head_size)
    rows_total = frames_dev * per_frame
    queries = grouped[:, :, :, 0].reshape(rows_total, heads_dev, head_size)
    keyvals = grouped[:, :, :, 1:3]
    clip_rows = lax.dynamic_slice_in_dim(clip_of, first_frame, frames_dev)
    block_rows = lax.dynamic_slice_in_dim(block_ids, first_frame, frames_dev)
    query_clip = jnp.repeat(clip_rows, per_frame)
    query_block = jnp.repeat(block_rows, per_frame)
    attended = attend_rows(queries, query_clip, query_block, keyvals, clip_of, block_ids)
    by_row = attended.reshape(frames_dev, height, width_grid, heads_dev * head_size)
    by_row = jnp.transpose(by_row, (1, 0, 2, 3)).reshape(
        height, frames_dev * width_grid, heads_dev * head_size
    )
    out_weight = w_out.reshape(heads_dev * head_size, w_out.shape[2])
    rows_here = height // lax.axis_size("head")
    summed_rows = lax.psum_scatter(
        jnp.dot(by_row, out_weight, preferred_element_type=jnp.float32).astype(jnp.bfloat16),
        "head",
        scatter_dimension=0,
        tiled=True,
    ).astype(jnp.float32)
    summed_rows = summed_rows.reshape(rows_here, frames_dev, width_grid, out_weight.shape[1])
    return jnp.transpose(summed_rows, (1, 0, 2, 3)).astype(jnp.bfloat16)


def turn(value, axis, steps):
    count = lax.axis_size(axis)
    return lax.ppermute(value, axis, [(i, (i + steps) % count) for i in range(count)])


def across(value, axis, bits):
    count = lax.axis_size(axis)
    return lax.ppermute(value, axis, [(i, i ^ bits) for i in range(count)])


def hop(lower, upper, axis, s):
    count = lax.axis_size(axis)
    lower = lax.ppermute(lower, axis, [(i, i + 1) for i in range(s - 1, count - 1)])
    upper = lax.ppermute(upper, axis, [(i, i - 1) for i in range(1, count - s + 1)])
    return lower, upper


def after(value, *others):
    def body(*refs):
        del refs

    anywhere = pl.BlockSpec(memory_space=pl.ANY)
    return pl.pallas_call(
        body,
        out_shape=jax.ShapeDtypeStruct(value.shape, value.dtype),
        in_specs=[anywhere] * (1 + len(others)),
        out_specs=anywhere,
        input_output_aliases={0: 0},
        name="after",
    )(value, *others)


def take_rows(weight, half, *ready):
    columns, rows, size = weight.shape
    part = columns // 3

    def body(half_ref, weight_ref, *refs):
        refs[-1][...] = weight_ref[...]

    return pl.pallas_call(
        body,
        out_shape=jax.ShapeDtypeStruct((columns, rows // 2, size), weight.dtype),
        grid_spec=pltpu.PrefetchScalarGridSpec(
            num_scalar_prefetch=1,
            grid=(3,),
            in_specs=[pl.BlockSpec((part, rows // 2, size), lambda h, half: (h, half[0], 0))]
            + [pl.BlockSpec(memory_space=pl.ANY)] * len(ready),
            out_specs=pl.BlockSpec((part, rows // 2, size), lambda h, half: (h, 0, 0)),
        ),
        cost_estimate=cost(0, 2 * weight.size),
        name="take_rows",
    )(half.reshape(1), weight, *ready)


def take_block(weight, row, column, shape, *ready):
    def body(at_ref, weight_ref, *refs):
        refs[-1][...] = weight_ref[...]

    return pl.pallas_call(
        body,
        out_shape=jax.ShapeDtypeStruct(shape, weight.dtype),
        grid_spec=pltpu.PrefetchScalarGridSpec(
            num_scalar_prefetch=1,
            grid=(1,),
            in_specs=[pl.BlockSpec(shape, lambda i, at: (at[0], at[1]))]
            + [pl.BlockSpec(memory_space=pl.ANY)] * len(ready),
            out_specs=pl.BlockSpec(shape, lambda i, at: (0, 0)),
        ),
        cost_estimate=cost(0, 4 * shape[0] * shape[1]),
        name="take_block",
    )(jnp.stack([row, column]), weight, *ready)


def conv_kernel(keep_ref, cols_ref, weight_ref, bias_ref, out_ref, acc_ref):
    step = pl.program_id(0)
    tap_a, tap_b = step // 3, step % 3
    frames, strip_rows, width = out_ref.shape[0], out_ref.shape[1], cols_ref.shape[2]
    pieces = []
    for t in range(frames):
        keep = keep_ref[tap_a * frames + t]
        for r in range(strip_rows):
            rows = cols_ref[tap_a + t, tap_b + 2 * r].astype(F32)
            pieces.append(jnp.where(keep > 0, rows, 0.0))
    lhs = jnp.concatenate(pieces, axis=0).astype(BF16)
    channels = weight_ref.shape[3]
    total = None
    for e in range(3):
        part = lax.dot_general(
            lhs[:, e * channels : (e + 1) * channels],
            weight_ref[0, e],
            (((1,), (1,)), ((), ())),
            preferred_element_type=F32,
        )
        total = part if total is None else total + part

    @pl.when(step == 0)
    def _():
        acc_ref[...] = total

    @pl.when(step > 0)
    def _():
        acc_ref[...] += total

    @pl.when(step == 8)
    def _():
        summed = acc_ref[...] + bias_ref[...]
        feature = summed / (1.0 + jnp.exp(-summed))
        for t in range(frames):
            for r in range(strip_rows):
                at = (t * strip_rows + r) * width
                out_ref[t, r] = feature[at : at + width].astype(BF16)


def pose_halos(pose_maps):
    devices, strips = lax.axis_size("frame"), lax.axis_size("head")
    last = pose_maps[:, -1:]
    upper_row = shifted(last, "head", 1)
    earlier = shifted(pose_maps, "frame", 1)
    corners = [
        (f * strips + z, (f + 1) * strips + z + 1) for f in range(devices - 1) for z in range(strips - 1)
    ]
    return upper_row, earlier, lax.ppermute(last, ("frame", "head"), corners)


def pose_feature(halos, pose_maps, conv_weight, conv_bias, start_of, first_frame):
    frames, rows, columns, channels = pose_maps.shape
    out_channels = conv_weight.shape[-1]
    upper_row, earlier, corner = halos
    extended = jnp.concatenate(
        [jnp.concatenate([corner, earlier], axis=1), jnp.concatenate([upper_row, pose_maps], axis=1)], axis=0
    )
    pairs = extended.reshape(2 * frames, rows + 1, columns // 2, 2 * channels)
    before = jnp.pad(pairs[:, :, :-1, channels:], ((0, 0), (0, 0), (1, 0), (0, 0)))
    cols = jnp.concatenate([before, pairs], axis=3)
    taps = jnp.transpose(conv_weight, (0, 1, 2, 4, 3)).reshape(9, 3, out_channels, channels)
    frame_ids = first_frame + jnp.arange(frames, dtype=jnp.int32)
    starts_here = lax.dynamic_slice_in_dim(start_of, first_frame, frames)
    keep = (frame_ids[None, :] - 2 + jnp.arange(3, dtype=jnp.int32)[:, None] >= starts_here[None, :])
    keep = keep.astype(jnp.int32).reshape(-1)
    out_shape = (frames, rows // 2, columns // 2, out_channels)
    tokens = frames * (rows // 2) * (columns // 2)
    feature = pl.pallas_call(
        conv_kernel,
        out_shape=jax.ShapeDtypeStruct(out_shape, BF16),
        grid_spec=pltpu.PrefetchScalarGridSpec(
            num_scalar_prefetch=1,
            grid=(9,),
            in_specs=[
                pl.BlockSpec(cols.shape, lambda i, k: (0, 0, 0, 0)),
                pl.BlockSpec((1, 3, out_channels, channels), lambda i, k: (i, 0, 0, 0)),
                pl.BlockSpec((1, out_channels), lambda i, k: (0, 0)),
            ],
            out_specs=pl.BlockSpec(out_shape, lambda i, k: (0, 0, 0, 0)),
            scratch_shapes=[pltpu.VMEM((tokens, out_channels), F32)],
        ),
        compiler_params=pltpu.CompilerParams(vmem_limit_bytes=24 * MIB),
        cost_estimate=cost(tokens * out_channels, 2 * tokens * out_channels),
        name="pose_conv",
    )(keep, cols, taps, conv_bias.reshape(1, -1))
    return feature.reshape(tokens, out_channels)


def project(own, lower, upper, features, pose_proj, order, sources, total, here, frames):
    strips = len(features)
    tokens = own.shape[0]
    channels = pose_proj.shape[0]
    columns, half, size = sources[-1].shape
    rows = strips * tokens
    per_frame = tokens // frames
    plan = [(a, b) for a, array in enumerate(sources) for b in range(array.shape[1] // half)]
    steps = len(plan)
    heads = columns // 3

    def body(order_ref, *refs):
        refs = list(refs)
        own_ref, lower_refs, upper_refs = refs[0], refs[1:strips], refs[strips : 2 * strips - 1]
        feature_refs = refs[2 * strips - 1 : 3 * strips - 1]
        proj_ref = refs[3 * strips - 1]
        source_refs = refs[3 * strips : 3 * strips + len(sources)]
        rest = refs[3 * strips + len(sources) :]
        held_ref, guided_ref, sems = rest[-3:]
        if total is None:
            sum_ref = rest[0]
        else:
            total_ref, last_ref, sum_ref = rest[0], rest[1 + PLANE], rest[2 + PLANE]
            message_refs = rest[1 : 1 + PLANE]
        step = pl.program_id(0)

        def fetch(k):
            a, b = plan[k]
            return pltpu.make_async_copy(
                source_refs[a].at[:, pl.ds(b * half, half)], held_ref.at[k % 2], sems.at[k % 2]
            )

        for k in range(steps):

            @pl.when(step == max(k - 1, 0))
            def _(k=k):
                fetch(k).start()

        feature = jnp.concatenate([ref[...] for ref in feature_refs], axis=0)
        added = jnp.dot(feature, proj_ref[...], preferred_element_type=F32)
        for s in range(strips):
            latent = own_ref[...].astype(F32)
            if s > 0:
                latent = lower_refs[s - 1][...].astype(F32) + upper_refs[strips - s - 1][...].astype(F32)
            guided = (latent + added[s * tokens : (s + 1) * tokens]).astype(BF16)
            for t in range(frames):
                at = (t * strips + s) * per_frame
                guided_ref[at : at + per_frame] = guided[t * per_frame : (t + 1) * per_frame]

        @pl.when(step == 0)
        def _():
            sum_ref[...] = jnp.zeros_like(sum_ref) if total is None else total_ref[...]

        for k in range(steps):

            @pl.when(step == k)
            def _(k=k):
                fetch(k).wait()

        slot = lax.rem(step, 2)
        for c in range(0, columns, 2):
            wide = min(2, columns - c)
            rhs = jnp.concatenate([held_ref[slot, c + w] for w in range(wide)], axis=1)
            sum_ref[:, c * size : (c + wide) * size] += jnp.dot(
                guided_ref[...], rhs, preferred_element_type=F32
            )

        if total is None:
            return

        @pl.when(step == steps - 1)
        def _():
            last = 3 * (heads - 1) * size
            last_ref[...] = sum_ref[:, last : last + size].astype(BF16)
            for r in range(PLANE):
                head = order_ref[steps] ^ r
                for j in range(3):
                    at = pl.multiple_of((3 * head + j) * size, size)
                    message_refs[r][j] = sum_ref[:, pl.ds(at, size)].astype(BF16)
                for j in range(1, 3):
                    at = last + j * size
                    message_refs[r][2 + j] = sum_ref[:, at : at + size].astype(BF16)

    piece = pl.BlockSpec((tokens, half), lambda i, order: (0, order[i]))
    in_specs = [piece] * (2 * strips - 1)
    in_specs += [pl.BlockSpec((tokens, channels), lambda i, order: (0, 0))] * strips
    in_specs += [pl.BlockSpec((channels, half), lambda i, order: (0, order[i]))]
    in_specs += [pl.BlockSpec(memory_space=pl.ANY)] * len(sources)
    operands = [own, *lower, *upper, *features, pose_proj, *sources]
    sums = pl.BlockSpec((rows, columns * size), lambda i, order: (0, 0))
    scratch = [
        pltpu.VMEM((2, columns, half, size), BF16),
        pltpu.VMEM((rows, half), BF16),
        pltpu.SemaphoreType.DMA((2,)),
    ]
    if total is None:
        out_shape, out_specs = jax.ShapeDtypeStruct((rows, columns * size), F32), sums
    else:
        in_specs.append(sums)
        operands.append(total)
        message = jax.ShapeDtypeStruct((5, rows, size), BF16)
        out_shape = (message,) * PLANE + (jax.ShapeDtypeStruct((rows, size), BF16),)
        out_specs = (pl.BlockSpec((5, rows, size), lambda i, order: (0, 0, 0)),) * PLANE
        out_specs += (pl.BlockSpec((rows, size), lambda i, order: (0, 0)),)
        scratch = [pltpu.VMEM((rows, columns * size), F32)] + scratch
    return pl.pallas_call(
        body,
        out_shape=out_shape,
        grid_spec=pltpu.PrefetchScalarGridSpec(
            num_scalar_prefetch=1, grid=(steps,), in_specs=in_specs, out_specs=out_specs, scratch_shapes=scratch
        ),
        compiler_params=pltpu.CompilerParams(vmem_limit_bytes=44 * MIB),
        cost_estimate=cost(0, 2 * rows * size),
        name="project",
    )(order, *operands)


def attend(messages, last_query, here, spans, frames, strips):
    rows, size = last_query.shape
    per_frame = rows // frames
    strip = per_frame // strips
    frame_count = PLANE * frames
    window = frame_count - 4 if frame_count > 4 else frame_count
    out_rows = (PLANE + 1) * frames * strip
    scale = size ** (-0.5)

    def body(table_ref, *refs):
        message_refs, last_ref = refs[:PLANE], refs[PLANE]
        out_refs, held_ref = refs[PLANE + 1 : PLANE + 1 + strips], refs[-1]
        here_at = table_ref[3 * frame_count]
        for r in range(PLANE):
            for t in range(frames):
                frame = (here_at ^ r) * frames + t
                for j in range(4):
                    held_ref[frame, j] = message_refs[r][j + 1, t * per_frame : (t + 1) * per_frame]

        def one(query, frame, kind, at):
            begin, low, high = table_ref[3 * frame], table_ref[3 * frame + 1], table_ref[3 * frame + 2]
            keys = held_ref[pl.ds(begin, window), kind].reshape(window * per_frame, size)
            values = held_ref[pl.ds(begin, window), kind + 1].reshape(window * per_frame, size)
            scores = lax.dot_general(query, keys, (((1,), (1,)), ((), ())), preferred_element_type=F32)
            place = lax.broadcasted_iota(jnp.int32, (1, window * per_frame), 1)
            seen = (place >= low * per_frame) & (place < high * per_frame)
            scores = jnp.where(seen, scores * scale, NEG_FILL)
            weights = jnp.exp(scores - jnp.max(scores, axis=1, keepdims=True))
            totals = jnp.sum(weights, axis=1, keepdims=True)
            mixed = jnp.dot(weights.astype(BF16), values, preferred_element_type=F32)
            result = (mixed / totals).astype(BF16)
            for s in range(strips):
                out_refs[s][at : at + strip] = result[s * strip : (s + 1) * strip]

        for r in range(PLANE):
            for t in range(frames):
                query = message_refs[r][0, t * per_frame : (t + 1) * per_frame]
                one(query, (here_at ^ r) * frames + t, 0, (r * frames + t) * strip)
        for t in range(frames):
            query = last_ref[t * per_frame : (t + 1) * per_frame]
            one(query, here_at * frames + t, 2, (PLANE * frames + t) * strip)

    table = jnp.concatenate([spans.reshape(-1), here.reshape(1)]).astype(jnp.int32)
    whole = pl.BlockSpec((5, rows, size), lambda i, table: (0, 0, 0))
    units = (PLANE + 1) * frames
    return pl.pallas_call(
        body,
        out_shape=(jax.ShapeDtypeStruct((out_rows, size), BF16),) * strips,
        grid_spec=pltpu.PrefetchScalarGridSpec(
            num_scalar_prefetch=1,
            grid=(1,),
            in_specs=[whole] * PLANE + [pl.BlockSpec((rows, size), lambda i, table: (0, 0))],
            out_specs=(pl.BlockSpec((out_rows, size), lambda i, table: (0, 0)),) * strips,
            scratch_shapes=[pltpu.VMEM((frame_count, 4, per_frame, size), BF16)],
        ),
        compiler_params=pltpu.CompilerParams(vmem_limit_bytes=40 * MIB),
        cost_estimate=cost(0, 2 * rows * size),
        name="attend",
    )(table, *messages, last_query)


def out_project(gathered, weights, here, group, core, tokens):
    groups, depth, columns = weights[0].shape
    size = gathered[0][0].shape[-1]
    heads = depth // size

    def body(at_ref, *refs):
        weight_refs = refs[2 * PLANE : 2 * PLANE + 2]
        out_ref, lhs_ref, sum_ref = refs[-3:]
        step = pl.program_id(0)
        for s in range(groups):

            @pl.when(step == s)
            def _(s=s):
                found = [refs[2 * q] if s == 0 else refs[2 * q + 1].at[s - 1] for q in range(PLANE)]
                for p in range(PLANE):
                    rows = slice(p * tokens, (p + 1) * tokens)
                    for q in range(PLANE):
                        at = (p ^ q) * tokens
                        lhs_ref[rows, q * size : (q + 1) * size] = found[q][at : at + tokens]
                    lhs_ref[rows, PLANE * size :] = found[p][PLANE * tokens :]

        here_at, core_at = at_ref[0], at_ref[2]
        for c in range(2):
            found = [
                weight_refs[c][0, pl.ds(pl.multiple_of((here_at ^ q) * size, size), size)] for q in range(PLANE)
            ]
            found.append(weight_refs[c][0, PLANE * size : heads * size])
            part = jnp.dot(lhs_ref[...], jnp.concatenate(found, axis=0), preferred_element_type=F32)
            part = part.astype(BF16).astype(F32)

            @pl.when(step == 0)
            def _(c=c, part=part):
                sum_ref[c] = part

            @pl.when(step > 0)
            def _(c=c, part=part):
                sum_ref[c] += part

        @pl.when(step == groups - 1)
        def _():
            for p in range(PLANE):
                for c in range(2):
                    at = pl.multiple_of((core_at ^ c) * columns, 128)
                    out_ref[p, :, pl.ds(at, columns)] = sum_ref[c, p * tokens : (p + 1) * tokens].astype(BF16)

    flat = [piece for pieces in gathered for piece in pieces]
    in_specs = [pl.BlockSpec(piece.shape, lambda g, at, n=piece.ndim: (0,) * n) for piece in flat]
    in_specs += [
        pl.BlockSpec((1, depth, columns), lambda g, at: (lax.rem(at[1] + g, groups), 0, 0))
    ] * 2
    return pl.pallas_call(
        body,
        out_shape=jax.ShapeDtypeStruct((PLANE, tokens, 2 * columns), BF16),
        grid_spec=pltpu.PrefetchScalarGridSpec(
            num_scalar_prefetch=1,
            grid=(groups,),
            in_specs=in_specs,
            out_specs=pl.BlockSpec((PLANE, tokens, 2 * columns), lambda g, at: (0, 0, 0)),
            scratch_shapes=[
                pltpu.VMEM((PLANE * tokens, depth), BF16),
                pltpu.VMEM((2, PLANE * tokens, columns), F32),
            ],
        ),
        compiler_params=pltpu.CompilerParams(vmem_limit_bytes=32 * MIB),
        cost_estimate=cost(
            4 * PLANE * tokens * groups * depth * columns, 2 * groups * depth * (2 * columns + PLANE * tokens)
        ),
        name="out_project",
    )(jnp.stack([here, group, core]), *flat, *weights)


def place_columns(pieces, here):
    tokens, columns = pieces[0].shape

    def body(here_ref, *refs):
        for r in range(PLANE):
            at = pl.multiple_of((here_ref[0] ^ r) * columns, 128)
            refs[-1][:, pl.ds(at, columns)] = refs[r][...]

    return pl.pallas_call(
        body,
        out_shape=jax.ShapeDtypeStruct((tokens, PLANE * columns), BF16),
        grid_spec=pltpu.PrefetchScalarGridSpec(
            num_scalar_prefetch=1,
            grid=(1,),
            in_specs=[pl.BlockSpec((tokens, columns), lambda i, here: (0, 0))] * PLANE,
            out_specs=pl.BlockSpec((tokens, PLANE * columns), lambda i, here: (0, 0)),
        ),
        cost_estimate=cost(0, 4 * tokens * PLANE * columns),
        name="place_columns",
    )(here.reshape(1), *pieces)


def shards(
    latent, pose_maps, conv_weight, conv_bias, pose_proj, w_qkv, w_out, clip_lengths, block_ids
):
    frame_count = block_ids.shape[0]
    frames, strip_rows, width_grid, model_width = latent.shape
    heads, head_size = w_qkv.shape[1], w_qkv.shape[3]
    strips = lax.axis_size("head")
    tokens = frames * strip_rows * width_grid
    here = lax.axis_index("frame").astype(jnp.int32)
    group = lax.axis_index("head").astype(jnp.int32)
    core = lax.axis_index("dp").astype(jnp.int32)
    clip_of, start_of = frame_tables(clip_lengths, frame_count)

    halos = pose_halos(pose_maps)

    weight = jnp.transpose(w_qkv, (1, 2, 0, 3)).reshape(3 * heads, -1, head_size)
    near_pairs = [(2 * f + c, 2 * (f ^ (1 + c)) + c) for f in range(PLANE) for c in range(2)]
    far_pairs = [(2 * f + c, 2 * (f ^ (2 - c)) + c) for f in range(PLANE) for c in range(2)]
    plane_axes = ("frame", "dp")
    own = latent.reshape(tokens, model_width)
    first = lax.ppermute(after(take_rows(weight, core), *halos), plane_axes, near_pairs)
    lower, upper = hop(own, own, "head", 1)
    second = lax.ppermute(take_rows(weight, 1 - core), plane_axes, near_pairs)
    lower, upper = [lower], [upper]

    columns = model_width // PLANE // 2
    depth = heads * head_size
    out_half = take_block(w_out.reshape(depth, model_width), jnp.int32(0), 2 * here + core, (depth, columns))

    start_of = after(start_of, lower[0], upper[0], out_half)
    feature = pose_feature(halos, pose_maps, conv_weight, conv_bias, start_of, here * frames)
    for s in range(2, strips):
        below, above = hop(lower[-1], upper[-1], "head", s)
        if s < strips - 1:
            below, above = after(below, feature), after(above, feature)
        lower.append(below)
        upper.append(above)
    feature = after(feature, lower[1], upper[1])
    features = [feature] + [turn(feature, "head", s) for s in range(1, strips)]
    second = after(second, *features[1:])
    first = after(first, second)
    out_half = after(out_half, lower[1], upper[1])
    far = lax.ppermute(first, plane_axes, far_pairs)
    other_first, other_second = across(first, "dp", 1), across(second, "dp", 1)

    here_next, here_other, here_far = here ^ (1 + core), here ^ (2 - core), here ^ 3
    order = [2 * here, 2 * here + 1, 2 * here_next + core, 2 * here_next + 1 - core]
    order += [2 * here_other + 1 - core, 2 * here_other + core, here]
    order = after(jnp.stack(order), out_half)
    sources = [weight, first, second, other_first, other_second]
    total = project(own, lower, upper, features, pose_proj, order, sources, None, here, frames)
    far = after(far, total)
    other_far = across(far, "dp", 1)
    order = jnp.stack([2 * here_far + core, 2 * here_far + 1 - core, here])
    *messages, last_query = project(
        own, lower, upper, features, pose_proj, order, [far, other_far], total, here, frames
    )
    messages = [messages[0]] + [across(messages[r], "frame", r) for r in range(1, PLANE)]

    same_clip = clip_of[:, None] == clip_of[None, :]
    counts = jnp.sum((same_clip & (block_ids[None, :] <= block_ids[:, None])).astype(jnp.int32), axis=1)
    window = frame_count - 4 if frame_count > 4 else frame_count
    begins = jnp.minimum(start_of, frame_count - window)
    spans = jnp.stack([begins, start_of - begins, start_of - begins + counts], axis=1)
    outs = attend(messages, last_query, here, spans, frames, strips)

    out_half = lax.all_gather(out_half, "head")
    out_half = after(out_half, outs[0])
    out_weights = [out_half, across(out_half, "dp", 1)]

    strip_heads = [outs[0]] + [turn(outs[s], "head", -s) for s in range(1, strips)]
    mine = [strip_heads[0], jnp.stack(strip_heads[1:])]
    gathered = [mine] + [[across(part, "frame", r) for part in mine] for r in range(1, PLANE)]
    done = out_project(gathered, out_weights, here, group, core, tokens)
    mine = [done[0]] + [across(done[r], "frame", r) for r in range(1, PLANE)]
    return place_columns(mine, here).reshape(latent.shape)


def solution(mesh):
    return jax.shard_map(
        shards if mesh.shape["frame"] == PLANE else plain_shards,
        mesh=mesh,
        in_specs=(
            P(("dp", "frame"), "head", None, None),
            P(("dp", "frame"), "head", None, None),
            P(),
            P(),
            P(),
            P("frame", "head", None, None),
            P("head", None, None),
            P("dp"),
            P("dp"),
        ),
        out_specs=P(("dp", "frame"), "head", None, None),
        check_vma=False,
    )
```

```python
import jax
import jax.numpy as jnp
from jax import lax
from jax.experimental import pallas as pl
from jax.experimental.pallas import tpu as pltpu
from jax.sharding import PartitionSpec as P

NEG_FILL = -1e30
MIB = 1 << 20
F32 = jnp.float32
BF16 = jnp.bfloat16
PLANE = 4


def cost(flops, moved, exps=0):
    return pl.CostEstimate(flops=int(flops), bytes_accessed=int(moved), transcendentals=int(exps))


def shifted(value, axis, steps):
    count = lax.axis_size(axis)
    leading, last = (max(0, -steps), min(count, count - steps))
    return lax.ppermute(value, axis, [(source, source + steps) for source in range(leading, last)])


def frame_tables(clip_lengths, frame_count):
    clip_ends = jnp.cumsum(clip_lengths)
    clip_starts = clip_ends - clip_lengths
    frame_index = jnp.arange(frame_count, dtype=jnp.int32)
    clip_of = jnp.sum((frame_index[:, None] >= clip_ends[None, :]).astype(jnp.int32), axis=1)
    clip_match = clip_of[:, None] == jnp.arange(clip_lengths.shape[0], dtype=jnp.int32)[None, :]
    start_of = jnp.sum(jnp.where(clip_match, clip_starts[None, :], 0), axis=1)
    return (clip_of, start_of)


def guide_features(latent, pose_maps, conv_weight, conv_bias, pose_proj, start_of, first_frame):
    frames_dev = pose_maps.shape[0]
    upper_row = shifted(pose_maps[:, -1:], "head", 1)
    rows_ext = jnp.concatenate([upper_row, pose_maps], axis=1)
    left_column = jnp.zeros(rows_ext.shape[:2] + (1, rows_ext.shape[3]), rows_ext.dtype)
    cols_ext = jnp.concatenate([left_column, rows_ext], axis=2)
    earlier = shifted(cols_ext, "frame", 1)
    extended = jnp.concatenate([earlier, cols_ext], axis=0)
    out_rows = pose_maps.shape[1] // 2
    out_cols = pose_maps.shape[2] // 2
    frame_ids = first_frame + jnp.arange(frames_dev, dtype=jnp.int32)
    starts_here = lax.dynamic_slice_in_dim(start_of, first_frame, frames_dev)
    tap_list = []
    for step_a in range(3):
        keep_mask = (frame_ids - 2 + step_a >= starts_here).astype(pose_maps.dtype)[
            :, None, None, None
        ]
        frames_tap = extended[step_a : step_a + frames_dev] * keep_mask
        for step_b in range(3):
            for step_e in range(3):
                tap_list.append(
                    frames_tap[
                        :,
                        step_b : step_b + 2 * out_rows - 1 : 2,
                        step_e : step_e + 2 * out_cols - 1 : 2,
                    ]
                )
    stacked = jnp.concatenate(tap_list, axis=3)
    kernel = conv_weight.reshape(-1, conv_weight.shape[-1])
    summed = jnp.dot(stacked, kernel, preferred_element_type=jnp.float32) + conv_bias
    feature = jax.nn.silu(summed).astype(jnp.bfloat16)
    guided = latent.astype(jnp.float32) + jnp.dot(
        feature, pose_proj, preferred_element_type=jnp.float32
    )
    return guided.astype(jnp.bfloat16)


def attend_rows(queries, query_clip, query_block, keyvals, clip_of, block_ids):
    heads_dev = queries.shape[1]
    rows_query = queries.shape[0]
    head_size = queries.shape[2]
    score_scale = head_size ** (-0.5)
    start_carry = (
        jnp.full((heads_dev, rows_query), NEG_FILL, jnp.float32),
        jnp.zeros((heads_dev, rows_query), jnp.float32),
        jnp.zeros((heads_dev, rows_query, head_size), jnp.float32),
    )

    def one_frame(running, frame_item):
        frame_kv, frame_id = frame_item
        key_clip = clip_of[frame_id]
        key_block = block_ids[frame_id]
        visible = (query_clip == key_clip) & (key_block <= query_block)
        run_max, run_total, run_acc = running
        scores = (
            jnp.einsum(
                "qhd,khd->hqk", queries, frame_kv[:, :, 0], preferred_element_type=jnp.float32
            )
            * score_scale
        )
        scores = jnp.where(visible[None, :, None], scores, NEG_FILL)
        new_max = jnp.maximum(run_max, jnp.max(scores, axis=2))
        factor = jnp.exp(run_max - new_max)
        weights = jnp.where(visible[None, :, None], jnp.exp(scores - new_max[:, :, None]), 0.0)
        new_total = run_total * factor + jnp.sum(weights, axis=2)
        new_acc = run_acc * factor[:, :, None] + jnp.einsum(
            "hqk,khd->hqd",
            weights.astype(jnp.bfloat16),
            frame_kv[:, :, 1],
            preferred_element_type=jnp.float32,
        )
        running = (new_max, new_total, new_acc)
        return (running, None)

    running = start_carry
    shard_piece = lax.all_gather(keyvals, "frame", axis=0, tiled=True)
    piece_frames = shard_piece.shape[0]
    frame_list = jnp.arange(piece_frames, dtype=jnp.int32)
    running, unused = lax.scan(one_frame, running, (shard_piece, frame_list))
    run_max, run_total, run_acc = running
    normalized = run_acc / run_total[:, :, None]
    return jnp.transpose(normalized, (1, 0, 2)).astype(jnp.bfloat16)


def plain_shards(
    latent, pose_maps, conv_weight, conv_bias, pose_proj, w_qkv, w_out, clip_lengths, block_ids
):
    frame_count = block_ids.shape[0]
    clip_of, start_of = frame_tables(clip_lengths, frame_count)
    frames_dev = latent.shape[0]
    first_frame = lax.axis_index("frame") * frames_dev
    guided = guide_features(
        latent, pose_maps, conv_weight, conv_bias, pose_proj, start_of, first_frame
    )
    whole_rows = lax.all_gather(guided, "head", axis=1, tiled=True)
    height = whole_rows.shape[1]
    width_grid = whole_rows.shape[2]
    model_width = whole_rows.shape[3]
    flat_tokens = whole_rows.reshape(-1, model_width)
    qkv_local = w_qkv.reshape(w_qkv.shape[0], -1)
    projected = jnp.dot(
        flat_tokens,
        lax.all_gather(qkv_local, "frame", axis=0, tiled=True),
        preferred_element_type=jnp.float32,
    ).astype(jnp.bfloat16)
    per_frame = height * width_grid
    heads_dev = w_qkv.shape[1]
    head_size = w_qkv.shape[3]
    grouped = projected.reshape(frames_dev, per_frame, heads_dev, 3, head_size)
    rows_total = frames_dev * per_frame
    queries = grouped[:, :, :, 0].reshape(rows_total, heads_dev, head_size)
    keyvals = grouped[:, :, :, 1:3]
    clip_rows = lax.dynamic_slice_in_dim(clip_of, first_frame, frames_dev)
    block_rows = lax.dynamic_slice_in_dim(block_ids, first_frame, frames_dev)
    query_clip = jnp.repeat(clip_rows, per_frame)
    query_block = jnp.repeat(block_rows, per_frame)
    attended = attend_rows(queries, query_clip, query_block, keyvals, clip_of, block_ids)
    by_row = attended.reshape(frames_dev, height, width_grid, heads_dev * head_size)
    by_row = jnp.transpose(by_row, (1, 0, 2, 3)).reshape(
        height, frames_dev * width_grid, heads_dev * head_size
    )
    out_weight = w_out.reshape(heads_dev * head_size, w_out.shape[2])
    rows_here = height // lax.axis_size("head")
    summed_rows = lax.psum_scatter(
        jnp.dot(by_row, out_weight, preferred_element_type=jnp.float32).astype(jnp.bfloat16),
        "head",
        scatter_dimension=0,
        tiled=True,
    ).astype(jnp.float32)
    summed_rows = summed_rows.reshape(rows_here, frames_dev, width_grid, out_weight.shape[1])
    return jnp.transpose(summed_rows, (1, 0, 2, 3)).astype(jnp.bfloat16)


def turn(value, axis, steps):
    count = lax.axis_size(axis)
    return lax.ppermute(value, axis, [(i, (i + steps) % count) for i in range(count)])


def across(value, axis, bits):
    count = lax.axis_size(axis)
    return lax.ppermute(value, axis, [(i, i ^ bits) for i in range(count)])


def hop(lower, upper, axis, s):
    count = lax.axis_size(axis)
    lower = lax.ppermute(lower, axis, [(i, i + 1) for i in range(s - 1, count - 1)])
    upper = lax.ppermute(upper, axis, [(i, i - 1) for i in range(1, count - s + 1)])
    return lower, upper


def after(value, *others):
    def body(*refs):
        del refs

    anywhere = pl.BlockSpec(memory_space=pl.ANY)
    return pl.pallas_call(
        body,
        out_shape=jax.ShapeDtypeStruct(value.shape, value.dtype),
        in_specs=[anywhere] * (1 + len(others)),
        out_specs=anywhere,
        input_output_aliases={0: 0},
        name="after",
    )(value, *others)


def take_rows(weight, half, *ready):
    columns, rows, size = weight.shape
    part = columns // 3

    def body(half_ref, weight_ref, *refs):
        refs[-1][...] = weight_ref[...]

    return pl.pallas_call(
        body,
        out_shape=jax.ShapeDtypeStruct((columns, rows // 2, size), weight.dtype),
        grid_spec=pltpu.PrefetchScalarGridSpec(
            num_scalar_prefetch=1,
            grid=(3,),
            in_specs=[pl.BlockSpec((part, rows // 2, size), lambda h, half: (h, half[0], 0))]
            + [pl.BlockSpec(memory_space=pl.ANY)] * len(ready),
            out_specs=pl.BlockSpec((part, rows // 2, size), lambda h, half: (h, 0, 0)),
        ),
        cost_estimate=cost(0, 2 * weight.size),
        name="take_rows",
    )(half.reshape(1), weight, *ready)


def take_block(weight, row, column, shape, *ready):
    def body(at_ref, weight_ref, *refs):
        refs[-1][...] = weight_ref[...]

    return pl.pallas_call(
        body,
        out_shape=jax.ShapeDtypeStruct(shape, weight.dtype),
        grid_spec=pltpu.PrefetchScalarGridSpec(
            num_scalar_prefetch=1,
            grid=(1,),
            in_specs=[pl.BlockSpec(shape, lambda i, at: (at[0], at[1]))]
            + [pl.BlockSpec(memory_space=pl.ANY)] * len(ready),
            out_specs=pl.BlockSpec(shape, lambda i, at: (0, 0)),
        ),
        cost_estimate=cost(0, 4 * shape[0] * shape[1]),
        name="take_block",
    )(jnp.stack([row, column]), weight, *ready)


def conv_kernel(keep_ref, cols_ref, weight_ref, bias_ref, out_ref, acc_ref):
    step = pl.program_id(0)
    tap_a, tap_b = step // 3, step % 3
    frames, strip_rows, width = out_ref.shape[0], out_ref.shape[1], cols_ref.shape[2]
    pieces = []
    for t in range(frames):
        keep = keep_ref[tap_a * frames + t]
        for r in range(strip_rows):
            rows = cols_ref[tap_a + t, tap_b + 2 * r].astype(F32)
            pieces.append(jnp.where(keep > 0, rows, 0.0))
    lhs = jnp.concatenate(pieces, axis=0).astype(BF16)
    channels = weight_ref.shape[3]
    total = None
    for e in range(3):
        part = lax.dot_general(
            lhs[:, e * channels : (e + 1) * channels],
            weight_ref[0, e],
            (((1,), (1,)), ((), ())),
            preferred_element_type=F32,
        )
        total = part if total is None else total + part

    @pl.when(step == 0)
    def _():
        acc_ref[...] = total

    @pl.when(step > 0)
    def _():
        acc_ref[...] += total

    @pl.when(step == 8)
    def _():
        summed = acc_ref[...] + bias_ref[...]
        feature = summed / (1.0 + jnp.exp(-summed))
        for t in range(frames):
            for r in range(strip_rows):
                at = (t * strip_rows + r) * width
                out_ref[t, r] = feature[at : at + width].astype(BF16)


def pose_feature(earlier, rows_above, pose_maps, conv_weight, conv_bias, start_of, first_frame):
    frames, rows, columns, channels = pose_maps.shape
    out_channels = conv_weight.shape[-1]
    extended = jnp.concatenate([earlier, pose_maps], axis=0)
    extended = jnp.concatenate([rows_above, extended], axis=1)
    pairs = extended.reshape(2 * frames, rows + 1, columns // 2, 2 * channels)
    before = jnp.pad(pairs[:, :, :-1, channels:], ((0, 0), (0, 0), (1, 0), (0, 0)))
    cols = jnp.concatenate([before, pairs], axis=3)
    taps = jnp.transpose(conv_weight, (0, 1, 2, 4, 3)).reshape(9, 3, out_channels, channels)
    frame_ids = first_frame + jnp.arange(frames, dtype=jnp.int32)
    starts_here = lax.dynamic_slice_in_dim(start_of, first_frame, frames)
    keep = (frame_ids[None, :] - 2 + jnp.arange(3, dtype=jnp.int32)[:, None] >= starts_here[None, :])
    keep = keep.astype(jnp.int32).reshape(-1)
    out_shape = (frames, rows // 2, columns // 2, out_channels)
    tokens = frames * (rows // 2) * (columns // 2)
    feature = pl.pallas_call(
        conv_kernel,
        out_shape=jax.ShapeDtypeStruct(out_shape, BF16),
        grid_spec=pltpu.PrefetchScalarGridSpec(
            num_scalar_prefetch=1,
            grid=(9,),
            in_specs=[
                pl.BlockSpec(cols.shape, lambda i, k: (0, 0, 0, 0)),
                pl.BlockSpec((1, 3, out_channels, channels), lambda i, k: (i, 0, 0, 0)),
                pl.BlockSpec((1, out_channels), lambda i, k: (0, 0)),
            ],
            out_specs=pl.BlockSpec(out_shape, lambda i, k: (0, 0, 0, 0)),
            scratch_shapes=[pltpu.VMEM((tokens, out_channels), F32)],
        ),
        compiler_params=pltpu.CompilerParams(vmem_limit_bytes=24 * MIB),
        cost_estimate=cost(tokens * out_channels, 2 * tokens * out_channels),
        name="pose_conv",
    )(keep, cols, taps, conv_bias.reshape(1, -1))
    return feature.reshape(tokens, out_channels)


def project(own, lower, upper, features, pose_proj, order, shards_of, total, frames):
    strips = len(features)
    tokens = own.shape[0]
    channels = pose_proj.shape[0]
    columns, size = shards_of[0][0].shape[0], shards_of[0][0].shape[2]
    depth = sum(array.shape[1] for array in shards_of[0])
    rows = strips * tokens
    per_frame = tokens // frames
    steps = len(shards_of)
    heads = columns // 3
    cuts = [(c, min(c + 4, columns)) for c in range(0, columns, 4)]
    flat = [array for shard in shards_of for array in shard]
    parts = len(shards_of[0])
    slots = min(2, steps)

    def body(order_ref, *refs):
        own_ref, lower_refs, upper_refs = refs[0], refs[1:strips], refs[strips : 2 * strips - 1]
        feature_refs = refs[2 * strips - 1 : 3 * strips - 1]
        proj_ref = refs[3 * strips - 1]
        source_refs = refs[3 * strips : 3 * strips + len(flat)]
        rest = refs[3 * strips + len(flat) :]
        held_ref, guided_ref, sems = rest[-3:]
        if total is None:
            sum_ref = rest[0]
        else:
            total_ref, last_ref, sum_ref = rest[0], rest[1 + PLANE], rest[2 + PLANE]
            message_refs = rest[1 : 1 + PLANE]
        step = pl.program_id(0)

        def fetch(k, n, part):
            low, high = cuts[n]
            length = depth // parts
            at = 0 if parts == 1 else pl.multiple_of((order_ref[steps + 1] ^ part) * length, 128)
            return pltpu.make_async_copy(
                source_refs[k * parts + part].at[low:high],
                held_ref.at[k % slots, low:high, pl.ds(at, length)],
                sems.at[k % slots, n, part],
            )

        def start(k):
            for n in range(len(cuts)):
                for part in range(parts):
                    fetch(k, n, part).start()

        for k in range(steps):

            @pl.when(step == max(k - 1, 0))
            def _(k=k):
                start(k)

        feature = jnp.concatenate([ref[...] for ref in feature_refs], axis=0)
        added = jnp.dot(feature, proj_ref[...], preferred_element_type=F32)
        for s in range(strips):
            latent = own_ref[...].astype(F32)
            if s > 0:
                latent = lower_refs[s - 1][...].astype(F32) + upper_refs[strips - s - 1][...].astype(F32)
            guided = (latent + added[s * tokens : (s + 1) * tokens]).astype(BF16)
            for t in range(frames):
                at = (t * strips + s) * per_frame
                guided_ref[at : at + per_frame] = guided[t * per_frame : (t + 1) * per_frame]

        slot = lax.rem(step, slots)
        for n, (low, high) in enumerate(cuts):
            for k in range(steps):

                @pl.when(step == k)
                def _(k=k, n=n):
                    for part in range(parts):
                        fetch(k, n, part).wait()

            rhs = jnp.concatenate([held_ref[slot, c] for c in range(low, high)], axis=1)
            part = jnp.dot(guided_ref[...], rhs, preferred_element_type=F32)
            lanes = slice(low * size, high * size)
            if total is not None:
                sum_ref[:, lanes] = total_ref[:, lanes] + part
                continue

            @pl.when(step == 0)
            def _(lanes=lanes, part=part):
                sum_ref[:, lanes] = part

            @pl.when(step > 0)
            def _(lanes=lanes, part=part):
                sum_ref[:, lanes] += part

        if total is None:
            return
        last = 3 * (heads - 1) * size
        last_ref[...] = sum_ref[:, last : last + size].astype(BF16)
        for r in range(PLANE):
            head = order_ref[steps] ^ r
            for j in range(3):
                at = pl.multiple_of((3 * head + j) * size, size)
                message_refs[r][j] = sum_ref[:, pl.ds(at, size)].astype(BF16)
            for j in range(1, 3):
                at = last + j * size
                message_refs[r][2 + j] = sum_ref[:, at : at + size].astype(BF16)

    piece = pl.BlockSpec((tokens, depth), lambda i, order: (0, order[i]))
    in_specs = [piece] * (2 * strips - 1)
    in_specs += [pl.BlockSpec((tokens, channels), lambda i, order: (0, 0))] * strips
    in_specs += [pl.BlockSpec((channels, depth), lambda i, order: (0, order[i]))]
    in_specs += [pl.BlockSpec(memory_space=pl.ANY)] * len(flat)
    operands = [own, *lower, *upper, *features, pose_proj, *flat]
    sums = pl.BlockSpec((rows, columns * size), lambda i, order: (0, 0))
    scratch = [
        pltpu.VMEM((slots, columns, depth, size), BF16),
        pltpu.VMEM((rows, depth), BF16),
        pltpu.SemaphoreType.DMA((slots, len(cuts), parts)),
    ]
    if total is None:
        out_shape, out_specs = jax.ShapeDtypeStruct((rows, columns * size), F32), sums
    else:
        assert steps == 1
        in_specs.append(sums)
        operands.append(total)
        message = jax.ShapeDtypeStruct((5, rows, size), BF16)
        out_shape = (message,) * PLANE + (jax.ShapeDtypeStruct((rows, size), BF16),)
        out_specs = (pl.BlockSpec((5, rows, size), lambda i, order: (0, 0, 0)),) * PLANE
        out_specs += (pl.BlockSpec((rows, size), lambda i, order: (0, 0)),)
        scratch = [pltpu.VMEM((rows, columns * size), F32)] + scratch
    return pl.pallas_call(
        body,
        out_shape=out_shape,
        grid_spec=pltpu.PrefetchScalarGridSpec(
            num_scalar_prefetch=1, grid=(steps,), in_specs=in_specs, out_specs=out_specs, scratch_shapes=scratch
        ),
        compiler_params=pltpu.CompilerParams(vmem_limit_bytes=44 * MIB),
        cost_estimate=cost(0, 2 * rows * size),
        name="project",
    )(order, *operands)


def attend(messages, last_query, here, spans, frames, strips):
    rows, size = last_query.shape
    per_frame = rows // frames
    strip = per_frame // strips
    frame_count = PLANE * frames
    window = frame_count - 4 if frame_count > 4 else frame_count
    out_rows = (PLANE + 1) * frames * strip
    scale = size ** (-0.5)

    def body(table_ref, *refs):
        message_refs, last_ref = refs[:PLANE], refs[PLANE]
        out_refs, held_ref = refs[PLANE + 1 : PLANE + 1 + strips], refs[-1]
        here_at = table_ref[3 * frame_count]
        for r in range(PLANE):
            for t in range(frames):
                frame = (here_at ^ r) * frames + t
                for j in range(4):
                    held_ref[frame, j] = message_refs[r][j + 1, t * per_frame : (t + 1) * per_frame]

        def one(query, frame, kind, at):
            begin, low, high = table_ref[3 * frame], table_ref[3 * frame + 1], table_ref[3 * frame + 2]
            keys = held_ref[pl.ds(begin, window), kind].reshape(window * per_frame, size)
            values = held_ref[pl.ds(begin, window), kind + 1].reshape(window * per_frame, size)
            scores = lax.dot_general(query, keys, (((1,), (1,)), ((), ())), preferred_element_type=F32)
            place = lax.broadcasted_iota(jnp.int32, (1, window * per_frame), 1)
            seen = (place >= low * per_frame) & (place < high * per_frame)
            scores = jnp.where(seen, scores * scale, NEG_FILL)
            weights = jnp.exp(scores - jnp.max(scores, axis=1, keepdims=True))
            totals = jnp.sum(weights, axis=1, keepdims=True)
            mixed = jnp.dot(weights.astype(BF16), values, preferred_element_type=F32)
            result = (mixed / totals).astype(BF16)
            for s in range(strips):
                out_refs[s][at : at + strip] = result[s * strip : (s + 1) * strip]

        for r in range(PLANE):
            for t in range(frames):
                query = message_refs[r][0, t * per_frame : (t + 1) * per_frame]
                one(query, (here_at ^ r) * frames + t, 0, (r * frames + t) * strip)
        for t in range(frames):
            query = last_ref[t * per_frame : (t + 1) * per_frame]
            one(query, here_at * frames + t, 2, (PLANE * frames + t) * strip)

    table = jnp.concatenate([spans.reshape(-1), here.reshape(1)]).astype(jnp.int32)
    whole = pl.BlockSpec((5, rows, size), lambda i, table: (0, 0, 0))
    units = (PLANE + 1) * frames
    return pl.pallas_call(
        body,
        out_shape=(jax.ShapeDtypeStruct((out_rows, size), BF16),) * strips,
        grid_spec=pltpu.PrefetchScalarGridSpec(
            num_scalar_prefetch=1,
            grid=(1,),
            in_specs=[whole] * PLANE + [pl.BlockSpec((rows, size), lambda i, table: (0, 0))],
            out_specs=(pl.BlockSpec((out_rows, size), lambda i, table: (0, 0)),) * strips,
            scratch_shapes=[pltpu.VMEM((frame_count, 4, per_frame, size), BF16)],
        ),
        compiler_params=pltpu.CompilerParams(vmem_limit_bytes=40 * MIB),
        cost_estimate=cost(0, 2 * rows * size),
        name="attend",
    )(table, *messages, last_query)


def out_project(gathered, weights, here, group, core, tokens):
    groups, depth, columns = weights[0].shape
    size = gathered[0].shape[2]
    heads = depth // size

    def body(at_ref, *refs):
        weight_refs = refs[PLANE : PLANE + 2]
        out_ref, lhs_ref, sum_ref = refs[-3:]
        step = pl.program_id(0)
        for p in range(PLANE):
            rows = slice(p * tokens, (p + 1) * tokens)
            for q in range(PLANE):
                at = (p ^ q) * tokens
                lhs_ref[rows, q * size : (q + 1) * size] = refs[q][0, at : at + tokens]
            lhs_ref[rows, PLANE * size :] = refs[p][0, PLANE * tokens :]

        here_at, core_at = at_ref[0], at_ref[2]
        for c in range(2):
            found = [
                weight_refs[c][0, pl.ds(pl.multiple_of((here_at ^ q) * size, size), size)] for q in range(PLANE)
            ]
            found.append(weight_refs[c][0, PLANE * size : heads * size])
            part = jnp.dot(lhs_ref[...], jnp.concatenate(found, axis=0), preferred_element_type=F32)
            part = part.astype(BF16).astype(F32)

            @pl.when(step == 0)
            def _(c=c, part=part):
                sum_ref[c] = part

            @pl.when(step > 0)
            def _(c=c, part=part):
                sum_ref[c] += part

        @pl.when(step == groups - 1)
        def _():
            for p in range(PLANE):
                for c in range(2):
                    at = pl.multiple_of((core_at ^ c) * columns, 128)
                    out_ref[p, :, pl.ds(at, columns)] = sum_ref[c, p * tokens : (p + 1) * tokens].astype(BF16)

    in_specs = [pl.BlockSpec((1,) + piece.shape[1:], lambda g, at: (g, 0, 0)) for piece in gathered]
    in_specs += [
        pl.BlockSpec((1, depth, columns), lambda g, at: (lax.rem(at[1] + g, groups), 0, 0))
    ] * 2
    return pl.pallas_call(
        body,
        out_shape=jax.ShapeDtypeStruct((PLANE, tokens, 2 * columns), BF16),
        grid_spec=pltpu.PrefetchScalarGridSpec(
            num_scalar_prefetch=1,
            grid=(groups,),
            in_specs=in_specs,
            out_specs=pl.BlockSpec((PLANE, tokens, 2 * columns), lambda g, at: (0, 0, 0)),
            scratch_shapes=[
                pltpu.VMEM((PLANE * tokens, depth), BF16),
                pltpu.VMEM((2, PLANE * tokens, columns), F32),
            ],
        ),
        compiler_params=pltpu.CompilerParams(vmem_limit_bytes=32 * MIB),
        cost_estimate=cost(0, 4 * PLANE * tokens * columns),
        name="out_project",
    )(jnp.stack([here, group, core]), *gathered, *weights)


def place_columns(pieces, here):
    tokens, columns = pieces[0].shape

    def body(here_ref, *refs):
        for r in range(PLANE):
            at = pl.multiple_of((here_ref[0] ^ r) * columns, 128)
            refs[-1][:, pl.ds(at, columns)] = refs[r][...]

    return pl.pallas_call(
        body,
        out_shape=jax.ShapeDtypeStruct((tokens, PLANE * columns), BF16),
        grid_spec=pltpu.PrefetchScalarGridSpec(
            num_scalar_prefetch=1,
            grid=(1,),
            in_specs=[pl.BlockSpec((tokens, columns), lambda i, here: (0, 0))] * PLANE,
            out_specs=pl.BlockSpec((tokens, PLANE * columns), lambda i, here: (0, 0)),
        ),
        cost_estimate=cost(0, 4 * tokens * PLANE * columns),
        name="place_columns",
    )(here.reshape(1), *pieces)


def shards(
    latent, pose_maps, conv_weight, conv_bias, pose_proj, w_qkv, w_out, clip_lengths, block_ids
):
    frame_count = block_ids.shape[0]
    frames, strip_rows, width_grid, model_width = latent.shape
    heads, head_size = w_qkv.shape[1], w_qkv.shape[3]
    strips = lax.axis_size("head")
    tokens = frames * strip_rows * width_grid
    here = lax.axis_index("frame").astype(jnp.int32)
    group = lax.axis_index("head").astype(jnp.int32)
    core = lax.axis_index("dp").astype(jnp.int32)
    clip_of, start_of = frame_tables(clip_lengths, frame_count)

    earlier = lax.all_gather(pose_maps, "frame")
    earlier = lax.dynamic_index_in_dim(earlier, jnp.maximum(here - 1, 0), keepdims=False)

    weight = jnp.transpose(w_qkv, (1, 2, 0, 3)).reshape(3 * heads, -1, head_size)
    near_pairs = [(2 * f + c, 2 * (f ^ (1 + c)) + c) for f in range(PLANE) for c in range(2)]
    far_pairs = [(2 * f + c, 2 * (f ^ (2 - c)) + c) for f in range(PLANE) for c in range(2)]
    plane_axes = ("frame", "dp")
    near = lax.ppermute(weight, plane_axes, near_pairs)

    own = latent.reshape(tokens, model_width)
    lower, upper = hop(own, own, "head", 1)
    lower, upper = [lower], [upper]
    last_rows = lax.all_gather(pose_maps[:, -1:], ("frame", "head"))
    before = jnp.maximum(here - 1, 0) * strips + jnp.maximum(group - 1, 0)
    above = jnp.maximum(here * strips + group - 1, 0)
    rows_above = jnp.concatenate(
        [lax.dynamic_index_in_dim(last_rows, at, keepdims=False) for at in (before, above)], axis=0
    )
    rows_above = jnp.where(group > 0, rows_above, jnp.zeros_like(rows_above))

    columns = model_width // PLANE // 2
    depth = heads * head_size
    out_half = take_block(w_out.reshape(depth, model_width), jnp.int32(0), 2 * here + core, (depth, columns))

    start_of = after(start_of, lower[0], upper[0], out_half)
    feature = pose_feature(earlier, rows_above, pose_maps, conv_weight, conv_bias, start_of, here * frames)
    for s in range(2, strips):
        below, above = hop(lower[-1], upper[-1], "head", s)
        if s < strips - 1:
            below, above = after(below, feature), after(above, feature)
        lower.append(below)
        upper.append(above)
    features = [feature] + [turn(feature, "head", s) for s in range(1, strips)]
    near = after(near, lower[1], upper[1], *features[1:])
    far = lax.ppermute(take_rows(near, core), plane_axes, far_pairs)
    other_near = across(near, "dp", 1)
    out_half = after(out_half, lower[-1], upper[-1])

    here_near, here_other, here_far = here ^ (1 + core), here ^ (2 - core), here ^ 3
    order = after(jnp.stack([here, here_near, here_other, here, core]), out_half)
    total = project(
        own, lower, upper, features, pose_proj, order, [(weight,), (near,), (other_near,)], None, frames
    )
    far = after(far, total)
    other_far = across(far, "dp", 1)
    order = jnp.stack([here_far, here, core])
    *messages, last_query = project(
        own, lower, upper, features, pose_proj, order, [(far, other_far)], total, frames
    )
    messages = [messages[0]] + [across(messages[r], "frame", r) for r in range(1, PLANE)]

    same_clip = clip_of[:, None] == clip_of[None, :]
    counts = jnp.sum((same_clip & (block_ids[None, :] <= block_ids[:, None])).astype(jnp.int32), axis=1)
    window = frame_count - 4 if frame_count > 4 else frame_count
    begins = jnp.minimum(start_of, frame_count - window)
    spans = jnp.stack([begins, start_of - begins, start_of - begins + counts], axis=1)
    outs = attend(messages, last_query, here, spans, frames, strips)

    out_half = after(lax.all_gather(out_half, "head"), outs[0])
    out_weights = [out_half, across(out_half, "dp", 1)]

    strip_heads = [outs[0]] + [turn(outs[s], "head", -s) for s in range(1, strips)]
    strip_heads = jnp.stack(strip_heads)
    gathered = [strip_heads] + [across(strip_heads, "frame", r) for r in range(1, PLANE)]
    done = out_project(gathered, out_weights, here, group, core, tokens)
    mine = [done[0]] + [across(done[r], "frame", r) for r in range(1, PLANE)]
    return place_columns(mine, here).reshape(latent.shape)


def solution(mesh):
    return jax.shard_map(
        shards if mesh.shape["frame"] == PLANE else plain_shards,
        mesh=mesh,
        in_specs=(
            P(("dp", "frame"), "head", None, None),
            P(("dp", "frame"), "head", None, None),
            P(),
            P(),
            P(),
            P("frame", "head", None, None),
            P("head", None, None),
            P("dp"),
            P("dp"),
        ),
        out_specs=P(("dp", "frame"), "head", None, None),
        check_vma=False,
    )
```

```python
import jax
import jax.numpy as jnp
from jax import lax
from jax.experimental import pallas as pl
from jax.experimental.pallas import tpu as pltpu
from jax.sharding import PartitionSpec as P

NEG_FILL = -1e30
MIB = 1 << 20
F32 = jnp.float32
BF16 = jnp.bfloat16
PLANE = 4


def cost(flops, moved, exps=0):
    return pl.CostEstimate(flops=int(flops), bytes_accessed=int(moved), transcendentals=int(exps))


def shifted(value, axis, steps):
    count = lax.axis_size(axis)
    leading, last = (max(0, -steps), min(count, count - steps))
    return lax.ppermute(value, axis, [(source, source + steps) for source in range(leading, last)])


def frame_tables(clip_lengths, frame_count):
    clip_ends = jnp.cumsum(clip_lengths)
    clip_starts = clip_ends - clip_lengths
    frame_index = jnp.arange(frame_count, dtype=jnp.int32)
    clip_of = jnp.sum((frame_index[:, None] >= clip_ends[None, :]).astype(jnp.int32), axis=1)
    clip_match = clip_of[:, None] == jnp.arange(clip_lengths.shape[0], dtype=jnp.int32)[None, :]
    start_of = jnp.sum(jnp.where(clip_match, clip_starts[None, :], 0), axis=1)
    return (clip_of, start_of)


def guide_features(latent, pose_maps, conv_weight, conv_bias, pose_proj, start_of, first_frame):
    frames_dev = pose_maps.shape[0]
    upper_row = shifted(pose_maps[:, -1:], "head", 1)
    rows_ext = jnp.concatenate([upper_row, pose_maps], axis=1)
    left_column = jnp.zeros(rows_ext.shape[:2] + (1, rows_ext.shape[3]), rows_ext.dtype)
    cols_ext = jnp.concatenate([left_column, rows_ext], axis=2)
    earlier = shifted(cols_ext, "frame", 1)
    extended = jnp.concatenate([earlier, cols_ext], axis=0)
    out_rows = pose_maps.shape[1] // 2
    out_cols = pose_maps.shape[2] // 2
    frame_ids = first_frame + jnp.arange(frames_dev, dtype=jnp.int32)
    starts_here = lax.dynamic_slice_in_dim(start_of, first_frame, frames_dev)
    tap_list = []
    for step_a in range(3):
        keep_mask = (frame_ids - 2 + step_a >= starts_here).astype(pose_maps.dtype)[
            :, None, None, None
        ]
        frames_tap = extended[step_a : step_a + frames_dev] * keep_mask
        for step_b in range(3):
            for step_e in range(3):
                tap_list.append(
                    frames_tap[
                        :,
                        step_b : step_b + 2 * out_rows - 1 : 2,
                        step_e : step_e + 2 * out_cols - 1 : 2,
                    ]
                )
    stacked = jnp.concatenate(tap_list, axis=3)
    kernel = conv_weight.reshape(-1, conv_weight.shape[-1])
    summed = jnp.dot(stacked, kernel, preferred_element_type=jnp.float32) + conv_bias
    feature = jax.nn.silu(summed).astype(jnp.bfloat16)
    guided = latent.astype(jnp.float32) + jnp.dot(
        feature, pose_proj, preferred_element_type=jnp.float32
    )
    return guided.astype(jnp.bfloat16)


def attend_rows(queries, query_clip, query_block, keyvals, clip_of, block_ids):
    heads_dev = queries.shape[1]
    rows_query = queries.shape[0]
    head_size = queries.shape[2]
    score_scale = head_size ** (-0.5)
    start_carry = (
        jnp.full((heads_dev, rows_query), NEG_FILL, jnp.float32),
        jnp.zeros((heads_dev, rows_query), jnp.float32),
        jnp.zeros((heads_dev, rows_query, head_size), jnp.float32),
    )

    def one_frame(running, frame_item):
        frame_kv, frame_id = frame_item
        key_clip = clip_of[frame_id]
        key_block = block_ids[frame_id]
        visible = (query_clip == key_clip) & (key_block <= query_block)
        run_max, run_total, run_acc = running
        scores = (
            jnp.einsum(
                "qhd,khd->hqk", queries, frame_kv[:, :, 0], preferred_element_type=jnp.float32
            )
            * score_scale
        )
        scores = jnp.where(visible[None, :, None], scores, NEG_FILL)
        new_max = jnp.maximum(run_max, jnp.max(scores, axis=2))
        factor = jnp.exp(run_max - new_max)
        weights = jnp.where(visible[None, :, None], jnp.exp(scores - new_max[:, :, None]), 0.0)
        new_total = run_total * factor + jnp.sum(weights, axis=2)
        new_acc = run_acc * factor[:, :, None] + jnp.einsum(
            "hqk,khd->hqd",
            weights.astype(jnp.bfloat16),
            frame_kv[:, :, 1],
            preferred_element_type=jnp.float32,
        )
        running = (new_max, new_total, new_acc)
        return (running, None)

    running = start_carry
    shard_piece = lax.all_gather(keyvals, "frame", axis=0, tiled=True)
    piece_frames = shard_piece.shape[0]
    frame_list = jnp.arange(piece_frames, dtype=jnp.int32)
    running, unused = lax.scan(one_frame, running, (shard_piece, frame_list))
    run_max, run_total, run_acc = running
    normalized = run_acc / run_total[:, :, None]
    return jnp.transpose(normalized, (1, 0, 2)).astype(jnp.bfloat16)


def plain_shards(
    latent, pose_maps, conv_weight, conv_bias, pose_proj, w_qkv, w_out, clip_lengths, block_ids
):
    frame_count = block_ids.shape[0]
    clip_of, start_of = frame_tables(clip_lengths, frame_count)
    frames_dev = latent.shape[0]
    first_frame = lax.axis_index("frame") * frames_dev
    guided = guide_features(
        latent, pose_maps, conv_weight, conv_bias, pose_proj, start_of, first_frame
    )
    whole_rows = lax.all_gather(guided, "head", axis=1, tiled=True)
    height = whole_rows.shape[1]
    width_grid = whole_rows.shape[2]
    model_width = whole_rows.shape[3]
    flat_tokens = whole_rows.reshape(-1, model_width)
    qkv_local = w_qkv.reshape(w_qkv.shape[0], -1)
    projected = jnp.dot(
        flat_tokens,
        lax.all_gather(qkv_local, "frame", axis=0, tiled=True),
        preferred_element_type=jnp.float32,
    ).astype(jnp.bfloat16)
    per_frame = height * width_grid
    heads_dev = w_qkv.shape[1]
    head_size = w_qkv.shape[3]
    grouped = projected.reshape(frames_dev, per_frame, heads_dev, 3, head_size)
    rows_total = frames_dev * per_frame
    queries = grouped[:, :, :, 0].reshape(rows_total, heads_dev, head_size)
    keyvals = grouped[:, :, :, 1:3]
    clip_rows = lax.dynamic_slice_in_dim(clip_of, first_frame, frames_dev)
    block_rows = lax.dynamic_slice_in_dim(block_ids, first_frame, frames_dev)
    query_clip = jnp.repeat(clip_rows, per_frame)
    query_block = jnp.repeat(block_rows, per_frame)
    attended = attend_rows(queries, query_clip, query_block, keyvals, clip_of, block_ids)
    by_row = attended.reshape(frames_dev, height, width_grid, heads_dev * head_size)
    by_row = jnp.transpose(by_row, (1, 0, 2, 3)).reshape(
        height, frames_dev * width_grid, heads_dev * head_size
    )
    out_weight = w_out.reshape(heads_dev * head_size, w_out.shape[2])
    rows_here = height // lax.axis_size("head")
    summed_rows = lax.psum_scatter(
        jnp.dot(by_row, out_weight, preferred_element_type=jnp.float32).astype(jnp.bfloat16),
        "head",
        scatter_dimension=0,
        tiled=True,
    ).astype(jnp.float32)
    summed_rows = summed_rows.reshape(rows_here, frames_dev, width_grid, out_weight.shape[1])
    return jnp.transpose(summed_rows, (1, 0, 2, 3)).astype(jnp.bfloat16)


def turn(value, axis, steps):
    count = lax.axis_size(axis)
    return lax.ppermute(value, axis, [(i, (i + steps) % count) for i in range(count)])


def across(value, axis, bits):
    count = lax.axis_size(axis)
    return lax.ppermute(value, axis, [(i, i ^ bits) for i in range(count)])


def hop(lower, upper, axis, s):
    count = lax.axis_size(axis)
    lower = lax.ppermute(lower, axis, [(i, i + 1) for i in range(s - 1, count - 1)])
    upper = lax.ppermute(upper, axis, [(i, i - 1) for i in range(1, count - s + 1)])
    return lower, upper


def after(value, *others):
    def body(*refs):
        del refs

    anywhere = pl.BlockSpec(memory_space=pl.ANY)
    return pl.pallas_call(
        body,
        out_shape=jax.ShapeDtypeStruct(value.shape, value.dtype),
        in_specs=[anywhere] * (1 + len(others)),
        out_specs=anywhere,
        input_output_aliases={0: 0},
        name="after",
    )(value, *others)


def take_rows(weight, half):
    columns, rows, size = weight.shape
    pieces = 5
    part = columns // pieces

    def body(half_ref, weight_ref, out_ref, sems):
        at = pl.multiple_of(half_ref[0] * (rows // 2), rows // 2)
        copies = [
            pltpu.make_async_copy(
                weight_ref.at[n * part : (n + 1) * part, pl.ds(at, rows // 2)],
                out_ref.at[n * part : (n + 1) * part],
                sems.at[n],
            )
            for n in range(pieces)
        ]
        for copy in copies:
            copy.start()
        for copy in copies:
            copy.wait()

    return pl.pallas_call(
        body,
        out_shape=jax.ShapeDtypeStruct((columns, rows // 2, size), weight.dtype),
        in_specs=[pl.BlockSpec(memory_space=pltpu.SMEM), pl.BlockSpec(memory_space=pl.ANY)],
        out_specs=pl.BlockSpec(memory_space=pl.ANY),
        scratch_shapes=[pltpu.SemaphoreType.DMA((pieces,))],
        cost_estimate=cost(0, 2 * weight.size),
        name="take_rows",
    )(half.reshape(1), weight)


def take_block(weight, row, column, shape, *ready):
    def body(at_ref, weight_ref, *refs):
        refs[-1][...] = weight_ref[...]

    return pl.pallas_call(
        body,
        out_shape=jax.ShapeDtypeStruct(shape, weight.dtype),
        grid_spec=pltpu.PrefetchScalarGridSpec(
            num_scalar_prefetch=1,
            grid=(1,),
            in_specs=[pl.BlockSpec(shape, lambda i, at: (at[0], at[1]))]
            + [pl.BlockSpec(memory_space=pl.ANY)] * len(ready),
            out_specs=pl.BlockSpec(shape, lambda i, at: (0, 0)),
        ),
        cost_estimate=cost(0, 4 * shape[0] * shape[1]),
        name="take_block",
    )(jnp.stack([row, column]), weight, *ready)


def conv_kernel(keep_ref, cols_ref, weight_ref, bias_ref, out_ref, acc_ref):
    step = pl.program_id(0)
    tap_a, tap_b = step // 3, step % 3
    frames, strip_rows, width = out_ref.shape[0], out_ref.shape[1], cols_ref.shape[2]
    pieces = []
    for t in range(frames):
        keep = keep_ref[tap_a * frames + t]
        for r in range(strip_rows):
            rows = cols_ref[tap_a + t, tap_b + 2 * r].astype(F32)
            pieces.append(jnp.where(keep > 0, rows, 0.0))
    lhs = jnp.concatenate(pieces, axis=0).astype(BF16)
    channels = weight_ref.shape[3]
    total = None
    for e in range(3):
        part = lax.dot_general(
            lhs[:, e * channels : (e + 1) * channels],
            weight_ref[0, e],
            (((1,), (1,)), ((), ())),
            preferred_element_type=F32,
        )
        total = part if total is None else total + part

    @pl.when(step == 0)
    def _():
        acc_ref[...] = total

    @pl.when(step > 0)
    def _():
        acc_ref[...] += total

    @pl.when(step == 8)
    def _():
        summed = acc_ref[...] + bias_ref[...]
        feature = summed / (1.0 + jnp.exp(-summed))
        for t in range(frames):
            for r in range(strip_rows):
                at = (t * strip_rows + r) * width
                out_ref[t, r] = feature[at : at + width].astype(BF16)


def pose_feature(extended, conv_weight, conv_bias, start_of, first_frame):
    frames, rows, columns, channels = extended.shape
    frames, rows = frames // 2, rows - 1
    out_channels = conv_weight.shape[-1]
    pairs = extended.reshape(2 * frames, rows + 1, columns // 2, 2 * channels)
    before = jnp.pad(pairs[:, :, :-1, channels:], ((0, 0), (0, 0), (1, 0), (0, 0)))
    cols = jnp.concatenate([before, pairs], axis=3)
    taps = jnp.transpose(conv_weight, (0, 1, 2, 4, 3)).reshape(9, 3, out_channels, channels)
    frame_ids = first_frame + jnp.arange(frames, dtype=jnp.int32)
    starts_here = lax.dynamic_slice_in_dim(start_of, first_frame, frames)
    keep = (frame_ids[None, :] - 2 + jnp.arange(3, dtype=jnp.int32)[:, None] >= starts_here[None, :])
    keep = keep.astype(jnp.int32).reshape(-1)
    out_shape = (frames, rows // 2, columns // 2, out_channels)
    tokens = frames * (rows // 2) * (columns // 2)
    feature = pl.pallas_call(
        conv_kernel,
        out_shape=jax.ShapeDtypeStruct(out_shape, BF16),
        grid_spec=pltpu.PrefetchScalarGridSpec(
            num_scalar_prefetch=1,
            grid=(9,),
            in_specs=[
                pl.BlockSpec(cols.shape, lambda i, k: (0, 0, 0, 0)),
                pl.BlockSpec((1, 3, out_channels, channels), lambda i, k: (i, 0, 0, 0)),
                pl.BlockSpec((1, out_channels), lambda i, k: (0, 0)),
            ],
            out_specs=pl.BlockSpec(out_shape, lambda i, k: (0, 0, 0, 0)),
            scratch_shapes=[pltpu.VMEM((tokens, out_channels), F32)],
        ),
        compiler_params=pltpu.CompilerParams(vmem_limit_bytes=24 * MIB),
        cost_estimate=cost(tokens * out_channels, 2 * tokens * out_channels),
        name="pose_conv",
    )(keep, cols, taps, conv_bias.reshape(1, -1))
    return feature.reshape(tokens, out_channels)


def project(own, lower, upper, features, pose_proj, order, shards_of, total, frames):
    strips = len(features)
    tokens = own.shape[0]
    channels = pose_proj.shape[0]
    columns, size = shards_of[0][0].shape[0], shards_of[0][0].shape[2]
    depth = sum(array.shape[1] for array in shards_of[0])
    rows = strips * tokens
    per_frame = tokens // frames
    steps = len(shards_of)
    heads = columns // 3
    cuts = [(c, min(c + 4, columns)) for c in range(0, columns, 4)]
    flat = [array for shard in shards_of for array in shard]
    parts = len(shards_of[0])
    slots = min(2, steps)

    def body(order_ref, *refs):
        own_ref, lower_refs, upper_refs = refs[0], refs[1:strips], refs[strips : 2 * strips - 1]
        feature_refs = refs[2 * strips - 1 : 3 * strips - 1]
        proj_ref = refs[3 * strips - 1]
        source_refs = refs[3 * strips : 3 * strips + len(flat)]
        rest = refs[3 * strips + len(flat) :]
        held_ref, guided_ref, sems = rest[-3:]
        if total is None:
            sum_ref = rest[0]
        else:
            total_ref, last_ref, sum_ref = rest[0], rest[1 + PLANE], rest[2 + PLANE]
            message_refs = rest[1 : 1 + PLANE]
        step = pl.program_id(0)

        def fetch(k, n, part):
            low, high = cuts[n]
            length = depth // parts
            at = 0 if parts == 1 else pl.multiple_of((order_ref[steps + 1] ^ part) * length, 128)
            return pltpu.make_async_copy(
                source_refs[k * parts + part].at[low:high],
                held_ref.at[k % slots, low:high, pl.ds(at, length)],
                sems.at[k % slots, n, part],
            )

        def start(k):
            for n in range(len(cuts)):
                for part in range(parts):
                    fetch(k, n, part).start()

        for k in range(steps):

            @pl.when(step == max(k - 1, 0))
            def _(k=k):
                start(k)

        feature = jnp.concatenate([ref[...] for ref in feature_refs], axis=0)
        added = jnp.dot(feature, proj_ref[...], preferred_element_type=F32)
        for s in range(strips):
            latent = own_ref[...].astype(F32)
            if s > 0:
                latent = lower_refs[s - 1][...].astype(F32) + upper_refs[strips - s - 1][...].astype(F32)
            guided = (latent + added[s * tokens : (s + 1) * tokens]).astype(BF16)
            for t in range(frames):
                at = (t * strips + s) * per_frame
                guided_ref[at : at + per_frame] = guided[t * per_frame : (t + 1) * per_frame]

        slot = lax.rem(step, slots)
        for n, (low, high) in enumerate(cuts):
            for k in range(steps):

                @pl.when(step == k)
                def _(k=k, n=n):
                    for part in range(parts):
                        fetch(k, n, part).wait()

            rhs = jnp.concatenate([held_ref[slot, c] for c in range(low, high)], axis=1)
            part = jnp.dot(guided_ref[...], rhs, preferred_element_type=F32)
            lanes = slice(low * size, high * size)
            if total is not None:
                sum_ref[:, lanes] = total_ref[:, lanes] + part
                continue

            @pl.when(step == 0)
            def _(lanes=lanes, part=part):
                sum_ref[:, lanes] = part

            @pl.when(step > 0)
            def _(lanes=lanes, part=part):
                sum_ref[:, lanes] += part

        if total is None:
            return
        last = 3 * (heads - 1) * size
        last_ref[...] = sum_ref[:, last : last + size].astype(BF16)
        for r in range(PLANE):
            head = order_ref[steps] ^ r
            for j in range(3):
                at = pl.multiple_of((3 * head + j) * size, size)
                message_refs[r][j] = sum_ref[:, pl.ds(at, size)].astype(BF16)
            for j in range(1, 3):
                at = last + j * size
                message_refs[r][2 + j] = sum_ref[:, at : at + size].astype(BF16)

    piece = pl.BlockSpec((tokens, depth), lambda i, order: (0, order[i]))
    in_specs = [piece] * (2 * strips - 1)
    in_specs += [pl.BlockSpec((tokens, channels), lambda i, order: (0, 0))] * strips
    in_specs += [pl.BlockSpec((channels, depth), lambda i, order: (0, order[i]))]
    in_specs += [pl.BlockSpec(memory_space=pl.ANY)] * len(flat)
    operands = [own, *lower, *upper, *features, pose_proj, *flat]
    sums = pl.BlockSpec((rows, columns * size), lambda i, order: (0, 0))
    scratch = [
        pltpu.VMEM((slots, columns, depth, size), BF16),
        pltpu.VMEM((rows, depth), BF16),
        pltpu.SemaphoreType.DMA((slots, len(cuts), parts)),
    ]
    if total is None:
        out_shape, out_specs = jax.ShapeDtypeStruct((rows, columns * size), F32), sums
    else:
        assert steps == 1
        in_specs.append(sums)
        operands.append(total)
        message = jax.ShapeDtypeStruct((5, rows, size), BF16)
        out_shape = (message,) * PLANE + (jax.ShapeDtypeStruct((rows, size), BF16),)
        out_specs = (pl.BlockSpec((5, rows, size), lambda i, order: (0, 0, 0)),) * PLANE
        out_specs += (pl.BlockSpec((rows, size), lambda i, order: (0, 0)),)
        scratch = [pltpu.VMEM((rows, columns * size), F32)] + scratch
    return pl.pallas_call(
        body,
        out_shape=out_shape,
        grid_spec=pltpu.PrefetchScalarGridSpec(
            num_scalar_prefetch=1, grid=(steps,), in_specs=in_specs, out_specs=out_specs, scratch_shapes=scratch
        ),
        compiler_params=pltpu.CompilerParams(vmem_limit_bytes=56 * MIB),
        cost_estimate=cost(0, 2 * rows * size),
        name="project",
    )(order, *operands)


def attend(messages, last_query, here, spans, frames, strips):
    rows, size = last_query.shape
    per_frame = rows // frames
    strip = per_frame // strips
    frame_count = PLANE * frames
    window = frame_count - 4 if frame_count > 4 else frame_count
    out_rows = (PLANE + 1) * frames * strip
    scale = size ** (-0.5)

    def body(table_ref, *refs):
        message_refs, last_ref = refs[:PLANE], refs[PLANE]
        out_refs, held_ref = refs[PLANE + 1 : PLANE + 1 + strips], refs[-1]
        here_at = table_ref[3 * frame_count]
        for r in range(PLANE):
            for t in range(frames):
                frame = (here_at ^ r) * frames + t
                for j in range(4):
                    held_ref[frame, j] = message_refs[r][j + 1, t * per_frame : (t + 1) * per_frame]

        def one(query, frame, kind, at):
            begin, low, high = table_ref[3 * frame], table_ref[3 * frame + 1], table_ref[3 * frame + 2]
            keys = held_ref[pl.ds(begin, window), kind].reshape(window * per_frame, size)
            values = held_ref[pl.ds(begin, window), kind + 1].reshape(window * per_frame, size)
            scores = lax.dot_general(query, keys, (((1,), (1,)), ((), ())), preferred_element_type=F32)
            place = lax.broadcasted_iota(jnp.int32, (1, window * per_frame), 1)
            seen = (place >= low * per_frame) & (place < high * per_frame)
            scores = jnp.where(seen, scores * scale, NEG_FILL)
            weights = jnp.exp(scores - jnp.max(scores, axis=1, keepdims=True))
            totals = jnp.sum(weights, axis=1, keepdims=True)
            mixed = jnp.dot(weights.astype(BF16), values, preferred_element_type=F32)
            result = (mixed / totals).astype(BF16)
            for s in range(strips):
                out_refs[s][at : at + strip] = result[s * strip : (s + 1) * strip]

        for r in range(PLANE):
            for t in range(frames):
                query = message_refs[r][0, t * per_frame : (t + 1) * per_frame]
                one(query, (here_at ^ r) * frames + t, 0, (r * frames + t) * strip)
        for t in range(frames):
            query = last_ref[t * per_frame : (t + 1) * per_frame]
            one(query, here_at * frames + t, 2, (PLANE * frames + t) * strip)

    table = jnp.concatenate([spans.reshape(-1), here.reshape(1)]).astype(jnp.int32)
    whole = pl.BlockSpec((5, rows, size), lambda i, table: (0, 0, 0))
    units = (PLANE + 1) * frames
    return pl.pallas_call(
        body,
        out_shape=(jax.ShapeDtypeStruct((out_rows, size), BF16),) * strips,
        grid_spec=pltpu.PrefetchScalarGridSpec(
            num_scalar_prefetch=1,
            grid=(1,),
            in_specs=[whole] * PLANE + [pl.BlockSpec((rows, size), lambda i, table: (0, 0))],
            out_specs=(pl.BlockSpec((out_rows, size), lambda i, table: (0, 0)),) * strips,
            scratch_shapes=[pltpu.VMEM((frame_count, 4, per_frame, size), BF16)],
        ),
        compiler_params=pltpu.CompilerParams(vmem_limit_bytes=40 * MIB),
        cost_estimate=cost(0, 2 * rows * size),
        name="attend",
    )(table, *messages, last_query)


def out_project(gathered, weights, here, group, core, tokens):
    groups, depth, columns = weights[0].shape
    size = gathered[0][0].shape[2]
    heads = depth // size

    def body(at_ref, *refs):
        weight_refs = refs[2 * PLANE : 2 * PLANE + 2]
        out_refs, lhs_ref, sum_ref = refs[2 * PLANE + 2 : -2], refs[-2], refs[-1]
        step = pl.program_id(0)
        def assemble(found):
            for p in range(PLANE):
                rows = slice(p * tokens, (p + 1) * tokens)
                for q in range(PLANE):
                    at = (p ^ q) * tokens
                    lhs_ref[rows, q * size : (q + 1) * size] = found[q][0, at : at + tokens]
                lhs_ref[rows, PLANE * size :] = found[p][0, PLANE * tokens :]

        pl.when(step == 0)(lambda: assemble(refs[0 : 2 * PLANE : 2]))
        pl.when(step > 0)(lambda: assemble(refs[1 : 2 * PLANE : 2]))

        here_at, core_at = at_ref[0], at_ref[2]
        for c in range(2):
            found = [
                weight_refs[c][0, pl.ds(pl.multiple_of((here_at ^ q) * size, size), size)] for q in range(PLANE)
            ]
            found.append(weight_refs[c][0, PLANE * size : heads * size])
            part = jnp.dot(lhs_ref[...], jnp.concatenate(found, axis=0), preferred_element_type=F32)
            part = part.astype(BF16).astype(F32)

            @pl.when(step == 0)
            def _(c=c, part=part):
                sum_ref[c] = part

            @pl.when(step > 0)
            def _(c=c, part=part):
                sum_ref[c] += part

        @pl.when(step == groups - 1)
        def _():
            for p in range(PLANE):
                for c in range(2):
                    at = pl.multiple_of((core_at ^ c) * columns, 128)
                    out_refs[p][:, pl.ds(at, columns)] = sum_ref[c, p * tokens : (p + 1) * tokens].astype(BF16)

    block = (1,) + gathered[0][0].shape[1:]
    in_specs = [
        pl.BlockSpec(block, lambda g, at: (0, 0, 0)),
        pl.BlockSpec(block, lambda g, at: (jnp.maximum(g - 1, 0), 0, 0)),
    ] * PLANE
    in_specs += [
        pl.BlockSpec((1, depth, columns), lambda g, at: (lax.rem(at[1] + g, groups), 0, 0))
    ] * 2
    return pl.pallas_call(
        body,
        out_shape=(jax.ShapeDtypeStruct((tokens, 2 * columns), BF16),) * PLANE,
        grid_spec=pltpu.PrefetchScalarGridSpec(
            num_scalar_prefetch=1,
            grid=(groups,),
            in_specs=in_specs,
            out_specs=(pl.BlockSpec((tokens, 2 * columns), lambda g, at: (0, 0)),) * PLANE,
            scratch_shapes=[
                pltpu.VMEM((PLANE * tokens, depth), BF16),
                pltpu.VMEM((2, PLANE * tokens, columns), F32),
            ],
        ),
        compiler_params=pltpu.CompilerParams(vmem_limit_bytes=56 * MIB),
        cost_estimate=cost(0, 4 * PLANE * tokens * columns),
        name="out_project",
    )(jnp.stack([here, group, core]), *[part for parts in gathered for part in parts], *weights)


def place_columns(pieces, here):
    tokens, columns = pieces[0].shape

    def body(here_ref, *refs):
        for r in range(PLANE):
            at = pl.multiple_of((here_ref[0] ^ r) * columns, 128)
            refs[-1][:, pl.ds(at, columns)] = refs[r][...]

    return pl.pallas_call(
        body,
        out_shape=jax.ShapeDtypeStruct((tokens, PLANE * columns), BF16),
        grid_spec=pltpu.PrefetchScalarGridSpec(
            num_scalar_prefetch=1,
            grid=(1,),
            in_specs=[pl.BlockSpec((tokens, columns), lambda i, here: (0, 0))] * PLANE,
            out_specs=pl.BlockSpec((tokens, PLANE * columns), lambda i, here: (0, 0)),
        ),
        cost_estimate=cost(0, 4 * tokens * PLANE * columns),
        name="place_columns",
    )(here.reshape(1), *pieces)


def shards(
    latent, pose_maps, conv_weight, conv_bias, pose_proj, w_qkv, w_out, clip_lengths, block_ids
):
    frame_count = block_ids.shape[0]
    frames, strip_rows, width_grid, model_width = latent.shape
    heads, head_size = w_qkv.shape[1], w_qkv.shape[3]
    strips = lax.axis_size("head")
    tokens = frames * strip_rows * width_grid
    here = lax.axis_index("frame").astype(jnp.int32)
    group = lax.axis_index("head").astype(jnp.int32)
    core = lax.axis_index("dp").astype(jnp.int32)
    clip_of, start_of = frame_tables(clip_lengths, frame_count)

    weight = jnp.transpose(w_qkv, (1, 2, 0, 3)).reshape(3 * heads, -1, head_size)
    near_pairs = [(2 * f + c, 2 * (f ^ (1 + c)) + c) for f in range(PLANE) for c in range(2)]
    far_pairs = [(2 * f + c, 2 * (f ^ (2 - c)) + c) for f in range(PLANE) for c in range(2)]
    plane_axes = ("frame", "dp")
    near = lax.ppermute(weight, plane_axes, near_pairs)

    own = latent.reshape(tokens, model_width)
    lower, upper = hop(own, own, "head", 1)
    lower, upper = [lower], [upper]
    rows_ext = jnp.concatenate([shifted(pose_maps[:, -1:], "head", 1), pose_maps], axis=1)
    earlier = shifted(rows_ext, "frame", 1)
    extended = jnp.concatenate([earlier, rows_ext], axis=0)
    lower[0], upper[0] = after(lower[0], rows_ext), after(upper[0], rows_ext)

    columns = model_width // PLANE // 2
    depth = heads * head_size
    out_half = take_block(w_out.reshape(depth, model_width), jnp.int32(0), 2 * here + core, (depth, columns))

    for s in range(2, strips):
        below, above = hop(lower[-1], upper[-1], "head", s)
        lower.append(below)
        upper.append(above)
    near = after(near, lower[1], upper[1])
    passed = after(take_rows(near, core), earlier)
    start_of = after(start_of, passed, out_half)
    feature = pose_feature(extended, conv_weight, conv_bias, start_of, here * frames)
    features = [feature] + [turn(feature, "head", s) for s in range(1, strips)]
    far = lax.ppermute(passed, plane_axes, far_pairs)
    other_near = across(near, "dp", 1)
    out_half = after(out_half, lower[-1], upper[-1])

    here_near, here_other, here_far = here ^ (1 + core), here ^ (2 - core), here ^ 3
    order = after(jnp.stack([here, here_near, here_other, here, core]), out_half)
    total = project(
        own, lower, upper, features, pose_proj, order, [(weight,), (near,), (other_near,)], None, frames
    )
    far = after(far, total)
    other_far = across(far, "dp", 1)
    order = jnp.stack([here_far, here, core])
    *messages, last_query = project(
        own, lower, upper, features, pose_proj, order, [(far, other_far)], total, frames
    )
    messages = [messages[0]] + [across(messages[r], "frame", r) for r in range(1, PLANE)]

    same_clip = clip_of[:, None] == clip_of[None, :]
    counts = jnp.sum((same_clip & (block_ids[None, :] <= block_ids[:, None])).astype(jnp.int32), axis=1)
    window = frame_count - 4 if frame_count > 4 else frame_count
    begins = jnp.minimum(start_of, frame_count - window)
    spans = jnp.stack([begins, start_of - begins, start_of - begins + counts], axis=1)
    outs = attend(messages, last_query, here, spans, frames, strips)

    out_half = after(lax.all_gather(out_half, "head"), outs[0])
    out_weights = [out_half, across(out_half, "dp", 1)]

    strip_heads = [outs[0]] + [turn(outs[s], "head", -s) for s in range(1, strips)]
    mine = [strip_heads[0][None], jnp.stack(strip_heads[1:])]
    gathered = [mine] + [[across(part, "frame", r) for part in mine] for r in range(1, PLANE)]
    done = out_project(gathered, out_weights, here, group, core, tokens)
    mine = [done[0]] + [across(done[r], "frame", r) for r in range(1, PLANE)]
    return place_columns(mine, here).reshape(latent.shape)


def solution(mesh):
    return jax.shard_map(
        shards if mesh.shape["frame"] == PLANE else plain_shards,
        mesh=mesh,
        in_specs=(
            P(("dp", "frame"), "head", None, None),
            P(("dp", "frame"), "head", None, None),
            P(),
            P(),
            P(),
            P("frame", "head", None, None),
            P("head", None, None),
            P("dp"),
            P("dp"),
        ),
        out_specs=P(("dp", "frame"), "head", None, None),
        check_vma=False,
    )
```

```python
import jax
import jax.numpy as jnp
from jax import lax
from jax.experimental import pallas as pl
from jax.experimental.pallas import tpu as pltpu
from jax.sharding import PartitionSpec as P

NEG_FILL = -1e30
MIB = 1 << 20
F32 = jnp.float32
BF16 = jnp.bfloat16
PLANE = 4
FIRST_COLUMNS = 8


def cost(flops, moved, exps=0):
    return pl.CostEstimate(flops=int(flops), bytes_accessed=int(moved), transcendentals=int(exps))


def shifted(value, axis, steps):
    count = lax.axis_size(axis)
    leading, last = (max(0, -steps), min(count, count - steps))
    return lax.ppermute(value, axis, [(source, source + steps) for source in range(leading, last)])


def frame_tables(clip_lengths, frame_count):
    clip_ends = jnp.cumsum(clip_lengths)
    clip_starts = clip_ends - clip_lengths
    frame_index = jnp.arange(frame_count, dtype=jnp.int32)
    clip_of = jnp.sum((frame_index[:, None] >= clip_ends[None, :]).astype(jnp.int32), axis=1)
    clip_match = clip_of[:, None] == jnp.arange(clip_lengths.shape[0], dtype=jnp.int32)[None, :]
    start_of = jnp.sum(jnp.where(clip_match, clip_starts[None, :], 0), axis=1)
    return (clip_of, start_of)


def guide_features(latent, pose_maps, conv_weight, conv_bias, pose_proj, start_of, first_frame):
    frames_dev = pose_maps.shape[0]
    upper_row = shifted(pose_maps[:, -1:], "head", 1)
    rows_ext = jnp.concatenate([upper_row, pose_maps], axis=1)
    left_column = jnp.zeros(rows_ext.shape[:2] + (1, rows_ext.shape[3]), rows_ext.dtype)
    cols_ext = jnp.concatenate([left_column, rows_ext], axis=2)
    earlier = shifted(cols_ext, "frame", 1)
    extended = jnp.concatenate([earlier, cols_ext], axis=0)
    out_rows = pose_maps.shape[1] // 2
    out_cols = pose_maps.shape[2] // 2
    frame_ids = first_frame + jnp.arange(frames_dev, dtype=jnp.int32)
    starts_here = lax.dynamic_slice_in_dim(start_of, first_frame, frames_dev)
    tap_list = []
    for step_a in range(3):
        keep_mask = (frame_ids - 2 + step_a >= starts_here).astype(pose_maps.dtype)[
            :, None, None, None
        ]
        frames_tap = extended[step_a : step_a + frames_dev] * keep_mask
        for step_b in range(3):
            for step_e in range(3):
                tap_list.append(
                    frames_tap[
                        :,
                        step_b : step_b + 2 * out_rows - 1 : 2,
                        step_e : step_e + 2 * out_cols - 1 : 2,
                    ]
                )
    stacked = jnp.concatenate(tap_list, axis=3)
    kernel = conv_weight.reshape(-1, conv_weight.shape[-1])
    summed = jnp.dot(stacked, kernel, preferred_element_type=jnp.float32) + conv_bias
    feature = jax.nn.silu(summed).astype(jnp.bfloat16)
    guided = latent.astype(jnp.float32) + jnp.dot(
        feature, pose_proj, preferred_element_type=jnp.float32
    )
    return guided.astype(jnp.bfloat16)


def attend_rows(queries, query_clip, query_block, keyvals, clip_of, block_ids):
    heads_dev = queries.shape[1]
    rows_query = queries.shape[0]
    head_size = queries.shape[2]
    score_scale = head_size ** (-0.5)
    start_carry = (
        jnp.full((heads_dev, rows_query), NEG_FILL, jnp.float32),
        jnp.zeros((heads_dev, rows_query), jnp.float32),
        jnp.zeros((heads_dev, rows_query, head_size), jnp.float32),
    )

    def one_frame(running, frame_item):
        frame_kv, frame_id = frame_item
        key_clip = clip_of[frame_id]
        key_block = block_ids[frame_id]
        visible = (query_clip == key_clip) & (key_block <= query_block)
        run_max, run_total, run_acc = running
        scores = (
            jnp.einsum(
                "qhd,khd->hqk", queries, frame_kv[:, :, 0], preferred_element_type=jnp.float32
            )
            * score_scale
        )
        scores = jnp.where(visible[None, :, None], scores, NEG_FILL)
        new_max = jnp.maximum(run_max, jnp.max(scores, axis=2))
        factor = jnp.exp(run_max - new_max)
        weights = jnp.where(visible[None, :, None], jnp.exp(scores - new_max[:, :, None]), 0.0)
        new_total = run_total * factor + jnp.sum(weights, axis=2)
        new_acc = run_acc * factor[:, :, None] + jnp.einsum(
            "hqk,khd->hqd",
            weights.astype(jnp.bfloat16),
            frame_kv[:, :, 1],
            preferred_element_type=jnp.float32,
        )
        running = (new_max, new_total, new_acc)
        return (running, None)

    running = start_carry
    shard_piece = lax.all_gather(keyvals, "frame", axis=0, tiled=True)
    piece_frames = shard_piece.shape[0]
    frame_list = jnp.arange(piece_frames, dtype=jnp.int32)
    running, unused = lax.scan(one_frame, running, (shard_piece, frame_list))
    run_max, run_total, run_acc = running
    normalized = run_acc / run_total[:, :, None]
    return jnp.transpose(normalized, (1, 0, 2)).astype(jnp.bfloat16)


def plain_shards(
    latent, pose_maps, conv_weight, conv_bias, pose_proj, w_qkv, w_out, clip_lengths, block_ids
):
    frame_count = block_ids.shape[0]
    clip_of, start_of = frame_tables(clip_lengths, frame_count)
    frames_dev = latent.shape[0]
    first_frame = lax.axis_index("frame") * frames_dev
    guided = guide_features(
        latent, pose_maps, conv_weight, conv_bias, pose_proj, start_of, first_frame
    )
    whole_rows = lax.all_gather(guided, "head", axis=1, tiled=True)
    height = whole_rows.shape[1]
    width_grid = whole_rows.shape[2]
    model_width = whole_rows.shape[3]
    flat_tokens = whole_rows.reshape(-1, model_width)
    qkv_local = w_qkv.reshape(w_qkv.shape[0], -1)
    projected = jnp.dot(
        flat_tokens,
        lax.all_gather(qkv_local, "frame", axis=0, tiled=True),
        preferred_element_type=jnp.float32,
    ).astype(jnp.bfloat16)
    per_frame = height * width_grid
    heads_dev = w_qkv.shape[1]
    head_size = w_qkv.shape[3]
    grouped = projected.reshape(frames_dev, per_frame, heads_dev, 3, head_size)
    rows_total = frames_dev * per_frame
    queries = grouped[:, :, :, 0].reshape(rows_total, heads_dev, head_size)
    keyvals = grouped[:, :, :, 1:3]
    clip_rows = lax.dynamic_slice_in_dim(clip_of, first_frame, frames_dev)
    block_rows = lax.dynamic_slice_in_dim(block_ids, first_frame, frames_dev)
    query_clip = jnp.repeat(clip_rows, per_frame)
    query_block = jnp.repeat(block_rows, per_frame)
    attended = attend_rows(queries, query_clip, query_block, keyvals, clip_of, block_ids)
    by_row = attended.reshape(frames_dev, height, width_grid, heads_dev * head_size)
    by_row = jnp.transpose(by_row, (1, 0, 2, 3)).reshape(
        height, frames_dev * width_grid, heads_dev * head_size
    )
    out_weight = w_out.reshape(heads_dev * head_size, w_out.shape[2])
    rows_here = height // lax.axis_size("head")
    summed_rows = lax.psum_scatter(
        jnp.dot(by_row, out_weight, preferred_element_type=jnp.float32).astype(jnp.bfloat16),
        "head",
        scatter_dimension=0,
        tiled=True,
    ).astype(jnp.float32)
    summed_rows = summed_rows.reshape(rows_here, frames_dev, width_grid, out_weight.shape[1])
    return jnp.transpose(summed_rows, (1, 0, 2, 3)).astype(jnp.bfloat16)


def turn(value, axis, steps):
    count = lax.axis_size(axis)
    return lax.ppermute(value, axis, [(i, (i + steps) % count) for i in range(count)])


def across(value, axis, bits):
    count = lax.axis_size(axis)
    return lax.ppermute(value, axis, [(i, i ^ bits) for i in range(count)])


def hop(lower, upper, axis, s):
    count = lax.axis_size(axis)
    lower = lax.ppermute(lower, axis, [(i, i + 1) for i in range(s - 1, count - 1)])
    upper = lax.ppermute(upper, axis, [(i, i - 1) for i in range(1, count - s + 1)])
    return lower, upper


def after(value, *others):
    def body(*refs):
        del refs

    anywhere = pl.BlockSpec(memory_space=pl.ANY)
    return pl.pallas_call(
        body,
        out_shape=jax.ShapeDtypeStruct(value.shape, value.dtype),
        in_specs=[anywhere] * (1 + len(others)),
        out_specs=anywhere,
        input_output_aliases={0: 0},
        name="after",
    )(value, *others)


def take_block(weight, row, column, shape, *ready):
    def body(at_ref, weight_ref, *refs):
        refs[-1][...] = weight_ref[...]

    return pl.pallas_call(
        body,
        out_shape=jax.ShapeDtypeStruct(shape, weight.dtype),
        grid_spec=pltpu.PrefetchScalarGridSpec(
            num_scalar_prefetch=1,
            grid=(1,),
            in_specs=[pl.BlockSpec(shape, lambda i, at: (at[0], at[1]))]
            + [pl.BlockSpec(memory_space=pl.ANY)] * len(ready),
            out_specs=pl.BlockSpec(shape, lambda i, at: (0, 0)),
        ),
        cost_estimate=cost(0, 4 * shape[0] * shape[1]),
        name="take_block",
    )(jnp.stack([row, column]), weight, *ready)


def conv_kernel(keep_ref, cols_ref, weight_ref, bias_ref, out_ref, acc_ref):
    step = pl.program_id(0)
    tap_a, tap_b = step // 3, step % 3
    frames, strip_rows, width = out_ref.shape[0], out_ref.shape[1], cols_ref.shape[2]
    pieces = []
    for t in range(frames):
        keep = keep_ref[tap_a * frames + t]
        for r in range(strip_rows):
            rows = cols_ref[tap_a + t, tap_b + 2 * r].astype(F32)
            pieces.append(jnp.where(keep > 0, rows, 0.0))
    lhs = jnp.concatenate(pieces, axis=0).astype(BF16)
    channels = weight_ref.shape[3]
    total = None
    for e in range(3):
        part = lax.dot_general(
            lhs[:, e * channels : (e + 1) * channels],
            weight_ref[0, e],
            (((1,), (1,)), ((), ())),
            preferred_element_type=F32,
        )
        total = part if total is None else total + part

    @pl.when(step == 0)
    def _():
        acc_ref[...] = total

    @pl.when(step > 0)
    def _():
        acc_ref[...] += total

    @pl.when(step == 8)
    def _():
        summed = acc_ref[...] + bias_ref[...]
        feature = summed / (1.0 + jnp.exp(-summed))
        for t in range(frames):
            for r in range(strip_rows):
                at = (t * strip_rows + r) * width
                out_ref[t, r] = feature[at : at + width].astype(BF16)


def pose_feature(extended, conv_weight, conv_bias, start_of, first_frame):
    frames, rows, columns, channels = extended.shape
    frames, rows = frames // 2, rows - 1
    out_channels = conv_weight.shape[-1]
    pairs = extended.reshape(2 * frames, rows + 1, columns // 2, 2 * channels)
    before = jnp.pad(pairs[:, :, :-1, channels:], ((0, 0), (0, 0), (1, 0), (0, 0)))
    cols = jnp.concatenate([before, pairs], axis=3)
    taps = jnp.transpose(conv_weight, (0, 1, 2, 4, 3)).reshape(9, 3, out_channels, channels)
    frame_ids = first_frame + jnp.arange(frames, dtype=jnp.int32)
    starts_here = lax.dynamic_slice_in_dim(start_of, first_frame, frames)
    keep = (frame_ids[None, :] - 2 + jnp.arange(3, dtype=jnp.int32)[:, None] >= starts_here[None, :])
    keep = keep.astype(jnp.int32).reshape(-1)
    out_shape = (frames, rows // 2, columns // 2, out_channels)
    tokens = frames * (rows // 2) * (columns // 2)
    feature = pl.pallas_call(
        conv_kernel,
        out_shape=jax.ShapeDtypeStruct(out_shape, BF16),
        grid_spec=pltpu.PrefetchScalarGridSpec(
            num_scalar_prefetch=1,
            grid=(9,),
            in_specs=[
                pl.BlockSpec(cols.shape, lambda i, k: (0, 0, 0, 0)),
                pl.BlockSpec((1, 3, out_channels, channels), lambda i, k: (i, 0, 0, 0)),
                pl.BlockSpec((1, out_channels), lambda i, k: (0, 0)),
            ],
            out_specs=pl.BlockSpec(out_shape, lambda i, k: (0, 0, 0, 0)),
            scratch_shapes=[pltpu.VMEM((tokens, out_channels), F32)],
        ),
        compiler_params=pltpu.CompilerParams(vmem_limit_bytes=24 * MIB),
        cost_estimate=cost(tokens * out_channels, 2 * tokens * out_channels),
        name="pose_conv",
    )(keep, cols, taps, conv_bias.reshape(1, -1))
    return feature.reshape(tokens, out_channels)


def project(own, lower, upper, features, pose_proj, order, shards_of, total, frames):
    strips = len(features)
    tokens = own.shape[0]
    channels = pose_proj.shape[0]
    rows = strips * tokens
    per_frame = tokens // frames
    steps = len(shards_of)
    flat = [array for kind, arrays in shards_of for array in arrays]
    size = flat[0].shape[2]
    columns = 3 * (PLANE + 1)
    heads = PLANE + 1
    depth = own.shape[1] // PLANE
    cuts = [(c, min(c + 4, columns)) for c in range(0, columns, 4)]
    parts = 2 if shards_of[0][0] == "rows" else 1
    slots = min(2, steps)

    def body(order_ref, *refs):
        own_ref, lower_refs, upper_refs = refs[0], refs[1:strips], refs[strips : 2 * strips - 1]
        feature_refs = refs[2 * strips - 1 : 3 * strips - 1]
        proj_ref = refs[3 * strips - 1]
        source_refs = refs[3 * strips : 3 * strips + len(flat)]
        rest = refs[3 * strips + len(flat) :]
        held_ref, guided_ref, sems = rest[-3:]
        if total is None:
            sum_ref = rest[0]
        else:
            total_ref, last_ref, sum_ref = rest[0], rest[1 + PLANE], rest[2 + PLANE]
            message_refs = rest[1 : 1 + PLANE]
        step = pl.program_id(0)

        def fetch(k, n, part):
            low, high = cuts[n]
            kind, arrays = shards_of[k]
            base = sum(len(other) for unused, other in shards_of[:k])
            length, at, shift = depth // parts, 0, 0
            if kind != "whole" and low >= FIRST_COLUMNS:
                base, shift = base + 1, FIRST_COLUMNS
            if kind == "rows":
                base += 2 * part
                at = pl.multiple_of((order_ref[steps + 1] ^ part) * length, 128)
            return pltpu.make_async_copy(
                source_refs[base].at[low - shift : high - shift],
                held_ref.at[k % slots, low:high, pl.ds(at, length)],
                sems.at[k % slots, n, part],
            )

        def start(k):
            for n in range(len(cuts)):
                for part in range(parts):
                    fetch(k, n, part).start()

        for k in range(steps):

            @pl.when(step == max(k - 1, 0))
            def _(k=k):
                start(k)

        feature = jnp.concatenate([ref[...] for ref in feature_refs], axis=0)
        added = jnp.dot(feature, proj_ref[...], preferred_element_type=F32)
        for s in range(strips):
            latent = own_ref[...].astype(F32)
            if s > 0:
                latent = lower_refs[s - 1][...].astype(F32) + upper_refs[strips - s - 1][...].astype(F32)
            guided = (latent + added[s * tokens : (s + 1) * tokens]).astype(BF16)
            for t in range(frames):
                at = (t * strips + s) * per_frame
                guided_ref[at : at + per_frame] = guided[t * per_frame : (t + 1) * per_frame]

        slot = lax.rem(step, slots)
        for n, (low, high) in enumerate(cuts):
            for k in range(steps):

                @pl.when(step == k)
                def _(k=k, n=n):
                    for part in range(parts):
                        fetch(k, n, part).wait()

            rhs = jnp.concatenate([held_ref[slot, c] for c in range(low, high)], axis=1)
            part = jnp.dot(guided_ref[...], rhs, preferred_element_type=F32)
            lanes = slice(low * size, high * size)
            if total is not None:
                sum_ref[:, lanes] = total_ref[:, lanes] + part
                continue

            @pl.when(step == 0)
            def _(lanes=lanes, part=part):
                sum_ref[:, lanes] = part

            @pl.when(step > 0)
            def _(lanes=lanes, part=part):
                sum_ref[:, lanes] += part

        if total is None:
            return
        last = 3 * (heads - 1) * size
        last_ref[...] = sum_ref[:, last : last + size].astype(BF16)
        for r in range(PLANE):
            head = order_ref[steps] ^ r
            for j in range(3):
                at = pl.multiple_of((3 * head + j) * size, size)
                message_refs[r][j] = sum_ref[:, pl.ds(at, size)].astype(BF16)
            for j in range(1, 3):
                at = last + j * size
                message_refs[r][2 + j] = sum_ref[:, at : at + size].astype(BF16)

    piece = pl.BlockSpec((tokens, depth), lambda i, order: (0, order[i]))
    in_specs = [piece] * (2 * strips - 1)
    in_specs += [pl.BlockSpec((tokens, channels), lambda i, order: (0, 0))] * strips
    in_specs += [pl.BlockSpec((channels, depth), lambda i, order: (0, order[i]))]
    in_specs += [pl.BlockSpec(memory_space=pl.ANY)] * len(flat)
    operands = [own, *lower, *upper, *features, pose_proj, *flat]
    sums = pl.BlockSpec((rows, columns * size), lambda i, order: (0, 0))
    scratch = [
        pltpu.VMEM((slots, columns, depth, size), BF16),
        pltpu.VMEM((rows, depth), BF16),
        pltpu.SemaphoreType.DMA((slots, len(cuts), parts)),
    ]
    if total is None:
        out_shape, out_specs = jax.ShapeDtypeStruct((rows, columns * size), F32), sums
    else:
        assert steps == 1
        in_specs.append(sums)
        operands.append(total)
        message = jax.ShapeDtypeStruct((5, rows, size), BF16)
        out_shape = (message,) * PLANE + (jax.ShapeDtypeStruct((rows, size), BF16),)
        out_specs = (pl.BlockSpec((5, rows, size), lambda i, order: (0, 0, 0)),) * PLANE
        out_specs += (pl.BlockSpec((rows, size), lambda i, order: (0, 0)),)
        scratch = [pltpu.VMEM((rows, columns * size), F32)] + scratch
    return pl.pallas_call(
        body,
        out_shape=out_shape,
        grid_spec=pltpu.PrefetchScalarGridSpec(
            num_scalar_prefetch=1, grid=(steps,), in_specs=in_specs, out_specs=out_specs, scratch_shapes=scratch
        ),
        compiler_params=pltpu.CompilerParams(vmem_limit_bytes=40 * MIB),
        cost_estimate=cost(0, 2 * rows * size),
        name="project",
    )(order, *operands)


def attend(messages, last_query, here, spans, frames, strips):
    rows, size = last_query.shape
    per_frame = rows // frames
    strip = per_frame // strips
    frame_count = PLANE * frames
    window = frame_count - 4 if frame_count > 4 else frame_count
    out_rows = (PLANE + 1) * frames * strip
    scale = size ** (-0.5)

    def body(table_ref, *refs):
        message_refs, last_ref = refs[:PLANE], refs[PLANE]
        out_refs, held_ref = refs[PLANE + 1 : PLANE + 1 + strips], refs[-1]
        here_at = table_ref[3 * frame_count]
        for r in range(PLANE):
            for t in range(frames):
                frame = (here_at ^ r) * frames + t
                for j in range(4):
                    held_ref[frame, j] = message_refs[r][j + 1, t * per_frame : (t + 1) * per_frame]

        def one(query, frame, kind, at):
            begin, low, high = table_ref[3 * frame], table_ref[3 * frame + 1], table_ref[3 * frame + 2]
            keys = held_ref[pl.ds(begin, window), kind].reshape(window * per_frame, size)
            values = held_ref[pl.ds(begin, window), kind + 1].reshape(window * per_frame, size)
            scores = lax.dot_general(query, keys, (((1,), (1,)), ((), ())), preferred_element_type=F32)
            place = lax.broadcasted_iota(jnp.int32, (1, window * per_frame), 1)
            seen = (place >= low * per_frame) & (place < high * per_frame)
            scores = jnp.where(seen, scores * scale, NEG_FILL)
            weights = jnp.exp(scores - jnp.max(scores, axis=1, keepdims=True))
            totals = jnp.sum(weights, axis=1, keepdims=True)
            mixed = jnp.dot(weights.astype(BF16), values, preferred_element_type=F32)
            result = (mixed / totals).astype(BF16)
            for s in range(strips):
                out_refs[s][at : at + strip] = result[s * strip : (s + 1) * strip]

        for r in range(PLANE):
            for t in range(frames):
                query = message_refs[r][0, t * per_frame : (t + 1) * per_frame]
                one(query, (here_at ^ r) * frames + t, 0, (r * frames + t) * strip)
        for t in range(frames):
            query = last_ref[t * per_frame : (t + 1) * per_frame]
            one(query, here_at * frames + t, 2, (PLANE * frames + t) * strip)

    table = jnp.concatenate([spans.reshape(-1), here.reshape(1)]).astype(jnp.int32)
    whole = pl.BlockSpec((5, rows, size), lambda i, table: (0, 0, 0))
    units = (PLANE + 1) * frames
    return pl.pallas_call(
        body,
        out_shape=(jax.ShapeDtypeStruct((out_rows, size), BF16),) * strips,
        grid_spec=pltpu.PrefetchScalarGridSpec(
            num_scalar_prefetch=1,
            grid=(1,),
            in_specs=[whole] * PLANE + [pl.BlockSpec((rows, size), lambda i, table: (0, 0))],
            out_specs=(pl.BlockSpec((out_rows, size), lambda i, table: (0, 0)),) * strips,
            scratch_shapes=[pltpu.VMEM((frame_count, 4, per_frame, size), BF16)],
        ),
        compiler_params=pltpu.CompilerParams(vmem_limit_bytes=40 * MIB),
        cost_estimate=cost(0, 2 * rows * size),
        name="attend",
    )(table, *messages, last_query)


def out_project(gathered, weights, here, group, core, tokens):
    groups, depth, columns = weights[0].shape
    size = gathered[0].shape[2]
    heads = depth // size

    def body(at_ref, *refs):
        weight_refs = refs[PLANE : PLANE + 2]
        out_refs, lhs_ref, sum_ref = refs[PLANE + 2 : -2], refs[-2], refs[-1]
        step = pl.program_id(0)
        for p in range(PLANE):
            rows = slice(p * tokens, (p + 1) * tokens)
            for q in range(PLANE):
                at = (p ^ q) * tokens
                lhs_ref[rows, q * size : (q + 1) * size] = refs[q][0, at : at + tokens]
            lhs_ref[rows, PLANE * size :] = refs[p][0, PLANE * tokens :]

        here_at, core_at = at_ref[0], at_ref[2]
        for c in range(2):
            found = [
                weight_refs[c][0, pl.ds(pl.multiple_of((here_at ^ q) * size, size), size)] for q in range(PLANE)
            ]
            found.append(weight_refs[c][0, PLANE * size : heads * size])
            part = jnp.dot(lhs_ref[...], jnp.concatenate(found, axis=0), preferred_element_type=F32)
            part = part.astype(BF16).astype(F32)

            @pl.when(step == 0)
            def _(c=c, part=part):
                sum_ref[c] = part

            @pl.when(step > 0)
            def _(c=c, part=part):
                sum_ref[c] += part

        @pl.when(step == groups - 1)
        def _():
            for p in range(PLANE):
                for c in range(2):
                    at = pl.multiple_of((core_at ^ c) * columns, 128)
                    out_refs[p][:, pl.ds(at, columns)] = sum_ref[c, p * tokens : (p + 1) * tokens].astype(BF16)

    in_specs = [pl.BlockSpec((1,) + piece.shape[1:], lambda g, at: (g, 0, 0)) for piece in gathered]
    in_specs += [
        pl.BlockSpec((1, depth, columns), lambda g, at: (lax.rem(at[1] + g, groups), 0, 0))
    ] * 2
    return pl.pallas_call(
        body,
        out_shape=(jax.ShapeDtypeStruct((tokens, 2 * columns), BF16),) * PLANE,
        grid_spec=pltpu.PrefetchScalarGridSpec(
            num_scalar_prefetch=1,
            grid=(groups,),
            in_specs=in_specs,
            out_specs=(pl.BlockSpec((tokens, 2 * columns), lambda g, at: (0, 0)),) * PLANE,
            scratch_shapes=[
                pltpu.VMEM((PLANE * tokens, depth), BF16),
                pltpu.VMEM((2, PLANE * tokens, columns), F32),
            ],
        ),
        compiler_params=pltpu.CompilerParams(vmem_limit_bytes=24 * MIB),
        cost_estimate=cost(0, 4 * PLANE * tokens * columns),
        name="out_project",
    )(jnp.stack([here, group, core]), *gathered, *weights)


def place_columns(pieces, here):
    tokens, columns = pieces[0].shape

    def body(here_ref, *refs):
        for r in range(PLANE):
            at = pl.multiple_of((here_ref[0] ^ r) * columns, 128)
            refs[-1][:, pl.ds(at, columns)] = refs[r][...]

    return pl.pallas_call(
        body,
        out_shape=jax.ShapeDtypeStruct((tokens, PLANE * columns), BF16),
        grid_spec=pltpu.PrefetchScalarGridSpec(
            num_scalar_prefetch=1,
            grid=(1,),
            in_specs=[pl.BlockSpec((tokens, columns), lambda i, here: (0, 0))] * PLANE,
            out_specs=pl.BlockSpec((tokens, PLANE * columns), lambda i, here: (0, 0)),
        ),
        cost_estimate=cost(0, 4 * tokens * PLANE * columns),
        name="place_columns",
    )(here.reshape(1), *pieces)


def shards(
    latent, pose_maps, conv_weight, conv_bias, pose_proj, w_qkv, w_out, clip_lengths, block_ids
):
    frame_count = block_ids.shape[0]
    frames, strip_rows, width_grid, model_width = latent.shape
    heads, head_size = w_qkv.shape[1], w_qkv.shape[3]
    strips = lax.axis_size("head")
    tokens = frames * strip_rows * width_grid
    here = lax.axis_index("frame").astype(jnp.int32)
    group = lax.axis_index("head").astype(jnp.int32)
    core = lax.axis_index("dp").astype(jnp.int32)
    clip_of, start_of = frame_tables(clip_lengths, frame_count)

    weight = jnp.transpose(w_qkv, (1, 2, 0, 3)).reshape(3 * heads, -1, head_size)
    near_pairs = [(2 * f + c, 2 * (f ^ (1 + c)) + c) for f in range(PLANE) for c in range(2)]
    far_pairs = [(2 * f + c, 2 * (f ^ (2 - c)) + c) for f in range(PLANE) for c in range(2)]
    plane_axes = ("frame", "dp")
    near_first = lax.ppermute(weight[:FIRST_COLUMNS], plane_axes, near_pairs)
    earlier = shifted(pose_maps, "frame", 1)

    own = latent.reshape(tokens, model_width)
    lower, upper = hop(own, own, "head", 1)
    lower, upper = [lower], [upper]
    near_rest = after(weight[FIRST_COLUMNS:], near_first, earlier, lower[0], upper[0])
    near_rest = lax.ppermute(near_rest, plane_axes, near_pairs)
    extended = jnp.concatenate([earlier, pose_maps], axis=0)
    rows_above = shifted(extended[:, -1:], "head", 1)
    extended = jnp.concatenate([rows_above, extended], axis=1)

    columns = model_width // PLANE // 2
    depth = heads * head_size
    out_half = take_block(w_out.reshape(depth, model_width), jnp.int32(0), 2 * here + core, (depth, columns))

    for s in range(2, strips):
        below, above = hop(lower[-1], upper[-1], "head", s)
        if s < strips - 1:
            below, above = after(below, rows_above), after(above, rows_above)
        lower.append(below)
        upper.append(above)
    start_of = after(start_of, lower[1], upper[1], out_half)
    feature = pose_feature(extended, conv_weight, conv_bias, start_of, here * frames)
    half_rows = weight.shape[1] // 2
    first_half = lax.dynamic_slice_in_dim(near_first, core * half_rows, half_rows, axis=1)
    first_half = after(first_half, lower[1])
    near_rest = after(near_rest, lower[1], upper[1], first_half)
    near = (near_first, near_rest)
    rest_half = lax.dynamic_slice_in_dim(near_rest, core * half_rows, half_rows, axis=1)
    rest_half = after(rest_half, feature)
    far = tuple(lax.ppermute(part, plane_axes, far_pairs) for part in (first_half, rest_half))
    feature = after(feature, near_rest)
    features = [feature] + [turn(feature, "head", s) for s in range(1, strips)]
    other = tuple(across(part, "dp", 1) for part in near)
    out_half = after(out_half, lower[-1], upper[-1])

    here_near, here_other, here_far = here ^ (1 + core), here ^ (2 - core), here ^ 3
    order = after(jnp.stack([here, here_near, here_other, here, core]), out_half)
    held = [("whole", (weight,)), ("columns", near), ("columns", other)]
    total = project(own, lower, upper, features, pose_proj, order, held, None, frames)
    far = tuple(after(part, total) for part in far)
    far += tuple(across(part, "dp", 1) for part in far)
    order = jnp.stack([here_far, here, core])
    *messages, last_query = project(
        own, lower, upper, features, pose_proj, order, [("rows", far)], total, frames
    )
    messages = [messages[0]] + [across(messages[r], "frame", r) for r in range(1, PLANE)]

    same_clip = clip_of[:, None] == clip_of[None, :]
    counts = jnp.sum((same_clip & (block_ids[None, :] <= block_ids[:, None])).astype(jnp.int32), axis=1)
    window = frame_count - 4 if frame_count > 4 else frame_count
    begins = jnp.minimum(start_of, frame_count - window)
    spans = jnp.stack([begins, start_of - begins, start_of - begins + counts], axis=1)
    outs = attend(messages, last_query, here, spans, frames, strips)

    out_half = after(lax.all_gather(out_half, "head"), outs[0])
    out_weights = [out_half, across(out_half, "dp", 1)]

    strip_heads = [outs[0]] + [turn(outs[s], "head", -s) for s in range(1, strips)]
    strip_heads = jnp.stack(strip_heads)
    gathered = [strip_heads] + [across(strip_heads, "frame", r) for r in range(1, PLANE)]
    done = out_project(gathered, out_weights, here, group, core, tokens)
    mine = [done[0]] + [across(done[r], "frame", r) for r in range(1, PLANE)]
    return place_columns(mine, here).reshape(latent.shape)


def solution(mesh):
    return jax.shard_map(
        shards if mesh.shape["frame"] == PLANE else plain_shards,
        mesh=mesh,
        in_specs=(
            P(("dp", "frame"), "head", None, None),
            P(("dp", "frame"), "head", None, None),
            P(),
            P(),
            P(),
            P("frame", "head", None, None),
            P("head", None, None),
            P("dp"),
            P("dp"),
        ),
        out_specs=P(("dp", "frame"), "head", None, None),
        check_vma=False,
    )
```

```python
import jax
import jax.numpy as jnp
from jax import lax
from jax.experimental import pallas as pl
from jax.experimental.pallas import tpu as pltpu
from jax.sharding import PartitionSpec as P

NEG_FILL = -1e30
MIB = 1 << 20
F32 = jnp.float32
BF16 = jnp.bfloat16
PLANE = 4
FIRST_COLUMNS = 8


def cost(flops, moved, exps=0):
    return pl.CostEstimate(flops=int(flops), bytes_accessed=int(moved), transcendentals=int(exps))


def shifted(value, axis, steps):
    count = lax.axis_size(axis)
    leading, last = (max(0, -steps), min(count, count - steps))
    return lax.ppermute(value, axis, [(source, source + steps) for source in range(leading, last)])


def frame_tables(clip_lengths, frame_count):
    clip_ends = jnp.cumsum(clip_lengths)
    clip_starts = clip_ends - clip_lengths
    frame_index = jnp.arange(frame_count, dtype=jnp.int32)
    clip_of = jnp.sum((frame_index[:, None] >= clip_ends[None, :]).astype(jnp.int32), axis=1)
    clip_match = clip_of[:, None] == jnp.arange(clip_lengths.shape[0], dtype=jnp.int32)[None, :]
    start_of = jnp.sum(jnp.where(clip_match, clip_starts[None, :], 0), axis=1)
    return (clip_of, start_of)


def guide_features(latent, pose_maps, conv_weight, conv_bias, pose_proj, start_of, first_frame):
    frames_dev = pose_maps.shape[0]
    upper_row = shifted(pose_maps[:, -1:], "head", 1)
    rows_ext = jnp.concatenate([upper_row, pose_maps], axis=1)
    left_column = jnp.zeros(rows_ext.shape[:2] + (1, rows_ext.shape[3]), rows_ext.dtype)
    cols_ext = jnp.concatenate([left_column, rows_ext], axis=2)
    earlier = shifted(cols_ext, "frame", 1)
    extended = jnp.concatenate([earlier, cols_ext], axis=0)
    out_rows = pose_maps.shape[1] // 2
    out_cols = pose_maps.shape[2] // 2
    frame_ids = first_frame + jnp.arange(frames_dev, dtype=jnp.int32)
    starts_here = lax.dynamic_slice_in_dim(start_of, first_frame, frames_dev)
    tap_list = []
    for step_a in range(3):
        keep_mask = (frame_ids - 2 + step_a >= starts_here).astype(pose_maps.dtype)[
            :, None, None, None
        ]
        frames_tap = extended[step_a : step_a + frames_dev] * keep_mask
        for step_b in range(3):
            for step_e in range(3):
                tap_list.append(
                    frames_tap[
                        :,
                        step_b : step_b + 2 * out_rows - 1 : 2,
                        step_e : step_e + 2 * out_cols - 1 : 2,
                    ]
                )
    stacked = jnp.concatenate(tap_list, axis=3)
    kernel = conv_weight.reshape(-1, conv_weight.shape[-1])
    summed = jnp.dot(stacked, kernel, preferred_element_type=jnp.float32) + conv_bias
    feature = jax.nn.silu(summed).astype(jnp.bfloat16)
    guided = latent.astype(jnp.float32) + jnp.dot(
        feature, pose_proj, preferred_element_type=jnp.float32
    )
    return guided.astype(jnp.bfloat16)


def attend_rows(queries, query_clip, query_block, keyvals, clip_of, block_ids):
    heads_dev = queries.shape[1]
    rows_query = queries.shape[0]
    head_size = queries.shape[2]
    score_scale = head_size ** (-0.5)
    start_carry = (
        jnp.full((heads_dev, rows_query), NEG_FILL, jnp.float32),
        jnp.zeros((heads_dev, rows_query), jnp.float32),
        jnp.zeros((heads_dev, rows_query, head_size), jnp.float32),
    )

    def one_frame(running, frame_item):
        frame_kv, frame_id = frame_item
        key_clip = clip_of[frame_id]
        key_block = block_ids[frame_id]
        visible = (query_clip == key_clip) & (key_block <= query_block)
        run_max, run_total, run_acc = running
        scores = (
            jnp.einsum(
                "qhd,khd->hqk", queries, frame_kv[:, :, 0], preferred_element_type=jnp.float32
            )
            * score_scale
        )
        scores = jnp.where(visible[None, :, None], scores, NEG_FILL)
        new_max = jnp.maximum(run_max, jnp.max(scores, axis=2))
        factor = jnp.exp(run_max - new_max)
        weights = jnp.where(visible[None, :, None], jnp.exp(scores - new_max[:, :, None]), 0.0)
        new_total = run_total * factor + jnp.sum(weights, axis=2)
        new_acc = run_acc * factor[:, :, None] + jnp.einsum(
            "hqk,khd->hqd",
            weights.astype(jnp.bfloat16),
            frame_kv[:, :, 1],
            preferred_element_type=jnp.float32,
        )
        running = (new_max, new_total, new_acc)
        return (running, None)

    running = start_carry
    shard_piece = lax.all_gather(keyvals, "frame", axis=0, tiled=True)
    piece_frames = shard_piece.shape[0]
    frame_list = jnp.arange(piece_frames, dtype=jnp.int32)
    running, unused = lax.scan(one_frame, running, (shard_piece, frame_list))
    run_max, run_total, run_acc = running
    normalized = run_acc / run_total[:, :, None]
    return jnp.transpose(normalized, (1, 0, 2)).astype(jnp.bfloat16)


def plain_shards(
    latent, pose_maps, conv_weight, conv_bias, pose_proj, w_qkv, w_out, clip_lengths, block_ids
):
    frame_count = block_ids.shape[0]
    clip_of, start_of = frame_tables(clip_lengths, frame_count)
    frames_dev = latent.shape[0]
    first_frame = lax.axis_index("frame") * frames_dev
    guided = guide_features(
        latent, pose_maps, conv_weight, conv_bias, pose_proj, start_of, first_frame
    )
    whole_rows = lax.all_gather(guided, "head", axis=1, tiled=True)
    height = whole_rows.shape[1]
    width_grid = whole_rows.shape[2]
    model_width = whole_rows.shape[3]
    flat_tokens = whole_rows.reshape(-1, model_width)
    qkv_local = w_qkv.reshape(w_qkv.shape[0], -1)
    projected = jnp.dot(
        flat_tokens,
        lax.all_gather(qkv_local, "frame", axis=0, tiled=True),
        preferred_element_type=jnp.float32,
    ).astype(jnp.bfloat16)
    per_frame = height * width_grid
    heads_dev = w_qkv.shape[1]
    head_size = w_qkv.shape[3]
    grouped = projected.reshape(frames_dev, per_frame, heads_dev, 3, head_size)
    rows_total = frames_dev * per_frame
    queries = grouped[:, :, :, 0].reshape(rows_total, heads_dev, head_size)
    keyvals = grouped[:, :, :, 1:3]
    clip_rows = lax.dynamic_slice_in_dim(clip_of, first_frame, frames_dev)
    block_rows = lax.dynamic_slice_in_dim(block_ids, first_frame, frames_dev)
    query_clip = jnp.repeat(clip_rows, per_frame)
    query_block = jnp.repeat(block_rows, per_frame)
    attended = attend_rows(queries, query_clip, query_block, keyvals, clip_of, block_ids)
    by_row = attended.reshape(frames_dev, height, width_grid, heads_dev * head_size)
    by_row = jnp.transpose(by_row, (1, 0, 2, 3)).reshape(
        height, frames_dev * width_grid, heads_dev * head_size
    )
    out_weight = w_out.reshape(heads_dev * head_size, w_out.shape[2])
    rows_here = height // lax.axis_size("head")
    summed_rows = lax.psum_scatter(
        jnp.dot(by_row, out_weight, preferred_element_type=jnp.float32).astype(jnp.bfloat16),
        "head",
        scatter_dimension=0,
        tiled=True,
    ).astype(jnp.float32)
    summed_rows = summed_rows.reshape(rows_here, frames_dev, width_grid, out_weight.shape[1])
    return jnp.transpose(summed_rows, (1, 0, 2, 3)).astype(jnp.bfloat16)


def turn(value, axis, steps):
    count = lax.axis_size(axis)
    return lax.ppermute(value, axis, [(i, (i + steps) % count) for i in range(count)])


def across(value, axis, bits):
    count = lax.axis_size(axis)
    return lax.ppermute(value, axis, [(i, i ^ bits) for i in range(count)])


def hop(lower, upper, axis, s):
    count = lax.axis_size(axis)
    lower = lax.ppermute(lower, axis, [(i, i + 1) for i in range(s - 1, count - 1)])
    upper = lax.ppermute(upper, axis, [(i, i - 1) for i in range(1, count - s + 1)])
    return lower, upper


def after(value, *others):
    def body(*refs):
        del refs

    anywhere = pl.BlockSpec(memory_space=pl.ANY)
    return pl.pallas_call(
        body,
        out_shape=jax.ShapeDtypeStruct(value.shape, value.dtype),
        in_specs=[anywhere] * (1 + len(others)),
        out_specs=anywhere,
        input_output_aliases={0: 0},
        name="after",
    )(value, *others)


def take_block(weight, row, column, shape, *ready):
    def body(at_ref, weight_ref, *refs):
        refs[-1][...] = weight_ref[...]

    return pl.pallas_call(
        body,
        out_shape=jax.ShapeDtypeStruct(shape, weight.dtype),
        grid_spec=pltpu.PrefetchScalarGridSpec(
            num_scalar_prefetch=1,
            grid=(1,),
            in_specs=[pl.BlockSpec(shape, lambda i, at: (at[0], at[1]))]
            + [pl.BlockSpec(memory_space=pl.ANY)] * len(ready),
            out_specs=pl.BlockSpec(shape, lambda i, at: (0, 0)),
        ),
        cost_estimate=cost(0, 4 * shape[0] * shape[1]),
        name="take_block",
    )(jnp.stack([row, column]), weight, *ready)


def conv_kernel(keep_ref, cols_ref, weight_ref, bias_ref, out_ref, acc_ref):
    step = pl.program_id(0)
    tap_a, tap_b = step // 3, step % 3
    frames, strip_rows, width = out_ref.shape[0], out_ref.shape[1], cols_ref.shape[2]
    pieces = []
    for t in range(frames):
        keep = keep_ref[tap_a * frames + t]
        for r in range(strip_rows):
            rows = cols_ref[tap_a + t, tap_b + 2 * r].astype(F32)
            pieces.append(jnp.where(keep > 0, rows, 0.0))
    lhs = jnp.concatenate(pieces, axis=0).astype(BF16)
    channels = weight_ref.shape[3]
    total = None
    for e in range(3):
        part = lax.dot_general(
            lhs[:, e * channels : (e + 1) * channels],
            weight_ref[0, e],
            (((1,), (1,)), ((), ())),
            preferred_element_type=F32,
        )
        total = part if total is None else total + part

    @pl.when(step == 0)
    def _():
        acc_ref[...] = total

    @pl.when(step > 0)
    def _():
        acc_ref[...] += total

    @pl.when(step == 8)
    def _():
        summed = acc_ref[...] + bias_ref[...]
        feature = summed / (1.0 + jnp.exp(-summed))
        for t in range(frames):
            for r in range(strip_rows):
                at = (t * strip_rows + r) * width
                out_ref[t, r] = feature[at : at + width].astype(BF16)


def pose_feature(extended, conv_weight, conv_bias, start_of, first_frame):
    frames, rows, columns, channels = extended.shape
    frames, rows = frames // 2, rows - 1
    out_channels = conv_weight.shape[-1]
    pairs = extended.reshape(2 * frames, rows + 1, columns // 2, 2 * channels)
    before = jnp.pad(pairs[:, :, :-1, channels:], ((0, 0), (0, 0), (1, 0), (0, 0)))
    cols = jnp.concatenate([before, pairs], axis=3)
    taps = jnp.transpose(conv_weight, (0, 1, 2, 4, 3)).reshape(9, 3, out_channels, channels)
    frame_ids = first_frame + jnp.arange(frames, dtype=jnp.int32)
    starts_here = lax.dynamic_slice_in_dim(start_of, first_frame, frames)
    keep = (frame_ids[None, :] - 2 + jnp.arange(3, dtype=jnp.int32)[:, None] >= starts_here[None, :])
    keep = keep.astype(jnp.int32).reshape(-1)
    out_shape = (frames, rows // 2, columns // 2, out_channels)
    tokens = frames * (rows // 2) * (columns // 2)
    feature = pl.pallas_call(
        conv_kernel,
        out_shape=jax.ShapeDtypeStruct(out_shape, BF16),
        grid_spec=pltpu.PrefetchScalarGridSpec(
            num_scalar_prefetch=1,
            grid=(9,),
            in_specs=[
                pl.BlockSpec(cols.shape, lambda i, k: (0, 0, 0, 0)),
                pl.BlockSpec((1, 3, out_channels, channels), lambda i, k: (i, 0, 0, 0)),
                pl.BlockSpec((1, out_channels), lambda i, k: (0, 0)),
            ],
            out_specs=pl.BlockSpec(out_shape, lambda i, k: (0, 0, 0, 0)),
            scratch_shapes=[pltpu.VMEM((tokens, out_channels), F32)],
        ),
        compiler_params=pltpu.CompilerParams(vmem_limit_bytes=24 * MIB),
        cost_estimate=cost(tokens * out_channels, 2 * tokens * out_channels),
        name="pose_conv",
    )(keep, cols, taps, conv_bias.reshape(1, -1))
    return feature.reshape(tokens, out_channels)


def project(own, lower, upper, features, pose_proj, order, shards_of, total, frames):
    strips = len(features)
    tokens = own.shape[0]
    channels = pose_proj.shape[0]
    rows = strips * tokens
    per_frame = tokens // frames
    steps = len(shards_of)
    flat = [array for kind, arrays in shards_of for array in arrays]
    size = flat[0].shape[2]
    columns = 3 * (PLANE + 1)
    heads = PLANE + 1
    depth = own.shape[1] // PLANE
    cuts = [(c, min(c + 4, columns)) for c in range(0, columns, 4)]
    parts = 2 if shards_of[0][0] == "rows" else 1
    slots = min(2, steps)

    def body(order_ref, *refs):
        own_ref, lower_refs, upper_refs = refs[0], refs[1:strips], refs[strips : 2 * strips - 1]
        feature_refs = refs[2 * strips - 1 : 3 * strips - 1]
        proj_ref = refs[3 * strips - 1]
        source_refs = refs[3 * strips : 3 * strips + len(flat)]
        rest = refs[3 * strips + len(flat) :]
        held_ref, guided_ref, sems = rest[-3:]
        if total is None:
            sum_ref = rest[0]
        else:
            total_ref, last_ref, sum_ref = rest[0], rest[1 + PLANE], rest[2 + PLANE]
            message_refs = rest[1 : 1 + PLANE]
        step = pl.program_id(0)

        def fetch(k, n, part):
            low, high = cuts[n]
            kind, arrays = shards_of[k]
            base = sum(len(other) for unused, other in shards_of[:k])
            length, at, shift = depth // parts, 0, 0
            if kind != "whole" and low >= FIRST_COLUMNS:
                base, shift = base + 1, FIRST_COLUMNS
            if kind == "rows":
                base += 2 * part
                at = pl.multiple_of((order_ref[steps + 1] ^ part) * length, 128)
            return pltpu.make_async_copy(
                source_refs[base].at[low - shift : high - shift],
                held_ref.at[k % slots, low:high, pl.ds(at, length)],
                sems.at[k % slots, n, part],
            )

        def start(k):
            for n in range(len(cuts)):
                for part in range(parts):
                    fetch(k, n, part).start()

        for k in range(steps):

            @pl.when(step == max(k - 1, 0))
            def _(k=k):
                start(k)

        feature = jnp.concatenate([ref[...] for ref in feature_refs], axis=0)
        added = jnp.dot(feature, proj_ref[...], preferred_element_type=F32)
        for s in range(strips):
            latent = own_ref[...].astype(F32)
            if s > 0:
                latent = lower_refs[s - 1][...].astype(F32) + upper_refs[strips - s - 1][...].astype(F32)
            guided = (latent + added[s * tokens : (s + 1) * tokens]).astype(BF16)
            for t in range(frames):
                at = (t * strips + s) * per_frame
                guided_ref[at : at + per_frame] = guided[t * per_frame : (t + 1) * per_frame]

        slot = lax.rem(step, slots)
        for n, (low, high) in enumerate(cuts):
            for k in range(steps):

                @pl.when(step == k)
                def _(k=k, n=n):
                    for part in range(parts):
                        fetch(k, n, part).wait()

            rhs = jnp.concatenate([held_ref[slot, c] for c in range(low, high)], axis=1)
            part = jnp.dot(guided_ref[...], rhs, preferred_element_type=F32)
            lanes = slice(low * size, high * size)
            if total is not None:
                sum_ref[:, lanes] = total_ref[:, lanes] + part
                continue

            @pl.when(step == 0)
            def _(lanes=lanes, part=part):
                sum_ref[:, lanes] = part

            @pl.when(step > 0)
            def _(lanes=lanes, part=part):
                sum_ref[:, lanes] += part

        if total is None:
            return
        last = 3 * (heads - 1) * size
        last_ref[...] = sum_ref[:, last : last + size].astype(BF16)
        for r in range(PLANE):
            head = order_ref[steps] ^ r
            for j in range(3):
                at = pl.multiple_of((3 * head + j) * size, size)
                message_refs[r][j] = sum_ref[:, pl.ds(at, size)].astype(BF16)
            for j in range(1, 3):
                at = last + j * size
                message_refs[r][2 + j] = sum_ref[:, at : at + size].astype(BF16)

    piece = pl.BlockSpec((tokens, depth), lambda i, order: (0, order[i]))
    in_specs = [piece] * (2 * strips - 1)
    in_specs += [pl.BlockSpec((tokens, channels), lambda i, order: (0, 0))] * strips
    in_specs += [pl.BlockSpec((channels, depth), lambda i, order: (0, order[i]))]
    in_specs += [pl.BlockSpec(memory_space=pl.ANY)] * len(flat)
    operands = [own, *lower, *upper, *features, pose_proj, *flat]
    sums = pl.BlockSpec((rows, columns * size), lambda i, order: (0, 0))
    scratch = [
        pltpu.VMEM((slots, columns, depth, size), BF16),
        pltpu.VMEM((rows, depth), BF16),
        pltpu.SemaphoreType.DMA((slots, len(cuts), parts)),
    ]
    if total is None:
        out_shape, out_specs = jax.ShapeDtypeStruct((rows, columns * size), F32), sums
    else:
        assert steps == 1
        in_specs.append(sums)
        operands.append(total)
        message = jax.ShapeDtypeStruct((5, rows, size), BF16)
        out_shape = (message,) * PLANE + (jax.ShapeDtypeStruct((rows, size), BF16),)
        out_specs = (pl.BlockSpec((5, rows, size), lambda i, order: (0, 0, 0)),) * PLANE
        out_specs += (pl.BlockSpec((rows, size), lambda i, order: (0, 0)),)
        scratch = [pltpu.VMEM((rows, columns * size), F32)] + scratch
    return pl.pallas_call(
        body,
        out_shape=out_shape,
        grid_spec=pltpu.PrefetchScalarGridSpec(
            num_scalar_prefetch=1, grid=(steps,), in_specs=in_specs, out_specs=out_specs, scratch_shapes=scratch
        ),
        compiler_params=pltpu.CompilerParams(vmem_limit_bytes=40 * MIB),
        cost_estimate=cost(0, 2 * rows * size),
        name="project",
    )(order, *operands)


def attend(messages, last_query, here, spans, frames, strips):
    rows, size = last_query.shape
    per_frame = rows // frames
    strip = per_frame // strips
    frame_count = PLANE * frames
    window = frame_count - 4 if frame_count > 4 else frame_count
    out_rows = (PLANE + 1) * frames * strip
    scale = size ** (-0.5)

    def body(table_ref, *refs):
        message_refs, last_ref = refs[:PLANE], refs[PLANE]
        out_refs, held_ref = refs[PLANE + 1 : PLANE + 1 + strips], refs[-1]
        here_at = table_ref[3 * frame_count]
        for r in range(PLANE):
            for t in range(frames):
                frame = (here_at ^ r) * frames + t
                for j in range(4):
                    held_ref[frame, j] = message_refs[r][j + 1, t * per_frame : (t + 1) * per_frame]

        def one(query, frame, kind, at):
            begin, low, high = table_ref[3 * frame], table_ref[3 * frame + 1], table_ref[3 * frame + 2]
            keys = held_ref[pl.ds(begin, window), kind].reshape(window * per_frame, size)
            values = held_ref[pl.ds(begin, window), kind + 1].reshape(window * per_frame, size)
            scores = lax.dot_general(query, keys, (((1,), (1,)), ((), ())), preferred_element_type=F32)
            place = lax.broadcasted_iota(jnp.int32, (1, window * per_frame), 1)
            seen = (place >= low * per_frame) & (place < high * per_frame)
            scores = jnp.where(seen, scores * scale, NEG_FILL)
            weights = jnp.exp(scores - jnp.max(scores, axis=1, keepdims=True))
            totals = jnp.sum(weights, axis=1, keepdims=True)
            mixed = jnp.dot(weights.astype(BF16), values, preferred_element_type=F32)
            result = (mixed / totals).astype(BF16)
            for s in range(strips):
                out_refs[s][at : at + strip] = result[s * strip : (s + 1) * strip]

        for r in range(PLANE):
            for t in range(frames):
                query = message_refs[r][0, t * per_frame : (t + 1) * per_frame]
                one(query, (here_at ^ r) * frames + t, 0, (r * frames + t) * strip)
        for t in range(frames):
            query = last_ref[t * per_frame : (t + 1) * per_frame]
            one(query, here_at * frames + t, 2, (PLANE * frames + t) * strip)

    table = jnp.concatenate([spans.reshape(-1), here.reshape(1)]).astype(jnp.int32)
    whole = pl.BlockSpec((5, rows, size), lambda i, table: (0, 0, 0))
    units = (PLANE + 1) * frames
    return pl.pallas_call(
        body,
        out_shape=(jax.ShapeDtypeStruct((out_rows, size), BF16),) * strips,
        grid_spec=pltpu.PrefetchScalarGridSpec(
            num_scalar_prefetch=1,
            grid=(1,),
            in_specs=[whole] * PLANE + [pl.BlockSpec((rows, size), lambda i, table: (0, 0))],
            out_specs=(pl.BlockSpec((out_rows, size), lambda i, table: (0, 0)),) * strips,
            scratch_shapes=[pltpu.VMEM((frame_count, 4, per_frame, size), BF16)],
        ),
        compiler_params=pltpu.CompilerParams(vmem_limit_bytes=40 * MIB),
        cost_estimate=cost(0, 2 * rows * size),
        name="attend",
    )(table, *messages, last_query)


def out_project(gathered, weights, here, group, core, tokens):
    groups, depth, columns = weights[0].shape
    size = gathered[0].shape[2]
    heads = depth // size

    def body(at_ref, *refs):
        weight_refs = refs[PLANE : PLANE + 2]
        out_refs, lhs_ref, sum_ref = refs[PLANE + 2 : -2], refs[-2], refs[-1]
        step = pl.program_id(0)
        for p in range(PLANE):
            rows = slice(p * tokens, (p + 1) * tokens)
            for q in range(PLANE):
                at = (p ^ q) * tokens
                lhs_ref[rows, q * size : (q + 1) * size] = refs[q][0, at : at + tokens]
            lhs_ref[rows, PLANE * size :] = refs[p][0, PLANE * tokens :]

        here_at, core_at = at_ref[0], at_ref[2]
        for c in range(2):
            found = [
                weight_refs[c][0, pl.ds(pl.multiple_of((here_at ^ q) * size, size), size)] for q in range(PLANE)
            ]
            found.append(weight_refs[c][0, PLANE * size : heads * size])
            part = jnp.dot(lhs_ref[...], jnp.concatenate(found, axis=0), preferred_element_type=F32)
            part = part.astype(BF16).astype(F32)

            @pl.when(step == 0)
            def _(c=c, part=part):
                sum_ref[c] = part

            @pl.when(step > 0)
            def _(c=c, part=part):
                sum_ref[c] += part

        @pl.when(step == groups - 1)
        def _():
            for p in range(PLANE):
                for c in range(2):
                    at = pl.multiple_of((core_at ^ c) * columns, 128)
                    out_refs[p][:, pl.ds(at, columns)] = sum_ref[c, p * tokens : (p + 1) * tokens].astype(BF16)

    in_specs = [pl.BlockSpec((1,) + piece.shape[1:], lambda g, at: (g, 0, 0)) for piece in gathered]
    in_specs += [
        pl.BlockSpec((1, depth, columns), lambda g, at: (lax.rem(at[1] + g, groups), 0, 0))
    ] * 2
    return pl.pallas_call(
        body,
        out_shape=(jax.ShapeDtypeStruct((tokens, 2 * columns), BF16),) * PLANE,
        grid_spec=pltpu.PrefetchScalarGridSpec(
            num_scalar_prefetch=1,
            grid=(groups,),
            in_specs=in_specs,
            out_specs=(pl.BlockSpec((tokens, 2 * columns), lambda g, at: (0, 0)),) * PLANE,
            scratch_shapes=[
                pltpu.VMEM((PLANE * tokens, depth), BF16),
                pltpu.VMEM((2, PLANE * tokens, columns), F32),
            ],
        ),
        compiler_params=pltpu.CompilerParams(vmem_limit_bytes=24 * MIB),
        cost_estimate=cost(0, 4 * PLANE * tokens * columns),
        name="out_project",
    )(jnp.stack([here, group, core]), *gathered, *weights)


def place_columns(pieces, here):
    tokens, columns = pieces[0].shape

    def body(here_ref, *refs):
        for r in range(PLANE):
            at = pl.multiple_of((here_ref[0] ^ r) * columns, 128)
            refs[-1][:, pl.ds(at, columns)] = refs[r][...]

    return pl.pallas_call(
        body,
        out_shape=jax.ShapeDtypeStruct((tokens, PLANE * columns), BF16),
        grid_spec=pltpu.PrefetchScalarGridSpec(
            num_scalar_prefetch=1,
            grid=(1,),
            in_specs=[pl.BlockSpec((tokens, columns), lambda i, here: (0, 0))] * PLANE,
            out_specs=pl.BlockSpec((tokens, PLANE * columns), lambda i, here: (0, 0)),
        ),
        cost_estimate=cost(0, 4 * tokens * PLANE * columns),
        name="place_columns",
    )(here.reshape(1), *pieces)


def shards(
    latent, pose_maps, conv_weight, conv_bias, pose_proj, w_qkv, w_out, clip_lengths, block_ids
):
    frame_count = block_ids.shape[0]
    frames, strip_rows, width_grid, model_width = latent.shape
    heads, head_size = w_qkv.shape[1], w_qkv.shape[3]
    strips = lax.axis_size("head")
    tokens = frames * strip_rows * width_grid
    here = lax.axis_index("frame").astype(jnp.int32)
    group = lax.axis_index("head").astype(jnp.int32)
    core = lax.axis_index("dp").astype(jnp.int32)
    clip_of, start_of = frame_tables(clip_lengths, frame_count)

    weight = jnp.transpose(w_qkv, (1, 2, 0, 3)).reshape(3 * heads, -1, head_size)
    near_pairs = [(2 * f + c, 2 * (f ^ (1 + c)) + c) for f in range(PLANE) for c in range(2)]
    far_pairs = [(2 * f + c, 2 * (f ^ (2 - c)) + c) for f in range(PLANE) for c in range(2)]
    plane_axes = ("frame", "dp")
    near_first = lax.ppermute(weight[:FIRST_COLUMNS], plane_axes, near_pairs)
    near_rest = weight[FIRST_COLUMNS:]
    earlier = shifted(after(pose_maps, near_rest), "frame", 1)

    own = latent.reshape(tokens, model_width)
    lower, upper = hop(own, own, "head", 1)
    lower, upper = [lower], [upper]
    lower[0], upper[0] = after(lower[0], earlier), after(upper[0], earlier)
    near_rest = after(near_rest, near_first, lower[0], upper[0])
    near_rest = lax.ppermute(near_rest, plane_axes, near_pairs)
    extended = jnp.concatenate([earlier, pose_maps], axis=0)
    rows_above = shifted(extended[:, -1:], "head", 1)
    extended = jnp.concatenate([rows_above, extended], axis=1)

    columns = model_width // PLANE // 2
    depth = heads * head_size
    out_half = take_block(w_out.reshape(depth, model_width), jnp.int32(0), 2 * here + core, (depth, columns))

    for s in range(2, strips):
        below, above = hop(lower[-1], upper[-1], "head", s)
        if s < strips - 1:
            below, above = after(below, rows_above), after(above, rows_above)
        lower.append(below)
        upper.append(above)
    start_of = after(start_of, lower[1], upper[1], out_half)
    feature = pose_feature(extended, conv_weight, conv_bias, start_of, here * frames)
    half_rows = weight.shape[1] // 2
    first_half = lax.dynamic_slice_in_dim(near_first, core * half_rows, half_rows, axis=1)
    first_half = after(first_half, lower[1])
    near_rest = after(near_rest, lower[1], upper[1], first_half)
    near = (near_first, near_rest)
    rest_half = lax.dynamic_slice_in_dim(near_rest, core * half_rows, half_rows, axis=1)
    rest_half = after(rest_half, feature)
    far = tuple(lax.ppermute(part, plane_axes, far_pairs) for part in (first_half, rest_half))
    feature = after(feature, near_rest)
    features = [feature] + [turn(feature, "head", s) for s in range(1, strips)]
    other = tuple(across(part, "dp", 1) for part in near)
    out_half = after(out_half, lower[-1], upper[-1], *features[1:])

    here_near, here_other, here_far = here ^ (1 + core), here ^ (2 - core), here ^ 3
    order = after(jnp.stack([here, here_near, here_other, here, core]), out_half)
    held = [("whole", (weight,)), ("columns", near), ("columns", other)]
    total = project(own, lower, upper, features, pose_proj, order, held, None, frames)
    far = tuple(after(part, total) for part in far)
    far += tuple(across(part, "dp", 1) for part in far)
    order = jnp.stack([here_far, here, core])
    *messages, last_query = project(
        own, lower, upper, features, pose_proj, order, [("rows", far)], total, frames
    )
    messages = [messages[0]] + [across(messages[r], "frame", r) for r in range(1, PLANE)]

    same_clip = clip_of[:, None] == clip_of[None, :]
    counts = jnp.sum((same_clip & (block_ids[None, :] <= block_ids[:, None])).astype(jnp.int32), axis=1)
    window = frame_count - 4 if frame_count > 4 else frame_count
    begins = jnp.minimum(start_of, frame_count - window)
    spans = jnp.stack([begins, start_of - begins, start_of - begins + counts], axis=1)
    outs = attend(messages, last_query, here, spans, frames, strips)

    out_half = after(lax.all_gather(out_half, "head"), outs[0])
    out_weights = [out_half, across(out_half, "dp", 1)]

    strip_heads = [outs[0]] + [turn(outs[s], "head", -s) for s in range(1, strips)]
    strip_heads = jnp.stack(strip_heads)
    gathered = [strip_heads] + [across(strip_heads, "frame", r) for r in range(1, PLANE)]
    done = out_project(gathered, out_weights, here, group, core, tokens)
    mine = [done[0]] + [across(done[r], "frame", r) for r in range(1, PLANE)]
    return place_columns(mine, here).reshape(latent.shape)


def solution(mesh):
    return jax.shard_map(
        shards if mesh.shape["frame"] == PLANE else plain_shards,
        mesh=mesh,
        in_specs=(
            P(("dp", "frame"), "head", None, None),
            P(("dp", "frame"), "head", None, None),
            P(),
            P(),
            P(),
            P("frame", "head", None, None),
            P("head", None, None),
            P("dp"),
            P("dp"),
        ),
        out_specs=P(("dp", "frame"), "head", None, None),
        check_vma=False,
    )
```

```python
import jax
import jax.numpy as jnp
from jax import lax
from jax.experimental import pallas as pl
from jax.experimental.pallas import tpu as pltpu
from jax.sharding import PartitionSpec as P

NEG_FILL = -1e30
MIB = 1 << 20
F32 = jnp.float32
BF16 = jnp.bfloat16
PLANE = 4
FIRST_COLUMNS = 8


def cost(flops, moved, exps=0):
    return pl.CostEstimate(flops=int(flops), bytes_accessed=int(moved), transcendentals=int(exps))


def shifted(value, axis, steps):
    count = lax.axis_size(axis)
    leading, last = (max(0, -steps), min(count, count - steps))
    return lax.ppermute(value, axis, [(source, source + steps) for source in range(leading, last)])


def frame_tables(clip_lengths, frame_count):
    clip_ends = jnp.cumsum(clip_lengths)
    clip_starts = clip_ends - clip_lengths
    frame_index = jnp.arange(frame_count, dtype=jnp.int32)
    clip_of = jnp.sum((frame_index[:, None] >= clip_ends[None, :]).astype(jnp.int32), axis=1)
    clip_match = clip_of[:, None] == jnp.arange(clip_lengths.shape[0], dtype=jnp.int32)[None, :]
    start_of = jnp.sum(jnp.where(clip_match, clip_starts[None, :], 0), axis=1)
    return (clip_of, start_of)


def guide_features(latent, pose_maps, conv_weight, conv_bias, pose_proj, start_of, first_frame):
    frames_dev = pose_maps.shape[0]
    upper_row = shifted(pose_maps[:, -1:], "head", 1)
    rows_ext = jnp.concatenate([upper_row, pose_maps], axis=1)
    left_column = jnp.zeros(rows_ext.shape[:2] + (1, rows_ext.shape[3]), rows_ext.dtype)
    cols_ext = jnp.concatenate([left_column, rows_ext], axis=2)
    earlier = shifted(cols_ext, "frame", 1)
    extended = jnp.concatenate([earlier, cols_ext], axis=0)
    out_rows = pose_maps.shape[1] // 2
    out_cols = pose_maps.shape[2] // 2
    frame_ids = first_frame + jnp.arange(frames_dev, dtype=jnp.int32)
    starts_here = lax.dynamic_slice_in_dim(start_of, first_frame, frames_dev)
    tap_list = []
    for step_a in range(3):
        keep_mask = (frame_ids - 2 + step_a >= starts_here).astype(pose_maps.dtype)[
            :, None, None, None
        ]
        frames_tap = extended[step_a : step_a + frames_dev] * keep_mask
        for step_b in range(3):
            for step_e in range(3):
                tap_list.append(
                    frames_tap[
                        :,
                        step_b : step_b + 2 * out_rows - 1 : 2,
                        step_e : step_e + 2 * out_cols - 1 : 2,
                    ]
                )
    stacked = jnp.concatenate(tap_list, axis=3)
    kernel = conv_weight.reshape(-1, conv_weight.shape[-1])
    summed = jnp.dot(stacked, kernel, preferred_element_type=jnp.float32) + conv_bias
    feature = jax.nn.silu(summed).astype(jnp.bfloat16)
    guided = latent.astype(jnp.float32) + jnp.dot(
        feature, pose_proj, preferred_element_type=jnp.float32
    )
    return guided.astype(jnp.bfloat16)


def attend_rows(queries, query_clip, query_block, keyvals, clip_of, block_ids):
    heads_dev = queries.shape[1]
    rows_query = queries.shape[0]
    head_size = queries.shape[2]
    score_scale = head_size ** (-0.5)
    start_carry = (
        jnp.full((heads_dev, rows_query), NEG_FILL, jnp.float32),
        jnp.zeros((heads_dev, rows_query), jnp.float32),
        jnp.zeros((heads_dev, rows_query, head_size), jnp.float32),
    )

    def one_frame(running, frame_item):
        frame_kv, frame_id = frame_item
        key_clip = clip_of[frame_id]
        key_block = block_ids[frame_id]
        visible = (query_clip == key_clip) & (key_block <= query_block)
        run_max, run_total, run_acc = running
        scores = (
            jnp.einsum(
                "qhd,khd->hqk", queries, frame_kv[:, :, 0], preferred_element_type=jnp.float32
            )
            * score_scale
        )
        scores = jnp.where(visible[None, :, None], scores, NEG_FILL)
        new_max = jnp.maximum(run_max, jnp.max(scores, axis=2))
        factor = jnp.exp(run_max - new_max)
        weights = jnp.where(visible[None, :, None], jnp.exp(scores - new_max[:, :, None]), 0.0)
        new_total = run_total * factor + jnp.sum(weights, axis=2)
        new_acc = run_acc * factor[:, :, None] + jnp.einsum(
            "hqk,khd->hqd",
            weights.astype(jnp.bfloat16),
            frame_kv[:, :, 1],
            preferred_element_type=jnp.float32,
        )
        running = (new_max, new_total, new_acc)
        return (running, None)

    running = start_carry
    shard_piece = lax.all_gather(keyvals, "frame", axis=0, tiled=True)
    piece_frames = shard_piece.shape[0]
    frame_list = jnp.arange(piece_frames, dtype=jnp.int32)
    running, unused = lax.scan(one_frame, running, (shard_piece, frame_list))
    run_max, run_total, run_acc = running
    normalized = run_acc / run_total[:, :, None]
    return jnp.transpose(normalized, (1, 0, 2)).astype(jnp.bfloat16)


def plain_shards(
    latent, pose_maps, conv_weight, conv_bias, pose_proj, w_qkv, w_out, clip_lengths, block_ids
):
    frame_count = block_ids.shape[0]
    clip_of, start_of = frame_tables(clip_lengths, frame_count)
    frames_dev = latent.shape[0]
    first_frame = lax.axis_index("frame") * frames_dev
    guided = guide_features(
        latent, pose_maps, conv_weight, conv_bias, pose_proj, start_of, first_frame
    )
    whole_rows = lax.all_gather(guided, "head", axis=1, tiled=True)
    height = whole_rows.shape[1]
    width_grid = whole_rows.shape[2]
    model_width = whole_rows.shape[3]
    flat_tokens = whole_rows.reshape(-1, model_width)
    qkv_local = w_qkv.reshape(w_qkv.shape[0], -1)
    projected = jnp.dot(
        flat_tokens,
        lax.all_gather(qkv_local, "frame", axis=0, tiled=True),
        preferred_element_type=jnp.float32,
    ).astype(jnp.bfloat16)
    per_frame = height * width_grid
    heads_dev = w_qkv.shape[1]
    head_size = w_qkv.shape[3]
    grouped = projected.reshape(frames_dev, per_frame, heads_dev, 3, head_size)
    rows_total = frames_dev * per_frame
    queries = grouped[:, :, :, 0].reshape(rows_total, heads_dev, head_size)
    keyvals = grouped[:, :, :, 1:3]
    clip_rows = lax.dynamic_slice_in_dim(clip_of, first_frame, frames_dev)
    block_rows = lax.dynamic_slice_in_dim(block_ids, first_frame, frames_dev)
    query_clip = jnp.repeat(clip_rows, per_frame)
    query_block = jnp.repeat(block_rows, per_frame)
    attended = attend_rows(queries, query_clip, query_block, keyvals, clip_of, block_ids)
    by_row = attended.reshape(frames_dev, height, width_grid, heads_dev * head_size)
    by_row = jnp.transpose(by_row, (1, 0, 2, 3)).reshape(
        height, frames_dev * width_grid, heads_dev * head_size
    )
    out_weight = w_out.reshape(heads_dev * head_size, w_out.shape[2])
    rows_here = height // lax.axis_size("head")
    summed_rows = lax.psum_scatter(
        jnp.dot(by_row, out_weight, preferred_element_type=jnp.float32).astype(jnp.bfloat16),
        "head",
        scatter_dimension=0,
        tiled=True,
    ).astype(jnp.float32)
    summed_rows = summed_rows.reshape(rows_here, frames_dev, width_grid, out_weight.shape[1])
    return jnp.transpose(summed_rows, (1, 0, 2, 3)).astype(jnp.bfloat16)


def turn(value, axis, steps):
    count = lax.axis_size(axis)
    return lax.ppermute(value, axis, [(i, (i + steps) % count) for i in range(count)])


def across(value, axis, bits):
    count = lax.axis_size(axis)
    return lax.ppermute(value, axis, [(i, i ^ bits) for i in range(count)])


def hop(lower, upper, axis, s):
    count = lax.axis_size(axis)
    lower = lax.ppermute(lower, axis, [(i, i + 1) for i in range(s - 1, count - 1)])
    upper = lax.ppermute(upper, axis, [(i, i - 1) for i in range(1, count - s + 1)])
    return lower, upper


def after(value, *others):
    def body(*refs):
        del refs

    anywhere = pl.BlockSpec(memory_space=pl.ANY)
    return pl.pallas_call(
        body,
        out_shape=jax.ShapeDtypeStruct(value.shape, value.dtype),
        in_specs=[anywhere] * (1 + len(others)),
        out_specs=anywhere,
        input_output_aliases={0: 0},
        name="after",
    )(value, *others)


def take_block(weight, row, column, shape, *ready):
    def body(at_ref, weight_ref, *refs):
        refs[-1][...] = weight_ref[...]

    return pl.pallas_call(
        body,
        out_shape=jax.ShapeDtypeStruct(shape, weight.dtype),
        grid_spec=pltpu.PrefetchScalarGridSpec(
            num_scalar_prefetch=1,
            grid=(1,),
            in_specs=[pl.BlockSpec(shape, lambda i, at: (at[0], at[1]))]
            + [pl.BlockSpec(memory_space=pl.ANY)] * len(ready),
            out_specs=pl.BlockSpec(shape, lambda i, at: (0, 0)),
        ),
        cost_estimate=cost(0, 4 * shape[0] * shape[1]),
        name="take_block",
    )(jnp.stack([row, column]), weight, *ready)


def conv_kernel(keep_ref, cols_ref, weight_ref, bias_ref, out_ref, acc_ref):
    step = pl.program_id(0)
    tap_a, tap_b = step // 3, step % 3
    frames, strip_rows, width = out_ref.shape[0], out_ref.shape[1], cols_ref.shape[2]
    pieces = []
    for t in range(frames):
        keep = keep_ref[tap_a * frames + t]
        for r in range(strip_rows):
            rows = cols_ref[tap_a + t, tap_b + 2 * r].astype(F32)
            pieces.append(jnp.where(keep > 0, rows, 0.0))
    lhs = jnp.concatenate(pieces, axis=0).astype(BF16)
    channels = weight_ref.shape[3]
    total = None
    for e in range(3):
        part = lax.dot_general(
            lhs[:, e * channels : (e + 1) * channels],
            weight_ref[0, e],
            (((1,), (1,)), ((), ())),
            preferred_element_type=F32,
        )
        total = part if total is None else total + part

    @pl.when(step == 0)
    def _():
        acc_ref[...] = total

    @pl.when(step > 0)
    def _():
        acc_ref[...] += total

    @pl.when(step == 8)
    def _():
        summed = acc_ref[...] + bias_ref[...]
        feature = summed / (1.0 + jnp.exp(-summed))
        for t in range(frames):
            for r in range(strip_rows):
                at = (t * strip_rows + r) * width
                out_ref[t, r] = feature[at : at + width].astype(BF16)


def pose_feature(extended, conv_weight, conv_bias, start_of, first_frame):
    frames, rows, columns, channels = extended.shape
    frames, rows = frames // 2, rows - 1
    out_channels = conv_weight.shape[-1]
    pairs = extended.reshape(2 * frames, rows + 1, columns // 2, 2 * channels)
    before = jnp.pad(pairs[:, :, :-1, channels:], ((0, 0), (0, 0), (1, 0), (0, 0)))
    cols = jnp.concatenate([before, pairs], axis=3)
    taps = jnp.transpose(conv_weight, (0, 1, 2, 4, 3)).reshape(9, 3, out_channels, channels)
    frame_ids = first_frame + jnp.arange(frames, dtype=jnp.int32)
    starts_here = lax.dynamic_slice_in_dim(start_of, first_frame, frames)
    keep = (frame_ids[None, :] - 2 + jnp.arange(3, dtype=jnp.int32)[:, None] >= starts_here[None, :])
    keep = keep.astype(jnp.int32).reshape(-1)
    out_shape = (frames, rows // 2, columns // 2, out_channels)
    tokens = frames * (rows // 2) * (columns // 2)
    feature = pl.pallas_call(
        conv_kernel,
        out_shape=jax.ShapeDtypeStruct(out_shape, BF16),
        grid_spec=pltpu.PrefetchScalarGridSpec(
            num_scalar_prefetch=1,
            grid=(9,),
            in_specs=[
                pl.BlockSpec(cols.shape, lambda i, k: (0, 0, 0, 0)),
                pl.BlockSpec((1, 3, out_channels, channels), lambda i, k: (i, 0, 0, 0)),
                pl.BlockSpec((1, out_channels), lambda i, k: (0, 0)),
            ],
            out_specs=pl.BlockSpec(out_shape, lambda i, k: (0, 0, 0, 0)),
            scratch_shapes=[pltpu.VMEM((tokens, out_channels), F32)],
        ),
        compiler_params=pltpu.CompilerParams(vmem_limit_bytes=24 * MIB),
        cost_estimate=cost(tokens * out_channels, 2 * tokens * out_channels),
        name="pose_conv",
    )(keep, cols, taps, conv_bias.reshape(1, -1))
    return feature.reshape(tokens, out_channels)


def project(own, lower, upper, features, pose_proj, order, shards_of, total, frames):
    strips = len(features)
    tokens = own.shape[0]
    channels = pose_proj.shape[0]
    rows = strips * tokens
    per_frame = tokens // frames
    steps = len(shards_of)
    flat = [array for kind, arrays in shards_of for array in arrays]
    size = flat[0].shape[2]
    columns = 3 * (PLANE + 1)
    heads = PLANE + 1
    depth = own.shape[1] // PLANE
    cuts = [(c, min(c + 4, columns)) for c in range(0, columns, 4)]
    parts = 2 if shards_of[0][0] == "rows" else 1
    slots = min(2, steps)

    def body(order_ref, *refs):
        own_ref, lower_refs, upper_refs = refs[0], refs[1:strips], refs[strips : 2 * strips - 1]
        feature_refs = refs[2 * strips - 1 : 3 * strips - 1]
        proj_ref = refs[3 * strips - 1]
        source_refs = refs[3 * strips : 3 * strips + len(flat)]
        rest = refs[3 * strips + len(flat) :]
        held_ref, guided_ref, sems = rest[-3:]
        if total is None:
            sum_ref = rest[0]
        else:
            total_ref, last_ref, sum_ref = rest[0], rest[1 + PLANE], rest[2 + PLANE]
            message_refs = rest[1 : 1 + PLANE]
        step = pl.program_id(0)

        def fetch(k, n, part):
            low, high = cuts[n]
            kind, arrays = shards_of[k]
            base = sum(len(other) for unused, other in shards_of[:k])
            length, at, shift = depth // parts, 0, 0
            if kind != "whole" and low >= FIRST_COLUMNS:
                base, shift = base + 1, FIRST_COLUMNS
            if kind == "rows":
                base += 2 * part
                at = pl.multiple_of((order_ref[steps + 1] ^ part) * length, 128)
            return pltpu.make_async_copy(
                source_refs[base].at[low - shift : high - shift],
                held_ref.at[k % slots, low:high, pl.ds(at, length)],
                sems.at[k % slots, n, part],
            )

        def start(k):
            for n in range(len(cuts)):
                for part in range(parts):
                    fetch(k, n, part).start()

        for k in range(steps):

            @pl.when(step == max(k - 1, 0))
            def _(k=k):
                start(k)

        feature = jnp.concatenate([ref[...] for ref in feature_refs], axis=0)
        added = jnp.dot(feature, proj_ref[...], preferred_element_type=F32)
        for s in range(strips):
            latent = own_ref[...].astype(F32)
            if s > 0:
                latent = lower_refs[s - 1][...].astype(F32) + upper_refs[strips - s - 1][...].astype(F32)
            guided = (latent + added[s * tokens : (s + 1) * tokens]).astype(BF16)
            for t in range(frames):
                at = (t * strips + s) * per_frame
                guided_ref[at : at + per_frame] = guided[t * per_frame : (t + 1) * per_frame]

        slot = lax.rem(step, slots)
        for n, (low, high) in enumerate(cuts):
            for k in range(steps):

                @pl.when(step == k)
                def _(k=k, n=n):
                    for part in range(parts):
                        fetch(k, n, part).wait()

            rhs = jnp.concatenate([held_ref[slot, c] for c in range(low, high)], axis=1)
            part = jnp.dot(guided_ref[...], rhs, preferred_element_type=F32)
            lanes = slice(low * size, high * size)
            if total is not None:
                sum_ref[:, lanes] = total_ref[:, lanes] + part
                continue

            @pl.when(step == 0)
            def _(lanes=lanes, part=part):
                sum_ref[:, lanes] = part

            @pl.when(step > 0)
            def _(lanes=lanes, part=part):
                sum_ref[:, lanes] += part

        if total is None:
            return
        last = 3 * (heads - 1) * size
        last_ref[...] = sum_ref[:, last : last + size].astype(BF16)
        for r in range(PLANE):
            head = order_ref[steps] ^ r
            for j in range(3):
                at = pl.multiple_of((3 * head + j) * size, size)
                message_refs[r][j] = sum_ref[:, pl.ds(at, size)].astype(BF16)
            for j in range(1, 3):
                at = last + j * size
                message_refs[r][2 + j] = sum_ref[:, at : at + size].astype(BF16)

    piece = pl.BlockSpec((tokens, depth), lambda i, order: (0, order[i]))
    in_specs = [piece] * (2 * strips - 1)
    in_specs += [pl.BlockSpec((tokens, channels), lambda i, order: (0, 0))] * strips
    in_specs += [pl.BlockSpec((channels, depth), lambda i, order: (0, order[i]))]
    in_specs += [pl.BlockSpec(memory_space=pl.ANY)] * len(flat)
    operands = [own, *lower, *upper, *features, pose_proj, *flat]
    sums = pl.BlockSpec((rows, columns * size), lambda i, order: (0, 0))
    scratch = [
        pltpu.VMEM((slots, columns, depth, size), BF16),
        pltpu.VMEM((rows, depth), BF16),
        pltpu.SemaphoreType.DMA((slots, len(cuts), parts)),
    ]
    if total is None:
        out_shape, out_specs = jax.ShapeDtypeStruct((rows, columns * size), F32), sums
    else:
        assert steps == 1
        in_specs.append(sums)
        operands.append(total)
        message = jax.ShapeDtypeStruct((5, rows, size), BF16)
        out_shape = (message,) * PLANE + (jax.ShapeDtypeStruct((rows, size), BF16),)
        out_specs = (pl.BlockSpec((5, rows, size), lambda i, order: (0, 0, 0)),) * PLANE
        out_specs += (pl.BlockSpec((rows, size), lambda i, order: (0, 0)),)
        scratch = [pltpu.VMEM((rows, columns * size), F32)] + scratch
    return pl.pallas_call(
        body,
        out_shape=out_shape,
        grid_spec=pltpu.PrefetchScalarGridSpec(
            num_scalar_prefetch=1, grid=(steps,), in_specs=in_specs, out_specs=out_specs, scratch_shapes=scratch
        ),
        compiler_params=pltpu.CompilerParams(vmem_limit_bytes=40 * MIB),
        cost_estimate=cost(0, 2 * rows * size),
        name="project",
    )(order, *operands)


def attend(messages, last_query, here, spans, frames, strips):
    rows, size = last_query.shape
    per_frame = rows // frames
    strip = per_frame // strips
    frame_count = PLANE * frames
    window = frame_count - 4 if frame_count > 4 else frame_count
    out_rows = (PLANE + 1) * frames * strip
    scale = size ** (-0.5)

    def body(table_ref, *refs):
        message_refs, last_ref = refs[:PLANE], refs[PLANE]
        out_refs, held_ref = refs[PLANE + 1 : PLANE + 1 + strips], refs[-1]
        here_at = table_ref[3 * frame_count]
        for r in range(PLANE):
            for t in range(frames):
                frame = (here_at ^ r) * frames + t
                for j in range(4):
                    held_ref[frame, j] = message_refs[r][j + 1, t * per_frame : (t + 1) * per_frame]

        def one(query, frame, kind, at):
            begin, low, high = table_ref[3 * frame], table_ref[3 * frame + 1], table_ref[3 * frame + 2]
            keys = held_ref[pl.ds(begin, window), kind].reshape(window * per_frame, size)
            values = held_ref[pl.ds(begin, window), kind + 1].reshape(window * per_frame, size)
            scores = lax.dot_general(query, keys, (((1,), (1,)), ((), ())), preferred_element_type=F32)
            place = lax.broadcasted_iota(jnp.int32, (1, window * per_frame), 1)
            seen = (place >= low * per_frame) & (place < high * per_frame)
            scores = jnp.where(seen, scores * scale, NEG_FILL)
            weights = jnp.exp(scores - jnp.max(scores, axis=1, keepdims=True))
            totals = jnp.sum(weights, axis=1, keepdims=True)
            mixed = jnp.dot(weights.astype(BF16), values, preferred_element_type=F32)
            result = (mixed / totals).astype(BF16)
            for s in range(strips):
                out_refs[s][at : at + strip] = result[s * strip : (s + 1) * strip]

        for r in range(PLANE):
            for t in range(frames):
                query = message_refs[r][0, t * per_frame : (t + 1) * per_frame]
                one(query, (here_at ^ r) * frames + t, 0, (r * frames + t) * strip)
        for t in range(frames):
            query = last_ref[t * per_frame : (t + 1) * per_frame]
            one(query, here_at * frames + t, 2, (PLANE * frames + t) * strip)

    table = jnp.concatenate([spans.reshape(-1), here.reshape(1)]).astype(jnp.int32)
    whole = pl.BlockSpec((5, rows, size), lambda i, table: (0, 0, 0))
    units = (PLANE + 1) * frames
    return pl.pallas_call(
        body,
        out_shape=(jax.ShapeDtypeStruct((out_rows, size), BF16),) * strips,
        grid_spec=pltpu.PrefetchScalarGridSpec(
            num_scalar_prefetch=1,
            grid=(1,),
            in_specs=[whole] * PLANE + [pl.BlockSpec((rows, size), lambda i, table: (0, 0))],
            out_specs=(pl.BlockSpec((out_rows, size), lambda i, table: (0, 0)),) * strips,
            scratch_shapes=[pltpu.VMEM((frame_count, 4, per_frame, size), BF16)],
        ),
        compiler_params=pltpu.CompilerParams(vmem_limit_bytes=40 * MIB),
        cost_estimate=cost(0, 2 * rows * size),
        name="attend",
    )(table, *messages, last_query)


def out_project(gathered, weights, here, group, core, tokens):
    groups, depth, columns = weights[0].shape
    size = gathered[0].shape[2]
    heads = depth // size

    def body(at_ref, *refs):
        weight_refs = refs[PLANE + 1 : PLANE + 3]
        out_refs, lhs_ref, sum_ref = refs[PLANE + 3 : -2], refs[-2], refs[-1]
        step = pl.program_id(0)
        def put(q, ref):
            for p in range(PLANE):
                at = (p ^ q) * tokens
                lhs_ref[p * tokens : (p + 1) * tokens, q * size : (q + 1) * size] = ref[0, at : at + tokens]
            lhs_ref[q * tokens : (q + 1) * tokens, PLANE * size :] = ref[0, PLANE * tokens :]

        for q in range(PLANE - 1):
            put(q, refs[q])
        pl.when(step < groups // 2)(lambda: put(PLANE - 1, refs[PLANE - 1]))
        pl.when(step >= groups // 2)(lambda: put(PLANE - 1, refs[PLANE]))
        here_at, core_at = at_ref[0], at_ref[2]
        for c in range(2):
            found = [
                weight_refs[c][0, pl.ds(pl.multiple_of((here_at ^ q) * size, size), size)] for q in range(PLANE)
            ]
            found.append(weight_refs[c][0, PLANE * size : heads * size])
            part = jnp.dot(lhs_ref[...], jnp.concatenate(found, axis=0), preferred_element_type=F32)
            part = part.astype(BF16).astype(F32)

            @pl.when(step == 0)
            def _(c=c, part=part):
                sum_ref[c] = part

            @pl.when(step > 0)
            def _(c=c, part=part):
                sum_ref[c] += part

        @pl.when(step == groups - 1)
        def _():
            for p in range(PLANE):
                for c in range(2):
                    at = pl.multiple_of((core_at ^ c) * columns, 128)
                    out_refs[p][:, pl.ds(at, columns)] = sum_ref[c, p * tokens : (p + 1) * tokens].astype(BF16)

    block = (1,) + gathered[0].shape[1:]
    in_specs = [pl.BlockSpec(block, lambda g, at: (g, 0, 0))] * (PLANE - 1)
    in_specs += [
        pl.BlockSpec(block, lambda g, at: (jnp.minimum(g, groups // 2 - 1), 0, 0)),
        pl.BlockSpec(block, lambda g, at: (jnp.maximum(g - groups // 2, 0), 0, 0)),
    ]
    in_specs += [
        pl.BlockSpec((1, depth, columns), lambda g, at: (lax.rem(at[1] + g, groups), 0, 0))
    ] * 2
    return pl.pallas_call(
        body,
        out_shape=(jax.ShapeDtypeStruct((tokens, 2 * columns), BF16),) * PLANE,
        grid_spec=pltpu.PrefetchScalarGridSpec(
            num_scalar_prefetch=1,
            grid=(groups,),
            in_specs=in_specs,
            out_specs=(pl.BlockSpec((tokens, 2 * columns), lambda g, at: (0, 0)),) * PLANE,
            scratch_shapes=[
                pltpu.VMEM((PLANE * tokens, depth), BF16),
                pltpu.VMEM((2, PLANE * tokens, columns), F32),
            ],
        ),
        compiler_params=pltpu.CompilerParams(vmem_limit_bytes=24 * MIB),
        cost_estimate=cost(0, 4 * PLANE * tokens * columns),
        name="out_project",
    )(jnp.stack([here, group, core]), *gathered, *weights)


def place_columns(pieces, here):
    tokens, columns = pieces[0].shape

    def body(here_ref, *refs):
        for r in range(PLANE):
            at = pl.multiple_of((here_ref[0] ^ r) * columns, 128)
            refs[-1][:, pl.ds(at, columns)] = refs[r][...]

    return pl.pallas_call(
        body,
        out_shape=jax.ShapeDtypeStruct((tokens, PLANE * columns), BF16),
        grid_spec=pltpu.PrefetchScalarGridSpec(
            num_scalar_prefetch=1,
            grid=(1,),
            in_specs=[pl.BlockSpec((tokens, columns), lambda i, here: (0, 0))] * PLANE,
            out_specs=pl.BlockSpec((tokens, PLANE * columns), lambda i, here: (0, 0)),
        ),
        cost_estimate=cost(0, 4 * tokens * PLANE * columns),
        name="place_columns",
    )(here.reshape(1), *pieces)


def shards(
    latent, pose_maps, conv_weight, conv_bias, pose_proj, w_qkv, w_out, clip_lengths, block_ids
):
    frame_count = block_ids.shape[0]
    frames, strip_rows, width_grid, model_width = latent.shape
    heads, head_size = w_qkv.shape[1], w_qkv.shape[3]
    strips = lax.axis_size("head")
    tokens = frames * strip_rows * width_grid
    here = lax.axis_index("frame").astype(jnp.int32)
    group = lax.axis_index("head").astype(jnp.int32)
    core = lax.axis_index("dp").astype(jnp.int32)
    clip_of, start_of = frame_tables(clip_lengths, frame_count)

    weight = jnp.transpose(w_qkv, (1, 2, 0, 3)).reshape(3 * heads, -1, head_size)
    near_pairs = [(2 * f + c, 2 * (f ^ (1 + c)) + c) for f in range(PLANE) for c in range(2)]
    far_pairs = [(2 * f + c, 2 * (f ^ (2 - c)) + c) for f in range(PLANE) for c in range(2)]
    plane_axes = ("frame", "dp")
    near_first = lax.ppermute(weight[:FIRST_COLUMNS], plane_axes, near_pairs)
    near_rest = weight[FIRST_COLUMNS:]
    earlier = shifted(after(pose_maps, near_rest), "frame", 1)

    own = latent.reshape(tokens, model_width)
    lower, upper = hop(own, own, "head", 1)
    lower, upper = [lower], [upper]
    near_rest = after(near_rest, near_first, earlier, lower[0], upper[0])
    near_rest = lax.ppermute(near_rest, plane_axes, near_pairs)
    extended = jnp.concatenate([earlier, pose_maps], axis=0)
    rows_above = shifted(extended[:, -1:], "head", 1)
    extended = jnp.concatenate([rows_above, extended], axis=1)

    columns = model_width // PLANE // 2
    depth = heads * head_size
    out_half = take_block(w_out.reshape(depth, model_width), jnp.int32(0), 2 * here + core, (depth, columns))

    for s in range(2, strips):
        below, above = hop(lower[-1], upper[-1], "head", s)
        if s < strips - 1:
            below, above = after(below, rows_above), after(above, rows_above)
        lower.append(below)
        upper.append(above)
    half_rows = weight.shape[1] // 2
    first_half = lax.dynamic_slice_in_dim(near_first, core * half_rows, half_rows, axis=1)
    near_rest = after(near_rest, lower[1], upper[1], first_half, out_half)
    near = (near_first, near_rest)
    rest_half = lax.dynamic_slice_in_dim(near_rest, core * half_rows, half_rows, axis=1)
    far = tuple(lax.ppermute(part, plane_axes, far_pairs) for part in (first_half, rest_half))
    start_of = after(start_of, rest_half)
    feature = pose_feature(extended, conv_weight, conv_bias, start_of, here * frames)
    features = [feature] + [turn(feature, "head", s) for s in range(1, strips)]
    other = tuple(across(part, "dp", 1) for part in near)
    out_half = after(out_half, lower[-1], upper[-1], *features[1:])

    here_near, here_other, here_far = here ^ (1 + core), here ^ (2 - core), here ^ 3
    order = after(jnp.stack([here, here_near, here_other, here, core]), out_half)
    held = [("whole", (weight,)), ("columns", near), ("columns", other)]
    total = project(own, lower, upper, features, pose_proj, order, held, None, frames)
    far = tuple(after(part, total) for part in far)
    far += tuple(across(part, "dp", 1) for part in far)
    order = jnp.stack([here_far, here, core])
    *messages, last_query = project(
        own, lower, upper, features, pose_proj, order, [("rows", far)], total, frames
    )
    messages = [messages[0]] + [across(messages[r], "frame", r) for r in range(1, PLANE)]

    same_clip = clip_of[:, None] == clip_of[None, :]
    counts = jnp.sum((same_clip & (block_ids[None, :] <= block_ids[:, None])).astype(jnp.int32), axis=1)
    window = frame_count - 4 if frame_count > 4 else frame_count
    begins = jnp.minimum(start_of, frame_count - window)
    spans = jnp.stack([begins, start_of - begins, start_of - begins + counts], axis=1)
    outs = attend(messages, last_query, here, spans, frames, strips)

    out_half = after(lax.all_gather(out_half, "head"), outs[0])
    out_weights = [out_half, across(out_half, "dp", 1)]

    strip_heads = [outs[0]] + [turn(outs[s], "head", -s) for s in range(1, strips)]
    strip_heads = after(jnp.stack(strip_heads), out_weights[1])
    from_x, from_y = across(strip_heads, "frame", 1), across(strip_heads, "frame", 2)
    middle = strips // 2
    gathered = [strip_heads, from_x, from_y]
    gathered += [across(from_y[:middle], "frame", 1), across(from_x[middle:], "frame", 2)]
    done = out_project(gathered, out_weights, here, group, core, tokens)
    mine = [done[0]] + [across(done[r], "frame", r) for r in range(1, PLANE)]
    return place_columns(mine, here).reshape(latent.shape)


def solution(mesh):
    return jax.shard_map(
        shards if mesh.shape["frame"] == PLANE else plain_shards,
        mesh=mesh,
        in_specs=(
            P(("dp", "frame"), "head", None, None),
            P(("dp", "frame"), "head", None, None),
            P(),
            P(),
            P(),
            P("frame", "head", None, None),
            P("head", None, None),
            P("dp"),
            P("dp"),
        ),
        out_specs=P(("dp", "frame"), "head", None, None),
        check_vma=False,
    )
```

```python
import jax
import jax.numpy as jnp
from jax import lax
from jax.experimental import pallas as pl
from jax.experimental.pallas import tpu as pltpu
from jax.sharding import PartitionSpec as P

NEG_FILL = -1e30
MIB = 1 << 20
F32 = jnp.float32
BF16 = jnp.bfloat16
PLANE = 4
FIRST_COLUMNS = 8


def cost(flops, moved, exps=0):
    return pl.CostEstimate(flops=int(flops), bytes_accessed=int(moved), transcendentals=int(exps))


def shifted(value, axis, steps):
    count = lax.axis_size(axis)
    leading, last = (max(0, -steps), min(count, count - steps))
    return lax.ppermute(value, axis, [(source, source + steps) for source in range(leading, last)])


def frame_tables(clip_lengths, frame_count):
    clip_ends = jnp.cumsum(clip_lengths)
    clip_starts = clip_ends - clip_lengths
    frame_index = jnp.arange(frame_count, dtype=jnp.int32)
    clip_of = jnp.sum((frame_index[:, None] >= clip_ends[None, :]).astype(jnp.int32), axis=1)
    clip_match = clip_of[:, None] == jnp.arange(clip_lengths.shape[0], dtype=jnp.int32)[None, :]
    start_of = jnp.sum(jnp.where(clip_match, clip_starts[None, :], 0), axis=1)
    return (clip_of, start_of)


def guide_features(latent, pose_maps, conv_weight, conv_bias, pose_proj, start_of, first_frame):
    frames_dev = pose_maps.shape[0]
    upper_row = shifted(pose_maps[:, -1:], "head", 1)
    rows_ext = jnp.concatenate([upper_row, pose_maps], axis=1)
    left_column = jnp.zeros(rows_ext.shape[:2] + (1, rows_ext.shape[3]), rows_ext.dtype)
    cols_ext = jnp.concatenate([left_column, rows_ext], axis=2)
    earlier = shifted(cols_ext, "frame", 1)
    extended = jnp.concatenate([earlier, cols_ext], axis=0)
    out_rows = pose_maps.shape[1] // 2
    out_cols = pose_maps.shape[2] // 2
    frame_ids = first_frame + jnp.arange(frames_dev, dtype=jnp.int32)
    starts_here = lax.dynamic_slice_in_dim(start_of, first_frame, frames_dev)
    tap_list = []
    for step_a in range(3):
        keep_mask = (frame_ids - 2 + step_a >= starts_here).astype(pose_maps.dtype)[
            :, None, None, None
        ]
        frames_tap = extended[step_a : step_a + frames_dev] * keep_mask
        for step_b in range(3):
            for step_e in range(3):
                tap_list.append(
                    frames_tap[
                        :,
                        step_b : step_b + 2 * out_rows - 1 : 2,
                        step_e : step_e + 2 * out_cols - 1 : 2,
                    ]
                )
    stacked = jnp.concatenate(tap_list, axis=3)
    kernel = conv_weight.reshape(-1, conv_weight.shape[-1])
    summed = jnp.dot(stacked, kernel, preferred_element_type=jnp.float32) + conv_bias
    feature = jax.nn.silu(summed).astype(jnp.bfloat16)
    guided = latent.astype(jnp.float32) + jnp.dot(
        feature, pose_proj, preferred_element_type=jnp.float32
    )
    return guided.astype(jnp.bfloat16)


def attend_rows(queries, query_clip, query_block, keyvals, clip_of, block_ids):
    heads_dev = queries.shape[1]
    rows_query = queries.shape[0]
    head_size = queries.shape[2]
    score_scale = head_size ** (-0.5)
    start_carry = (
        jnp.full((heads_dev, rows_query), NEG_FILL, jnp.float32),
        jnp.zeros((heads_dev, rows_query), jnp.float32),
        jnp.zeros((heads_dev, rows_query, head_size), jnp.float32),
    )

    def one_frame(running, frame_item):
        frame_kv, frame_id = frame_item
        key_clip = clip_of[frame_id]
        key_block = block_ids[frame_id]
        visible = (query_clip == key_clip) & (key_block <= query_block)
        run_max, run_total, run_acc = running
        scores = (
            jnp.einsum(
                "qhd,khd->hqk", queries, frame_kv[:, :, 0], preferred_element_type=jnp.float32
            )
            * score_scale
        )
        scores = jnp.where(visible[None, :, None], scores, NEG_FILL)
        new_max = jnp.maximum(run_max, jnp.max(scores, axis=2))
        factor = jnp.exp(run_max - new_max)
        weights = jnp.where(visible[None, :, None], jnp.exp(scores - new_max[:, :, None]), 0.0)
        new_total = run_total * factor + jnp.sum(weights, axis=2)
        new_acc = run_acc * factor[:, :, None] + jnp.einsum(
            "hqk,khd->hqd",
            weights.astype(jnp.bfloat16),
            frame_kv[:, :, 1],
            preferred_element_type=jnp.float32,
        )
        running = (new_max, new_total, new_acc)
        return (running, None)

    running = start_carry
    shard_piece = lax.all_gather(keyvals, "frame", axis=0, tiled=True)
    piece_frames = shard_piece.shape[0]
    frame_list = jnp.arange(piece_frames, dtype=jnp.int32)
    running, unused = lax.scan(one_frame, running, (shard_piece, frame_list))
    run_max, run_total, run_acc = running
    normalized = run_acc / run_total[:, :, None]
    return jnp.transpose(normalized, (1, 0, 2)).astype(jnp.bfloat16)


def plain_shards(
    latent, pose_maps, conv_weight, conv_bias, pose_proj, w_qkv, w_out, clip_lengths, block_ids
):
    frame_count = block_ids.shape[0]
    clip_of, start_of = frame_tables(clip_lengths, frame_count)
    frames_dev = latent.shape[0]
    first_frame = lax.axis_index("frame") * frames_dev
    guided = guide_features(
        latent, pose_maps, conv_weight, conv_bias, pose_proj, start_of, first_frame
    )
    whole_rows = lax.all_gather(guided, "head", axis=1, tiled=True)
    height = whole_rows.shape[1]
    width_grid = whole_rows.shape[2]
    model_width = whole_rows.shape[3]
    flat_tokens = whole_rows.reshape(-1, model_width)
    qkv_local = w_qkv.reshape(w_qkv.shape[0], -1)
    projected = jnp.dot(
        flat_tokens,
        lax.all_gather(qkv_local, "frame", axis=0, tiled=True),
        preferred_element_type=jnp.float32,
    ).astype(jnp.bfloat16)
    per_frame = height * width_grid
    heads_dev = w_qkv.shape[1]
    head_size = w_qkv.shape[3]
    grouped = projected.reshape(frames_dev, per_frame, heads_dev, 3, head_size)
    rows_total = frames_dev * per_frame
    queries = grouped[:, :, :, 0].reshape(rows_total, heads_dev, head_size)
    keyvals = grouped[:, :, :, 1:3]
    clip_rows = lax.dynamic_slice_in_dim(clip_of, first_frame, frames_dev)
    block_rows = lax.dynamic_slice_in_dim(block_ids, first_frame, frames_dev)
    query_clip = jnp.repeat(clip_rows, per_frame)
    query_block = jnp.repeat(block_rows, per_frame)
    attended = attend_rows(queries, query_clip, query_block, keyvals, clip_of, block_ids)
    by_row = attended.reshape(frames_dev, height, width_grid, heads_dev * head_size)
    by_row = jnp.transpose(by_row, (1, 0, 2, 3)).reshape(
        height, frames_dev * width_grid, heads_dev * head_size
    )
    out_weight = w_out.reshape(heads_dev * head_size, w_out.shape[2])
    rows_here = height // lax.axis_size("head")
    summed_rows = lax.psum_scatter(
        jnp.dot(by_row, out_weight, preferred_element_type=jnp.float32).astype(jnp.bfloat16),
        "head",
        scatter_dimension=0,
        tiled=True,
    ).astype(jnp.float32)
    summed_rows = summed_rows.reshape(rows_here, frames_dev, width_grid, out_weight.shape[1])
    return jnp.transpose(summed_rows, (1, 0, 2, 3)).astype(jnp.bfloat16)


def turn(value, axis, steps):
    count = lax.axis_size(axis)
    return lax.ppermute(value, axis, [(i, (i + steps) % count) for i in range(count)])


def across(value, axis, bits):
    count = lax.axis_size(axis)
    return lax.ppermute(value, axis, [(i, i ^ bits) for i in range(count)])


def hop(lower, upper, axis, s):
    count = lax.axis_size(axis)
    lower = lax.ppermute(lower, axis, [(i, i + 1) for i in range(s - 1, count - 1)])
    upper = lax.ppermute(upper, axis, [(i, i - 1) for i in range(1, count - s + 1)])
    return lower, upper


def after(value, *others):
    def body(*refs):
        del refs

    anywhere = pl.BlockSpec(memory_space=pl.ANY)
    return pl.pallas_call(
        body,
        out_shape=jax.ShapeDtypeStruct(value.shape, value.dtype),
        in_specs=[anywhere] * (1 + len(others)),
        out_specs=anywhere,
        input_output_aliases={0: 0},
        name="after",
    )(value, *others)


def take_block(weight, row, column, shape, *ready):
    def body(at_ref, weight_ref, *refs):
        refs[-1][...] = weight_ref[...]

    return pl.pallas_call(
        body,
        out_shape=jax.ShapeDtypeStruct(shape, weight.dtype),
        grid_spec=pltpu.PrefetchScalarGridSpec(
            num_scalar_prefetch=1,
            grid=(1,),
            in_specs=[pl.BlockSpec(shape, lambda i, at: (at[0], at[1]))]
            + [pl.BlockSpec(memory_space=pl.ANY)] * len(ready),
            out_specs=pl.BlockSpec(shape, lambda i, at: (0, 0)),
        ),
        cost_estimate=cost(0, 4 * shape[0] * shape[1]),
        name="take_block",
    )(jnp.stack([row, column]), weight, *ready)


def conv_kernel(keep_ref, cols_ref, weight_ref, bias_ref, out_ref, acc_ref):
    step = pl.program_id(0)
    tap_a, tap_b = step // 3, step % 3
    frames, strip_rows, width = out_ref.shape[0], out_ref.shape[1], cols_ref.shape[2]
    pieces = []
    for t in range(frames):
        keep = keep_ref[tap_a * frames + t]
        for r in range(strip_rows):
            rows = cols_ref[tap_a + t, tap_b + 2 * r].astype(F32)
            pieces.append(jnp.where(keep > 0, rows, 0.0))
    lhs = jnp.concatenate(pieces, axis=0).astype(BF16)
    channels = weight_ref.shape[3]
    total = None
    for e in range(3):
        part = lax.dot_general(
            lhs[:, e * channels : (e + 1) * channels],
            weight_ref[0, e],
            (((1,), (1,)), ((), ())),
            preferred_element_type=F32,
        )
        total = part if total is None else total + part

    @pl.when(step == 0)
    def _():
        acc_ref[...] = total

    @pl.when(step > 0)
    def _():
        acc_ref[...] += total

    @pl.when(step == 8)
    def _():
        summed = acc_ref[...] + bias_ref[...]
        feature = summed / (1.0 + jnp.exp(-summed))
        for t in range(frames):
            for r in range(strip_rows):
                at = (t * strip_rows + r) * width
                out_ref[t, r] = feature[at : at + width].astype(BF16)


def pose_feature(extended, conv_weight, conv_bias, start_of, first_frame):
    frames, rows, columns, channels = extended.shape
    frames, rows = frames // 2, rows - 1
    out_channels = conv_weight.shape[-1]
    pairs = extended.reshape(2 * frames, rows + 1, columns // 2, 2 * channels)
    before = jnp.pad(pairs[:, :, :-1, channels:], ((0, 0), (0, 0), (1, 0), (0, 0)))
    cols = jnp.concatenate([before, pairs], axis=3)
    taps = jnp.transpose(conv_weight, (0, 1, 2, 4, 3)).reshape(9, 3, out_channels, channels)
    frame_ids = first_frame + jnp.arange(frames, dtype=jnp.int32)
    starts_here = lax.dynamic_slice_in_dim(start_of, first_frame, frames)
    keep = (frame_ids[None, :] - 2 + jnp.arange(3, dtype=jnp.int32)[:, None] >= starts_here[None, :])
    keep = keep.astype(jnp.int32).reshape(-1)
    out_shape = (frames, rows // 2, columns // 2, out_channels)
    tokens = frames * (rows // 2) * (columns // 2)
    feature = pl.pallas_call(
        conv_kernel,
        out_shape=jax.ShapeDtypeStruct(out_shape, BF16),
        grid_spec=pltpu.PrefetchScalarGridSpec(
            num_scalar_prefetch=1,
            grid=(9,),
            in_specs=[
                pl.BlockSpec(cols.shape, lambda i, k: (0, 0, 0, 0)),
                pl.BlockSpec((1, 3, out_channels, channels), lambda i, k: (i, 0, 0, 0)),
                pl.BlockSpec((1, out_channels), lambda i, k: (0, 0)),
            ],
            out_specs=pl.BlockSpec(out_shape, lambda i, k: (0, 0, 0, 0)),
            scratch_shapes=[pltpu.VMEM((tokens, out_channels), F32)],
        ),
        compiler_params=pltpu.CompilerParams(vmem_limit_bytes=24 * MIB),
        cost_estimate=cost(tokens * out_channels, 2 * tokens * out_channels),
        name="pose_conv",
    )(keep, cols, taps, conv_bias.reshape(1, -1))
    return feature.reshape(tokens, out_channels)


def project(own, lower, upper, features, pose_proj, order, shards_of, total, frames):
    strips = len(features)
    tokens = own.shape[0]
    channels = pose_proj.shape[0]
    rows = strips * tokens
    per_frame = tokens // frames
    steps = len(shards_of)
    flat = [array for kind, arrays in shards_of for array in arrays]
    size = flat[0].shape[2]
    columns = 3 * (PLANE + 1)
    heads = PLANE + 1
    depth = own.shape[1] // PLANE
    cuts = [(c, min(c + 4, columns)) for c in range(0, columns, 4)]
    parts = 2 if shards_of[0][0] == "rows" else 1
    slots = min(2, steps)

    def body(order_ref, *refs):
        own_ref, lower_refs, upper_refs = refs[0], refs[1:strips], refs[strips : 2 * strips - 1]
        feature_refs = refs[2 * strips - 1 : 3 * strips - 1]
        proj_ref = refs[3 * strips - 1]
        source_refs = refs[3 * strips : 3 * strips + len(flat)]
        rest = refs[3 * strips + len(flat) :]
        held_ref, guided_ref, sems = rest[-3:]
        if total is None:
            sum_ref = rest[0]
        else:
            total_ref, last_ref, sum_ref = rest[0], rest[1 + PLANE], rest[2 + PLANE]
            message_refs = rest[1 : 1 + PLANE]
        step = pl.program_id(0)

        def fetch(k, n, part):
            low, high = cuts[n]
            kind, arrays = shards_of[k]
            base = sum(len(other) for unused, other in shards_of[:k])
            length, at, shift = depth // parts, 0, 0
            if kind != "whole" and low >= FIRST_COLUMNS:
                base, shift = base + 1, FIRST_COLUMNS
            if kind == "rows":
                base += 2 * part
                at = pl.multiple_of((order_ref[steps + 1] ^ part) * length, 128)
            return pltpu.make_async_copy(
                source_refs[base].at[low - shift : high - shift],
                held_ref.at[k % slots, low:high, pl.ds(at, length)],
                sems.at[k % slots, n, part],
            )

        def start(k):
            for n in range(len(cuts)):
                for part in range(parts):
                    fetch(k, n, part).start()

        for k in range(steps):

            @pl.when(step == max(k - 1, 0))
            def _(k=k):
                start(k)

        feature = jnp.concatenate([ref[...] for ref in feature_refs], axis=0)
        added = jnp.dot(feature, proj_ref[...], preferred_element_type=F32)
        for s in range(strips):
            latent = own_ref[...].astype(F32)
            if s > 0:
                latent = lower_refs[s - 1][...].astype(F32) + upper_refs[strips - s - 1][...].astype(F32)
            guided = (latent + added[s * tokens : (s + 1) * tokens]).astype(BF16)
            for t in range(frames):
                at = (t * strips + s) * per_frame
                guided_ref[at : at + per_frame] = guided[t * per_frame : (t + 1) * per_frame]

        slot = lax.rem(step, slots)
        for n, (low, high) in enumerate(cuts):
            for k in range(steps):

                @pl.when(step == k)
                def _(k=k, n=n):
                    for part in range(parts):
                        fetch(k, n, part).wait()

            rhs = jnp.concatenate([held_ref[slot, c] for c in range(low, high)], axis=1)
            part = jnp.dot(guided_ref[...], rhs, preferred_element_type=F32)
            lanes = slice(low * size, high * size)
            if total is not None:
                sum_ref[:, lanes] = total_ref[:, lanes] + part
                continue

            @pl.when(step == 0)
            def _(lanes=lanes, part=part):
                sum_ref[:, lanes] = part

            @pl.when(step > 0)
            def _(lanes=lanes, part=part):
                sum_ref[:, lanes] += part

        if total is None:
            return
        last = 3 * (heads - 1) * size
        last_ref[...] = sum_ref[:, last : last + size].astype(BF16)
        for r in range(PLANE):
            head = order_ref[steps] ^ r
            for j in range(3):
                at = pl.multiple_of((3 * head + j) * size, size)
                message_refs[r][j] = sum_ref[:, pl.ds(at, size)].astype(BF16)
            for j in range(1, 3):
                at = last + j * size
                message_refs[r][2 + j] = sum_ref[:, at : at + size].astype(BF16)

    piece = pl.BlockSpec((tokens, depth), lambda i, order: (0, order[i]))
    in_specs = [piece] * (2 * strips - 1)
    in_specs += [pl.BlockSpec((tokens, channels), lambda i, order: (0, 0))] * strips
    in_specs += [pl.BlockSpec((channels, depth), lambda i, order: (0, order[i]))]
    in_specs += [pl.BlockSpec(memory_space=pl.ANY)] * len(flat)
    operands = [own, *lower, *upper, *features, pose_proj, *flat]
    sums = pl.BlockSpec((rows, columns * size), lambda i, order: (0, 0))
    scratch = [
        pltpu.VMEM((slots, columns, depth, size), BF16),
        pltpu.VMEM((rows, depth), BF16),
        pltpu.SemaphoreType.DMA((slots, len(cuts), parts)),
    ]
    if total is None:
        out_shape, out_specs = jax.ShapeDtypeStruct((rows, columns * size), F32), sums
    else:
        assert steps == 1
        in_specs.append(sums)
        operands.append(total)
        message = jax.ShapeDtypeStruct((5, rows, size), BF16)
        out_shape = (message,) * PLANE + (jax.ShapeDtypeStruct((rows, size), BF16),)
        out_specs = (pl.BlockSpec((5, rows, size), lambda i, order: (0, 0, 0)),) * PLANE
        out_specs += (pl.BlockSpec((rows, size), lambda i, order: (0, 0)),)
        scratch = [pltpu.VMEM((rows, columns * size), F32)] + scratch
    return pl.pallas_call(
        body,
        out_shape=out_shape,
        grid_spec=pltpu.PrefetchScalarGridSpec(
            num_scalar_prefetch=1, grid=(steps,), in_specs=in_specs, out_specs=out_specs, scratch_shapes=scratch
        ),
        compiler_params=pltpu.CompilerParams(vmem_limit_bytes=40 * MIB),
        cost_estimate=cost(0, 2 * rows * size),
        name="project",
    )(order, *operands)


def attend(messages, last_query, here, spans, frames, strips):
    rows, size = last_query.shape
    per_frame = rows // frames
    strip = per_frame // strips
    frame_count = PLANE * frames
    window = frame_count - 4 if frame_count > 4 else frame_count
    out_rows = (PLANE + 1) * frames * strip
    scale = size ** (-0.5)

    def body(table_ref, *refs):
        message_refs, last_ref = refs[:PLANE], refs[PLANE]
        out_refs, held_ref = refs[PLANE + 1 : PLANE + 1 + strips], refs[-1]
        here_at = table_ref[3 * frame_count]
        for r in range(PLANE):
            for t in range(frames):
                frame = (here_at ^ r) * frames + t
                for j in range(4):
                    held_ref[frame, j] = message_refs[r][j + 1, t * per_frame : (t + 1) * per_frame]

        def one(query, frame, kind, at):
            begin, low, high = table_ref[3 * frame], table_ref[3 * frame + 1], table_ref[3 * frame + 2]
            keys = held_ref[pl.ds(begin, window), kind].reshape(window * per_frame, size)
            values = held_ref[pl.ds(begin, window), kind + 1].reshape(window * per_frame, size)
            scores = lax.dot_general(query, keys, (((1,), (1,)), ((), ())), preferred_element_type=F32)
            place = lax.broadcasted_iota(jnp.int32, (1, window * per_frame), 1)
            seen = (place >= low * per_frame) & (place < high * per_frame)
            scores = jnp.where(seen, scores * scale, NEG_FILL)
            weights = jnp.exp(scores - jnp.max(scores, axis=1, keepdims=True))
            totals = jnp.sum(weights, axis=1, keepdims=True)
            mixed = jnp.dot(weights.astype(BF16), values, preferred_element_type=F32)
            result = (mixed / totals).astype(BF16)
            for s in range(strips):
                out_refs[s][at : at + strip] = result[s * strip : (s + 1) * strip]

        for r in range(PLANE):
            for t in range(frames):
                query = message_refs[r][0, t * per_frame : (t + 1) * per_frame]
                one(query, (here_at ^ r) * frames + t, 0, (r * frames + t) * strip)
        for t in range(frames):
            query = last_ref[t * per_frame : (t + 1) * per_frame]
            one(query, here_at * frames + t, 2, (PLANE * frames + t) * strip)

    table = jnp.concatenate([spans.reshape(-1), here.reshape(1)]).astype(jnp.int32)
    whole = pl.BlockSpec((5, rows, size), lambda i, table: (0, 0, 0))
    units = (PLANE + 1) * frames
    return pl.pallas_call(
        body,
        out_shape=(jax.ShapeDtypeStruct((out_rows, size), BF16),) * strips,
        grid_spec=pltpu.PrefetchScalarGridSpec(
            num_scalar_prefetch=1,
            grid=(1,),
            in_specs=[whole] * PLANE + [pl.BlockSpec((rows, size), lambda i, table: (0, 0))],
            out_specs=(pl.BlockSpec((out_rows, size), lambda i, table: (0, 0)),) * strips,
            scratch_shapes=[pltpu.VMEM((frame_count, 4, per_frame, size), BF16)],
        ),
        compiler_params=pltpu.CompilerParams(vmem_limit_bytes=40 * MIB),
        cost_estimate=cost(0, 2 * rows * size),
        name="attend",
    )(table, *messages, last_query)


def out_project(gathered, weights, here, group, core, tokens):
    groups, depth, columns = weights[0].shape
    size = gathered[0].shape[2]
    heads = depth // size

    def body(at_ref, *refs):
        weight_refs = refs[PLANE : PLANE + 2]
        out_refs, lhs_ref, sum_ref = refs[PLANE + 2 : -2], refs[-2], refs[-1]
        step = pl.program_id(0)
        for p in range(PLANE):
            rows = slice(p * tokens, (p + 1) * tokens)
            for q in range(PLANE):
                at = (p ^ q) * tokens
                lhs_ref[rows, q * size : (q + 1) * size] = refs[q][0, at : at + tokens]
            lhs_ref[rows, PLANE * size :] = refs[p][0, PLANE * tokens :]

        here_at, core_at = at_ref[0], at_ref[2]
        for c in range(2):
            found = [
                weight_refs[c][0, pl.ds(pl.multiple_of((here_at ^ q) * size, size), size)] for q in range(PLANE)
            ]
            found.append(weight_refs[c][0, PLANE * size : heads * size])
            part = jnp.dot(lhs_ref[...], jnp.concatenate(found, axis=0), preferred_element_type=F32)
            part = part.astype(BF16).astype(F32)

            @pl.when(step == 0)
            def _(c=c, part=part):
                sum_ref[c] = part

            @pl.when(step > 0)
            def _(c=c, part=part):
                sum_ref[c] += part

        @pl.when(step == groups - 1)
        def _():
            for p in range(PLANE):
                for c in range(2):
                    at = pl.multiple_of((core_at ^ c) * columns, 128)
                    out_refs[p][:, pl.ds(at, columns)] = sum_ref[c, p * tokens : (p + 1) * tokens].astype(BF16)

    in_specs = [pl.BlockSpec((1,) + piece.shape[1:], lambda g, at: (g, 0, 0)) for piece in gathered]
    in_specs += [
        pl.BlockSpec((1, depth, columns), lambda g, at: (lax.rem(at[1] + g, groups), 0, 0))
    ] * 2
    return pl.pallas_call(
        body,
        out_shape=(jax.ShapeDtypeStruct((tokens, 2 * columns), BF16),) * PLANE,
        grid_spec=pltpu.PrefetchScalarGridSpec(
            num_scalar_prefetch=1,
            grid=(groups,),
            in_specs=in_specs,
            out_specs=(pl.BlockSpec((tokens, 2 * columns), lambda g, at: (0, 0)),) * PLANE,
            scratch_shapes=[
                pltpu.VMEM((PLANE * tokens, depth), BF16),
                pltpu.VMEM((2, PLANE * tokens, columns), F32),
            ],
        ),
        compiler_params=pltpu.CompilerParams(vmem_limit_bytes=24 * MIB),
        cost_estimate=cost(0, 4 * PLANE * tokens * columns),
        name="out_project",
    )(jnp.stack([here, group, core]), *gathered, *weights)


def place_columns(pieces, here):
    tokens, columns = pieces[0].shape

    def body(here_ref, *refs):
        for r in range(PLANE):
            at = pl.multiple_of((here_ref[0] ^ r) * columns, 128)
            refs[-1][:, pl.ds(at, columns)] = refs[r][...]

    return pl.pallas_call(
        body,
        out_shape=jax.ShapeDtypeStruct((tokens, PLANE * columns), BF16),
        grid_spec=pltpu.PrefetchScalarGridSpec(
            num_scalar_prefetch=1,
            grid=(1,),
            in_specs=[pl.BlockSpec((tokens, columns), lambda i, here: (0, 0))] * PLANE,
            out_specs=pl.BlockSpec((tokens, PLANE * columns), lambda i, here: (0, 0)),
        ),
        cost_estimate=cost(0, 4 * tokens * PLANE * columns),
        name="place_columns",
    )(here.reshape(1), *pieces)


def shards(
    latent, pose_maps, conv_weight, conv_bias, pose_proj, w_qkv, w_out, clip_lengths, block_ids
):
    frame_count = block_ids.shape[0]
    frames, strip_rows, width_grid, model_width = latent.shape
    heads, head_size = w_qkv.shape[1], w_qkv.shape[3]
    strips = lax.axis_size("head")
    tokens = frames * strip_rows * width_grid
    here = lax.axis_index("frame").astype(jnp.int32)
    group = lax.axis_index("head").astype(jnp.int32)
    core = lax.axis_index("dp").astype(jnp.int32)
    clip_of, start_of = frame_tables(clip_lengths, frame_count)

    weight = jnp.transpose(w_qkv, (1, 2, 0, 3)).reshape(3 * heads, -1, head_size)
    near_pairs = [(2 * f + c, 2 * (f ^ (1 + c)) + c) for f in range(PLANE) for c in range(2)]
    far_pairs = [(2 * f + c, 2 * (f ^ (2 - c)) + c) for f in range(PLANE) for c in range(2)]
    plane_axes = ("frame", "dp")
    earlier = shifted(pose_maps, "frame", 1)
    near_first = lax.ppermute(after(weight[:FIRST_COLUMNS], earlier), plane_axes, near_pairs)
    near_rest = lax.ppermute(after(weight[FIRST_COLUMNS:], earlier), plane_axes, near_pairs)

    own = latent.reshape(tokens, model_width)
    lower, upper = hop(own, own, "head", 1)
    extended = jnp.concatenate([earlier, pose_maps], axis=0)
    rows_above = shifted(extended[:, -1:], "head", 1)
    extended = jnp.concatenate([rows_above, extended], axis=1)
    lower, upper = [after(lower, rows_above)], [after(upper, rows_above)]

    columns = model_width // PLANE // 2
    depth = heads * head_size
    out_half = take_block(w_out.reshape(depth, model_width), jnp.int32(0), 2 * here + core, (depth, columns))

    start_of = after(start_of, lower[0], upper[0], out_half)
    feature = pose_feature(extended, conv_weight, conv_bias, start_of, here * frames)
    features = [feature] + [turn(feature, "head", s) for s in range(1, strips)]
    half_rows = weight.shape[1] // 2
    first_half = lax.dynamic_slice_in_dim(near_first, core * half_rows, half_rows, axis=1)
    for s in range(2, strips):
        below, above = hop(lower[-1], upper[-1], "head", s)
        if s < strips - 1:
            below, above = after(below, *features[1:], first_half), after(above, *features[1:])
        lower.append(below)
        upper.append(above)
    near_rest = after(near_rest, lower[1], upper[1])
    near = (near_first, near_rest)
    rest_half = lax.dynamic_slice_in_dim(near_rest, core * half_rows, half_rows, axis=1)
    far = tuple(lax.ppermute(part, plane_axes, far_pairs) for part in (first_half, rest_half))
    other = tuple(across(part, "dp", 1) for part in near)
    out_half = after(out_half, lower[-1], upper[-1])

    here_near, here_other, here_far = here ^ (1 + core), here ^ (2 - core), here ^ 3
    order = after(jnp.stack([here, here_near, here_other, here, core]), out_half)
    held = [("whole", (weight,)), ("columns", near), ("columns", other)]
    total = project(own, lower, upper, features, pose_proj, order, held, None, frames)
    far = tuple(after(part, total) for part in far)
    far += tuple(across(part, "dp", 1) for part in far)
    order = jnp.stack([here_far, here, core])
    *messages, last_query = project(
        own, lower, upper, features, pose_proj, order, [("rows", far)], total, frames
    )
    messages = [messages[0]] + [across(messages[r], "frame", r) for r in range(1, PLANE)]

    same_clip = clip_of[:, None] == clip_of[None, :]
    counts = jnp.sum((same_clip & (block_ids[None, :] <= block_ids[:, None])).astype(jnp.int32), axis=1)
    window = frame_count - 4 if frame_count > 4 else frame_count
    begins = jnp.minimum(start_of, frame_count - window)
    spans = jnp.stack([begins, start_of - begins, start_of - begins + counts], axis=1)
    outs = attend(messages, last_query, here, spans, frames, strips)

    out_half = after(lax.all_gather(out_half, "head"), outs[0])
    out_weights = [out_half, across(out_half, "dp", 1)]

    strip_heads = [outs[0]] + [turn(outs[s], "head", -s) for s in range(1, strips)]
    strip_heads = after(jnp.stack(strip_heads), out_weights[1])
    gathered = [strip_heads] + [across(strip_heads, "frame", r) for r in range(1, PLANE)]
    done = out_project(gathered, out_weights, here, group, core, tokens)
    mine = [done[0]] + [across(done[r], "frame", r) for r in range(1, PLANE)]
    return place_columns(mine, here).reshape(latent.shape)


def solution(mesh):
    return jax.shard_map(
        shards if mesh.shape["frame"] == PLANE else plain_shards,
        mesh=mesh,
        in_specs=(
            P(("dp", "frame"), "head", None, None),
            P(("dp", "frame"), "head", None, None),
            P(),
            P(),
            P(),
            P("frame", "head", None, None),
            P("head", None, None),
            P("dp"),
            P("dp"),
        ),
        out_specs=P(("dp", "frame"), "head", None, None),
        check_vma=False,
    )
```

```python
import jax
import jax.numpy as jnp
from jax import lax
from jax.experimental import pallas as pl
from jax.experimental.pallas import tpu as pltpu
from jax.sharding import PartitionSpec as P

NEG_FILL = -1e30
MIB = 1 << 20
F32 = jnp.float32
BF16 = jnp.bfloat16
PLANE = 4
FIRST_COLUMNS = 8


def cost(flops, moved, exps=0):
    return pl.CostEstimate(flops=int(flops), bytes_accessed=int(moved), transcendentals=int(exps))


def shifted(value, axis, steps):
    count = lax.axis_size(axis)
    leading, last = (max(0, -steps), min(count, count - steps))
    return lax.ppermute(value, axis, [(source, source + steps) for source in range(leading, last)])


def frame_tables(clip_lengths, frame_count):
    clip_ends = jnp.cumsum(clip_lengths)
    clip_starts = clip_ends - clip_lengths
    frame_index = jnp.arange(frame_count, dtype=jnp.int32)
    clip_of = jnp.sum((frame_index[:, None] >= clip_ends[None, :]).astype(jnp.int32), axis=1)
    clip_match = clip_of[:, None] == jnp.arange(clip_lengths.shape[0], dtype=jnp.int32)[None, :]
    start_of = jnp.sum(jnp.where(clip_match, clip_starts[None, :], 0), axis=1)
    return (clip_of, start_of)


def guide_features(latent, pose_maps, conv_weight, conv_bias, pose_proj, start_of, first_frame):
    frames_dev = pose_maps.shape[0]
    upper_row = shifted(pose_maps[:, -1:], "head", 1)
    rows_ext = jnp.concatenate([upper_row, pose_maps], axis=1)
    left_column = jnp.zeros(rows_ext.shape[:2] + (1, rows_ext.shape[3]), rows_ext.dtype)
    cols_ext = jnp.concatenate([left_column, rows_ext], axis=2)
    earlier = shifted(cols_ext, "frame", 1)
    extended = jnp.concatenate([earlier, cols_ext], axis=0)
    out_rows = pose_maps.shape[1] // 2
    out_cols = pose_maps.shape[2] // 2
    frame_ids = first_frame + jnp.arange(frames_dev, dtype=jnp.int32)
    starts_here = lax.dynamic_slice_in_dim(start_of, first_frame, frames_dev)
    tap_list = []
    for step_a in range(3):
        keep_mask = (frame_ids - 2 + step_a >= starts_here).astype(pose_maps.dtype)[
            :, None, None, None
        ]
        frames_tap = extended[step_a : step_a + frames_dev] * keep_mask
        for step_b in range(3):
            for step_e in range(3):
                tap_list.append(
                    frames_tap[
                        :,
                        step_b : step_b + 2 * out_rows - 1 : 2,
                        step_e : step_e + 2 * out_cols - 1 : 2,
                    ]
                )
    stacked = jnp.concatenate(tap_list, axis=3)
    kernel = conv_weight.reshape(-1, conv_weight.shape[-1])
    summed = jnp.dot(stacked, kernel, preferred_element_type=jnp.float32) + conv_bias
    feature = jax.nn.silu(summed).astype(jnp.bfloat16)
    guided = latent.astype(jnp.float32) + jnp.dot(
        feature, pose_proj, preferred_element_type=jnp.float32
    )
    return guided.astype(jnp.bfloat16)


def attend_rows(queries, query_clip, query_block, keyvals, clip_of, block_ids):
    heads_dev = queries.shape[1]
    rows_query = queries.shape[0]
    head_size = queries.shape[2]
    score_scale = head_size ** (-0.5)
    start_carry = (
        jnp.full((heads_dev, rows_query), NEG_FILL, jnp.float32),
        jnp.zeros((heads_dev, rows_query), jnp.float32),
        jnp.zeros((heads_dev, rows_query, head_size), jnp.float32),
    )

    def one_frame(running, frame_item):
        frame_kv, frame_id = frame_item
        key_clip = clip_of[frame_id]
        key_block = block_ids[frame_id]
        visible = (query_clip == key_clip) & (key_block <= query_block)
        run_max, run_total, run_acc = running
        scores = (
            jnp.einsum(
                "qhd,khd->hqk", queries, frame_kv[:, :, 0], preferred_element_type=jnp.float32
            )
            * score_scale
        )
        scores = jnp.where(visible[None, :, None], scores, NEG_FILL)
        new_max = jnp.maximum(run_max, jnp.max(scores, axis=2))
        factor = jnp.exp(run_max - new_max)
        weights = jnp.where(visible[None, :, None], jnp.exp(scores - new_max[:, :, None]), 0.0)
        new_total = run_total * factor + jnp.sum(weights, axis=2)
        new_acc = run_acc * factor[:, :, None] + jnp.einsum(
            "hqk,khd->hqd",
            weights.astype(jnp.bfloat16),
            frame_kv[:, :, 1],
            preferred_element_type=jnp.float32,
        )
        running = (new_max, new_total, new_acc)
        return (running, None)

    running = start_carry
    shard_piece = lax.all_gather(keyvals, "frame", axis=0, tiled=True)
    piece_frames = shard_piece.shape[0]
    frame_list = jnp.arange(piece_frames, dtype=jnp.int32)
    running, unused = lax.scan(one_frame, running, (shard_piece, frame_list))
    run_max, run_total, run_acc = running
    normalized = run_acc / run_total[:, :, None]
    return jnp.transpose(normalized, (1, 0, 2)).astype(jnp.bfloat16)


def plain_shards(
    latent, pose_maps, conv_weight, conv_bias, pose_proj, w_qkv, w_out, clip_lengths, block_ids
):
    frame_count = block_ids.shape[0]
    clip_of, start_of = frame_tables(clip_lengths, frame_count)
    frames_dev = latent.shape[0]
    first_frame = lax.axis_index("frame") * frames_dev
    guided = guide_features(
        latent, pose_maps, conv_weight, conv_bias, pose_proj, start_of, first_frame
    )
    whole_rows = lax.all_gather(guided, "head", axis=1, tiled=True)
    height = whole_rows.shape[1]
    width_grid = whole_rows.shape[2]
    model_width = whole_rows.shape[3]
    flat_tokens = whole_rows.reshape(-1, model_width)
    qkv_local = w_qkv.reshape(w_qkv.shape[0], -1)
    projected = jnp.dot(
        flat_tokens,
        lax.all_gather(qkv_local, "frame", axis=0, tiled=True),
        preferred_element_type=jnp.float32,
    ).astype(jnp.bfloat16)
    per_frame = height * width_grid
    heads_dev = w_qkv.shape[1]
    head_size = w_qkv.shape[3]
    grouped = projected.reshape(frames_dev, per_frame, heads_dev, 3, head_size)
    rows_total = frames_dev * per_frame
    queries = grouped[:, :, :, 0].reshape(rows_total, heads_dev, head_size)
    keyvals = grouped[:, :, :, 1:3]
    clip_rows = lax.dynamic_slice_in_dim(clip_of, first_frame, frames_dev)
    block_rows = lax.dynamic_slice_in_dim(block_ids, first_frame, frames_dev)
    query_clip = jnp.repeat(clip_rows, per_frame)
    query_block = jnp.repeat(block_rows, per_frame)
    attended = attend_rows(queries, query_clip, query_block, keyvals, clip_of, block_ids)
    by_row = attended.reshape(frames_dev, height, width_grid, heads_dev * head_size)
    by_row = jnp.transpose(by_row, (1, 0, 2, 3)).reshape(
        height, frames_dev * width_grid, heads_dev * head_size
    )
    out_weight = w_out.reshape(heads_dev * head_size, w_out.shape[2])
    rows_here = height // lax.axis_size("head")
    summed_rows = lax.psum_scatter(
        jnp.dot(by_row, out_weight, preferred_element_type=jnp.float32).astype(jnp.bfloat16),
        "head",
        scatter_dimension=0,
        tiled=True,
    ).astype(jnp.float32)
    summed_rows = summed_rows.reshape(rows_here, frames_dev, width_grid, out_weight.shape[1])
    return jnp.transpose(summed_rows, (1, 0, 2, 3)).astype(jnp.bfloat16)


def turn(value, axis, steps):
    count = lax.axis_size(axis)
    return lax.ppermute(value, axis, [(i, (i + steps) % count) for i in range(count)])


def across(value, axis, bits):
    count = lax.axis_size(axis)
    return lax.ppermute(value, axis, [(i, i ^ bits) for i in range(count)])


def hop(lower, upper, axis, s):
    count = lax.axis_size(axis)
    lower = lax.ppermute(lower, axis, [(i, i + 1) for i in range(s - 1, count - 1)])
    upper = lax.ppermute(upper, axis, [(i, i - 1) for i in range(1, count - s + 1)])
    return lower, upper


def after(value, *others):
    def body(*refs):
        del refs

    anywhere = pl.BlockSpec(memory_space=pl.ANY)
    return pl.pallas_call(
        body,
        out_shape=jax.ShapeDtypeStruct(value.shape, value.dtype),
        in_specs=[anywhere] * (1 + len(others)),
        out_specs=anywhere,
        input_output_aliases={0: 0},
        name="after",
    )(value, *others)


def take_block(weight, row, column, shape, *ready):
    def body(at_ref, weight_ref, *refs):
        refs[-1][...] = weight_ref[...]

    return pl.pallas_call(
        body,
        out_shape=jax.ShapeDtypeStruct(shape, weight.dtype),
        grid_spec=pltpu.PrefetchScalarGridSpec(
            num_scalar_prefetch=1,
            grid=(1,),
            in_specs=[pl.BlockSpec(shape, lambda i, at: (at[0], at[1]))]
            + [pl.BlockSpec(memory_space=pl.ANY)] * len(ready),
            out_specs=pl.BlockSpec(shape, lambda i, at: (0, 0)),
        ),
        cost_estimate=cost(0, 4 * shape[0] * shape[1]),
        name="take_block",
    )(jnp.stack([row, column]), weight, *ready)


def conv_kernel(keep_ref, cols_ref, weight_ref, bias_ref, out_ref, acc_ref):
    step = pl.program_id(0)
    tap_a, tap_b = step // 3, step % 3
    frames, strip_rows, width = out_ref.shape[0], out_ref.shape[1], cols_ref.shape[2]
    pieces = []
    for t in range(frames):
        keep = keep_ref[tap_a * frames + t]
        for r in range(strip_rows):
            rows = cols_ref[tap_a + t, tap_b + 2 * r].astype(F32)
            pieces.append(jnp.where(keep > 0, rows, 0.0))
    lhs = jnp.concatenate(pieces, axis=0).astype(BF16)
    channels = weight_ref.shape[3]
    total = None
    for e in range(3):
        part = lax.dot_general(
            lhs[:, e * channels : (e + 1) * channels],
            weight_ref[0, e],
            (((1,), (1,)), ((), ())),
            preferred_element_type=F32,
        )
        total = part if total is None else total + part

    @pl.when(step == 0)
    def _():
        acc_ref[...] = total

    @pl.when(step > 0)
    def _():
        acc_ref[...] += total

    @pl.when(step == 8)
    def _():
        summed = acc_ref[...] + bias_ref[...]
        feature = summed / (1.0 + jnp.exp(-summed))
        for t in range(frames):
            for r in range(strip_rows):
                at = (t * strip_rows + r) * width
                out_ref[t, r] = feature[at : at + width].astype(BF16)


def pose_feature(extended, conv_weight, conv_bias, start_of, first_frame):
    frames, rows, columns, channels = extended.shape
    frames, rows = frames // 2, rows - 1
    out_channels = conv_weight.shape[-1]
    pairs = extended.reshape(2 * frames, rows + 1, columns // 2, 2 * channels)
    before = jnp.pad(pairs[:, :, :-1, channels:], ((0, 0), (0, 0), (1, 0), (0, 0)))
    cols = jnp.concatenate([before, pairs], axis=3)
    taps = jnp.transpose(conv_weight, (0, 1, 2, 4, 3)).reshape(9, 3, out_channels, channels)
    frame_ids = first_frame + jnp.arange(frames, dtype=jnp.int32)
    starts_here = lax.dynamic_slice_in_dim(start_of, first_frame, frames)
    keep = (frame_ids[None, :] - 2 + jnp.arange(3, dtype=jnp.int32)[:, None] >= starts_here[None, :])
    keep = keep.astype(jnp.int32).reshape(-1)
    out_shape = (frames, rows // 2, columns // 2, out_channels)
    tokens = frames * (rows // 2) * (columns // 2)
    feature = pl.pallas_call(
        conv_kernel,
        out_shape=jax.ShapeDtypeStruct(out_shape, BF16),
        grid_spec=pltpu.PrefetchScalarGridSpec(
            num_scalar_prefetch=1,
            grid=(9,),
            in_specs=[
                pl.BlockSpec(cols.shape, lambda i, k: (0, 0, 0, 0)),
                pl.BlockSpec((1, 3, out_channels, channels), lambda i, k: (i, 0, 0, 0)),
                pl.BlockSpec((1, out_channels), lambda i, k: (0, 0)),
            ],
            out_specs=pl.BlockSpec(out_shape, lambda i, k: (0, 0, 0, 0)),
            scratch_shapes=[pltpu.VMEM((tokens, out_channels), F32)],
        ),
        compiler_params=pltpu.CompilerParams(vmem_limit_bytes=24 * MIB),
        cost_estimate=cost(tokens * out_channels, 2 * tokens * out_channels),
        name="pose_conv",
    )(keep, cols, taps, conv_bias.reshape(1, -1))
    return feature.reshape(tokens, out_channels)


def guide(own, feature, pose_proj):
    tokens, width = own.shape
    channels = pose_proj.shape[0]
    wide = width // 4

    def body(own_ref, feature_ref, proj_ref, out_ref):
        added = jnp.dot(feature_ref[...], proj_ref[...], preferred_element_type=F32)
        out_ref[...] = (own_ref[...].astype(F32) + added).astype(BF16)

    return pl.pallas_call(
        body,
        out_shape=jax.ShapeDtypeStruct(own.shape, BF16),
        grid=(4,),
        in_specs=[
            pl.BlockSpec((tokens, wide), lambda i: (0, i)),
            pl.BlockSpec((tokens, channels), lambda i: (0, 0)),
            pl.BlockSpec((channels, wide), lambda i: (0, i)),
        ],
        out_specs=pl.BlockSpec((tokens, wide), lambda i: (0, i)),
        compiler_params=pltpu.CompilerParams(vmem_limit_bytes=16 * MIB),
        cost_estimate=cost(tokens * width, 2 * tokens * width),
        name="guide",
    )(own, feature, pose_proj)


def project(own, lower, upper, order, shards_of, total, frames):
    strips = len(lower) + 1
    tokens = own.shape[0]
    rows = strips * tokens
    per_frame = tokens // frames
    steps = len(shards_of)
    flat = [array for kind, arrays in shards_of for array in arrays]
    size = flat[0].shape[2]
    columns = 3 * (PLANE + 1)
    heads = PLANE + 1
    depth = own.shape[1] // PLANE
    cuts = [(c, min(c + 4, columns)) for c in range(0, columns, 4)]
    parts = 2 if shards_of[0][0] == "rows" else 1
    slots = min(2, steps)

    def body(order_ref, *refs):
        own_ref, lower_refs, upper_refs = refs[0], refs[1:strips], refs[strips : 2 * strips - 1]
        source_refs = refs[2 * strips - 1 : 2 * strips - 1 + len(flat)]
        rest = refs[2 * strips - 1 + len(flat) :]
        held_ref, guided_ref, sems = rest[-3:]
        if total is None:
            sum_ref = rest[0]
        else:
            total_ref, last_ref, sum_ref = rest[0], rest[1 + PLANE], rest[2 + PLANE]
            message_refs = rest[1 : 1 + PLANE]
        step = pl.program_id(0)

        def fetch(k, n, part):
            low, high = cuts[n]
            kind, arrays = shards_of[k]
            base = sum(len(other) for unused, other in shards_of[:k])
            length, at, shift = depth // parts, 0, 0
            if kind != "whole" and low >= FIRST_COLUMNS:
                base, shift = base + 1, FIRST_COLUMNS
            if kind == "rows":
                base += 2 * part
                at = pl.multiple_of((order_ref[steps + 1] ^ part) * length, 128)
            return pltpu.make_async_copy(
                source_refs[base].at[low - shift : high - shift],
                held_ref.at[k % slots, low:high, pl.ds(at, length)],
                sems.at[k % slots, n, part],
            )

        def start(k):
            for n in range(len(cuts)):
                for part in range(parts):
                    fetch(k, n, part).start()

        for k in range(steps):

            @pl.when(step == max(k - 1, 0))
            def _(k=k):
                start(k)

        for s in range(strips):
            found = own_ref[...]
            if s > 0:
                found = lower_refs[s - 1][...].astype(F32) + upper_refs[strips - s - 1][...].astype(F32)
                found = found.astype(BF16)
            for t in range(frames):
                at = (t * strips + s) * per_frame
                guided_ref[at : at + per_frame] = found[t * per_frame : (t + 1) * per_frame]

        slot = lax.rem(step, slots)
        for n, (low, high) in enumerate(cuts):
            for k in range(steps):

                @pl.when(step == k)
                def _(k=k, n=n):
                    for part in range(parts):
                        fetch(k, n, part).wait()

            rhs = jnp.concatenate([held_ref[slot, c] for c in range(low, high)], axis=1)
            part = jnp.dot(guided_ref[...], rhs, preferred_element_type=F32)
            lanes = slice(low * size, high * size)
            if total is not None:
                sum_ref[:, lanes] = total_ref[:, lanes] + part
                continue

            @pl.when(step == 0)
            def _(lanes=lanes, part=part):
                sum_ref[:, lanes] = part

            @pl.when(step > 0)
            def _(lanes=lanes, part=part):
                sum_ref[:, lanes] += part

        if total is None:
            return
        last = 3 * (heads - 1) * size
        last_ref[...] = sum_ref[:, last : last + size].astype(BF16)
        for r in range(PLANE):
            head = order_ref[steps] ^ r
            for j in range(3):
                at = pl.multiple_of((3 * head + j) * size, size)
                message_refs[r][j] = sum_ref[:, pl.ds(at, size)].astype(BF16)
            for j in range(1, 3):
                at = last + j * size
                message_refs[r][2 + j] = sum_ref[:, at : at + size].astype(BF16)

    piece = pl.BlockSpec((tokens, depth), lambda i, order: (0, order[i]))
    in_specs = [piece] * (2 * strips - 1)
    in_specs += [pl.BlockSpec(memory_space=pl.ANY)] * len(flat)
    operands = [own, *lower, *upper, *flat]
    sums = pl.BlockSpec((rows, columns * size), lambda i, order: (0, 0))
    scratch = [
        pltpu.VMEM((slots, columns, depth, size), BF16),
        pltpu.VMEM((rows, depth), BF16),
        pltpu.SemaphoreType.DMA((slots, len(cuts), parts)),
    ]
    if total is None:
        out_shape, out_specs = jax.ShapeDtypeStruct((rows, columns * size), F32), sums
    else:
        assert steps == 1
        in_specs.append(sums)
        operands.append(total)
        message = jax.ShapeDtypeStruct((5, rows, size), BF16)
        out_shape = (message,) * PLANE + (jax.ShapeDtypeStruct((rows, size), BF16),)
        out_specs = (pl.BlockSpec((5, rows, size), lambda i, order: (0, 0, 0)),) * PLANE
        out_specs += (pl.BlockSpec((rows, size), lambda i, order: (0, 0)),)
        scratch = [pltpu.VMEM((rows, columns * size), F32)] + scratch
    return pl.pallas_call(
        body,
        out_shape=out_shape,
        grid_spec=pltpu.PrefetchScalarGridSpec(
            num_scalar_prefetch=1, grid=(steps,), in_specs=in_specs, out_specs=out_specs, scratch_shapes=scratch
        ),
        compiler_params=pltpu.CompilerParams(vmem_limit_bytes=40 * MIB),
        cost_estimate=cost(0, 2 * rows * size),
        name="project",
    )(order, *operands)


def attend(messages, last_query, here, spans, frames, strips):
    rows, size = last_query.shape
    per_frame = rows // frames
    strip = per_frame // strips
    frame_count = PLANE * frames
    window = frame_count - 4 if frame_count > 4 else frame_count
    out_rows = (PLANE + 1) * frames * strip
    scale = size ** (-0.5)

    def body(table_ref, *refs):
        message_refs, last_ref = refs[:PLANE], refs[PLANE]
        out_refs, held_ref = refs[PLANE + 1 : PLANE + 1 + strips], refs[-1]
        here_at = table_ref[3 * frame_count]
        for r in range(PLANE):
            for t in range(frames):
                frame = (here_at ^ r) * frames + t
                for j in range(4):
                    held_ref[frame, j] = message_refs[r][j + 1, t * per_frame : (t + 1) * per_frame]

        def one(query, frame, kind, at):
            begin, low, high = table_ref[3 * frame], table_ref[3 * frame + 1], table_ref[3 * frame + 2]
            keys = held_ref[pl.ds(begin, window), kind].reshape(window * per_frame, size)
            values = held_ref[pl.ds(begin, window), kind + 1].reshape(window * per_frame, size)
            scores = lax.dot_general(query, keys, (((1,), (1,)), ((), ())), preferred_element_type=F32)
            place = lax.broadcasted_iota(jnp.int32, (1, window * per_frame), 1)
            seen = (place >= low * per_frame) & (place < high * per_frame)
            scores = jnp.where(seen, scores * scale, NEG_FILL)
            weights = jnp.exp(scores - jnp.max(scores, axis=1, keepdims=True))
            totals = jnp.sum(weights, axis=1, keepdims=True)
            mixed = jnp.dot(weights.astype(BF16), values, preferred_element_type=F32)
            result = (mixed / totals).astype(BF16)
            for s in range(strips):
                out_refs[s][at : at + strip] = result[s * strip : (s + 1) * strip]

        for r in range(PLANE):
            for t in range(frames):
                query = message_refs[r][0, t * per_frame : (t + 1) * per_frame]
                one(query, (here_at ^ r) * frames + t, 0, (r * frames + t) * strip)
        for t in range(frames):
            query = last_ref[t * per_frame : (t + 1) * per_frame]
            one(query, here_at * frames + t, 2, (PLANE * frames + t) * strip)

    table = jnp.concatenate([spans.reshape(-1), here.reshape(1)]).astype(jnp.int32)
    whole = pl.BlockSpec((5, rows, size), lambda i, table: (0, 0, 0))
    units = (PLANE + 1) * frames
    return pl.pallas_call(
        body,
        out_shape=(jax.ShapeDtypeStruct((out_rows, size), BF16),) * strips,
        grid_spec=pltpu.PrefetchScalarGridSpec(
            num_scalar_prefetch=1,
            grid=(1,),
            in_specs=[whole] * PLANE + [pl.BlockSpec((rows, size), lambda i, table: (0, 0))],
            out_specs=(pl.BlockSpec((out_rows, size), lambda i, table: (0, 0)),) * strips,
            scratch_shapes=[pltpu.VMEM((frame_count, 4, per_frame, size), BF16)],
        ),
        compiler_params=pltpu.CompilerParams(vmem_limit_bytes=40 * MIB),
        cost_estimate=cost(0, 2 * rows * size),
        name="attend",
    )(table, *messages, last_query)


def out_project(gathered, weights, here, group, core, tokens):
    groups, depth, columns = weights[0].shape
    size = gathered[0].shape[2]
    heads = depth // size

    def body(at_ref, *refs):
        weight_refs = refs[PLANE : PLANE + 2]
        out_refs, lhs_ref, sum_ref = refs[PLANE + 2 : -2], refs[-2], refs[-1]
        step = pl.program_id(0)
        for p in range(PLANE):
            rows = slice(p * tokens, (p + 1) * tokens)
            for q in range(PLANE):
                at = (p ^ q) * tokens
                lhs_ref[rows, q * size : (q + 1) * size] = refs[q][0, at : at + tokens]
            lhs_ref[rows, PLANE * size :] = refs[p][0, PLANE * tokens :]

        here_at, core_at = at_ref[0], at_ref[2]
        for c in range(2):
            found = [
                weight_refs[c][0, pl.ds(pl.multiple_of((here_at ^ q) * size, size), size)] for q in range(PLANE)
            ]
            found.append(weight_refs[c][0, PLANE * size : heads * size])
            part = jnp.dot(lhs_ref[...], jnp.concatenate(found, axis=0), preferred_element_type=F32)
            part = part.astype(BF16).astype(F32)

            @pl.when(step == 0)
            def _(c=c, part=part):
                sum_ref[c] = part

            @pl.when(step > 0)
            def _(c=c, part=part):
                sum_ref[c] += part

        @pl.when(step == groups - 1)
        def _():
            for p in range(PLANE):
                for c in range(2):
                    at = pl.multiple_of((core_at ^ c) * columns, 128)
                    out_refs[p][:, pl.ds(at, columns)] = sum_ref[c, p * tokens : (p + 1) * tokens].astype(BF16)

    in_specs = [pl.BlockSpec((1,) + piece.shape[1:], lambda g, at: (g, 0, 0)) for piece in gathered]
    in_specs += [
        pl.BlockSpec((1, depth, columns), lambda g, at: (lax.rem(at[1] + g, groups), 0, 0))
    ] * 2
    return pl.pallas_call(
        body,
        out_shape=(jax.ShapeDtypeStruct((tokens, 2 * columns), BF16),) * PLANE,
        grid_spec=pltpu.PrefetchScalarGridSpec(
            num_scalar_prefetch=1,
            grid=(groups,),
            in_specs=in_specs,
            out_specs=(pl.BlockSpec((tokens, 2 * columns), lambda g, at: (0, 0)),) * PLANE,
            scratch_shapes=[
                pltpu.VMEM((PLANE * tokens, depth), BF16),
                pltpu.VMEM((2, PLANE * tokens, columns), F32),
            ],
        ),
        compiler_params=pltpu.CompilerParams(vmem_limit_bytes=24 * MIB),
        cost_estimate=cost(0, 4 * PLANE * tokens * columns),
        name="out_project",
    )(jnp.stack([here, group, core]), *gathered, *weights)


def place_columns(pieces, here):
    tokens, columns = pieces[0].shape

    def body(here_ref, *refs):
        for r in range(PLANE):
            at = pl.multiple_of((here_ref[0] ^ r) * columns, 128)
            refs[-1][:, pl.ds(at, columns)] = refs[r][...]

    return pl.pallas_call(
        body,
        out_shape=jax.ShapeDtypeStruct((tokens, PLANE * columns), BF16),
        grid_spec=pltpu.PrefetchScalarGridSpec(
            num_scalar_prefetch=1,
            grid=(1,),
            in_specs=[pl.BlockSpec((tokens, columns), lambda i, here: (0, 0))] * PLANE,
            out_specs=pl.BlockSpec((tokens, PLANE * columns), lambda i, here: (0, 0)),
        ),
        cost_estimate=cost(0, 4 * tokens * PLANE * columns),
        name="place_columns",
    )(here.reshape(1), *pieces)


def shards(
    latent, pose_maps, conv_weight, conv_bias, pose_proj, w_qkv, w_out, clip_lengths, block_ids
):
    frame_count = block_ids.shape[0]
    frames, strip_rows, width_grid, model_width = latent.shape
    heads, head_size = w_qkv.shape[1], w_qkv.shape[3]
    strips = lax.axis_size("head")
    tokens = frames * strip_rows * width_grid
    here = lax.axis_index("frame").astype(jnp.int32)
    group = lax.axis_index("head").astype(jnp.int32)
    core = lax.axis_index("dp").astype(jnp.int32)
    clip_of, start_of = frame_tables(clip_lengths, frame_count)

    weight = jnp.transpose(w_qkv, (1, 2, 0, 3)).reshape(3 * heads, -1, head_size)
    near_pairs = [(2 * f + c, 2 * (f ^ (1 + c)) + c) for f in range(PLANE) for c in range(2)]
    far_pairs = [(2 * f + c, 2 * (f ^ (2 - c)) + c) for f in range(PLANE) for c in range(2)]
    plane_axes = ("frame", "dp")
    earlier = shifted(pose_maps, "frame", 1)
    near_first = lax.ppermute(after(weight[:FIRST_COLUMNS], earlier), plane_axes, near_pairs)
    near_rest = lax.ppermute(after(weight[FIRST_COLUMNS:], earlier), plane_axes, near_pairs)

    extended = jnp.concatenate([earlier, pose_maps], axis=0)
    extended = jnp.concatenate([shifted(extended[:, -1:], "head", 1), extended], axis=1)
    feature = pose_feature(extended, conv_weight, conv_bias, start_of, here * frames)
    own = guide(latent.reshape(tokens, model_width), feature, pose_proj)
    lower, upper = hop(own, own, "head", 1)
    lower, upper = [lower], [upper]
    columns = model_width // PLANE // 2
    depth = heads * head_size
    out_half = take_block(w_out.reshape(depth, model_width), jnp.int32(0), 2 * here + core, (depth, columns))

    half_rows = weight.shape[1] // 2
    first_half = lax.dynamic_slice_in_dim(near_first, core * half_rows, half_rows, axis=1)
    near_rest = after(near_rest, lower[0], upper[0], first_half, out_half)
    near = (near_first, near_rest)
    rest_half = lax.dynamic_slice_in_dim(near_rest, core * half_rows, half_rows, axis=1)
    for s in range(2, strips):
        below, above = hop(lower[-1], upper[-1], "head", s)
        if s < strips - 1:
            below, above = after(below, rest_half), after(above, rest_half)
        lower.append(below)
        upper.append(above)
    far = tuple(lax.ppermute(part, plane_axes, far_pairs) for part in (first_half, rest_half))
    other = tuple(across(part, "dp", 1) for part in near)
    out_half = after(out_half, lower[-1], upper[-1])

    here_near, here_other, here_far = here ^ (1 + core), here ^ (2 - core), here ^ 3
    order = after(jnp.stack([here, here_near, here_other, here, core]), out_half)
    held = [("whole", (weight,)), ("columns", near), ("columns", other)]
    total = project(own, lower, upper, order, held, None, frames)
    far = tuple(after(part, lower[-1], upper[-1]) for part in far)
    far += tuple(across(part, "dp", 1) for part in far)
    order = jnp.stack([here_far, here, core])
    *messages, last_query = project(
        own, lower, upper, order, [("rows", far)], total, frames
    )
    messages = [messages[0]] + [across(messages[r], "frame", r) for r in range(1, PLANE)]

    same_clip = clip_of[:, None] == clip_of[None, :]
    counts = jnp.sum((same_clip & (block_ids[None, :] <= block_ids[:, None])).astype(jnp.int32), axis=1)
    window = frame_count - 4 if frame_count > 4 else frame_count
    begins = jnp.minimum(start_of, frame_count - window)
    spans = jnp.stack([begins, start_of - begins, start_of - begins + counts], axis=1)
    outs = attend(messages, last_query, here, spans, frames, strips)

    out_half = after(lax.all_gather(out_half, "head"), outs[0])
    out_weights = [out_half, across(out_half, "dp", 1)]

    strip_heads = [outs[0]] + [turn(outs[s], "head", -s) for s in range(1, strips)]
    strip_heads = after(jnp.stack(strip_heads), out_weights[1])
    gathered = [strip_heads] + [across(strip_heads, "frame", r) for r in range(1, PLANE)]
    done = out_project(gathered, out_weights, here, group, core, tokens)
    mine = [done[0]] + [across(done[r], "frame", r) for r in range(1, PLANE)]
    return place_columns(mine, here).reshape(latent.shape)


def solution(mesh):
    return jax.shard_map(
        shards if mesh.shape["frame"] == PLANE else plain_shards,
        mesh=mesh,
        in_specs=(
            P(("dp", "frame"), "head", None, None),
            P(("dp", "frame"), "head", None, None),
            P(),
            P(),
            P(),
            P("frame", "head", None, None),
            P("head", None, None),
            P("dp"),
            P("dp"),
        ),
        out_specs=P(("dp", "frame"), "head", None, None),
        check_vma=False,
    )
```

```python
import jax
import jax.numpy as jnp
from jax import lax
from jax.experimental import pallas as pl
from jax.experimental.pallas import tpu as pltpu
from jax.sharding import PartitionSpec as P

NEG_FILL = -1e30
MIB = 1 << 20
F32 = jnp.float32
BF16 = jnp.bfloat16
PLANE = 4
FIRST_COLUMNS = 8


def cost(flops, moved, exps=0):
    return pl.CostEstimate(flops=int(flops), bytes_accessed=int(moved), transcendentals=int(exps))


def shifted(value, axis, steps):
    count = lax.axis_size(axis)
    leading, last = (max(0, -steps), min(count, count - steps))
    return lax.ppermute(value, axis, [(source, source + steps) for source in range(leading, last)])


def frame_tables(clip_lengths, frame_count):
    clip_ends = jnp.cumsum(clip_lengths)
    clip_starts = clip_ends - clip_lengths
    frame_index = jnp.arange(frame_count, dtype=jnp.int32)
    clip_of = jnp.sum((frame_index[:, None] >= clip_ends[None, :]).astype(jnp.int32), axis=1)
    clip_match = clip_of[:, None] == jnp.arange(clip_lengths.shape[0], dtype=jnp.int32)[None, :]
    start_of = jnp.sum(jnp.where(clip_match, clip_starts[None, :], 0), axis=1)
    return (clip_of, start_of)


def guide_features(latent, pose_maps, conv_weight, conv_bias, pose_proj, start_of, first_frame):
    frames_dev = pose_maps.shape[0]
    upper_row = shifted(pose_maps[:, -1:], "head", 1)
    rows_ext = jnp.concatenate([upper_row, pose_maps], axis=1)
    left_column = jnp.zeros(rows_ext.shape[:2] + (1, rows_ext.shape[3]), rows_ext.dtype)
    cols_ext = jnp.concatenate([left_column, rows_ext], axis=2)
    earlier = shifted(cols_ext, "frame", 1)
    extended = jnp.concatenate([earlier, cols_ext], axis=0)
    out_rows = pose_maps.shape[1] // 2
    out_cols = pose_maps.shape[2] // 2
    frame_ids = first_frame + jnp.arange(frames_dev, dtype=jnp.int32)
    starts_here = lax.dynamic_slice_in_dim(start_of, first_frame, frames_dev)
    tap_list = []
    for step_a in range(3):
        keep_mask = (frame_ids - 2 + step_a >= starts_here).astype(pose_maps.dtype)[
            :, None, None, None
        ]
        frames_tap = extended[step_a : step_a + frames_dev] * keep_mask
        for step_b in range(3):
            for step_e in range(3):
                tap_list.append(
                    frames_tap[
                        :,
                        step_b : step_b + 2 * out_rows - 1 : 2,
                        step_e : step_e + 2 * out_cols - 1 : 2,
                    ]
                )
    stacked = jnp.concatenate(tap_list, axis=3)
    kernel = conv_weight.reshape(-1, conv_weight.shape[-1])
    summed = jnp.dot(stacked, kernel, preferred_element_type=jnp.float32) + conv_bias
    feature = jax.nn.silu(summed).astype(jnp.bfloat16)
    guided = latent.astype(jnp.float32) + jnp.dot(
        feature, pose_proj, preferred_element_type=jnp.float32
    )
    return guided.astype(jnp.bfloat16)


def attend_rows(queries, query_clip, query_block, keyvals, clip_of, block_ids):
    heads_dev = queries.shape[1]
    rows_query = queries.shape[0]
    head_size = queries.shape[2]
    score_scale = head_size ** (-0.5)
    start_carry = (
        jnp.full((heads_dev, rows_query), NEG_FILL, jnp.float32),
        jnp.zeros((heads_dev, rows_query), jnp.float32),
        jnp.zeros((heads_dev, rows_query, head_size), jnp.float32),
    )

    def one_frame(running, frame_item):
        frame_kv, frame_id = frame_item
        key_clip = clip_of[frame_id]
        key_block = block_ids[frame_id]
        visible = (query_clip == key_clip) & (key_block <= query_block)
        run_max, run_total, run_acc = running
        scores = (
            jnp.einsum(
                "qhd,khd->hqk", queries, frame_kv[:, :, 0], preferred_element_type=jnp.float32
            )
            * score_scale
        )
        scores = jnp.where(visible[None, :, None], scores, NEG_FILL)
        new_max = jnp.maximum(run_max, jnp.max(scores, axis=2))
        factor = jnp.exp(run_max - new_max)
        weights = jnp.where(visible[None, :, None], jnp.exp(scores - new_max[:, :, None]), 0.0)
        new_total = run_total * factor + jnp.sum(weights, axis=2)
        new_acc = run_acc * factor[:, :, None] + jnp.einsum(
            "hqk,khd->hqd",
            weights.astype(jnp.bfloat16),
            frame_kv[:, :, 1],
            preferred_element_type=jnp.float32,
        )
        running = (new_max, new_total, new_acc)
        return (running, None)

    running = start_carry
    shard_piece = lax.all_gather(keyvals, "frame", axis=0, tiled=True)
    piece_frames = shard_piece.shape[0]
    frame_list = jnp.arange(piece_frames, dtype=jnp.int32)
    running, unused = lax.scan(one_frame, running, (shard_piece, frame_list))
    run_max, run_total, run_acc = running
    normalized = run_acc / run_total[:, :, None]
    return jnp.transpose(normalized, (1, 0, 2)).astype(jnp.bfloat16)


def plain_shards(
    latent, pose_maps, conv_weight, conv_bias, pose_proj, w_qkv, w_out, clip_lengths, block_ids
):
    frame_count = block_ids.shape[0]
    clip_of, start_of = frame_tables(clip_lengths, frame_count)
    frames_dev = latent.shape[0]
    first_frame = lax.axis_index("frame") * frames_dev
    guided = guide_features(
        latent, pose_maps, conv_weight, conv_bias, pose_proj, start_of, first_frame
    )
    whole_rows = lax.all_gather(guided, "head", axis=1, tiled=True)
    height = whole_rows.shape[1]
    width_grid = whole_rows.shape[2]
    model_width = whole_rows.shape[3]
    flat_tokens = whole_rows.reshape(-1, model_width)
    qkv_local = w_qkv.reshape(w_qkv.shape[0], -1)
    projected = jnp.dot(
        flat_tokens,
        lax.all_gather(qkv_local, "frame", axis=0, tiled=True),
        preferred_element_type=jnp.float32,
    ).astype(jnp.bfloat16)
    per_frame = height * width_grid
    heads_dev = w_qkv.shape[1]
    head_size = w_qkv.shape[3]
    grouped = projected.reshape(frames_dev, per_frame, heads_dev, 3, head_size)
    rows_total = frames_dev * per_frame
    queries = grouped[:, :, :, 0].reshape(rows_total, heads_dev, head_size)
    keyvals = grouped[:, :, :, 1:3]
    clip_rows = lax.dynamic_slice_in_dim(clip_of, first_frame, frames_dev)
    block_rows = lax.dynamic_slice_in_dim(block_ids, first_frame, frames_dev)
    query_clip = jnp.repeat(clip_rows, per_frame)
    query_block = jnp.repeat(block_rows, per_frame)
    attended = attend_rows(queries, query_clip, query_block, keyvals, clip_of, block_ids)
    by_row = attended.reshape(frames_dev, height, width_grid, heads_dev * head_size)
    by_row = jnp.transpose(by_row, (1, 0, 2, 3)).reshape(
        height, frames_dev * width_grid, heads_dev * head_size
    )
    out_weight = w_out.reshape(heads_dev * head_size, w_out.shape[2])
    rows_here = height // lax.axis_size("head")
    summed_rows = lax.psum_scatter(
        jnp.dot(by_row, out_weight, preferred_element_type=jnp.float32).astype(jnp.bfloat16),
        "head",
        scatter_dimension=0,
        tiled=True,
    ).astype(jnp.float32)
    summed_rows = summed_rows.reshape(rows_here, frames_dev, width_grid, out_weight.shape[1])
    return jnp.transpose(summed_rows, (1, 0, 2, 3)).astype(jnp.bfloat16)


def turn(value, axis, steps):
    count = lax.axis_size(axis)
    return lax.ppermute(value, axis, [(i, (i + steps) % count) for i in range(count)])


def across(value, axis, bits):
    count = lax.axis_size(axis)
    return lax.ppermute(value, axis, [(i, i ^ bits) for i in range(count)])


def hop(lower, upper, axis, s):
    count = lax.axis_size(axis)
    lower = lax.ppermute(lower, axis, [(i, i + 1) for i in range(s - 1, count - 1)])
    upper = lax.ppermute(upper, axis, [(i, i - 1) for i in range(1, count - s + 1)])
    return lower, upper


def after(value, *others):
    def body(*refs):
        del refs

    anywhere = pl.BlockSpec(memory_space=pl.ANY)
    return pl.pallas_call(
        body,
        out_shape=jax.ShapeDtypeStruct(value.shape, value.dtype),
        in_specs=[anywhere] * (1 + len(others)),
        out_specs=anywhere,
        input_output_aliases={0: 0},
        name="after",
    )(value, *others)


def take_block(weight, row, column, shape, *ready):
    def body(at_ref, weight_ref, *refs):
        refs[-1][...] = weight_ref[...]

    return pl.pallas_call(
        body,
        out_shape=jax.ShapeDtypeStruct(shape, weight.dtype),
        grid_spec=pltpu.PrefetchScalarGridSpec(
            num_scalar_prefetch=1,
            grid=(1,),
            in_specs=[pl.BlockSpec(shape, lambda i, at: (at[0], at[1]))]
            + [pl.BlockSpec(memory_space=pl.ANY)] * len(ready),
            out_specs=pl.BlockSpec(shape, lambda i, at: (0, 0)),
        ),
        cost_estimate=cost(0, 4 * shape[0] * shape[1]),
        name="take_block",
    )(jnp.stack([row, column]), weight, *ready)


def conv_kernel(keep_ref, cols_ref, weight_ref, bias_ref, out_ref, acc_ref):
    step = pl.program_id(0)
    tap_a, tap_b = step // 3, step % 3
    frames, strip_rows, width = out_ref.shape[0], out_ref.shape[1], cols_ref.shape[2]
    pieces = []
    for t in range(frames):
        keep = keep_ref[tap_a * frames + t]
        for r in range(strip_rows):
            rows = cols_ref[tap_a + t, tap_b + 2 * r].astype(F32)
            pieces.append(jnp.where(keep > 0, rows, 0.0))
    lhs = jnp.concatenate(pieces, axis=0).astype(BF16)
    channels = weight_ref.shape[3]
    total = None
    for e in range(3):
        part = lax.dot_general(
            lhs[:, e * channels : (e + 1) * channels],
            weight_ref[0, e],
            (((1,), (1,)), ((), ())),
            preferred_element_type=F32,
        )
        total = part if total is None else total + part

    @pl.when(step == 0)
    def _():
        acc_ref[...] = total

    @pl.when(step > 0)
    def _():
        acc_ref[...] += total

    @pl.when(step == 8)
    def _():
        summed = acc_ref[...] + bias_ref[...]
        feature = summed / (1.0 + jnp.exp(-summed))
        for t in range(frames):
            for r in range(strip_rows):
                at = (t * strip_rows + r) * width
                out_ref[t, r] = feature[at : at + width].astype(BF16)


def pose_feature(extended, conv_weight, conv_bias, start_of, first_frame):
    frames, rows, columns, channels = extended.shape
    frames, rows = frames // 2, rows - 1
    out_channels = conv_weight.shape[-1]
    pairs = extended.reshape(2 * frames, rows + 1, columns // 2, 2 * channels)
    before = jnp.pad(pairs[:, :, :-1, channels:], ((0, 0), (0, 0), (1, 0), (0, 0)))
    cols = jnp.concatenate([before, pairs], axis=3)
    taps = jnp.transpose(conv_weight, (0, 1, 2, 4, 3)).reshape(9, 3, out_channels, channels)
    frame_ids = first_frame + jnp.arange(frames, dtype=jnp.int32)
    starts_here = lax.dynamic_slice_in_dim(start_of, first_frame, frames)
    keep = (frame_ids[None, :] - 2 + jnp.arange(3, dtype=jnp.int32)[:, None] >= starts_here[None, :])
    keep = keep.astype(jnp.int32).reshape(-1)
    out_shape = (frames, rows // 2, columns // 2, out_channels)
    tokens = frames * (rows // 2) * (columns // 2)
    feature = pl.pallas_call(
        conv_kernel,
        out_shape=jax.ShapeDtypeStruct(out_shape, BF16),
        grid_spec=pltpu.PrefetchScalarGridSpec(
            num_scalar_prefetch=1,
            grid=(9,),
            in_specs=[
                pl.BlockSpec(cols.shape, lambda i, k: (0, 0, 0, 0)),
                pl.BlockSpec((1, 3, out_channels, channels), lambda i, k: (i, 0, 0, 0)),
                pl.BlockSpec((1, out_channels), lambda i, k: (0, 0)),
            ],
            out_specs=pl.BlockSpec(out_shape, lambda i, k: (0, 0, 0, 0)),
            scratch_shapes=[pltpu.VMEM((tokens, out_channels), F32)],
        ),
        compiler_params=pltpu.CompilerParams(vmem_limit_bytes=24 * MIB),
        cost_estimate=cost(tokens * out_channels, 2 * tokens * out_channels),
        name="pose_conv",
    )(keep, cols, taps, conv_bias.reshape(1, -1))
    return feature.reshape(tokens, out_channels)


def guide(own, feature, pose_proj):
    tokens, width = own.shape
    channels = pose_proj.shape[0]
    wide = width // 4

    def body(own_ref, feature_ref, proj_ref, out_ref):
        added = jnp.dot(feature_ref[...], proj_ref[...], preferred_element_type=F32)
        out_ref[...] = (own_ref[...].astype(F32) + added).astype(BF16)

    return pl.pallas_call(
        body,
        out_shape=jax.ShapeDtypeStruct(own.shape, BF16),
        grid=(4,),
        in_specs=[
            pl.BlockSpec((tokens, wide), lambda i: (0, i)),
            pl.BlockSpec((tokens, channels), lambda i: (0, 0)),
            pl.BlockSpec((channels, wide), lambda i: (0, i)),
        ],
        out_specs=pl.BlockSpec((tokens, wide), lambda i: (0, i)),
        compiler_params=pltpu.CompilerParams(vmem_limit_bytes=16 * MIB),
        cost_estimate=cost(tokens * width, 2 * tokens * width),
        name="guide",
    )(own, feature, pose_proj)


def project(own, lower, upper, order, shards_of, total, frames):
    strips = len(lower) + 1
    tokens = own.shape[0]
    rows = strips * tokens
    per_frame = tokens // frames
    steps = len(shards_of)
    flat = [array for kind, arrays in shards_of for array in arrays]
    size = flat[0].shape[2]
    columns = 3 * (PLANE + 1)
    heads = PLANE + 1
    depth = own.shape[1] // PLANE
    cuts = [(c, min(c + 4, columns)) for c in range(0, columns, 4)]
    parts = 2 if shards_of[0][0] == "rows" else 1
    slots = min(2, steps)

    def body(order_ref, *refs):
        own_ref, lower_refs, upper_refs = refs[0], refs[1:strips], refs[strips : 2 * strips - 1]
        source_refs = refs[2 * strips - 1 : 2 * strips - 1 + len(flat)]
        rest = refs[2 * strips - 1 + len(flat) :]
        held_ref, guided_ref, sems = rest[-3:]
        if total is None:
            sum_ref = rest[0]
        else:
            total_ref, last_ref, sum_ref = rest[0], rest[1 + PLANE], rest[2 + PLANE]
            message_refs = rest[1 : 1 + PLANE]
        step = pl.program_id(0)

        def fetch(k, n, part):
            low, high = cuts[n]
            kind, arrays = shards_of[k]
            base = sum(len(other) for unused, other in shards_of[:k])
            length, at, shift = depth // parts, 0, 0
            if kind != "whole" and low >= FIRST_COLUMNS:
                base, shift = base + 1, FIRST_COLUMNS
            if kind == "rows":
                base += 2 * part
                at = pl.multiple_of((order_ref[steps + 1] ^ part) * length, 128)
            return pltpu.make_async_copy(
                source_refs[base].at[low - shift : high - shift],
                held_ref.at[k % slots, low:high, pl.ds(at, length)],
                sems.at[k % slots, n, part],
            )

        def start(k):
            for n in range(len(cuts)):
                for part in range(parts):
                    fetch(k, n, part).start()

        for k in range(steps):

            @pl.when(step == max(k - 1, 0))
            def _(k=k):
                start(k)

        for s in range(strips):
            found = own_ref[...]
            if s > 0:
                found = lower_refs[s - 1][...].astype(F32) + upper_refs[strips - s - 1][...].astype(F32)
                found = found.astype(BF16)
            for t in range(frames):
                at = (t * strips + s) * per_frame
                guided_ref[at : at + per_frame] = found[t * per_frame : (t + 1) * per_frame]

        slot = lax.rem(step, slots)
        for n, (low, high) in enumerate(cuts):
            for k in range(steps):

                @pl.when(step == k)
                def _(k=k, n=n):
                    for part in range(parts):
                        fetch(k, n, part).wait()

            rhs = jnp.concatenate([held_ref[slot, c] for c in range(low, high)], axis=1)
            part = jnp.dot(guided_ref[...], rhs, preferred_element_type=F32)
            lanes = slice(low * size, high * size)
            if total is not None:
                sum_ref[:, lanes] = total_ref[:, lanes] + part
                continue

            @pl.when(step == 0)
            def _(lanes=lanes, part=part):
                sum_ref[:, lanes] = part

            @pl.when(step > 0)
            def _(lanes=lanes, part=part):
                sum_ref[:, lanes] += part

        if total is None:
            return
        last = 3 * (heads - 1) * size
        last_ref[...] = sum_ref[:, last : last + size].astype(BF16)
        for r in range(PLANE):
            head = order_ref[steps] ^ r
            for j in range(3):
                at = pl.multiple_of((3 * head + j) * size, size)
                message_refs[r][j] = sum_ref[:, pl.ds(at, size)].astype(BF16)
            for j in range(1, 3):
                at = last + j * size
                message_refs[r][2 + j] = sum_ref[:, at : at + size].astype(BF16)

    piece = pl.BlockSpec((tokens, depth), lambda i, order: (0, order[i]))
    in_specs = [piece] * (2 * strips - 1)
    in_specs += [pl.BlockSpec(memory_space=pl.ANY)] * len(flat)
    operands = [own, *lower, *upper, *flat]
    sums = pl.BlockSpec((rows, columns * size), lambda i, order: (0, 0))
    scratch = [
        pltpu.VMEM((slots, columns, depth, size), BF16),
        pltpu.VMEM((rows, depth), BF16),
        pltpu.SemaphoreType.DMA((slots, len(cuts), parts)),
    ]
    if total is None:
        out_shape, out_specs = jax.ShapeDtypeStruct((rows, columns * size), F32), sums
    else:
        assert steps == 1
        in_specs.append(sums)
        operands.append(total)
        message = jax.ShapeDtypeStruct((5, rows, size), BF16)
        out_shape = (message,) * PLANE + (jax.ShapeDtypeStruct((rows, size), BF16),)
        out_specs = (pl.BlockSpec((5, rows, size), lambda i, order: (0, 0, 0)),) * PLANE
        out_specs += (pl.BlockSpec((rows, size), lambda i, order: (0, 0)),)
        scratch = [pltpu.VMEM((rows, columns * size), F32)] + scratch
    return pl.pallas_call(
        body,
        out_shape=out_shape,
        grid_spec=pltpu.PrefetchScalarGridSpec(
            num_scalar_prefetch=1, grid=(steps,), in_specs=in_specs, out_specs=out_specs, scratch_shapes=scratch
        ),
        compiler_params=pltpu.CompilerParams(vmem_limit_bytes=40 * MIB),
        cost_estimate=cost(0, 2 * rows * size),
        name="project",
    )(order, *operands)


def attend(messages, last_query, here, spans, frames, strips):
    rows, size = last_query.shape
    per_frame = rows // frames
    strip = per_frame // strips
    frame_count = PLANE * frames
    window = frame_count - 4 if frame_count > 4 else frame_count
    out_rows = (PLANE + 1) * frames * strip
    scale = size ** (-0.5)

    def body(table_ref, *refs):
        message_refs, last_ref = refs[:PLANE], refs[PLANE]
        out_refs, held_ref = refs[PLANE + 1 : PLANE + 1 + strips], refs[-1]
        here_at = table_ref[3 * frame_count]
        for r in range(PLANE):
            for t in range(frames):
                frame = (here_at ^ r) * frames + t
                for j in range(4):
                    held_ref[frame, j] = message_refs[r][j + 1, t * per_frame : (t + 1) * per_frame]

        def one(query, frame, kind, at):
            begin, low, high = table_ref[3 * frame], table_ref[3 * frame + 1], table_ref[3 * frame + 2]
            keys = held_ref[pl.ds(begin, window), kind].reshape(window * per_frame, size)
            values = held_ref[pl.ds(begin, window), kind + 1].reshape(window * per_frame, size)
            scores = lax.dot_general(query, keys, (((1,), (1,)), ((), ())), preferred_element_type=F32)
            place = lax.broadcasted_iota(jnp.int32, (1, window * per_frame), 1)
            seen = (place >= low * per_frame) & (place < high * per_frame)
            scores = jnp.where(seen, scores * scale, NEG_FILL)
            weights = jnp.exp(scores - jnp.max(scores, axis=1, keepdims=True))
            totals = jnp.sum(weights, axis=1, keepdims=True)
            mixed = jnp.dot(weights.astype(BF16), values, preferred_element_type=F32)
            result = (mixed / totals).astype(BF16)
            for s in range(strips):
                out_refs[s][at : at + strip] = result[s * strip : (s + 1) * strip]

        for r in range(PLANE):
            for t in range(frames):
                query = message_refs[r][0, t * per_frame : (t + 1) * per_frame]
                one(query, (here_at ^ r) * frames + t, 0, (r * frames + t) * strip)
        for t in range(frames):
            query = last_ref[t * per_frame : (t + 1) * per_frame]
            one(query, here_at * frames + t, 2, (PLANE * frames + t) * strip)

    table = jnp.concatenate([spans.reshape(-1), here.reshape(1)]).astype(jnp.int32)
    whole = pl.BlockSpec((5, rows, size), lambda i, table: (0, 0, 0))
    units = (PLANE + 1) * frames
    return pl.pallas_call(
        body,
        out_shape=(jax.ShapeDtypeStruct((out_rows, size), BF16),) * strips,
        grid_spec=pltpu.PrefetchScalarGridSpec(
            num_scalar_prefetch=1,
            grid=(1,),
            in_specs=[whole] * PLANE + [pl.BlockSpec((rows, size), lambda i, table: (0, 0))],
            out_specs=(pl.BlockSpec((out_rows, size), lambda i, table: (0, 0)),) * strips,
            scratch_shapes=[pltpu.VMEM((frame_count, 4, per_frame, size), BF16)],
        ),
        compiler_params=pltpu.CompilerParams(vmem_limit_bytes=40 * MIB),
        cost_estimate=cost(0, 2 * rows * size),
        name="attend",
    )(table, *messages, last_query)


def out_project(gathered, weights, here, group, core, tokens):
    groups, depth, columns = weights[0].shape
    size = gathered[0].shape[2]
    heads = depth // size

    def body(at_ref, *refs):
        weight_refs = refs[PLANE : PLANE + 2]
        out_refs, lhs_ref, sum_ref = refs[PLANE + 2 : -2], refs[-2], refs[-1]
        step = pl.program_id(0)
        for p in range(PLANE):
            rows = slice(p * tokens, (p + 1) * tokens)
            for q in range(PLANE):
                at = (p ^ q) * tokens
                lhs_ref[rows, q * size : (q + 1) * size] = refs[q][0, at : at + tokens]
            lhs_ref[rows, PLANE * size :] = refs[p][0, PLANE * tokens :]

        here_at, core_at = at_ref[0], at_ref[2]
        for c in range(2):
            found = [
                weight_refs[c][0, pl.ds(pl.multiple_of((here_at ^ q) * size, size), size)] for q in range(PLANE)
            ]
            found.append(weight_refs[c][0, PLANE * size : heads * size])
            part = jnp.dot(lhs_ref[...], jnp.concatenate(found, axis=0), preferred_element_type=F32)
            part = part.astype(BF16).astype(F32)

            @pl.when(step == 0)
            def _(c=c, part=part):
                sum_ref[c] = part

            @pl.when(step > 0)
            def _(c=c, part=part):
                sum_ref[c] += part

        @pl.when(step == groups - 1)
        def _():
            for p in range(PLANE):
                for c in range(2):
                    at = pl.multiple_of((core_at ^ c) * columns, 128)
                    out_refs[p][:, pl.ds(at, columns)] = sum_ref[c, p * tokens : (p + 1) * tokens].astype(BF16)

    in_specs = [pl.BlockSpec((1,) + piece.shape[1:], lambda g, at: (g, 0, 0)) for piece in gathered]
    in_specs += [
        pl.BlockSpec((1, depth, columns), lambda g, at: (lax.rem(at[1] + g, groups), 0, 0))
    ] * 2
    return pl.pallas_call(
        body,
        out_shape=(jax.ShapeDtypeStruct((tokens, 2 * columns), BF16),) * PLANE,
        grid_spec=pltpu.PrefetchScalarGridSpec(
            num_scalar_prefetch=1,
            grid=(groups,),
            in_specs=in_specs,
            out_specs=(pl.BlockSpec((tokens, 2 * columns), lambda g, at: (0, 0)),) * PLANE,
            scratch_shapes=[
                pltpu.VMEM((PLANE * tokens, depth), BF16),
                pltpu.VMEM((2, PLANE * tokens, columns), F32),
            ],
        ),
        compiler_params=pltpu.CompilerParams(vmem_limit_bytes=24 * MIB),
        cost_estimate=cost(0, 4 * PLANE * tokens * columns),
        name="out_project",
    )(jnp.stack([here, group, core]), *gathered, *weights)


def place_columns(pieces, here):
    tokens, columns = pieces[0].shape

    def body(here_ref, *refs):
        for r in range(PLANE):
            at = pl.multiple_of((here_ref[0] ^ r) * columns, 128)
            refs[-1][:, pl.ds(at, columns)] = refs[r][...]

    return pl.pallas_call(
        body,
        out_shape=jax.ShapeDtypeStruct((tokens, PLANE * columns), BF16),
        grid_spec=pltpu.PrefetchScalarGridSpec(
            num_scalar_prefetch=1,
            grid=(1,),
            in_specs=[pl.BlockSpec((tokens, columns), lambda i, here: (0, 0))] * PLANE,
            out_specs=pl.BlockSpec((tokens, PLANE * columns), lambda i, here: (0, 0)),
        ),
        cost_estimate=cost(0, 4 * tokens * PLANE * columns),
        name="place_columns",
    )(here.reshape(1), *pieces)


def shards(
    latent, pose_maps, conv_weight, conv_bias, pose_proj, w_qkv, w_out, clip_lengths, block_ids
):
    frame_count = block_ids.shape[0]
    frames, strip_rows, width_grid, model_width = latent.shape
    heads, head_size = w_qkv.shape[1], w_qkv.shape[3]
    strips = lax.axis_size("head")
    tokens = frames * strip_rows * width_grid
    here = lax.axis_index("frame").astype(jnp.int32)
    group = lax.axis_index("head").astype(jnp.int32)
    core = lax.axis_index("dp").astype(jnp.int32)
    clip_of, start_of = frame_tables(clip_lengths, frame_count)

    weight = jnp.transpose(w_qkv, (1, 2, 0, 3)).reshape(3 * heads, -1, head_size)
    near_pairs = [(2 * f + c, 2 * (f ^ (1 + c)) + c) for f in range(PLANE) for c in range(2)]
    far_pairs = [(2 * f + c, 2 * (f ^ (2 - c)) + c) for f in range(PLANE) for c in range(2)]
    plane_axes = ("frame", "dp")
    earlier = shifted(pose_maps, "frame", 1)
    near_first = lax.ppermute(after(weight[:FIRST_COLUMNS], earlier), plane_axes, near_pairs)
    extended = jnp.concatenate([earlier, pose_maps], axis=0)
    extended = jnp.concatenate([shifted(extended[:, -1:], "head", 1), extended], axis=1)
    feature = pose_feature(extended, conv_weight, conv_bias, start_of, here * frames)
    own = guide(latent.reshape(tokens, model_width), feature, pose_proj)
    near_rest = lax.ppermute(after(weight[FIRST_COLUMNS:], own), plane_axes, near_pairs)
    lower, upper = hop(own, own, "head", 1)
    lower, upper = [lower], [upper]
    columns = model_width // PLANE // 2
    depth = heads * head_size
    out_half = take_block(w_out.reshape(depth, model_width), jnp.int32(0), 2 * here + core, (depth, columns))

    half_rows = weight.shape[1] // 2
    near_first = after(near_first, lower[0], upper[0], out_half)
    first_half = lax.dynamic_slice_in_dim(near_first, core * half_rows, half_rows, axis=1)
    far_first = lax.ppermute(first_half, plane_axes, far_pairs)
    near_rest = after(near_rest, first_half)
    near = (near_first, near_rest)
    rest_half = lax.dynamic_slice_in_dim(near_rest, core * half_rows, half_rows, axis=1)
    for s in range(2, strips):
        below, above = hop(lower[-1], upper[-1], "head", s)
        if s < strips - 1:
            below, above = after(below, rest_half, far_first), after(above, rest_half, far_first)
        lower.append(below)
        upper.append(above)
    far = (far_first, lax.ppermute(rest_half, plane_axes, far_pairs))
    other = tuple(across(part, "dp", 1) for part in near)
    out_half = after(out_half, lower[-1], upper[-1])

    here_near, here_other, here_far = here ^ (1 + core), here ^ (2 - core), here ^ 3
    order = after(jnp.stack([here, here_near, here_other, here, core]), out_half, *far)
    held = [("whole", (weight,)), ("columns", near), ("columns", other)]
    total = project(own, lower, upper, order, held, None, frames)
    far += tuple(across(part, "dp", 1) for part in far)
    order = jnp.stack([here_far, here, core])
    *messages, last_query = project(
        own, lower, upper, order, [("rows", far)], total, frames
    )
    messages = [messages[0]] + [across(messages[r], "frame", r) for r in range(1, PLANE)]

    same_clip = clip_of[:, None] == clip_of[None, :]
    counts = jnp.sum((same_clip & (block_ids[None, :] <= block_ids[:, None])).astype(jnp.int32), axis=1)
    window = frame_count - 4 if frame_count > 4 else frame_count
    begins = jnp.minimum(start_of, frame_count - window)
    spans = jnp.stack([begins, start_of - begins, start_of - begins + counts], axis=1)
    outs = attend(messages, last_query, here, spans, frames, strips)

    out_half = after(lax.all_gather(out_half, "head"), outs[0])
    out_weights = [out_half, across(out_half, "dp", 1)]

    strip_heads = [outs[0]] + [turn(outs[s], "head", -s) for s in range(1, strips)]
    strip_heads = after(jnp.stack(strip_heads), out_weights[1])
    gathered = [strip_heads] + [across(strip_heads, "frame", r) for r in range(1, PLANE)]
    done = out_project(gathered, out_weights, here, group, core, tokens)
    mine = [done[0]] + [across(done[r], "frame", r) for r in range(1, PLANE)]
    return place_columns(mine, here).reshape(latent.shape)


def solution(mesh):
    return jax.shard_map(
        shards if mesh.shape["frame"] == PLANE else plain_shards,
        mesh=mesh,
        in_specs=(
            P(("dp", "frame"), "head", None, None),
            P(("dp", "frame"), "head", None, None),
            P(),
            P(),
            P(),
            P("frame", "head", None, None),
            P("head", None, None),
            P("dp"),
            P("dp"),
        ),
        out_specs=P(("dp", "frame"), "head", None, None),
        check_vma=False,
    )
```

```python
import jax
import jax.numpy as jnp
from jax import lax
from jax.experimental import pallas as pl
from jax.experimental.pallas import tpu as pltpu
from jax.sharding import PartitionSpec as P

NEG_FILL = -1e30
MIB = 1 << 20
F32 = jnp.float32
BF16 = jnp.bfloat16
PLANE = 4
FIRST_COLUMNS = 8


def cost(flops, moved, exps=0):
    return pl.CostEstimate(flops=int(flops), bytes_accessed=int(moved), transcendentals=int(exps))


def shifted(value, axis, steps):
    count = lax.axis_size(axis)
    leading, last = (max(0, -steps), min(count, count - steps))
    return lax.ppermute(value, axis, [(source, source + steps) for source in range(leading, last)])


def frame_tables(clip_lengths, frame_count):
    clip_ends = jnp.cumsum(clip_lengths)
    clip_starts = clip_ends - clip_lengths
    frame_index = jnp.arange(frame_count, dtype=jnp.int32)
    clip_of = jnp.sum((frame_index[:, None] >= clip_ends[None, :]).astype(jnp.int32), axis=1)
    clip_match = clip_of[:, None] == jnp.arange(clip_lengths.shape[0], dtype=jnp.int32)[None, :]
    start_of = jnp.sum(jnp.where(clip_match, clip_starts[None, :], 0), axis=1)
    return (clip_of, start_of)


def guide_features(latent, pose_maps, conv_weight, conv_bias, pose_proj, start_of, first_frame):
    frames_dev = pose_maps.shape[0]
    upper_row = shifted(pose_maps[:, -1:], "head", 1)
    rows_ext = jnp.concatenate([upper_row, pose_maps], axis=1)
    left_column = jnp.zeros(rows_ext.shape[:2] + (1, rows_ext.shape[3]), rows_ext.dtype)
    cols_ext = jnp.concatenate([left_column, rows_ext], axis=2)
    earlier = shifted(cols_ext, "frame", 1)
    extended = jnp.concatenate([earlier, cols_ext], axis=0)
    out_rows = pose_maps.shape[1] // 2
    out_cols = pose_maps.shape[2] // 2
    frame_ids = first_frame + jnp.arange(frames_dev, dtype=jnp.int32)
    starts_here = lax.dynamic_slice_in_dim(start_of, first_frame, frames_dev)
    tap_list = []
    for step_a in range(3):
        keep_mask = (frame_ids - 2 + step_a >= starts_here).astype(pose_maps.dtype)[
            :, None, None, None
        ]
        frames_tap = extended[step_a : step_a + frames_dev] * keep_mask
        for step_b in range(3):
            for step_e in range(3):
                tap_list.append(
                    frames_tap[
                        :,
                        step_b : step_b + 2 * out_rows - 1 : 2,
                        step_e : step_e + 2 * out_cols - 1 : 2,
                    ]
                )
    stacked = jnp.concatenate(tap_list, axis=3)
    kernel = conv_weight.reshape(-1, conv_weight.shape[-1])
    summed = jnp.dot(stacked, kernel, preferred_element_type=jnp.float32) + conv_bias
    feature = jax.nn.silu(summed).astype(jnp.bfloat16)
    guided = latent.astype(jnp.float32) + jnp.dot(
        feature, pose_proj, preferred_element_type=jnp.float32
    )
    return guided.astype(jnp.bfloat16)


def attend_rows(queries, query_clip, query_block, keyvals, clip_of, block_ids):
    heads_dev = queries.shape[1]
    rows_query = queries.shape[0]
    head_size = queries.shape[2]
    score_scale = head_size ** (-0.5)
    start_carry = (
        jnp.full((heads_dev, rows_query), NEG_FILL, jnp.float32),
        jnp.zeros((heads_dev, rows_query), jnp.float32),
        jnp.zeros((heads_dev, rows_query, head_size), jnp.float32),
    )

    def one_frame(running, frame_item):
        frame_kv, frame_id = frame_item
        key_clip = clip_of[frame_id]
        key_block = block_ids[frame_id]
        visible = (query_clip == key_clip) & (key_block <= query_block)
        run_max, run_total, run_acc = running
        scores = (
            jnp.einsum(
                "qhd,khd->hqk", queries, frame_kv[:, :, 0], preferred_element_type=jnp.float32
            )
            * score_scale
        )
        scores = jnp.where(visible[None, :, None], scores, NEG_FILL)
        new_max = jnp.maximum(run_max, jnp.max(scores, axis=2))
        factor = jnp.exp(run_max - new_max)
        weights = jnp.where(visible[None, :, None], jnp.exp(scores - new_max[:, :, None]), 0.0)
        new_total = run_total * factor + jnp.sum(weights, axis=2)
        new_acc = run_acc * factor[:, :, None] + jnp.einsum(
            "hqk,khd->hqd",
            weights.astype(jnp.bfloat16),
            frame_kv[:, :, 1],
            preferred_element_type=jnp.float32,
        )
        running = (new_max, new_total, new_acc)
        return (running, None)

    running = start_carry
    shard_piece = lax.all_gather(keyvals, "frame", axis=0, tiled=True)
    piece_frames = shard_piece.shape[0]
    frame_list = jnp.arange(piece_frames, dtype=jnp.int32)
    running, unused = lax.scan(one_frame, running, (shard_piece, frame_list))
    run_max, run_total, run_acc = running
    normalized = run_acc / run_total[:, :, None]
    return jnp.transpose(normalized, (1, 0, 2)).astype(jnp.bfloat16)


def plain_shards(
    latent, pose_maps, conv_weight, conv_bias, pose_proj, w_qkv, w_out, clip_lengths, block_ids
):
    frame_count = block_ids.shape[0]
    clip_of, start_of = frame_tables(clip_lengths, frame_count)
    frames_dev = latent.shape[0]
    first_frame = lax.axis_index("frame") * frames_dev
    guided = guide_features(
        latent, pose_maps, conv_weight, conv_bias, pose_proj, start_of, first_frame
    )
    whole_rows = lax.all_gather(guided, "head", axis=1, tiled=True)
    height = whole_rows.shape[1]
    width_grid = whole_rows.shape[2]
    model_width = whole_rows.shape[3]
    flat_tokens = whole_rows.reshape(-1, model_width)
    qkv_local = w_qkv.reshape(w_qkv.shape[0], -1)
    projected = jnp.dot(
        flat_tokens,
        lax.all_gather(qkv_local, "frame", axis=0, tiled=True),
        preferred_element_type=jnp.float32,
    ).astype(jnp.bfloat16)
    per_frame = height * width_grid
    heads_dev = w_qkv.shape[1]
    head_size = w_qkv.shape[3]
    grouped = projected.reshape(frames_dev, per_frame, heads_dev, 3, head_size)
    rows_total = frames_dev * per_frame
    queries = grouped[:, :, :, 0].reshape(rows_total, heads_dev, head_size)
    keyvals = grouped[:, :, :, 1:3]
    clip_rows = lax.dynamic_slice_in_dim(clip_of, first_frame, frames_dev)
    block_rows = lax.dynamic_slice_in_dim(block_ids, first_frame, frames_dev)
    query_clip = jnp.repeat(clip_rows, per_frame)
    query_block = jnp.repeat(block_rows, per_frame)
    attended = attend_rows(queries, query_clip, query_block, keyvals, clip_of, block_ids)
    by_row = attended.reshape(frames_dev, height, width_grid, heads_dev * head_size)
    by_row = jnp.transpose(by_row, (1, 0, 2, 3)).reshape(
        height, frames_dev * width_grid, heads_dev * head_size
    )
    out_weight = w_out.reshape(heads_dev * head_size, w_out.shape[2])
    rows_here = height // lax.axis_size("head")
    summed_rows = lax.psum_scatter(
        jnp.dot(by_row, out_weight, preferred_element_type=jnp.float32).astype(jnp.bfloat16),
        "head",
        scatter_dimension=0,
        tiled=True,
    ).astype(jnp.float32)
    summed_rows = summed_rows.reshape(rows_here, frames_dev, width_grid, out_weight.shape[1])
    return jnp.transpose(summed_rows, (1, 0, 2, 3)).astype(jnp.bfloat16)


def turn(value, axis, steps):
    count = lax.axis_size(axis)
    return lax.ppermute(value, axis, [(i, (i + steps) % count) for i in range(count)])


def across(value, axis, bits):
    count = lax.axis_size(axis)
    return lax.ppermute(value, axis, [(i, i ^ bits) for i in range(count)])


def hop(lower, upper, axis, s):
    count = lax.axis_size(axis)
    lower = lax.ppermute(lower, axis, [(i, i + 1) for i in range(s - 1, count - 1)])
    upper = lax.ppermute(upper, axis, [(i, i - 1) for i in range(1, count - s + 1)])
    return lower, upper


def after(value, *others):
    def body(*refs):
        del refs

    anywhere = pl.BlockSpec(memory_space=pl.ANY)
    return pl.pallas_call(
        body,
        out_shape=jax.ShapeDtypeStruct(value.shape, value.dtype),
        in_specs=[anywhere] * (1 + len(others)),
        out_specs=anywhere,
        input_output_aliases={0: 0},
        name="after",
    )(value, *others)


def take_block(weight, row, column, shape, *ready):
    def body(at_ref, weight_ref, *refs):
        refs[-1][...] = weight_ref[...]

    return pl.pallas_call(
        body,
        out_shape=jax.ShapeDtypeStruct(shape, weight.dtype),
        grid_spec=pltpu.PrefetchScalarGridSpec(
            num_scalar_prefetch=1,
            grid=(1,),
            in_specs=[pl.BlockSpec(shape, lambda i, at: (at[0], at[1]))]
            + [pl.BlockSpec(memory_space=pl.ANY)] * len(ready),
            out_specs=pl.BlockSpec(shape, lambda i, at: (0, 0)),
        ),
        cost_estimate=cost(0, 4 * shape[0] * shape[1]),
        name="take_block",
    )(jnp.stack([row, column]), weight, *ready)


def conv_kernel(keep_ref, cols_ref, weight_ref, bias_ref, out_ref, acc_ref):
    step = pl.program_id(0)
    tap_a, tap_b = step // 3, step % 3
    frames, strip_rows, width = out_ref.shape[0], out_ref.shape[1], cols_ref.shape[2]
    pieces = []
    for t in range(frames):
        keep = keep_ref[tap_a * frames + t]
        for r in range(strip_rows):
            rows = cols_ref[tap_a + t, tap_b + 2 * r].astype(F32)
            pieces.append(jnp.where(keep > 0, rows, 0.0))
    lhs = jnp.concatenate(pieces, axis=0).astype(BF16)
    channels = weight_ref.shape[3]
    total = None
    for e in range(3):
        part = lax.dot_general(
            lhs[:, e * channels : (e + 1) * channels],
            weight_ref[0, e],
            (((1,), (1,)), ((), ())),
            preferred_element_type=F32,
        )
        total = part if total is None else total + part

    @pl.when(step == 0)
    def _():
        acc_ref[...] = total

    @pl.when(step > 0)
    def _():
        acc_ref[...] += total

    @pl.when(step == 8)
    def _():
        summed = acc_ref[...] + bias_ref[...]
        feature = summed / (1.0 + jnp.exp(-summed))
        for t in range(frames):
            for r in range(strip_rows):
                at = (t * strip_rows + r) * width
                out_ref[t, r] = feature[at : at + width].astype(BF16)


def pose_feature(extended, conv_weight, conv_bias, start_of, first_frame):
    frames, rows, columns, channels = extended.shape
    frames, rows = frames // 2, rows - 1
    out_channels = conv_weight.shape[-1]
    pairs = extended.reshape(2 * frames, rows + 1, columns // 2, 2 * channels)
    before = jnp.pad(pairs[:, :, :-1, channels:], ((0, 0), (0, 0), (1, 0), (0, 0)))
    cols = jnp.concatenate([before, pairs], axis=3)
    taps = jnp.transpose(conv_weight, (0, 1, 2, 4, 3)).reshape(9, 3, out_channels, channels)
    frame_ids = first_frame + jnp.arange(frames, dtype=jnp.int32)
    starts_here = lax.dynamic_slice_in_dim(start_of, first_frame, frames)
    keep = (frame_ids[None, :] - 2 + jnp.arange(3, dtype=jnp.int32)[:, None] >= starts_here[None, :])
    keep = keep.astype(jnp.int32).reshape(-1)
    out_shape = (frames, rows // 2, columns // 2, out_channels)
    tokens = frames * (rows // 2) * (columns // 2)
    feature = pl.pallas_call(
        conv_kernel,
        out_shape=jax.ShapeDtypeStruct(out_shape, BF16),
        grid_spec=pltpu.PrefetchScalarGridSpec(
            num_scalar_prefetch=1,
            grid=(9,),
            in_specs=[
                pl.BlockSpec(cols.shape, lambda i, k: (0, 0, 0, 0)),
                pl.BlockSpec((1, 3, out_channels, channels), lambda i, k: (i, 0, 0, 0)),
                pl.BlockSpec((1, out_channels), lambda i, k: (0, 0)),
            ],
            out_specs=pl.BlockSpec(out_shape, lambda i, k: (0, 0, 0, 0)),
            scratch_shapes=[pltpu.VMEM((tokens, out_channels), F32)],
        ),
        compiler_params=pltpu.CompilerParams(vmem_limit_bytes=24 * MIB),
        cost_estimate=cost(tokens * out_channels, 2 * tokens * out_channels),
        name="pose_conv",
    )(keep, cols, taps, conv_bias.reshape(1, -1))
    return feature.reshape(tokens, out_channels)


def guide(own, feature, pose_proj):
    tokens, width = own.shape
    channels = pose_proj.shape[0]
    wide = width // 4

    def body(own_ref, feature_ref, proj_ref, out_ref):
        added = jnp.dot(feature_ref[...], proj_ref[...], preferred_element_type=F32)
        out_ref[...] = (own_ref[...].astype(F32) + added).astype(BF16)

    return pl.pallas_call(
        body,
        out_shape=jax.ShapeDtypeStruct(own.shape, BF16),
        grid=(4,),
        in_specs=[
            pl.BlockSpec((tokens, wide), lambda i: (0, i)),
            pl.BlockSpec((tokens, channels), lambda i: (0, 0)),
            pl.BlockSpec((channels, wide), lambda i: (0, i)),
        ],
        out_specs=pl.BlockSpec((tokens, wide), lambda i: (0, i)),
        compiler_params=pltpu.CompilerParams(vmem_limit_bytes=16 * MIB),
        cost_estimate=cost(tokens * width, 2 * tokens * width),
        name="guide",
    )(own, feature, pose_proj)


def project(own, lower, upper, order, shards_of, total, frames):
    strips = len(lower) + 1
    tokens = own.shape[0]
    rows = strips * tokens
    per_frame = tokens // frames
    steps = len(shards_of)
    flat = [array for kind, arrays in shards_of for array in arrays]
    size = flat[0].shape[2]
    columns = 3 * (PLANE + 1)
    heads = PLANE + 1
    depth = own.shape[1] // PLANE
    cuts = [(c, min(c + 4, columns)) for c in range(0, columns, 4)]
    parts = 2 if shards_of[0][0] == "rows" else 1
    slots = min(2, steps)

    def body(order_ref, *refs):
        own_ref, lower_refs, upper_refs = refs[0], refs[1:strips], refs[strips : 2 * strips - 1]
        source_refs = refs[2 * strips - 1 : 2 * strips - 1 + len(flat)]
        rest = refs[2 * strips - 1 + len(flat) :]
        held_ref, guided_ref, sems = rest[-3:]
        if total is None:
            sum_ref = rest[0]
        else:
            total_ref, last_ref, sum_ref = rest[0], rest[1 + PLANE], rest[2 + PLANE]
            message_refs = rest[1 : 1 + PLANE]
        step = pl.program_id(0)

        def fetch(k, n, part):
            low, high = cuts[n]
            kind, arrays = shards_of[k]
            base = sum(len(other) for unused, other in shards_of[:k])
            length, at, shift = depth // parts, 0, 0
            if kind == "columns" and low >= FIRST_COLUMNS:
                base, shift = base + 1, FIRST_COLUMNS
            if kind == "rows":
                base += part
                at = pl.multiple_of((order_ref[steps + 1] ^ part) * length, 128)
            return pltpu.make_async_copy(
                source_refs[base].at[low - shift : high - shift],
                held_ref.at[k % slots, low:high, pl.ds(at, length)],
                sems.at[k % slots, n, part],
            )

        def start(k):
            for n in range(len(cuts)):
                for part in range(parts):
                    fetch(k, n, part).start()

        for k in range(steps):

            @pl.when(step == max(k - 1, 0))
            def _(k=k):
                start(k)

        for s in range(strips):
            found = own_ref[...]
            if s > 0:
                found = lower_refs[s - 1][...].astype(F32) + upper_refs[strips - s - 1][...].astype(F32)
                found = found.astype(BF16)
            for t in range(frames):
                at = (t * strips + s) * per_frame
                guided_ref[at : at + per_frame] = found[t * per_frame : (t + 1) * per_frame]

        slot = lax.rem(step, slots)
        for n, (low, high) in enumerate(cuts):
            for k in range(steps):

                @pl.when(step == k)
                def _(k=k, n=n):
                    for part in range(parts):
                        fetch(k, n, part).wait()

            rhs = jnp.concatenate([held_ref[slot, c] for c in range(low, high)], axis=1)
            part = jnp.dot(guided_ref[...], rhs, preferred_element_type=F32)
            lanes = slice(low * size, high * size)
            if total is not None:
                sum_ref[:, lanes] = total_ref[:, lanes] + part
                continue

            @pl.when(step == 0)
            def _(lanes=lanes, part=part):
                sum_ref[:, lanes] = part

            @pl.when(step > 0)
            def _(lanes=lanes, part=part):
                sum_ref[:, lanes] += part

        if total is None:
            return
        last = 3 * (heads - 1) * size
        last_ref[...] = sum_ref[:, last : last + size].astype(BF16)
        for r in range(PLANE):
            head = order_ref[steps] ^ r
            for j in range(3):
                at = pl.multiple_of((3 * head + j) * size, size)
                message_refs[r][j] = sum_ref[:, pl.ds(at, size)].astype(BF16)
            for j in range(1, 3):
                at = last + j * size
                message_refs[r][2 + j] = sum_ref[:, at : at + size].astype(BF16)

    piece = pl.BlockSpec((tokens, depth), lambda i, order: (0, order[i]))
    in_specs = [piece] * (2 * strips - 1)
    in_specs += [pl.BlockSpec(memory_space=pl.ANY)] * len(flat)
    operands = [own, *lower, *upper, *flat]
    sums = pl.BlockSpec((rows, columns * size), lambda i, order: (0, 0))
    scratch = [
        pltpu.VMEM((slots, columns, depth, size), BF16),
        pltpu.VMEM((rows, depth), BF16),
        pltpu.SemaphoreType.DMA((slots, len(cuts), parts)),
    ]
    if total is None:
        out_shape, out_specs = jax.ShapeDtypeStruct((rows, columns * size), F32), sums
    else:
        assert steps == 1
        in_specs.append(sums)
        operands.append(total)
        message = jax.ShapeDtypeStruct((5, rows, size), BF16)
        out_shape = (message,) * PLANE + (jax.ShapeDtypeStruct((rows, size), BF16),)
        out_specs = (pl.BlockSpec((5, rows, size), lambda i, order: (0, 0, 0)),) * PLANE
        out_specs += (pl.BlockSpec((rows, size), lambda i, order: (0, 0)),)
        scratch = [pltpu.VMEM((rows, columns * size), F32)] + scratch
    return pl.pallas_call(
        body,
        out_shape=out_shape,
        grid_spec=pltpu.PrefetchScalarGridSpec(
            num_scalar_prefetch=1, grid=(steps,), in_specs=in_specs, out_specs=out_specs, scratch_shapes=scratch
        ),
        compiler_params=pltpu.CompilerParams(vmem_limit_bytes=40 * MIB),
        cost_estimate=cost(0, 2 * rows * size),
        name="project",
    )(order, *operands)


def attend(messages, last_query, here, spans, frames, strips):
    rows, size = last_query.shape
    per_frame = rows // frames
    strip = per_frame // strips
    frame_count = PLANE * frames
    window = frame_count - 4 if frame_count > 4 else frame_count
    out_rows = (PLANE + 1) * frames * strip
    scale = size ** (-0.5)

    def body(table_ref, *refs):
        message_refs, last_ref = refs[:PLANE], refs[PLANE]
        out_refs, held_ref = refs[PLANE + 1 : PLANE + 1 + strips], refs[-1]
        here_at = table_ref[3 * frame_count]
        for r in range(PLANE):
            for t in range(frames):
                frame = (here_at ^ r) * frames + t
                for j in range(4):
                    held_ref[frame, j] = message_refs[r][j + 1, t * per_frame : (t + 1) * per_frame]

        def one(query, frame, kind, at):
            begin, low, high = table_ref[3 * frame], table_ref[3 * frame + 1], table_ref[3 * frame + 2]
            keys = held_ref[pl.ds(begin, window), kind].reshape(window * per_frame, size)
            values = held_ref[pl.ds(begin, window), kind + 1].reshape(window * per_frame, size)
            scores = lax.dot_general(query, keys, (((1,), (1,)), ((), ())), preferred_element_type=F32)
            place = lax.broadcasted_iota(jnp.int32, (1, window * per_frame), 1)
            seen = (place >= low * per_frame) & (place < high * per_frame)
            scores = jnp.where(seen, scores * scale, NEG_FILL)
            weights = jnp.exp(scores - jnp.max(scores, axis=1, keepdims=True))
            totals = jnp.sum(weights, axis=1, keepdims=True)
            mixed = jnp.dot(weights.astype(BF16), values, preferred_element_type=F32)
            result = (mixed / totals).astype(BF16)
            for s in range(strips):
                out_refs[s][at : at + strip] = result[s * strip : (s + 1) * strip]

        for r in range(PLANE):
            for t in range(frames):
                query = message_refs[r][0, t * per_frame : (t + 1) * per_frame]
                one(query, (here_at ^ r) * frames + t, 0, (r * frames + t) * strip)
        for t in range(frames):
            query = last_ref[t * per_frame : (t + 1) * per_frame]
            one(query, here_at * frames + t, 2, (PLANE * frames + t) * strip)

    table = jnp.concatenate([spans.reshape(-1), here.reshape(1)]).astype(jnp.int32)
    whole = pl.BlockSpec((5, rows, size), lambda i, table: (0, 0, 0))
    units = (PLANE + 1) * frames
    return pl.pallas_call(
        body,
        out_shape=(jax.ShapeDtypeStruct((out_rows, size), BF16),) * strips,
        grid_spec=pltpu.PrefetchScalarGridSpec(
            num_scalar_prefetch=1,
            grid=(1,),
            in_specs=[whole] * PLANE + [pl.BlockSpec((rows, size), lambda i, table: (0, 0))],
            out_specs=(pl.BlockSpec((out_rows, size), lambda i, table: (0, 0)),) * strips,
            scratch_shapes=[pltpu.VMEM((frame_count, 4, per_frame, size), BF16)],
        ),
        compiler_params=pltpu.CompilerParams(vmem_limit_bytes=40 * MIB),
        cost_estimate=cost(0, 2 * rows * size),
        name="attend",
    )(table, *messages, last_query)


def out_project(gathered, weights, here, group, core, tokens):
    groups, depth, columns = weights[0].shape
    size = gathered[0].shape[2]
    heads = depth // size

    def body(at_ref, *refs):
        weight_refs = refs[PLANE : PLANE + 2]
        out_refs, lhs_ref, sum_ref = refs[PLANE + 2 : -2], refs[-2], refs[-1]
        step = pl.program_id(0)
        for p in range(PLANE):
            rows = slice(p * tokens, (p + 1) * tokens)
            for q in range(PLANE):
                at = (p ^ q) * tokens
                lhs_ref[rows, q * size : (q + 1) * size] = refs[q][0, at : at + tokens]
            lhs_ref[rows, PLANE * size :] = refs[p][0, PLANE * tokens :]

        here_at, core_at = at_ref[0], at_ref[2]
        for c in range(2):
            found = [
                weight_refs[c][0, pl.ds(pl.multiple_of((here_at ^ q) * size, size), size)] for q in range(PLANE)
            ]
            found.append(weight_refs[c][0, PLANE * size : heads * size])
            part = jnp.dot(lhs_ref[...], jnp.concatenate(found, axis=0), preferred_element_type=F32)
            part = part.astype(BF16).astype(F32)

            @pl.when(step == 0)
            def _(c=c, part=part):
                sum_ref[c] = part

            @pl.when(step > 0)
            def _(c=c, part=part):
                sum_ref[c] += part

        @pl.when(step == groups - 1)
        def _():
            for p in range(PLANE):
                for c in range(2):
                    at = pl.multiple_of((core_at ^ c) * columns, 128)
                    out_refs[p][:, pl.ds(at, columns)] = sum_ref[c, p * tokens : (p + 1) * tokens].astype(BF16)

    in_specs = [pl.BlockSpec((1,) + piece.shape[1:], lambda g, at: (g, 0, 0)) for piece in gathered]
    in_specs += [
        pl.BlockSpec((1, depth, columns), lambda g, at: (lax.rem(at[1] + g, groups), 0, 0))
    ] * 2
    return pl.pallas_call(
        body,
        out_shape=(jax.ShapeDtypeStruct((tokens, 2 * columns), BF16),) * PLANE,
        grid_spec=pltpu.PrefetchScalarGridSpec(
            num_scalar_prefetch=1,
            grid=(groups,),
            in_specs=in_specs,
            out_specs=(pl.BlockSpec((tokens, 2 * columns), lambda g, at: (0, 0)),) * PLANE,
            scratch_shapes=[
                pltpu.VMEM((PLANE * tokens, depth), BF16),
                pltpu.VMEM((2, PLANE * tokens, columns), F32),
            ],
        ),
        compiler_params=pltpu.CompilerParams(vmem_limit_bytes=24 * MIB),
        cost_estimate=cost(0, 4 * PLANE * tokens * columns),
        name="out_project",
    )(jnp.stack([here, group, core]), *gathered, *weights)


def place_columns(pieces, here):
    tokens, columns = pieces[0].shape

    def body(here_ref, *refs):
        for r in range(PLANE):
            at = pl.multiple_of((here_ref[0] ^ r) * columns, 128)
            refs[-1][:, pl.ds(at, columns)] = refs[r][...]

    return pl.pallas_call(
        body,
        out_shape=jax.ShapeDtypeStruct((tokens, PLANE * columns), BF16),
        grid_spec=pltpu.PrefetchScalarGridSpec(
            num_scalar_prefetch=1,
            grid=(1,),
            in_specs=[pl.BlockSpec((tokens, columns), lambda i, here: (0, 0))] * PLANE,
            out_specs=pl.BlockSpec((tokens, PLANE * columns), lambda i, here: (0, 0)),
        ),
        cost_estimate=cost(0, 4 * tokens * PLANE * columns),
        name="place_columns",
    )(here.reshape(1), *pieces)


def shards(
    latent, pose_maps, conv_weight, conv_bias, pose_proj, w_qkv, w_out, clip_lengths, block_ids
):
    frame_count = block_ids.shape[0]
    frames, strip_rows, width_grid, model_width = latent.shape
    heads, head_size = w_qkv.shape[1], w_qkv.shape[3]
    strips = lax.axis_size("head")
    tokens = frames * strip_rows * width_grid
    here = lax.axis_index("frame").astype(jnp.int32)
    group = lax.axis_index("head").astype(jnp.int32)
    core = lax.axis_index("dp").astype(jnp.int32)
    clip_of, start_of = frame_tables(clip_lengths, frame_count)

    weight = jnp.transpose(w_qkv, (1, 2, 0, 3)).reshape(3 * heads, -1, head_size)
    near_pairs = [(2 * f + c, 2 * (f ^ (1 + c)) + c) for f in range(PLANE) for c in range(2)]
    far_pairs = [(2 * f + c, 2 * (f ^ (2 - c)) + c) for f in range(PLANE) for c in range(2)]
    plane_axes = ("frame", "dp")
    earlier = shifted(pose_maps, "frame", 1)
    near_first = lax.ppermute(after(weight[:FIRST_COLUMNS], earlier), plane_axes, near_pairs)
    extended = jnp.concatenate([earlier, pose_maps], axis=0)
    extended = jnp.concatenate([shifted(extended[:, -1:], "head", 1), extended], axis=1)
    feature = pose_feature(extended, conv_weight, conv_bias, start_of, here * frames)
    own = guide(latent.reshape(tokens, model_width), feature, pose_proj)
    near_rest = lax.ppermute(after(weight[FIRST_COLUMNS:], own), plane_axes, near_pairs)
    lower, upper = hop(own, own, "head", 1)
    lower, upper = [lower], [upper]
    columns = model_width // PLANE // 2
    depth = heads * head_size
    out_half = take_block(w_out.reshape(depth, model_width), jnp.int32(0), 2 * here + core, (depth, columns))

    half_rows = weight.shape[1] // 2
    near = (near_first, after(near_rest, lower[0], upper[0], out_half))
    passed = jnp.concatenate(
        [lax.dynamic_slice_in_dim(part, core * half_rows, half_rows, axis=1) for part in near], axis=0
    )
    far = lax.ppermute(passed, plane_axes, far_pairs)
    for s in range(2, strips):
        below, above = hop(lower[-1], upper[-1], "head", s)
        if s < strips - 1:
            below, above = after(below, passed), after(above, passed)
        lower.append(below)
        upper.append(above)
    other = tuple(across(part, "dp", 1) for part in near)
    out_half = after(out_half, lower[-1], upper[-1])

    here_near, here_other, here_far = here ^ (1 + core), here ^ (2 - core), here ^ 3
    order = after(jnp.stack([here, here_near, here_other, here, core]), out_half)
    held = [("whole", (weight,)), ("columns", near), ("columns", other)]
    total = project(own, lower, upper, order, held, None, frames)
    far = (far, across(far, "dp", 1))
    order = jnp.stack([here_far, here, core])
    *messages, last_query = project(
        own, lower, upper, order, [("rows", far)], total, frames
    )
    messages = [messages[0]] + [across(messages[r], "frame", r) for r in range(1, PLANE)]

    same_clip = clip_of[:, None] == clip_of[None, :]
    counts = jnp.sum((same_clip & (block_ids[None, :] <= block_ids[:, None])).astype(jnp.int32), axis=1)
    window = frame_count - 4 if frame_count > 4 else frame_count
    begins = jnp.minimum(start_of, frame_count - window)
    spans = jnp.stack([begins, start_of - begins, start_of - begins + counts], axis=1)
    outs = attend(messages, last_query, here, spans, frames, strips)

    out_half = after(lax.all_gather(out_half, "head"), outs[0])
    out_weights = [out_half, across(out_half, "dp", 1)]

    strip_heads = [outs[0]] + [turn(outs[s], "head", -s) for s in range(1, strips)]
    strip_heads = after(jnp.stack(strip_heads), out_weights[1])
    gathered = [strip_heads] + [across(strip_heads, "frame", r) for r in range(1, PLANE)]
    done = out_project(gathered, out_weights, here, group, core, tokens)
    mine = [done[0]] + [across(done[r], "frame", r) for r in range(1, PLANE)]
    return place_columns(mine, here).reshape(latent.shape)


def solution(mesh):
    return jax.shard_map(
        shards if mesh.shape["frame"] == PLANE else plain_shards,
        mesh=mesh,
        in_specs=(
            P(("dp", "frame"), "head", None, None),
            P(("dp", "frame"), "head", None, None),
            P(),
            P(),
            P(),
            P("frame", "head", None, None),
            P("head", None, None),
            P("dp"),
            P("dp"),
        ),
        out_specs=P(("dp", "frame"), "head", None, None),
        check_vma=False,
    )
```

```python
import jax
import jax.numpy as jnp
from jax import lax
from jax.experimental import pallas as pl
from jax.experimental.pallas import tpu as pltpu
from jax.sharding import PartitionSpec as P

NEG_FILL = -1e30
MIB = 1 << 20
F32 = jnp.float32
BF16 = jnp.bfloat16
PLANE = 4
FIRST_COLUMNS = 8


def cost(flops, moved, exps=0):
    return pl.CostEstimate(flops=int(flops), bytes_accessed=int(moved), transcendentals=int(exps))


def shifted(value, axis, steps):
    count = lax.axis_size(axis)
    leading, last = (max(0, -steps), min(count, count - steps))
    return lax.ppermute(value, axis, [(source, source + steps) for source in range(leading, last)])


def frame_tables(clip_lengths, frame_count):
    clip_ends = jnp.cumsum(clip_lengths)
    clip_starts = clip_ends - clip_lengths
    frame_index = jnp.arange(frame_count, dtype=jnp.int32)
    clip_of = jnp.sum((frame_index[:, None] >= clip_ends[None, :]).astype(jnp.int32), axis=1)
    clip_match = clip_of[:, None] == jnp.arange(clip_lengths.shape[0], dtype=jnp.int32)[None, :]
    start_of = jnp.sum(jnp.where(clip_match, clip_starts[None, :], 0), axis=1)
    return (clip_of, start_of)


def guide_features(latent, pose_maps, conv_weight, conv_bias, pose_proj, start_of, first_frame):
    frames_dev = pose_maps.shape[0]
    upper_row = shifted(pose_maps[:, -1:], "head", 1)
    rows_ext = jnp.concatenate([upper_row, pose_maps], axis=1)
    left_column = jnp.zeros(rows_ext.shape[:2] + (1, rows_ext.shape[3]), rows_ext.dtype)
    cols_ext = jnp.concatenate([left_column, rows_ext], axis=2)
    earlier = shifted(cols_ext, "frame", 1)
    extended = jnp.concatenate([earlier, cols_ext], axis=0)
    out_rows = pose_maps.shape[1] // 2
    out_cols = pose_maps.shape[2] // 2
    frame_ids = first_frame + jnp.arange(frames_dev, dtype=jnp.int32)
    starts_here = lax.dynamic_slice_in_dim(start_of, first_frame, frames_dev)
    tap_list = []
    for step_a in range(3):
        keep_mask = (frame_ids - 2 + step_a >= starts_here).astype(pose_maps.dtype)[
            :, None, None, None
        ]
        frames_tap = extended[step_a : step_a + frames_dev] * keep_mask
        for step_b in range(3):
            for step_e in range(3):
                tap_list.append(
                    frames_tap[
                        :,
                        step_b : step_b + 2 * out_rows - 1 : 2,
                        step_e : step_e + 2 * out_cols - 1 : 2,
                    ]
                )
    stacked = jnp.concatenate(tap_list, axis=3)
    kernel = conv_weight.reshape(-1, conv_weight.shape[-1])
    summed = jnp.dot(stacked, kernel, preferred_element_type=jnp.float32) + conv_bias
    feature = jax.nn.silu(summed).astype(jnp.bfloat16)
    guided = latent.astype(jnp.float32) + jnp.dot(
        feature, pose_proj, preferred_element_type=jnp.float32
    )
    return guided.astype(jnp.bfloat16)


def attend_rows(queries, query_clip, query_block, keyvals, clip_of, block_ids):
    heads_dev = queries.shape[1]
    rows_query = queries.shape[0]
    head_size = queries.shape[2]
    score_scale = head_size ** (-0.5)
    start_carry = (
        jnp.full((heads_dev, rows_query), NEG_FILL, jnp.float32),
        jnp.zeros((heads_dev, rows_query), jnp.float32),
        jnp.zeros((heads_dev, rows_query, head_size), jnp.float32),
    )

    def one_frame(running, frame_item):
        frame_kv, frame_id = frame_item
        key_clip = clip_of[frame_id]
        key_block = block_ids[frame_id]
        visible = (query_clip == key_clip) & (key_block <= query_block)
        run_max, run_total, run_acc = running
        scores = (
            jnp.einsum(
                "qhd,khd->hqk", queries, frame_kv[:, :, 0], preferred_element_type=jnp.float32
            )
            * score_scale
        )
        scores = jnp.where(visible[None, :, None], scores, NEG_FILL)
        new_max = jnp.maximum(run_max, jnp.max(scores, axis=2))
        factor = jnp.exp(run_max - new_max)
        weights = jnp.where(visible[None, :, None], jnp.exp(scores - new_max[:, :, None]), 0.0)
        new_total = run_total * factor + jnp.sum(weights, axis=2)
        new_acc = run_acc * factor[:, :, None] + jnp.einsum(
            "hqk,khd->hqd",
            weights.astype(jnp.bfloat16),
            frame_kv[:, :, 1],
            preferred_element_type=jnp.float32,
        )
        running = (new_max, new_total, new_acc)
        return (running, None)

    running = start_carry
    shard_piece = lax.all_gather(keyvals, "frame", axis=0, tiled=True)
    piece_frames = shard_piece.shape[0]
    frame_list = jnp.arange(piece_frames, dtype=jnp.int32)
    running, unused = lax.scan(one_frame, running, (shard_piece, frame_list))
    run_max, run_total, run_acc = running
    normalized = run_acc / run_total[:, :, None]
    return jnp.transpose(normalized, (1, 0, 2)).astype(jnp.bfloat16)


def plain_shards(
    latent, pose_maps, conv_weight, conv_bias, pose_proj, w_qkv, w_out, clip_lengths, block_ids
):
    frame_count = block_ids.shape[0]
    clip_of, start_of = frame_tables(clip_lengths, frame_count)
    frames_dev = latent.shape[0]
    first_frame = lax.axis_index("frame") * frames_dev
    guided = guide_features(
        latent, pose_maps, conv_weight, conv_bias, pose_proj, start_of, first_frame
    )
    whole_rows = lax.all_gather(guided, "head", axis=1, tiled=True)
    height = whole_rows.shape[1]
    width_grid = whole_rows.shape[2]
    model_width = whole_rows.shape[3]
    flat_tokens = whole_rows.reshape(-1, model_width)
    qkv_local = w_qkv.reshape(w_qkv.shape[0], -1)
    projected = jnp.dot(
        flat_tokens,
        lax.all_gather(qkv_local, "frame", axis=0, tiled=True),
        preferred_element_type=jnp.float32,
    ).astype(jnp.bfloat16)
    per_frame = height * width_grid
    heads_dev = w_qkv.shape[1]
    head_size = w_qkv.shape[3]
    grouped = projected.reshape(frames_dev, per_frame, heads_dev, 3, head_size)
    rows_total = frames_dev * per_frame
    queries = grouped[:, :, :, 0].reshape(rows_total, heads_dev, head_size)
    keyvals = grouped[:, :, :, 1:3]
    clip_rows = lax.dynamic_slice_in_dim(clip_of, first_frame, frames_dev)
    block_rows = lax.dynamic_slice_in_dim(block_ids, first_frame, frames_dev)
    query_clip = jnp.repeat(clip_rows, per_frame)
    query_block = jnp.repeat(block_rows, per_frame)
    attended = attend_rows(queries, query_clip, query_block, keyvals, clip_of, block_ids)
    by_row = attended.reshape(frames_dev, height, width_grid, heads_dev * head_size)
    by_row = jnp.transpose(by_row, (1, 0, 2, 3)).reshape(
        height, frames_dev * width_grid, heads_dev * head_size
    )
    out_weight = w_out.reshape(heads_dev * head_size, w_out.shape[2])
    rows_here = height // lax.axis_size("head")
    summed_rows = lax.psum_scatter(
        jnp.dot(by_row, out_weight, preferred_element_type=jnp.float32).astype(jnp.bfloat16),
        "head",
        scatter_dimension=0,
        tiled=True,
    ).astype(jnp.float32)
    summed_rows = summed_rows.reshape(rows_here, frames_dev, width_grid, out_weight.shape[1])
    return jnp.transpose(summed_rows, (1, 0, 2, 3)).astype(jnp.bfloat16)


def turn(value, axis, steps):
    count = lax.axis_size(axis)
    return lax.ppermute(value, axis, [(i, (i + steps) % count) for i in range(count)])


def across(value, axis, bits):
    count = lax.axis_size(axis)
    return lax.ppermute(value, axis, [(i, i ^ bits) for i in range(count)])


def hop(lower, upper, axis, s):
    count = lax.axis_size(axis)
    lower = lax.ppermute(lower, axis, [(i, i + 1) for i in range(s - 1, count - 1)])
    upper = lax.ppermute(upper, axis, [(i, i - 1) for i in range(1, count - s + 1)])
    return lower, upper


def after(value, *others):
    def body(*refs):
        del refs

    anywhere = pl.BlockSpec(memory_space=pl.ANY)
    return pl.pallas_call(
        body,
        out_shape=jax.ShapeDtypeStruct(value.shape, value.dtype),
        in_specs=[anywhere] * (1 + len(others)),
        out_specs=anywhere,
        input_output_aliases={0: 0},
        name="after",
    )(value, *others)


def take_block(weight, row, column, shape, *ready):
    def body(at_ref, weight_ref, *refs):
        refs[-1][...] = weight_ref[...]

    return pl.pallas_call(
        body,
        out_shape=jax.ShapeDtypeStruct(shape, weight.dtype),
        grid_spec=pltpu.PrefetchScalarGridSpec(
            num_scalar_prefetch=1,
            grid=(1,),
            in_specs=[pl.BlockSpec(shape, lambda i, at: (at[0], at[1]))]
            + [pl.BlockSpec(memory_space=pl.ANY)] * len(ready),
            out_specs=pl.BlockSpec(shape, lambda i, at: (0, 0)),
        ),
        cost_estimate=cost(0, 4 * shape[0] * shape[1]),
        name="take_block",
    )(jnp.stack([row, column]), weight, *ready)


def conv_kernel(keep_ref, cols_ref, weight_ref, bias_ref, out_ref, acc_ref):
    step = pl.program_id(0)
    tap_a, tap_b = step // 3, step % 3
    frames, strip_rows, width = out_ref.shape[0], out_ref.shape[1], cols_ref.shape[2]
    pieces = []
    for t in range(frames):
        keep = keep_ref[tap_a * frames + t]
        for r in range(strip_rows):
            rows = cols_ref[tap_a + t, tap_b + 2 * r].astype(F32)
            pieces.append(jnp.where(keep > 0, rows, 0.0))
    lhs = jnp.concatenate(pieces, axis=0).astype(BF16)
    channels = weight_ref.shape[3]
    total = None
    for e in range(3):
        part = lax.dot_general(
            lhs[:, e * channels : (e + 1) * channels],
            weight_ref[0, e],
            (((1,), (1,)), ((), ())),
            preferred_element_type=F32,
        )
        total = part if total is None else total + part

    @pl.when(step == 0)
    def _():
        acc_ref[...] = total

    @pl.when(step > 0)
    def _():
        acc_ref[...] += total

    @pl.when(step == 8)
    def _():
        summed = acc_ref[...] + bias_ref[...]
        feature = summed / (1.0 + jnp.exp(-summed))
        for t in range(frames):
            for r in range(strip_rows):
                at = (t * strip_rows + r) * width
                out_ref[t, r] = feature[at : at + width].astype(BF16)


def pose_feature(extended, conv_weight, conv_bias, start_of, first_frame):
    frames, rows, columns, channels = extended.shape
    frames, rows = frames // 2, rows - 1
    out_channels = conv_weight.shape[-1]
    pairs = extended.reshape(2 * frames, rows + 1, columns // 2, 2 * channels)
    before = jnp.pad(pairs[:, :, :-1, channels:], ((0, 0), (0, 0), (1, 0), (0, 0)))
    cols = jnp.concatenate([before, pairs], axis=3)
    taps = jnp.transpose(conv_weight, (0, 1, 2, 4, 3)).reshape(9, 3, out_channels, channels)
    frame_ids = first_frame + jnp.arange(frames, dtype=jnp.int32)
    starts_here = lax.dynamic_slice_in_dim(start_of, first_frame, frames)
    keep = (frame_ids[None, :] - 2 + jnp.arange(3, dtype=jnp.int32)[:, None] >= starts_here[None, :])
    keep = keep.astype(jnp.int32).reshape(-1)
    out_shape = (frames, rows // 2, columns // 2, out_channels)
    tokens = frames * (rows // 2) * (columns // 2)
    feature = pl.pallas_call(
        conv_kernel,
        out_shape=jax.ShapeDtypeStruct(out_shape, BF16),
        grid_spec=pltpu.PrefetchScalarGridSpec(
            num_scalar_prefetch=1,
            grid=(9,),
            in_specs=[
                pl.BlockSpec(cols.shape, lambda i, k: (0, 0, 0, 0)),
                pl.BlockSpec((1, 3, out_channels, channels), lambda i, k: (i, 0, 0, 0)),
                pl.BlockSpec((1, out_channels), lambda i, k: (0, 0)),
            ],
            out_specs=pl.BlockSpec(out_shape, lambda i, k: (0, 0, 0, 0)),
            scratch_shapes=[pltpu.VMEM((tokens, out_channels), F32)],
        ),
        compiler_params=pltpu.CompilerParams(vmem_limit_bytes=24 * MIB),
        cost_estimate=cost(tokens * out_channels, 2 * tokens * out_channels),
        name="pose_conv",
    )(keep, cols, taps, conv_bias.reshape(1, -1))
    return feature.reshape(tokens, out_channels)


def guide(own, feature, pose_proj):
    tokens, width = own.shape
    channels = pose_proj.shape[0]
    wide = width // 4

    def body(own_ref, feature_ref, proj_ref, out_ref):
        added = jnp.dot(feature_ref[...], proj_ref[...], preferred_element_type=F32)
        out_ref[...] = (own_ref[...].astype(F32) + added).astype(BF16)

    return pl.pallas_call(
        body,
        out_shape=jax.ShapeDtypeStruct(own.shape, BF16),
        grid=(4,),
        in_specs=[
            pl.BlockSpec((tokens, wide), lambda i: (0, i)),
            pl.BlockSpec((tokens, channels), lambda i: (0, 0)),
            pl.BlockSpec((channels, wide), lambda i: (0, i)),
        ],
        out_specs=pl.BlockSpec((tokens, wide), lambda i: (0, i)),
        compiler_params=pltpu.CompilerParams(vmem_limit_bytes=16 * MIB),
        cost_estimate=cost(tokens * width, 2 * tokens * width),
        name="guide",
    )(own, feature, pose_proj)


def project(own, lower, upper, order, shards_of, total, frames):
    strips = len(lower) + 1
    tokens = own.shape[0]
    rows = strips * tokens
    per_frame = tokens // frames
    steps = len(shards_of)
    flat = [array for kind, arrays in shards_of for array in arrays]
    size = flat[0].shape[2]
    columns = 3 * (PLANE + 1)
    heads = PLANE + 1
    depth = own.shape[1] // PLANE
    cuts = [(c, min(c + 4, columns)) for c in range(0, columns, 4)]
    parts = 2 if shards_of[0][0] == "rows" else 1
    slots = min(2, steps)

    def body(order_ref, *refs):
        own_ref, lower_refs, upper_refs = refs[0], refs[1:strips], refs[strips : 2 * strips - 1]
        source_refs = refs[2 * strips - 1 : 2 * strips - 1 + len(flat)]
        rest = refs[2 * strips - 1 + len(flat) :]
        held_ref, guided_ref, sems = rest[-3:]
        if total is None:
            sum_ref = rest[0]
        else:
            total_ref, last_ref, sum_ref = rest[0], rest[1 + PLANE], rest[2 + PLANE]
            message_refs = rest[1 : 1 + PLANE]
        step = pl.program_id(0)

        def fetch(k, n, part):
            low, high = cuts[n]
            kind, arrays = shards_of[k]
            base = sum(len(other) for unused, other in shards_of[:k])
            length, at, shift = depth // parts, 0, 0
            if kind == "columns" and low >= FIRST_COLUMNS:
                base, shift = base + 1, FIRST_COLUMNS
            if kind == "rows":
                base += part
                at = pl.multiple_of((order_ref[steps + 1] ^ part) * length, 128)
            return pltpu.make_async_copy(
                source_refs[base].at[low - shift : high - shift],
                held_ref.at[k % slots, low:high, pl.ds(at, length)],
                sems.at[k % slots, n, part],
            )

        def start(k):
            for n in range(len(cuts)):
                for part in range(parts):
                    fetch(k, n, part).start()

        for k in range(steps):

            @pl.when(step == max(k - 1, 0))
            def _(k=k):
                start(k)

        for s in range(strips):
            found = own_ref[...]
            if s > 0:
                found = lower_refs[s - 1][...].astype(F32) + upper_refs[strips - s - 1][...].astype(F32)
                found = found.astype(BF16)
            for t in range(frames):
                at = (t * strips + s) * per_frame
                guided_ref[at : at + per_frame] = found[t * per_frame : (t + 1) * per_frame]

        slot = lax.rem(step, slots)
        for n, (low, high) in enumerate(cuts):
            for k in range(steps):

                @pl.when(step == k)
                def _(k=k, n=n):
                    for part in range(parts):
                        fetch(k, n, part).wait()

            rhs = jnp.concatenate([held_ref[slot, c] for c in range(low, high)], axis=1)
            part = jnp.dot(guided_ref[...], rhs, preferred_element_type=F32)
            lanes = slice(low * size, high * size)
            if total is not None:
                sum_ref[:, lanes] = total_ref[:, lanes] + part
                continue

            @pl.when(step == 0)
            def _(lanes=lanes, part=part):
                sum_ref[:, lanes] = part

            @pl.when(step > 0)
            def _(lanes=lanes, part=part):
                sum_ref[:, lanes] += part

        if total is None:
            return
        last = 3 * (heads - 1) * size
        last_ref[...] = sum_ref[:, last : last + size].astype(BF16)
        for r in range(PLANE):
            head = order_ref[steps] ^ r
            for j in range(3):
                at = pl.multiple_of((3 * head + j) * size, size)
                message_refs[r][j] = sum_ref[:, pl.ds(at, size)].astype(BF16)
            for j in range(1, 3):
                at = last + j * size
                message_refs[r][2 + j] = sum_ref[:, at : at + size].astype(BF16)

    piece = pl.BlockSpec((tokens, depth), lambda i, order: (0, order[i]))
    in_specs = [piece] * (2 * strips - 1)
    in_specs += [pl.BlockSpec(memory_space=pl.ANY)] * len(flat)
    operands = [own, *lower, *upper, *flat]
    sums = pl.BlockSpec((rows, columns * size), lambda i, order: (0, 0))
    scratch = [
        pltpu.VMEM((slots, columns, depth, size), BF16),
        pltpu.VMEM((rows, depth), BF16),
        pltpu.SemaphoreType.DMA((slots, len(cuts), parts)),
    ]
    if total is None:
        out_shape, out_specs = jax.ShapeDtypeStruct((rows, columns * size), F32), sums
    else:
        assert steps == 1
        in_specs.append(sums)
        operands.append(total)
        message = jax.ShapeDtypeStruct((5, rows, size), BF16)
        out_shape = (message,) * PLANE + (jax.ShapeDtypeStruct((rows, size), BF16),)
        out_specs = (pl.BlockSpec((5, rows, size), lambda i, order: (0, 0, 0)),) * PLANE
        out_specs += (pl.BlockSpec((rows, size), lambda i, order: (0, 0)),)
        scratch = [pltpu.VMEM((rows, columns * size), F32)] + scratch
    return pl.pallas_call(
        body,
        out_shape=out_shape,
        grid_spec=pltpu.PrefetchScalarGridSpec(
            num_scalar_prefetch=1, grid=(steps,), in_specs=in_specs, out_specs=out_specs, scratch_shapes=scratch
        ),
        compiler_params=pltpu.CompilerParams(vmem_limit_bytes=40 * MIB),
        cost_estimate=cost(0, 2 * rows * size),
        name="project",
    )(order, *operands)


def attend(messages, last_query, here, spans, frames, strips):
    rows, size = last_query.shape
    per_frame = rows // frames
    strip = per_frame // strips
    frame_count = PLANE * frames
    window = frame_count - 4 if frame_count > 4 else frame_count
    out_rows = (PLANE + 1) * frames * strip
    scale = size ** (-0.5)

    def body(table_ref, *refs):
        message_refs, last_ref = refs[:PLANE], refs[PLANE]
        out_refs, held_ref = refs[PLANE + 1 : PLANE + 1 + strips], refs[-1]
        here_at = table_ref[3 * frame_count]
        for r in range(PLANE):
            for t in range(frames):
                frame = (here_at ^ r) * frames + t
                for j in range(4):
                    held_ref[frame, j] = message_refs[r][j + 1, t * per_frame : (t + 1) * per_frame]

        def one(query, frame, kind, at):
            begin, low, high = table_ref[3 * frame], table_ref[3 * frame + 1], table_ref[3 * frame + 2]
            keys = held_ref[pl.ds(begin, window), kind].reshape(window * per_frame, size)
            values = held_ref[pl.ds(begin, window), kind + 1].reshape(window * per_frame, size)
            scores = lax.dot_general(query, keys, (((1,), (1,)), ((), ())), preferred_element_type=F32)
            place = lax.broadcasted_iota(jnp.int32, (1, window * per_frame), 1)
            seen = (place >= low * per_frame) & (place < high * per_frame)
            scores = jnp.where(seen, scores * scale, NEG_FILL)
            weights = jnp.exp(scores - jnp.max(scores, axis=1, keepdims=True))
            totals = jnp.sum(weights, axis=1, keepdims=True)
            mixed = jnp.dot(weights.astype(BF16), values, preferred_element_type=F32)
            result = (mixed / totals).astype(BF16)
            for s in range(strips):
                out_refs[s][at : at + strip] = result[s * strip : (s + 1) * strip]

        for r in range(PLANE):
            for t in range(frames):
                query = message_refs[r][0, t * per_frame : (t + 1) * per_frame]
                one(query, (here_at ^ r) * frames + t, 0, (r * frames + t) * strip)
        for t in range(frames):
            query = last_ref[t * per_frame : (t + 1) * per_frame]
            one(query, here_at * frames + t, 2, (PLANE * frames + t) * strip)

    table = jnp.concatenate([spans.reshape(-1), here.reshape(1)]).astype(jnp.int32)
    whole = pl.BlockSpec((5, rows, size), lambda i, table: (0, 0, 0))
    units = (PLANE + 1) * frames
    return pl.pallas_call(
        body,
        out_shape=(jax.ShapeDtypeStruct((out_rows, size), BF16),) * strips,
        grid_spec=pltpu.PrefetchScalarGridSpec(
            num_scalar_prefetch=1,
            grid=(1,),
            in_specs=[whole] * PLANE + [pl.BlockSpec((rows, size), lambda i, table: (0, 0))],
            out_specs=(pl.BlockSpec((out_rows, size), lambda i, table: (0, 0)),) * strips,
            scratch_shapes=[pltpu.VMEM((frame_count, 4, per_frame, size), BF16)],
        ),
        compiler_params=pltpu.CompilerParams(vmem_limit_bytes=40 * MIB),
        cost_estimate=cost(0, 2 * rows * size),
        name="attend",
    )(table, *messages, last_query)


def out_project(gathered, weights, here, group, core, tokens):
    groups, depth, columns = weights[0].shape
    size = gathered[0].shape[2]
    heads = depth // size

    def body(at_ref, *refs):
        weight_refs = refs[PLANE : PLANE + 2]
        out_refs, lhs_ref, sum_ref = refs[PLANE + 2 : -2], refs[-2], refs[-1]
        step = pl.program_id(0)
        for p in range(PLANE):
            rows = slice(p * tokens, (p + 1) * tokens)
            for q in range(PLANE):
                at = (p ^ q) * tokens
                lhs_ref[rows, q * size : (q + 1) * size] = refs[q][0, at : at + tokens]
            lhs_ref[rows, PLANE * size :] = refs[p][0, PLANE * tokens :]

        here_at, core_at = at_ref[0], at_ref[2]
        for c in range(2):
            found = [
                weight_refs[c][0, pl.ds(pl.multiple_of((here_at ^ q) * size, size), size)] for q in range(PLANE)
            ]
            found.append(weight_refs[c][0, PLANE * size : heads * size])
            part = jnp.dot(lhs_ref[...], jnp.concatenate(found, axis=0), preferred_element_type=F32)
            part = part.astype(BF16).astype(F32)

            @pl.when(step == 0)
            def _(c=c, part=part):
                sum_ref[c] = part

            @pl.when(step > 0)
            def _(c=c, part=part):
                sum_ref[c] += part

        @pl.when(step == groups - 1)
        def _():
            for p in range(PLANE):
                for c in range(2):
                    at = pl.multiple_of((core_at ^ c) * columns, 128)
                    out_refs[p][:, pl.ds(at, columns)] = sum_ref[c, p * tokens : (p + 1) * tokens].astype(BF16)

    in_specs = [pl.BlockSpec((1,) + piece.shape[1:], lambda g, at: (g, 0, 0)) for piece in gathered]
    in_specs += [
        pl.BlockSpec((1, depth, columns), lambda g, at: (lax.rem(at[1] + g, groups), 0, 0))
    ] * 2
    return pl.pallas_call(
        body,
        out_shape=(jax.ShapeDtypeStruct((tokens, 2 * columns), BF16),) * PLANE,
        grid_spec=pltpu.PrefetchScalarGridSpec(
            num_scalar_prefetch=1,
            grid=(groups,),
            in_specs=in_specs,
            out_specs=(pl.BlockSpec((tokens, 2 * columns), lambda g, at: (0, 0)),) * PLANE,
            scratch_shapes=[
                pltpu.VMEM((PLANE * tokens, depth), BF16),
                pltpu.VMEM((2, PLANE * tokens, columns), F32),
            ],
        ),
        compiler_params=pltpu.CompilerParams(vmem_limit_bytes=24 * MIB),
        cost_estimate=cost(0, 4 * PLANE * tokens * columns),
        name="out_project",
    )(jnp.stack([here, group, core]), *gathered, *weights)


def place_columns(pieces, here):
    tokens, columns = pieces[0].shape

    def body(here_ref, *refs):
        for r in range(PLANE):
            at = pl.multiple_of((here_ref[0] ^ r) * columns, 128)
            refs[-1][:, pl.ds(at, columns)] = refs[r][...]

    return pl.pallas_call(
        body,
        out_shape=jax.ShapeDtypeStruct((tokens, PLANE * columns), BF16),
        grid_spec=pltpu.PrefetchScalarGridSpec(
            num_scalar_prefetch=1,
            grid=(1,),
            in_specs=[pl.BlockSpec((tokens, columns), lambda i, here: (0, 0))] * PLANE,
            out_specs=pl.BlockSpec((tokens, PLANE * columns), lambda i, here: (0, 0)),
        ),
        cost_estimate=cost(0, 4 * tokens * PLANE * columns),
        name="place_columns",
    )(here.reshape(1), *pieces)


def shards(
    latent, pose_maps, conv_weight, conv_bias, pose_proj, w_qkv, w_out, clip_lengths, block_ids
):
    frame_count = block_ids.shape[0]
    frames, strip_rows, width_grid, model_width = latent.shape
    heads, head_size = w_qkv.shape[1], w_qkv.shape[3]
    strips = lax.axis_size("head")
    tokens = frames * strip_rows * width_grid
    here = lax.axis_index("frame").astype(jnp.int32)
    group = lax.axis_index("head").astype(jnp.int32)
    core = lax.axis_index("dp").astype(jnp.int32)
    clip_of, start_of = frame_tables(clip_lengths, frame_count)

    weight = jnp.transpose(w_qkv, (1, 2, 0, 3)).reshape(3 * heads, -1, head_size)
    near_pairs = [(2 * f + c, 2 * (f ^ (1 + c)) + c) for f in range(PLANE) for c in range(2)]
    far_pairs = [(2 * f + c, 2 * (f ^ (2 - c)) + c) for f in range(PLANE) for c in range(2)]
    plane_axes = ("frame", "dp")
    earlier = shifted(pose_maps, "frame", 1)
    near_first = lax.ppermute(after(weight[:FIRST_COLUMNS], earlier), plane_axes, near_pairs)
    extended = jnp.concatenate([earlier, pose_maps], axis=0)
    extended = jnp.concatenate([shifted(extended[:, -1:], "head", 1), extended], axis=1)
    feature = pose_feature(extended, conv_weight, conv_bias, start_of, here * frames)
    own = guide(latent.reshape(tokens, model_width), feature, pose_proj)
    near_rest = lax.ppermute(after(weight[FIRST_COLUMNS:], own), plane_axes, near_pairs)
    lower, upper = hop(own, own, "head", 1)
    lower, upper = [lower], [upper]
    columns = model_width // PLANE // 2
    depth = heads * head_size
    out_half = take_block(w_out.reshape(depth, model_width), jnp.int32(0), 2 * here + core, (depth, columns))

    half_rows = weight.shape[1] // 2
    near = (near_first, after(near_rest, lower[0], upper[0], out_half))
    passed = jnp.concatenate(
        [lax.dynamic_slice_in_dim(part, core * half_rows, half_rows, axis=1) for part in near], axis=0
    )
    far = lax.ppermute(passed, plane_axes, far_pairs)
    for s in range(2, strips):
        below, above = hop(lower[-1], upper[-1], "head", s)
        if s < strips - 1:
            below, above = after(below, passed), after(above, passed)
        lower.append(below)
        upper.append(above)
    other = tuple(across(part, "dp", 1) for part in near)
    out_half = after(out_half, lower[-1], upper[-1])

    here_near, here_other, here_far = here ^ (1 + core), here ^ (2 - core), here ^ 3
    order = after(jnp.stack([here, here_near, here_other, here, core]), out_half)
    held = [("whole", (weight,)), ("columns", near), ("columns", other)]
    total = project(own, lower, upper, order, held, None, frames)
    far = after(far, total)
    far = (far, across(far, "dp", 1))
    order = jnp.stack([here_far, here, core])
    *messages, last_query = project(
        own, lower, upper, order, [("rows", far)], total, frames
    )
    messages = [messages[0]] + [across(messages[r], "frame", r) for r in range(1, PLANE)]

    same_clip = clip_of[:, None] == clip_of[None, :]
    counts = jnp.sum((same_clip & (block_ids[None, :] <= block_ids[:, None])).astype(jnp.int32), axis=1)
    window = frame_count - 4 if frame_count > 4 else frame_count
    begins = jnp.minimum(start_of, frame_count - window)
    spans = jnp.stack([begins, start_of - begins, start_of - begins + counts], axis=1)
    outs = attend(messages, last_query, here, spans, frames, strips)

    out_half = after(lax.all_gather(out_half, "head"), outs[0])
    out_weights = [out_half, across(out_half, "dp", 1)]

    strip_heads = [outs[0]] + [turn(outs[s], "head", -s) for s in range(1, strips)]
    strip_heads = after(jnp.stack(strip_heads), out_weights[1])
    gathered = [strip_heads] + [across(strip_heads, "frame", r) for r in range(1, PLANE)]
    done = out_project(gathered, out_weights, here, group, core, tokens)
    mine = [done[0]] + [across(done[r], "frame", r) for r in range(1, PLANE)]
    return place_columns(mine, here).reshape(latent.shape)


def solution(mesh):
    return jax.shard_map(
        shards if mesh.shape["frame"] == PLANE else plain_shards,
        mesh=mesh,
        in_specs=(
            P(("dp", "frame"), "head", None, None),
            P(("dp", "frame"), "head", None, None),
            P(),
            P(),
            P(),
            P("frame", "head", None, None),
            P("head", None, None),
            P("dp"),
            P("dp"),
        ),
        out_specs=P(("dp", "frame"), "head", None, None),
        check_vma=False,
    )
```
